32 devices in a mesh: ctx: 8 (over z, x), tp: 4 (over y, core).
Axes of the slice: x: 2, y: 2, z: 4, core: 2. Of those that a mesh axis runs over, the one named last changes fastest.
Arguments:
- clean: bfloat16 [8192, 128], P('ctx'), may hold values from -5 to 5
- noise: bfloat16 [8192, 128], P('ctx'), may hold values from -5 to 5
- levels: int32 [32], replicated, may hold values from 0 to 999
- lengths: int32 [4], replicated, may hold values from 1 to 16, as said below
- order: int32 [16], replicated, may hold values from 0 to 15, as said below
- step: int32 [1], replicated, may hold values from 1 to 20
- w_attn: float32 [4, 1024, 1024], P(None, 'ctx', 'tp'), may hold values from -0.46875 to 0.46875
- m_attn: float32 [4, 1024, 1024], P(None, 'ctx', 'tp'), may hold values from -1.4901161e-07 to 1.4901161e-07
- v_attn: float32 [4, 1024, 1024], P(None, 'ctx', 'tp'), may hold values from 5.2286e-17 to 2.09144e-16
- w_mlp: float32 [2, 1024, 4096], P(None, 'ctx', 'tp'), may hold values from -0.15625 to 0.15625
- m_mlp: float32 [2, 1024, 4096], P(None, 'ctx', 'tp'), may hold values from -1.4901161e-07 to 1.4901161e-07
- v_mlp: float32 [2, 1024, 4096], P(None, 'ctx', 'tp'), may hold values from 5.2286e-17 to 2.09144e-16
- w_mod: float32 [1024, 6144], P('ctx'), may hold values from -0.1875 to 0.1875
- m_mod: float32 [1024, 6144], P('ctx'), may hold values from -1.4901161e-07 to 1.4901161e-07
- v_mod: float32 [1024, 6144], P('ctx'), may hold values from 5.2286e-17 to 2.09144e-16
- w_io: float32 [2, 128, 1024], P(None, None, 'ctx'), may hold values from -0.44194174 to 0.44194174
- m_io: float32 [2, 128, 1024], P(None, None, 'ctx'), may hold values from -1.3810679e-06 to 1.3810679e-06
- v_io: float32 [2, 128, 1024], P(None, None, 'ctx'), may hold values from 6.0796738e-17 to 2.5177002e-14
- vectors: float32 [8, 1024], P(None, 'ctx'), may hold values from -1.5 to 1.5
- m_vec: float32 [8, 1024], P(None, 'ctx'), may hold values from -1.4901161e-07 to 1.4901161e-07
- v_vec: float32 [8, 1024], P(None, 'ctx'), may hold values from 5.2286e-17 to 2.09144e-16
Outputs:
- loss_value: float32 [], replicated
- grad_norm: float32 [], replicated
- new_w_attn: float32 [4, 1024, 1024], P(None, 'ctx', 'tp')
- new_m_attn: float32 [4, 1024, 1024], P(None, 'ctx', 'tp')
- new_v_attn: float32 [4, 1024, 1024], P(None, 'ctx', 'tp')
- copy_attn: bfloat16 [4, 1024, 1024], P(None, 'ctx', 'tp')
- new_w_mlp: float32 [2, 1024, 4096], P(None, 'ctx', 'tp')
- new_m_mlp: float32 [2, 1024, 4096], P(None, 'ctx', 'tp')
- new_v_mlp: float32 [2, 1024, 4096], P(None, 'ctx', 'tp')
- copy_mlp: bfloat16 [2, 1024, 4096], P(None, 'ctx', 'tp')
- new_w_mod: float32 [1024, 6144], P('ctx')
- new_m_mod: float32 [1024, 6144], P('ctx')
- new_v_mod: float32 [1024, 6144], P('ctx')
- copy_mod: bfloat16 [1024, 6144], P('ctx')
- new_w_io: float32 [2, 128, 1024], P(None, None, 'ctx')
- new_m_io: float32 [2, 128, 1024], P(None, None, 'ctx')
- new_v_embed: float32 [128, 1024], P(None, 'ctx')
- new_v_head: float32 [128, 1024], P(None, 'ctx')
- copy_io: bfloat16 [2, 128, 1024], P(None, None, 'ctx')
- new_vectors: float32 [8, 1024], P(None, 'ctx')
- new_m_vec: float32 [8, 1024], P(None, 'ctx')
- new_v_vec: float32 [8, 1024], P(None, 'ctx')
- copy_vec: bfloat16 [8, 1024], P(None, 'ctx')
The draws below stay inside these ranges and needn't reach their ends.
Inputs may be any that keep to these rules, and one draw needn't show every extreme that they name: `lengths`: clips are runs of consecutive logical frames in the given order; the longest has exactly 16 frames. `order`: each logical stretch appears once; storage stretches 0, 8 and 15 hold frames of one clip of 16 frames.
All inputs are finite; a program needn't handle non-finite values.
Results may differ from the reference program's by a relative error of at most 0.017.
Values may be sent and summed in bfloat16 or wider, within the bound.
No kernel may reach another device: no remote copies, remote signals or barrier semaphores. Data moves between devices by JAX's collectives and lax.ppermute only.
A program may use at most 320 MiB of HBM per device.

```python
import math
import jax
import jax.numpy as jnp
from jax import lax

D = 1024
HEADS = 16
HD = 64
FF = 4096
PF = 128
GRID = 16
PATCHES = 256
LEVELS = 1000
FRAMES = 32
TOKENS = 8192
STRETCHES = 16
CH_FR = 2
CH_ROWS = 512
MOST_CLIP = 16
CLIPS = 4


def scaled_normal(key, shape, scales):
    base = jnp.clip(jax.random.normal(key, shape, jnp.float32), -5.0, 5.0)
    return base * scales


def length_table(key):
    key = jax.random.fold_in(key, 3)
    full_count = min(CLIPS, (FRAMES - CLIPS) // (MOST_CLIP - 1))
    short_count = CLIPS - full_count
    extra_frames = FRAMES - full_count * MOST_CLIP - short_count
    pick_key, place_key = jax.random.split(key)
    table = jnp.full((CLIPS,), MOST_CLIP, jnp.int32)
    if short_count > 0:
        counts = jnp.ones((short_count,), jnp.int32)
        if extra_frames > 0:
            picks = jax.random.randint(pick_key, (extra_frames,), 0, short_count)
            hits = (picks[:, None] == jnp.arange(short_count, dtype=jnp.int32)[None, :]).astype(jnp.int32)
            counts = counts + jnp.sum(hits, axis=0).astype(jnp.int32)
        table = table.at[full_count:].set(counts)
    return table[jax.random.permutation(place_key, CLIPS)]


def place_stretch(table, slot, wanted):
    slots = jnp.arange(STRETCHES, dtype=jnp.int32)
    where_now = jnp.sum(jnp.where(table == wanted, slots, 0)).astype(jnp.int32)
    held = jnp.sum(jnp.where(slots == slot, table, 0)).astype(jnp.int32)
    return jnp.where(slots == slot, wanted, jnp.where(slots == where_now, held, table)).astype(jnp.int32)


def order_table(key):
    lengths = length_table(key)
    table = jax.random.permutation(jax.random.fold_in(key, 101), STRETCHES).astype(jnp.int32)
    clip_ids = jnp.arange(CLIPS, dtype=jnp.int32)
    longest = jnp.min(jnp.where(lengths == MOST_CLIP, clip_ids, CLIPS)).astype(jnp.int32)
    first_frame = jnp.sum(jnp.where(clip_ids < longest, lengths, 0)).astype(jnp.int32)
    first_stretch = first_frame // CH_FR
    last_stretch = (first_frame + MOST_CLIP - 1) // CH_FR
    table = place_stretch(table, 0, first_stretch)
    table = place_stretch(table, STRETCHES // 2, first_stretch + 1)
    table = place_stretch(table, STRETCHES - 1, last_stretch)
    return table


def patch_signs(key):
    stretch_table = order_table(key)
    rows = jnp.arange(TOKENS, dtype=jnp.int32)
    within = rows % CH_ROWS
    logical_frame = stretch_table[rows // CH_ROWS] * CH_FR + within // PATCHES
    column = within % PATCHES % GRID
    return (1 - 2 * ((column + logical_frame) % 2)).astype(jnp.float32)


def io_sigmas():
    head_size = 0.0009 / (PF * D) ** 0.5
    return jnp.array([0.8 * head_size * (PF / TOKENS) ** 0.5, head_size], jnp.float32)


def draw_order(key, part):
    return order_table(key)


def draw_lengths(key, part):
    return length_table(key)


def draw_clean(key, part):
    signs = patch_signs(key)
    key = jax.random.fold_in(key, 1)
    base = jnp.clip(jax.random.normal(key, (TOKENS, PF), jnp.float32), -5.0, 5.0)
    return (base * signs[:, None]).astype(jnp.bfloat16)


def draw_noise(key, part):
    signs = patch_signs(key)
    key = jax.random.fold_in(key, 2)
    base = jnp.clip(jax.random.normal(key, (TOKENS, PF), jnp.float32), -5.0, 5.0)
    return (base * signs[:, None]).astype(jnp.bfloat16)


def draw_w_attn(key, part):
    key = jax.random.fold_in(key, 4)
    scales = jnp.array([1.3, 1.3, 1.0, 3.0], jnp.float32) / D ** 0.5
    return scaled_normal(key, (4, D, D), scales[:, None, None])


def draw_w_mlp(key, part):
    key = jax.random.fold_in(key, 5)
    scales = jnp.array([D ** (-0.5), FF ** (-0.5)], jnp.float32)
    return scaled_normal(key, (2, D, FF), scales[:, None, None])


def draw_w_io(key, part):
    key = jax.random.fold_in(key, 6)
    scales = jnp.array([PF ** (-0.5), D ** (-0.5)], jnp.float32)
    return scaled_normal(key, (2, PF, D), scales[:, None, None])


def draw_m_io(key, part):
    key = jax.random.fold_in(key, 11)
    return scaled_normal(key, (2, PF, D), 0.111 * io_sigmas()[:, None, None])


def draw_v_io(key, part):
    key = jax.random.fold_in(key, 12)
    unit = jax.random.uniform(key, (2, PF, D), jnp.float32, 0.0, 1.0)
    factor = 1.001 * jnp.exp(unit * jnp.log(4.0))
    sigmas = io_sigmas()
    return 0.001 * factor * (sigmas * sigmas)[:, None, None]


def draw_vectors(key, part):
    first_key, second_key = jax.random.split(jax.random.fold_in(key, 7))
    spread = 0.3 * jnp.clip(jax.random.normal(first_key, (8, D), jnp.float32), -5.0, 5.0)
    levelled = jax.random.uniform(second_key, (8, D), jnp.float32, 0.5, 1.5)
    row_ids = jnp.arange(8)
    picked = (row_ids == 2) | (row_ids == 5) | (row_ids == 7)
    return jnp.where(picked[:, None], levelled, spread)


def with_ends(values, rng, low, largest):
    index_at = [jax.random.randint(jax.random.fold_in(rng, axis), (), 0, length) for axis, length in enumerate(values.shape)]
    main_axis = values.shape.index(max(values.shape))
    beside = index_at[:main_axis] + [(index_at[main_axis] + 1) % values.shape[main_axis]] + index_at[main_axis + 1:]
    return values.at[tuple(index_at)].set(low).at[tuple(beside)].set(largest)


def block_scale(stream_key, shape, cuts, low, high):
    level = 1.0
    for axis_at, blocks in cuts:
        heights = jax.random.uniform(jax.random.fold_in(jax.random.fold_in(stream_key, 6), axis_at), (blocks,), jnp.float32, low / len(cuts), high / len(cuts))
        level = level * jnp.repeat(jnp.exp(heights), shape[axis_at] // blocks).reshape((-1,) + (1,) * (len(shape) - 1 - axis_at))
    return level


def gaussian(stream_key, shape, deviation, bound, shards=(), held_as=jnp.bfloat16):
    level = block_scale(stream_key, shape, shards, -0.22, 0.18) if shards else 1.0
    result = jax.random.normal(stream_key, shape, jnp.float32) * deviation * level
    return jnp.minimum(jnp.maximum(result, -bound), bound).astype(held_as)


def setup_inputs(seed: int = 0) -> dict:
    splits = jax.random.split(jax.random.key(seed), 22)
    return {
        "clean": draw_clean(jax.random.fold_in(splits[21], 71), 0),
        "noise": draw_noise(jax.random.fold_in(splits[21], 71), 0),
        "levels": with_ends(jax.random.randint(splits[2], (FRAMES,), 0, LEVELS), jax.random.fold_in(splits[2], 1), 0, LEVELS - 1).astype(jnp.int32),
        "lengths": draw_lengths(jax.random.fold_in(splits[21], 71), 0),
        "order": draw_order(jax.random.fold_in(splits[21], 71), 0),
        "step": jax.random.randint(splits[5], (1,), 1, 21).astype(jnp.int32),
        "w_attn": draw_w_attn(jax.random.fold_in(splits[21], 71), 0),
        "m_attn": gaussian(splits[7], (4, D, D), (0.000111 / (10 * D * D + 2 * D * FF + 2 * PF * D + 8 * D) ** 0.5), 1.4901161193847656e-07, ((1, 8), (2, 4)), jnp.float32),
        "v_attn": jnp.clip(jnp.exp(math.log(2.091440019707727e-16) - 1.3862944 * jax.random.uniform(splits[8], (4, D, D), jnp.float32) ** block_scale(splits[8], (4, D, D), ((1, 8), (2, 4)), -0.2, 0.2)), 5.2286000492693174e-17, 2.091440019707727e-16),
        "w_mlp": draw_w_mlp(jax.random.fold_in(splits[21], 71), 0),
        "m_mlp": gaussian(splits[10], (2, D, FF), (0.000111 / (10 * D * D + 2 * D * FF + 2 * PF * D + 8 * D) ** 0.5), 1.4901161193847656e-07, ((1, 8), (2, 4)), jnp.float32),
        "v_mlp": jnp.clip(jnp.exp(math.log(2.091440019707727e-16) - 1.3862944 * jax.random.uniform(splits[11], (2, D, FF), jnp.float32) ** block_scale(splits[11], (2, D, FF), ((1, 8), (2, 4)), -0.2, 0.2)), 5.2286000492693174e-17, 2.091440019707727e-16),
        "w_mod": gaussian(splits[12], (D, 6 * D), D ** -0.5, 0.1875, ((0, 8),), jnp.float32),
        "m_mod": gaussian(splits[13], (D, 6 * D), (0.000111 / (10 * D * D + 2 * D * FF + 2 * PF * D + 8 * D) ** 0.5), 1.4901161193847656e-07, ((0, 8),), jnp.float32),
        "v_mod": jnp.clip(jnp.exp(math.log(2.091440019707727e-16) - 1.3862944 * jax.random.uniform(splits[14], (D, 6 * D), jnp.float32) ** block_scale(splits[14], (D, 6 * D), ((0, 8),), -0.2, 0.2)), 5.2286000492693174e-17, 2.091440019707727e-16),
        "w_io": draw_w_io(jax.random.fold_in(splits[21], 71), 0),
        "m_io": draw_m_io(jax.random.fold_in(splits[21], 71), 0),
        "v_io": draw_v_io(jax.random.fold_in(splits[21], 71), 0),
        "vectors": draw_vectors(jax.random.fold_in(splits[21], 71), 0),
        "m_vec": gaussian(splits[19], (8, D), (0.000111 / (10 * D * D + 2 * D * FF + 2 * PF * D + 8 * D) ** 0.5), 1.4901161193847656e-07, ((1, 8),), jnp.float32),
        "v_vec": jnp.clip(jnp.exp(math.log(2.091440019707727e-16) - 1.3862944 * jax.random.uniform(splits[20], (8, D), jnp.float32) ** block_scale(splits[20], (8, D), ((1, 8),), -0.2, 0.2)), 5.2286000492693174e-17, 2.091440019707727e-16),
    }


highest = lax.Precision.HIGHEST
ln_eps = 1e-06
snr_limit = 5.0
clip_limit = 0.001
beta_one = 0.9
beta_two = 0.999
adam_eps = 1e-08
rate_matrix = 0.05
rate_vector = 0.3
decay_rate = 0.1

@jax.custom_vjp
def low(v):
    return lax.optimization_barrier(v.astype(jnp.bfloat16)).astype(jnp.float32)

@jax.custom_vjp
def low_back(v):
    return v

def low_keep(v):
    return (low(v), None)

def low_pass(kept, grad):
    return (grad,)

def back_keep(v):
    return (v, None)

def back_low(kept, grad):
    return (low(grad),)
low.defvjp(low_keep, low_pass)
low_back.defvjp(back_keep, back_low)

def clip_starts(frame_ids, lengths):
    clip_ends = jnp.cumsum(lengths).astype(jnp.int32)
    before = (clip_ends[None, :] <= frame_ids[:, None]).astype(jnp.int32)
    return lax.optimization_barrier(jnp.sum(before * lengths[None, :], axis=1)).astype(jnp.int32)

def plan(levels):
    fraction = (levels.astype(jnp.float32) + 1.0) / (LEVELS + 1.0)
    signal_scale = jnp.cos(0.5 * math.pi * fraction)
    noise_scale = jnp.sin(0.5 * math.pi * fraction)
    snr_value = signal_scale * signal_scale / (noise_scale * noise_scale)
    weight = jnp.minimum(snr_value, snr_limit) / (snr_value + 1.0)
    return (signal_scale, noise_scale, weight)

def condition(levels, width):
    half_dim = width // 2
    frequency = jnp.exp(-math.log(10000.0) * jnp.arange(half_dim, dtype=jnp.float32) / half_dim)
    angle_tab = levels.astype(jnp.float32)[:, None] * frequency[None, :]
    return jax.nn.silu(jnp.concatenate([jnp.cos(angle_tab), jnp.sin(angle_tab)], axis=1))

def rope_tables(time_pos, height_pos, width_pos, head_dim):
    pair_count = head_dim // 2
    time_pairs = head_dim // 8
    height_pairs = (pair_count - time_pairs) // 2
    width_pairs = pair_count - time_pairs - height_pairs

    def angles(position, count):
        frequency = 10000.0 ** (-jnp.arange(count, dtype=jnp.float32) / count)
        return position.astype(jnp.float32)[:, None] * frequency[None, :]
    angle_tab = jnp.concatenate([angles(time_pos, time_pairs), angles(height_pos, height_pairs), angles(width_pos, width_pairs)], axis=1)
    return (jnp.cos(angle_tab), jnp.sin(angle_tab))

def rotate(values, cosine, sine):
    half_dim = values.shape[-1] // 2
    first_half = values[..., :half_dim]
    second_half = values[..., half_dim:]
    cosine = cosine[:, None, :]
    sine = sine[:, None, :]
    return jnp.concatenate([first_half * cosine - second_half * sine, second_half * cosine + first_half * sine], axis=-1)

def layer_norm(values):
    centred = values - lax.optimization_barrier(jnp.mean(values, axis=-1, keepdims=True))
    return centred * lax.rsqrt(lax.optimization_barrier(jnp.mean(centred * centred, axis=-1, keepdims=True)) + ln_eps)

def attend(query, key_all, value_all, starts):
    window = MOST_CLIP
    padding = jnp.zeros((window - 1, PATCHES, HEADS, HD), jnp.float32)
    key_pad = jnp.concatenate([padding, key_all], axis=0)
    value_pad = jnp.concatenate([padding, value_all], axis=0)
    scale = HD ** (-0.5)

    @jax.checkpoint
    def per_frame(frame):
        query_frame = lax.dynamic_index_in_dim(query, frame, 0, keepdims=False)
        key_win = lax.dynamic_slice_in_dim(key_pad, frame, window, 0).reshape(window * PATCHES, HEADS, HD)
        value_win = lax.dynamic_slice_in_dim(value_pad, frame, window, 0).reshape(window * PATCHES, HEADS, HD)
        key_frames = frame - window + 1 + jnp.arange(window, dtype=jnp.int32)
        allowed = key_frames >= lax.dynamic_index_in_dim(starts, frame, 0, keepdims=False)
        allowed_keys = jnp.repeat(allowed, PATCHES)
        scores = jnp.einsum('phe,khe->hpk', query_frame, key_win, precision=highest) * scale
        scores = low_back(jnp.where(allowed_keys[None, None, :], scores, -1e+30))
        probs = jax.nn.softmax(scores, axis=-1)
        return jnp.einsum('hpk,khe->phe', low(probs), value_win, precision=highest)
    return lax.map(per_frame, jnp.arange(FRAMES, dtype=jnp.int32))

def forward(w_attn, w_mlp, w_mod, w_io, vectors, clean, noise, levels, lengths):
    attn_w = low(w_attn)
    mlp_w = low(w_mlp)
    mod_w = low(w_mod)
    io_w = low(w_io)
    vec_w = low(vectors)
    signal_scale, noise_scale, weight = plan(levels)
    signal_col = signal_scale[:, None, None]
    noise_col = noise_scale[:, None, None]
    noisy = signal_col * clean + noise_col * noise
    target = signal_col * noise - noise_col * clean
    tok_count = FRAMES * PATCHES
    noisy_low = low(noisy.reshape(tok_count, PF))
    embedded = low_back(jnp.dot(noisy_low, io_w[0], precision=highest)) + vec_w[6]
    cond_low = low(condition(levels, D))
    modulate = low_back(jnp.dot(cond_low, mod_w, precision=highest)) + vec_w[:6].reshape(6 * D)
    modulate = modulate.reshape(FRAMES, 6, 1, D)
    frame_ids = jnp.arange(FRAMES, dtype=jnp.int32)
    starts = clip_starts(frame_ids, lengths)
    patch_ids = jnp.arange(PATCHES, dtype=jnp.int32)
    time_pos = jnp.repeat(frame_ids - starts, PATCHES)
    height_pos = jnp.tile(patch_ids // GRID, FRAMES)
    width_pos = jnp.tile(patch_ids % GRID, FRAMES)
    cosine, sine = rope_tables(time_pos, height_pos, width_pos, HD)
    resid = embedded.reshape(FRAMES, PATCHES, D)
    normed = layer_norm(resid) * (1.0 + modulate[:, 1]) + modulate[:, 0]
    hidden_one = low(normed.reshape(tok_count, D))
    query = low(rotate(low_back(jnp.dot(hidden_one, attn_w[0], precision=highest)).reshape(tok_count, HEADS, HD), cosine, sine))
    keys = low(rotate(low_back(jnp.dot(hidden_one, attn_w[1], precision=highest)).reshape(tok_count, HEADS, HD), cosine, sine))
    values = low_back(low(jnp.dot(hidden_one, attn_w[2], precision=highest)))
    head_shape = (FRAMES, PATCHES, HEADS, HD)
    mixed = attend(query.reshape(head_shape), keys.reshape(head_shape), values.reshape(head_shape), starts)
    mixed = low_back(low(mixed.reshape(tok_count, D)))
    attn_out = low_back(jnp.dot(mixed, attn_w[3].T, precision=highest))
    resid = resid + modulate[:, 2] * attn_out.reshape(FRAMES, PATCHES, D)
    normed = layer_norm(resid) * (1.0 + modulate[:, 4]) + modulate[:, 3]
    hidden_two = low(normed.reshape(tok_count, D))
    upward = low_back(jnp.dot(hidden_two, mlp_w[0], precision=highest))
    activ = low(jax.nn.gelu(upward, approximate=False))
    mlp_out = low_back(jnp.dot(activ, mlp_w[1].T, precision=highest))
    resid = resid + modulate[:, 5] * mlp_out.reshape(FRAMES, PATCHES, D)
    final = low((layer_norm(resid) * vec_w[7]).reshape(tok_count, D))
    pred = low_back(jnp.dot(final, io_w[1].T, precision=highest))
    error = lax.optimization_barrier(jnp.mean((pred.reshape(FRAMES, PATCHES, PF) - target) ** 2, axis=2))
    return jnp.sum(weight[:, None] * error) / (PATCHES * jnp.sum(weight))

def adam(weight_now, first_mom, second_mom, grad, factor, count, rate, decay):
    grad = grad * factor
    first_mom = beta_one * first_mom + (1.0 - beta_one) * grad
    second_mom = beta_two * second_mom + (1.0 - beta_two) * grad * grad
    first_hat = first_mom / (1.0 - beta_one ** count)
    second_hat = second_mom / (1.0 - beta_two ** count)
    updated = weight_now - rate * (first_hat / (jnp.sqrt(second_hat) + adam_eps) + decay * weight_now)
    return (updated, first_mom, second_mom, updated.astype(jnp.bfloat16))

def reference(clean, noise, levels, lengths, order, step, w_attn, m_attn, v_attn, w_mlp, m_mlp, v_mlp, w_mod, m_mod, v_mod, w_io, m_io, v_io, vectors, m_vec, v_vec):
    inverse = jnp.zeros((STRETCHES,), jnp.int32).at[order].set(jnp.arange(STRETCHES, dtype=jnp.int32))

    def logical(data):
        return data.astype(jnp.float32).reshape(STRETCHES, CH_ROWS, PF)[inverse].reshape(FRAMES, PATCHES, PF)
    clean_log = logical(clean)
    noise_log = logical(noise)
    loss_value, pullback = jax.vjp(lambda *params: forward(*params, clean_log, noise_log, levels, lengths), w_attn, w_mlp, w_mod, w_io, vectors)
    grads = pullback(jnp.ones_like(loss_value))
    total = sum((jnp.sum(piece * piece) for piece in grads))
    grad_norm = jnp.sqrt(total)
    factor = jnp.minimum(1.0, clip_limit / (grad_norm + 1e-06))
    count = step[0].astype(jnp.float32)
    attn_new = adam(w_attn, m_attn, v_attn, grads[0], factor, count, rate_matrix, decay_rate)
    mlp_new = adam(w_mlp, m_mlp, v_mlp, grads[1], factor, count, rate_matrix, decay_rate)
    mod_new = adam(w_mod, m_mod, v_mod, grads[2], factor, count, rate_matrix, decay_rate)
    io_new = adam(w_io, m_io, v_io, grads[3], factor, count, rate_matrix, decay_rate)
    vec_new = adam(vectors, m_vec, v_vec, grads[4], factor, count, rate_vector, 0.0)
    return (loss_value, grad_norm, attn_new[0], attn_new[1], attn_new[2], attn_new[3], mlp_new[0], mlp_new[1], mlp_new[2], mlp_new[3], mod_new[0], mod_new[1], mod_new[2], mod_new[3], io_new[0], io_new[1], io_new[2][0], io_new[2][1], io_new[3], vec_new[0], vec_new[1], vec_new[2], vec_new[3])
```

```python
import math

import jax
import jax.numpy as jnp
from jax import lax
from jax.experimental import pallas as pl
from jax.experimental.pallas import tpu as pltpu
from jax.sharding import PartitionSpec as P

D = 1024
HD = 64
GRID = 16
PATCHES = 256
LEVELS = 1000


ln_eps = 1e-06
snr_limit = 5.0
clip_limit = 0.001
beta_one = 0.9
beta_two = 0.999
adam_eps = 1e-08
rate_matrix = 0.05
rate_vector = 0.3
decay_rate = 0.1
neg_large = -1e30


def clip_starts(frame_ids, lengths):
    clip_ends = jnp.cumsum(lengths)
    before = (clip_ends[None, :] <= frame_ids[:, None]).astype(jnp.int32)
    return jnp.sum(before * lengths[None, :], axis=1)


def plan(levels):
    fraction = (levels.astype(jnp.float32) + 1.0) / (LEVELS + 1.0)
    signal_scale = jnp.cos(0.5 * math.pi * fraction)
    noise_scale = jnp.sin(0.5 * math.pi * fraction)
    snr_value = signal_scale * signal_scale / (noise_scale * noise_scale)
    weight = jnp.minimum(snr_value, snr_limit) / (snr_value + 1.0)
    return (signal_scale, noise_scale, weight)


def condition(levels, width):
    half_dim = width // 2
    frequency = jnp.exp(-math.log(10000.0) * jnp.arange(half_dim, dtype=jnp.float32) / half_dim)
    angle_tab = levels.astype(jnp.float32)[:, None] * frequency[None, :]
    return jax.nn.silu(jnp.concatenate([jnp.cos(angle_tab), jnp.sin(angle_tab)], axis=1))


def rope_tables(time_pos, height_pos, width_pos, head_dim):
    pair_count = head_dim // 2
    time_pairs = head_dim // 8
    height_pairs = (pair_count - time_pairs) // 2
    width_pairs = pair_count - time_pairs - height_pairs

    def angles(position, count):
        frequency = 10000.0 ** (-jnp.arange(count, dtype=jnp.float32) / count)
        return position.astype(jnp.float32)[:, None] * frequency[None, :]

    angle_tab = jnp.concatenate(
        [
            angles(time_pos, time_pairs),
            angles(height_pos, height_pairs),
            angles(width_pos, width_pairs),
        ],
        axis=1,
    )
    return (jnp.cos(angle_tab), jnp.sin(angle_tab))


def rotate(values, cosine, sine):
    half_dim = values.shape[-1] // 2
    first_half = values[..., :half_dim]
    second_half = values[..., half_dim:]
    cosine = cosine[:, None, :]
    sine = sine[:, None, :]
    return jnp.concatenate(
        [first_half * cosine - second_half * sine, second_half * cosine + first_half * sine],
        axis=-1,
    )


def rotate_back(grads, cosine, sine):
    half_dim = grads.shape[-1] // 2
    first_half = grads[..., :half_dim]
    second_half = grads[..., half_dim:]
    cosine = cosine[:, None, :]
    sine = sine[:, None, :]
    return jnp.concatenate(
        [first_half * cosine + second_half * sine, second_half * cosine - first_half * sine],
        axis=-1,
    )


def layer_norm(values):
    centred = values - jnp.mean(values, axis=-1, keepdims=True)
    inv_std = lax.rsqrt(jnp.mean(centred * centred, axis=-1, keepdims=True) + ln_eps)
    return (centred * inv_std, inv_std)


def norm_back(grad_in, normed, inv_std):
    mean_grad = jnp.mean(grad_in, axis=-1, keepdims=True)
    mean_proj = jnp.mean(grad_in * normed, axis=-1, keepdims=True)
    return inv_std * (grad_in - mean_grad - normed * mean_proj)


def gelu_slope(values):
    return 0.5 * (1.0 + lax.erf(values / math.sqrt(2.0))) + values * jnp.exp(
        -0.5 * values * values
    ) / math.sqrt(2.0 * math.pi)


def stretch_mask(query_stretch, key_stretch, stretch_frames, lengths):
    offsets = jnp.arange(stretch_frames, dtype=jnp.int32)
    query_frames = query_stretch * stretch_frames + offsets
    key_frames = key_stretch * stretch_frames + offsets
    starts = clip_starts(query_frames, lengths)
    return (key_frames[None, :] <= query_frames[:, None]) & (key_frames[None, :] >= starts[:, None])


def expand_mask(allowed):
    return jnp.repeat(jnp.repeat(allowed, PATCHES, axis=0), PATCHES, axis=1)


def online_step(current, query_block, key_block, value_block, keep, scale):
    run_max, run_sum, run_acc = current
    scores = (
        jnp.einsum("qhe,khe->hqk", query_block, key_block, preferred_element_type=jnp.float32)
        * scale
    )
    scores = jnp.where(keep[None], scores, neg_large)
    new_max = jnp.maximum(run_max, jnp.max(scores, axis=-1))
    probs = jnp.where(keep[None], jnp.exp(scores - new_max[..., None]), 0.0)
    shrink = jnp.exp(run_max - new_max)
    run_sum = run_sum * shrink + jnp.sum(probs, axis=-1)
    added = jnp.einsum(
        "hqk,khe->qhe", probs.astype(jnp.bfloat16), value_block, preferred_element_type=jnp.float32
    )
    run_acc = run_acc * jnp.transpose(shrink)[:, :, None] + added
    return (new_max, run_sum, run_acc)


def pair_grads(
    query_block, grad_block, lse_block, delta_block, key_block, value_block, keep, scale
):
    scores = (
        jnp.einsum("qhe,khe->hqk", query_block, key_block, preferred_element_type=jnp.float32)
        * scale
    )
    probs = jnp.where(keep[None], jnp.exp(scores - lse_block[..., None]), 0.0)
    grad_probs = jnp.einsum(
        "qhe,khe->hqk", grad_block, value_block, preferred_element_type=jnp.float32
    )
    grad_scores = (probs * (grad_probs - delta_block[..., None])).astype(jnp.bfloat16)
    grad_query = (
        jnp.einsum("hqk,khe->qhe", grad_scores, key_block, preferred_element_type=jnp.float32)
        * scale
    )
    grad_key = (
        jnp.einsum("hqk,qhe->khe", grad_scores, query_block, preferred_element_type=jnp.float32)
        * scale
    )
    grad_value = jnp.einsum(
        "hqk,qhe->khe", probs.astype(jnp.bfloat16), grad_block, preferred_element_type=jnp.float32
    )
    return (grad_query, grad_key, grad_value)


def adam(weight_now, first_mom, second_mom, grad, factor, count, rate, decay):
    grad = grad * factor
    first_mom = beta_one * first_mom + (1.0 - beta_one) * grad
    second_mom = beta_two * second_mom + (1.0 - beta_two) * grad * grad
    first_hat = first_mom / (1.0 - beta_one**count)
    second_hat = second_mom / (1.0 - beta_two**count)
    updated = weight_now - rate * (
        first_hat / (jnp.sqrt(second_hat) + adam_eps) + decay * weight_now
    )
    return (updated, first_mom, second_mom, updated.astype(jnp.bfloat16))


def shards(
    clean,
    noise,
    levels,
    lengths,
    order,
    step,
    w_attn,
    m_attn,
    v_attn,
    w_mlp,
    m_mlp,
    v_mlp,
    w_mod,
    m_mod,
    v_mod,
    w_io,
    m_io,
    v_io,
    vectors,
    m_vec,
    v_vec,
):
    ctx_count = lax.axis_size("ctx")
    ctx_index = lax.axis_index("ctx")
    tp_index = lax.axis_index("tp")
    tok_rows = clean.shape[0]
    feat_dim = clean.shape[1]
    frames_dev = tok_rows // PATCHES
    stretch_frames = frames_dev // 2
    stretch_rows = stretch_frames * PATCHES
    scale = HD ** (-0.5)
    bfloat = jnp.bfloat16
    single = jnp.float32
    attn_w, mlp_w, mod_w, io_w, vec_low = (
        lax.all_gather(w_attn.astype(bfloat), "ctx", axis=1, tiled=True),
        lax.all_gather(w_mlp.astype(bfloat), "ctx", axis=1, tiled=True),
        lax.all_gather(w_mod.astype(bfloat), "ctx", axis=0, tiled=True),
        lax.all_gather(w_io.astype(bfloat), "ctx", axis=2, tiled=True),
        lax.all_gather(vectors.astype(bfloat), "ctx", axis=1, tiled=True),
    )
    vec_w = vec_low.astype(single)
    local_width = attn_w.shape[2]
    heads_dev = local_width // HD
    frame_count = levels.shape[0]
    local_stretches = lax.dynamic_slice_in_dim(order, 2 * ctx_index, 2, 0)
    frame_ids = (
        local_stretches[:, None] * stretch_frames
        + jnp.arange(stretch_frames, dtype=jnp.int32)[None, :]
    ).reshape(frames_dev)
    table_hit = frame_ids[:, None] == jnp.arange(frame_count, dtype=jnp.int32)[None, :]
    frame_levels = jnp.sum(jnp.where(table_hit, levels[None, :], 0), axis=1)
    starts = clip_starts(frame_ids, lengths)
    signal_scale, noise_scale, weight = plan(frame_levels)
    signal_col = signal_scale[:, None, None]
    noise_col = noise_scale[:, None, None]
    clean_full = clean.astype(single).reshape(frames_dev, PATCHES, feat_dim)
    noise_full = noise.astype(single).reshape(frames_dev, PATCHES, feat_dim)
    noisy = signal_col * clean_full + noise_col * noise_full
    target = signal_col * noise_full - noise_col * clean_full
    noisy_low = noisy.reshape(tok_rows, feat_dim).astype(bfloat)
    embedded = jnp.dot(noisy_low, io_w[0], preferred_element_type=single) + vec_w[6]
    cond_low = condition(frame_levels, D).astype(bfloat)
    modulate = (
        jnp.dot(cond_low, mod_w, preferred_element_type=single) + vec_w[:6].reshape(6 * D)
    ).reshape(frames_dev, 6, 1, D)
    patch_ids = jnp.arange(PATCHES, dtype=jnp.int32)
    time_pos = jnp.repeat(frame_ids - starts, PATCHES)
    height_pos = jnp.tile(patch_ids // GRID, frames_dev)
    width_pos = jnp.tile(patch_ids % GRID, frames_dev)
    cosine, sine = rope_tables(time_pos, height_pos, width_pos, HD)
    resid_in = embedded.reshape(frames_dev, PATCHES, D)
    normed_one, inv_one = layer_norm(resid_in)
    hidden_one = (
        (normed_one * (1.0 + modulate[:, 1]) + modulate[:, 0]).reshape(tok_rows, D).astype(bfloat)
    )
    query_pre = jnp.dot(hidden_one, attn_w[0], preferred_element_type=single).reshape(
        tok_rows, heads_dev, HD
    )
    key_pre = jnp.dot(hidden_one, attn_w[1], preferred_element_type=single).reshape(
        tok_rows, heads_dev, HD
    )
    query_low = rotate(query_pre, cosine, sine).astype(bfloat)
    key_low = rotate(key_pre, cosine, sine).astype(bfloat)
    value_low = (
        jnp.dot(hidden_one, attn_w[2], preferred_element_type=single)
        .astype(bfloat)
        .reshape(tok_rows, heads_dev, HD)
    )
    query_stretches = query_low.reshape(2, stretch_rows, heads_dev, HD)
    init_state = (
        jnp.full((2, heads_dev, stretch_rows), neg_large, single),
        jnp.zeros((2, heads_dev, stretch_rows), single),
        jnp.zeros((2, stretch_rows, heads_dev, HD), single),
    )
    key_flat = key_low.reshape(tok_rows, local_width)
    value_flat = value_low.reshape(tok_rows, local_width)
    carry_state = init_state
    key_piece = lax.all_gather(key_flat, "ctx", axis=0, tiled=True)
    value_piece = lax.all_gather(value_flat, "ctx", axis=0, tiled=True)

    def per_stretch(block_num, carry_state):
        key_block = lax.dynamic_slice_in_dim(
            key_piece, block_num * stretch_rows, stretch_rows, 0
        ).reshape(stretch_rows, heads_dev, HD)
        value_block = lax.dynamic_slice_in_dim(
            value_piece, block_num * stretch_rows, stretch_rows, 0
        ).reshape(stretch_rows, heads_dev, HD)
        key_stretch = lax.dynamic_index_in_dim(order, block_num, 0, keepdims=False)
        updated = []
        for half_num in range(2):
            allowed = stretch_mask(local_stretches[half_num], key_stretch, stretch_frames, lengths)
            current = (carry_state[0][half_num], carry_state[1][half_num], carry_state[2][half_num])
            current = lax.cond(
                jnp.any(allowed),
                lambda cur, keep_mask: online_step(
                    cur,
                    query_stretches[half_num],
                    key_block,
                    value_block,
                    expand_mask(keep_mask),
                    scale,
                ),
                lambda cur, keep_mask: cur,
                current,
                allowed,
            )
            updated.append(current)
        return tuple((jnp.stack([updated[0][member], updated[1][member]]) for member in range(3)))

    run_max, run_sum, run_acc = lax.fori_loop(
        0, key_piece.shape[0] // stretch_rows, per_stretch, carry_state
    )
    mix_rows = (run_acc / jnp.transpose(run_sum, (0, 2, 1))[..., None]).reshape(
        tok_rows, heads_dev, HD
    )
    lse_stretches = run_max + jnp.log(run_sum)
    mix_low = mix_rows.reshape(tok_rows, local_width).astype(bfloat)
    attn_out = lax.psum(
        jnp.einsum("rh,dh->rd", mix_low, attn_w[3], preferred_element_type=single).astype(
            jnp.bfloat16
        ),
        "tp",
    ).astype(jnp.float32)
    attn_full = attn_out.reshape(frames_dev, PATCHES, D)
    resid_mid = resid_in + modulate[:, 2] * attn_full
    normed_two, inv_two = layer_norm(resid_mid)
    hidden_two = (
        (normed_two * (1.0 + modulate[:, 4]) + modulate[:, 3]).reshape(tok_rows, D).astype(bfloat)
    )
    upward = jnp.dot(hidden_two, mlp_w[0], preferred_element_type=single)
    activ_low = jax.nn.gelu(upward, approximate=False).astype(bfloat)
    mlp_out = lax.psum(
        jnp.einsum("rf,df->rd", activ_low, mlp_w[1], preferred_element_type=single).astype(
            jnp.bfloat16
        ),
        "tp",
    ).astype(jnp.float32)
    mlp_full = mlp_out.reshape(frames_dev, PATCHES, D)
    resid_out = resid_mid + modulate[:, 5] * mlp_full
    normed_three, inv_three = layer_norm(resid_out)
    final_low = (normed_three * vec_w[7]).reshape(tok_rows, D).astype(bfloat)
    pred = jnp.einsum("rd,pd->rp", final_low, io_w[1], preferred_element_type=single)
    diff = pred.reshape(frames_dev, PATCHES, feat_dim) - target
    error = jnp.mean(diff * diff, axis=2)
    weight_sum, error_sum = lax.psum(
        (PATCHES * jnp.sum(weight), jnp.sum(weight[:, None] * error)), "ctx"
    )
    loss_value = error_sum / weight_sum
    grad_pred = (
        (2.0 / feat_dim * weight[:, None, None] * diff / weight_sum)
        .reshape(tok_rows, feat_dim)
        .astype(bfloat)
    )
    grad_head = jnp.einsum("rp,rd->pd", grad_pred, final_low, preferred_element_type=single)
    grad_final = jnp.einsum("rp,pd->rd", grad_pred, io_w[1], preferred_element_type=single).reshape(
        frames_dev, PATCHES, D
    )
    grad_gain = jnp.sum(grad_final * normed_three, axis=(0, 1))
    grad_three = norm_back(grad_final * vec_w[7], normed_three, inv_three)
    grad_mlp_low = (modulate[:, 5] * grad_three).reshape(tok_rows, D).astype(bfloat)
    grad_gate_two = jnp.sum(grad_three * mlp_full, axis=1)
    grad_activ = jnp.einsum("rd,df->rf", grad_mlp_low, mlp_w[1], preferred_element_type=single)
    grad_down = jnp.einsum("rd,rf->df", grad_mlp_low, activ_low, preferred_element_type=single)
    grad_up_low = (grad_activ * gelu_slope(upward)).astype(bfloat)
    grad_up = jnp.einsum("rd,rf->df", hidden_two, grad_up_low, preferred_element_type=single)
    grad_hidden_two = lax.psum(
        jnp.einsum("rf,df->rd", grad_up_low, mlp_w[0], preferred_element_type=single).astype(
            jnp.bfloat16
        ),
        "tp",
    ).astype(jnp.float32)
    grad_hidden_two = grad_hidden_two.reshape(frames_dev, PATCHES, D)
    grad_shift_two = jnp.sum(grad_hidden_two, axis=1)
    grad_scale_two = jnp.sum(grad_hidden_two * normed_two, axis=1)
    grad_mid = grad_three + norm_back(grad_hidden_two * (1.0 + modulate[:, 4]), normed_two, inv_two)
    grad_attn_low = (modulate[:, 2] * grad_mid).reshape(tok_rows, D).astype(bfloat)
    grad_gate_one = jnp.sum(grad_mid * attn_full, axis=1)
    grad_outproj = jnp.einsum("rd,rh->dh", grad_attn_low, mix_low, preferred_element_type=single)
    grad_mix_low = jnp.einsum(
        "rd,dh->rh", grad_attn_low, attn_w[3], preferred_element_type=single
    ).astype(bfloat)
    delta_rows = jnp.sum(
        grad_mix_low.astype(single).reshape(tok_rows, heads_dev, HD) * mix_rows, axis=2
    )
    grad_stretches = grad_mix_low.reshape(2, stretch_rows, heads_dev, HD)
    delta_stretches = jnp.transpose(delta_rows.reshape(2, stretch_rows, heads_dev), (0, 2, 1))

    def span_back(key_block, value_block, key_stretch, grad_query_acc):
        key_sum = jnp.zeros((stretch_rows, heads_dev, HD), single)
        value_sum = jnp.zeros((stretch_rows, heads_dev, HD), single)
        query_parts = []
        for half_num in range(2):
            allowed = stretch_mask(local_stretches[half_num], key_stretch, stretch_frames, lengths)
            result = lax.cond(
                jnp.any(allowed),
                lambda keep_mask: pair_grads(
                    query_stretches[half_num],
                    grad_stretches[half_num],
                    lse_stretches[half_num],
                    delta_stretches[half_num],
                    key_block,
                    value_block,
                    expand_mask(keep_mask),
                    scale,
                ),
                lambda keep_mask: (jnp.zeros((stretch_rows, heads_dev, HD), single),) * 3,
                allowed,
            )
            query_parts.append(grad_query_acc[half_num] + result[0])
            key_sum = key_sum + result[1]
            value_sum = value_sum + result[2]
        return (
            jnp.stack(query_parts),
            key_sum.reshape(stretch_rows, local_width),
            value_sum.reshape(stretch_rows, local_width),
        )

    init_back = (
        jnp.zeros((2, stretch_rows, heads_dev, HD), single),
        jnp.zeros((ctx_count * tok_rows, local_width), single),
        jnp.zeros((ctx_count * tok_rows, local_width), single),
    )
    carry_state = init_back
    fold_key_piece = lax.all_gather(key_flat, "ctx", axis=0, tiled=True)
    fold_value_piece = lax.all_gather(value_flat, "ctx", axis=0, tiled=True)

    def per_stretch(block_num, carry_state):
        grad_query_acc, grad_keys_all, grad_values_all = carry_state
        key_block = lax.dynamic_slice_in_dim(
            fold_key_piece, block_num * stretch_rows, stretch_rows, 0
        ).reshape(stretch_rows, heads_dev, HD)
        value_block = lax.dynamic_slice_in_dim(
            fold_value_piece, block_num * stretch_rows, stretch_rows, 0
        ).reshape(stretch_rows, heads_dev, HD)
        key_stretch = lax.dynamic_index_in_dim(order, block_num, 0, keepdims=False)
        grad_query_acc, key_sum, value_sum = span_back(
            key_block, value_block, key_stretch, grad_query_acc
        )
        place = block_num * stretch_rows
        grad_keys_all = lax.dynamic_update_slice_in_dim(grad_keys_all, key_sum, place, 0)
        grad_values_all = lax.dynamic_update_slice_in_dim(grad_values_all, value_sum, place, 0)
        return (grad_query_acc, grad_keys_all, grad_values_all)

    grad_query_acc, grad_keys_all, grad_values_all = lax.fori_loop(
        0, fold_key_piece.shape[0] // stretch_rows, per_stretch, carry_state
    )
    grad_keys, grad_values = (
        lax.psum_scatter(
            grad_keys_all.astype(jnp.bfloat16), "ctx", scatter_dimension=0, tiled=True
        ).astype(jnp.float32),
        lax.psum_scatter(
            grad_values_all.astype(jnp.bfloat16), "ctx", scatter_dimension=0, tiled=True
        ).astype(jnp.float32),
    )
    grad_query = grad_query_acc.reshape(tok_rows, local_width)
    query_back = (
        rotate_back(grad_query.reshape(tok_rows, heads_dev, HD), cosine, sine)
        .reshape(tok_rows, local_width)
        .astype(bfloat)
    )
    key_back = (
        rotate_back(grad_keys.reshape(tok_rows, heads_dev, HD), cosine, sine)
        .reshape(tok_rows, local_width)
        .astype(bfloat)
    )
    value_back = grad_values.astype(bfloat)
    grad_wq = jnp.einsum("rd,rh->dh", hidden_one, query_back, preferred_element_type=single)
    grad_wk = jnp.einsum("rd,rh->dh", hidden_one, key_back, preferred_element_type=single)
    grad_wv = jnp.einsum("rd,rh->dh", hidden_one, value_back, preferred_element_type=single)
    partial_one = (
        jnp.einsum("rh,dh->rd", query_back, attn_w[0], preferred_element_type=single)
        + jnp.einsum("rh,dh->rd", key_back, attn_w[1], preferred_element_type=single)
        + jnp.einsum("rh,dh->rd", value_back, attn_w[2], preferred_element_type=single)
    )
    grad_hidden_one = (
        lax.psum(partial_one.astype(jnp.bfloat16), "tp")
        .astype(jnp.float32)
        .reshape(frames_dev, PATCHES, D)
    )
    grad_shift_one = jnp.sum(grad_hidden_one, axis=1)
    grad_scale_one = jnp.sum(grad_hidden_one * normed_one, axis=1)
    grad_in = grad_mid + norm_back(grad_hidden_one * (1.0 + modulate[:, 1]), normed_one, inv_one)
    grad_mod = jnp.stack(
        [
            grad_shift_one,
            grad_scale_one,
            grad_gate_one,
            grad_shift_two,
            grad_scale_two,
            grad_gate_two,
        ],
        axis=1,
    )
    grad_mod_w = jnp.einsum(
        "fd,fc->dc",
        cond_low,
        grad_mod.reshape(frames_dev, 6 * D).astype(bfloat),
        preferred_element_type=single,
    )
    grad_in_low = grad_in.reshape(tok_rows, D).astype(bfloat)
    grad_embed = jnp.einsum("rp,rd->pd", noisy_low, grad_in_low, preferred_element_type=single)
    grad_vec = jnp.concatenate(
        [jnp.sum(grad_mod, axis=0), jnp.sum(grad_in, axis=(0, 1))[None], grad_gain[None]], axis=0
    )
    grad_attn = jnp.stack([grad_wq, grad_wk, grad_wv, grad_outproj])
    grad_mlp = jnp.stack([grad_up, grad_down])
    grad_io = jnp.stack([grad_embed, grad_head])
    red_attn, red_mlp, red_mod, red_io, red_vec = (
        lax.psum_scatter(
            grad_attn.astype(jnp.bfloat16), "ctx", scatter_dimension=1, tiled=True
        ).astype(jnp.float32),
        lax.psum_scatter(
            grad_mlp.astype(jnp.bfloat16), "ctx", scatter_dimension=1, tiled=True
        ).astype(jnp.float32),
        lax.psum_scatter(
            grad_mod_w.astype(jnp.bfloat16), "ctx", scatter_dimension=0, tiled=True
        ).astype(jnp.float32),
        lax.psum_scatter(
            grad_io.astype(jnp.bfloat16), "ctx", scatter_dimension=2, tiled=True
        ).astype(jnp.float32),
        lax.psum_scatter(
            grad_vec.astype(jnp.bfloat16), "ctx", scatter_dimension=1, tiled=True
        ).astype(jnp.float32),
    )
    shared_sq = jnp.sum(red_mod * red_mod) + jnp.sum(red_io * red_io) + jnp.sum(red_vec * red_vec)
    own_sq = (
        jnp.sum(red_attn * red_attn)
        + jnp.sum(red_mlp * red_mlp)
        + jnp.where(tp_index == 0, shared_sq, 0.0)
    )
    grad_norm = jnp.sqrt(lax.psum(own_sq, ("ctx", "tp")))
    factor = jnp.minimum(1.0, clip_limit / (grad_norm + 1e-06))
    count = step[0].astype(single)
    attn_new = adam(w_attn, m_attn, v_attn, red_attn, factor, count, rate_matrix, decay_rate)
    mlp_new = adam(w_mlp, m_mlp, v_mlp, red_mlp, factor, count, rate_matrix, decay_rate)
    mod_new = adam(w_mod, m_mod, v_mod, red_mod, factor, count, rate_matrix, decay_rate)
    io_new = adam(w_io, m_io, v_io, red_io, factor, count, rate_matrix, decay_rate)
    vec_new = adam(vectors, m_vec, v_vec, red_vec, factor, count, rate_vector, 0.0)
    return (
        loss_value,
        grad_norm,
        attn_new[0],
        attn_new[1],
        attn_new[2],
        attn_new[3],
        mlp_new[0],
        mlp_new[1],
        mlp_new[2],
        mlp_new[3],
        mod_new[0],
        mod_new[1],
        mod_new[2],
        mod_new[3],
        io_new[0],
        io_new[1],
        io_new[2][0],
        io_new[2][1],
        io_new[3],
        vec_new[0],
        vec_new[1],
        vec_new[2],
        vec_new[3],
    )


RING = (0, 1, 3, 5, 7, 6, 4, 2)
RING_NEXT = tuple((RING[i], RING[(i + 1) % 8]) for i in range(8))
RING_PREV = tuple((b, a) for a, b in RING_NEXT)
HALF_SLOTS = 16
QKV_ROWS = 768
FRONT_ROWS = 912
NT = (((1,), (1,)), ((), ()))
TN = (((0,), (0,)), ((), ()))


def swap(values, axis, bit):
    size = 8 if axis == "ctx" else 4
    return lax.ppermute(values, axis, [(i, i ^ bit) for i in range(size)])


def ring_position(index):
    z, x = index // 2, index % 2
    return jnp.where(x == 1, z + 1, (8 - z) % 8)


def ring_member(position):
    position = position % 8
    return jnp.where(
        position == 0, 0, jnp.where(position <= 4, 2 * position - 1, 2 * (8 - position))
    )


def ring_gather(shard):
    half = shard.shape[0] // 2
    ahead = [shard]
    behind = [shard]
    for _ in range(3):
        ahead.append(lax.ppermute(ahead[-1], "ctx", RING_NEXT))
        behind.append(lax.ppermute(behind[-1], "ctx", RING_PREV))
    first = lax.ppermute(ahead[-1][:half], "ctx", RING_NEXT)
    second = lax.ppermute(behind[-1][half:], "ctx", RING_PREV)
    return ahead + behind[1:] + [jnp.concatenate([first, second], axis=0)]


def ring_offsets(ctx_index):
    position = ring_position(ctx_index)
    return [ring_member(position + 8 + offset) for offset in (0, -1, -2, -3, 1, 2, 3, 4)]


def reduce_blocks(blocks, ctx_index, wire):
    x = ctx_index % 2
    z = ctx_index // 2
    pairs = blocks.reshape((4, 2) + blocks.shape[1:])
    first, second = pairs[:, 0], pairs[:, 1]
    even = x == 0
    away = jnp.where(even, second, first).astype(wire)
    held = jnp.where(even, first, second) + swap(away, "ctx", 1).astype(jnp.float32)
    total = lax.dynamic_index_in_dim(held, z, 0, keepdims=False)
    low = held.astype(wire)
    for bit in (1, 2, 3):
        piece = lax.dynamic_index_in_dim(low, z ^ bit, 0, keepdims=False)
        total = total + swap(piece, "ctx", 2 * bit).astype(jnp.float32)
    return total


def spread_frames(own):
    core = swap(own, "tp", 1)
    across = swap(own, "tp", 2)
    return [own, core, across, swap(across, "tp", 1)]


def sum_frames(parts):
    low = jnp.stack([parts[1], parts[3]]).astype(jnp.bfloat16)
    came = swap(low, "tp", 1)
    across = (parts[2] + came[1].astype(jnp.float32)).astype(jnp.bfloat16)
    return parts[0] + came[0].astype(jnp.float32) + swap(across, "tp", 2).astype(jnp.float32)


def reorder_four(items, index):
    low_bit = (index & 1) == 1
    high_bit = (index & 2) == 2
    once = [jnp.where(low_bit, items[k ^ 1], items[k]) for k in range(4)]
    return [jnp.where(high_bit, once[k ^ 2], once[k]) for k in range(4)]


def sum_all(values):
    for axis, bit in (("tp", 1), ("tp", 2), ("ctx", 1), ("ctx", 2), ("ctx", 4)):
        values = values + swap(values, axis, bit)
    return values


def front_kernel(meta, *refs):
    shards_in = refs[:8]
    noisy, shift_scale, cosine, sine, weights, hidden, resid, heads, work = refs[8:]
    for place in range(8):
        weights[:, pl.ds(pl.multiple_of(meta[place] * 128, 128), 128)] = shards_in[place][...]
    embed = weights[QKV_ROWS : QKV_ROWS + 128, :]
    vec_rows = weights[QKV_ROWS + 128 : FRONT_ROWS, :].astype(jnp.float32)
    for frame in range(4):
        values = jnp.dot(noisy[frame], embed, preferred_element_type=jnp.float32) + vec_rows[6:7]
        if frame == 0:
            resid[...] = values
        centred = values - jnp.mean(values, axis=-1, keepdims=True)
        normed = centred * lax.rsqrt(jnp.mean(centred * centred, axis=-1, keepdims=True) + ln_eps)
        shift = shift_scale[frame, 0:1, :] + vec_rows[0:1]
        scale = shift_scale[frame, 1:2, :] + vec_rows[1:2]
        low = (normed * (1.0 + scale) + shift).astype(jnp.bfloat16)
        hidden[frame] = low
        mixed = lax.dot_general(
            weights[0:QKV_ROWS, :], low, NT, preferred_element_type=jnp.float32
        )
        cos_now = cosine[meta[8 + frame]]
        sin_now = sine[meta[8 + frame]]
        for head in range(4):
            base = 192 * head
            where_to = meta[12 + head]
            cols = slice(256 * frame, 256 * frame + 256)
            for part in range(2):
                upper = mixed[base + 64 * part : base + 64 * part + 32]
                lower = mixed[base + 64 * part + 32 : base + 64 * part + 64]
                heads[where_to, 64 * part : 64 * part + 32, cols] = (
                    upper * cos_now - lower * sin_now
                ).astype(jnp.bfloat16)
                heads[where_to, 64 * part + 32 : 64 * part + 64, cols] = (
                    lower * cos_now + upper * sin_now
                ).astype(jnp.bfloat16)
            heads[where_to, 128:192, cols] = mixed[base + 128 : base + 192].astype(jnp.bfloat16)


def call_front(meta, shard_list, noisy, shift_scale, cosine, sine):
    vmem = pl.BlockSpec(memory_space=pltpu.VMEM)
    return pl.pallas_call(
        front_kernel,
        out_shape=(
            jax.ShapeDtypeStruct((FRONT_ROWS, D), jnp.bfloat16),
            jax.ShapeDtypeStruct((4, PATCHES, D), jnp.bfloat16),
            jax.ShapeDtypeStruct((PATCHES, D), jnp.float32),
            jax.ShapeDtypeStruct((4, 192, 4 * PATCHES), jnp.bfloat16),
        ),
        in_specs=[pl.BlockSpec(memory_space=pltpu.SMEM)] + [vmem] * 12,
        out_specs=(vmem,) * 4,
        scratch_shapes=[pltpu.VMEM((8, 128), jnp.float32)],
        compiler_params=pltpu.CompilerParams(vmem_limit_bytes=40 * 2**20),
        cost_estimate=pl.CostEstimate(flops=2 * 10**9, bytes_accessed=10**7, transcendentals=0),
        name="front",
    )(meta, *shard_list, noisy, shift_scale, cosine, sine)


def turn(block):
    return block.astype(jnp.float32).T.astype(jnp.bfloat16)


def query_rows(meta, pair):
    first = 2 * pair
    start_first = first - meta[2 + first]
    start_second = first + 1 - meta[3 + first]
    left = lax.broadcasted_iota(jnp.int32, (1, 2 * PATCHES), 1) < PATCHES
    upto = jnp.where(left, first, first + 1)
    since = jnp.where(left, start_first, start_second)
    return jnp.minimum(start_first, start_second), since, upto


def attend_kernel(meta, *refs):
    blocks = refs[:4]
    outs = refs[4:8]
    lse, mixed, query, key, value = refs[8:]
    for member in range(4):
        for frame in range(4):
            slot = 4 * (meta[0] ^ member) + (meta[1] ^ frame)
            cols = slice(256 * frame, 256 * frame + 256)
            lanes = pl.ds(pl.multiple_of((slot % 2) * 256, 256), 256)
            query[slot // 2, :, lanes] = blocks[member][0:64, cols] * 0.125
            key[slot] = turn(blocks[member][64:128, cols])
            value[slot] = blocks[member][128:192, cols]

    def per_pair(pair, carry):
        low, since, upto = query_rows(meta, pair)
        wanted = query[pair]

        def per_key(slot, state):
            top, total, acc = state
            bias = jnp.where((slot >= since) & (slot <= upto), 0.0, neg_large)
            scores = jnp.dot(key[slot], wanted, preferred_element_type=jnp.float32) + bias
            new_top = jnp.maximum(top, jnp.max(scores, axis=0, keepdims=True))
            probs = jnp.exp(scores - new_top)
            shrink = jnp.exp(top - new_top)
            total = total * shrink + jnp.sum(probs, axis=0, keepdims=True)
            acc = acc * shrink + jnp.dot(
                value[slot], probs.astype(jnp.bfloat16), preferred_element_type=jnp.float32
            )
            return (new_top, total, acc)

        top, total, acc = lax.fori_loop(
            low,
            2 * pair + 2,
            per_key,
            (
                jnp.full((1, 2 * PATCHES), neg_large, jnp.float32),
                jnp.zeros((1, 2 * PATCHES), jnp.float32),
                jnp.zeros((HD, 2 * PATCHES), jnp.float32),
            ),
        )
        lse[pair] = top + jnp.log(total)
        mixed[pair] = acc / total
        return carry

    lax.fori_loop(0, 8, per_pair, 0)
    for member in range(4):
        for frame in range(4):
            slot = 4 * (meta[0] ^ member) + (meta[1] ^ frame)
            lanes = pl.ds(pl.multiple_of((slot % 2) * 256, 256), 256)
            outs[member][:, 256 * frame : 256 * frame + 256] = mixed[slot // 2, :, lanes].astype(
                jnp.bfloat16
            )


def call_attend(meta, blocks):
    vmem = pl.BlockSpec(memory_space=pltpu.VMEM)
    result = pl.pallas_call(
        attend_kernel,
        out_shape=tuple(jax.ShapeDtypeStruct((HD, 4 * PATCHES), jnp.bfloat16) for _ in range(4))
        + (
            jax.ShapeDtypeStruct((8, 1, 2 * PATCHES), jnp.float32),
            jax.ShapeDtypeStruct((8, HD, 2 * PATCHES), jnp.float32),
        ),
        in_specs=[pl.BlockSpec(memory_space=pltpu.SMEM)] + [vmem] * 4,
        out_specs=(vmem,) * 6,
        scratch_shapes=[
            pltpu.VMEM((8, HD, 2 * PATCHES), jnp.bfloat16),
            pltpu.VMEM((16, PATCHES, HD), jnp.bfloat16),
            pltpu.VMEM((16, HD, PATCHES), jnp.bfloat16),
        ],
        compiler_params=pltpu.CompilerParams(vmem_limit_bytes=40 * 2**20),
        cost_estimate=pl.CostEstimate(flops=9 * 10**9, bytes_accessed=5 * 10**6, transcendentals=10**7),
        name="attend",
    )(meta, *blocks)
    return list(result[:4]), result[4], result[5]


def attend_back_kernel(meta, *refs):
    blocks = refs[:4]
    grads = refs[4:8]
    lse, mixed, cosine, sine = refs[8:12]
    outs = refs[12:16]
    query, query_flat, key, key_flat, value_flat, grad, grad_flat, sum_key, sum_value, sum_query = (
        refs[16:]
    )
    for member in range(4):
        for frame in range(4):
            slot = 4 * (meta[0] ^ member) + (meta[1] ^ frame)
            cols = slice(256 * frame, 256 * frame + 256)
            place = pl.ds(pl.multiple_of((slot % 2) * 256, 256), 256)
            part = blocks[member][0:64, cols] * 0.125
            query[slot // 2, :, place] = part
            query_flat[slot // 2, place, :] = turn(part)
            part = blocks[member][64:128, cols]
            key[slot] = part
            key_flat[slot] = turn(part)
            value_flat[slot] = turn(blocks[member][128:192, cols])
            part = grads[member][:, cols]
            grad[slot // 2, :, place] = part
            grad_flat[slot // 2, place, :] = turn(part)
    sum_key[...] = jnp.zeros_like(sum_key)
    sum_value[...] = jnp.zeros_like(sum_value)

    def per_pair(pair, carry):
        low, since, upto = query_rows(meta, pair)
        wanted = query[pair]
        wanted_grad = grad[pair]
        delta = jnp.sum(wanted_grad.astype(jnp.float32) * mixed[pair], axis=0, keepdims=True)
        level = lse[pair]

        def per_key(slot, acc):
            bias = jnp.where((slot >= since) & (slot <= upto), -level, neg_large)
            scores = jnp.dot(key_flat[slot], wanted, preferred_element_type=jnp.float32)
            probs = jnp.exp(scores + bias)
            grad_probs = jnp.dot(
                value_flat[slot], wanted_grad, preferred_element_type=jnp.float32
            )
            grad_scores = (probs * (grad_probs - delta)).astype(jnp.bfloat16)
            sum_value[slot] += jnp.dot(
                probs.astype(jnp.bfloat16), grad_flat[pair], preferred_element_type=jnp.float32
            )
            sum_key[slot] += jnp.dot(
                grad_scores, query_flat[pair], preferred_element_type=jnp.float32
            )
            return acc + jnp.dot(key[slot], grad_scores, preferred_element_type=jnp.float32)

        sum_query[pair] = lax.fori_loop(
            low, 2 * pair + 2, per_key, jnp.zeros((HD, 2 * PATCHES), jnp.float32)
        )
        return carry

    lax.fori_loop(0, 8, per_pair, 0)
    for member in range(4):
        for frame in range(4):
            slot = 4 * (meta[0] ^ member) + (meta[1] ^ frame)
            cols = slice(256 * frame, 256 * frame + 256)
            place = pl.ds(pl.multiple_of((slot % 2) * 256, 256), 256)
            cos_now = cosine[slot]
            sin_now = sine[slot]
            for base, part in (
                (0, sum_query[slot // 2, :, place] * 0.125),
                (64, sum_key[slot].T),
            ):
                upper = part[0:32]
                lower = part[32:64]
                outs[member][base : base + 32, cols] = (
                    upper * cos_now + lower * sin_now
                ).astype(jnp.bfloat16)
                outs[member][base + 32 : base + 64, cols] = (
                    lower * cos_now - upper * sin_now
                ).astype(jnp.bfloat16)
            outs[member][128:192, cols] = sum_value[slot].T.astype(jnp.bfloat16)


def call_attend_back(meta, blocks, grads, lse, mixed, cosine, sine):
    vmem = pl.BlockSpec(memory_space=pltpu.VMEM)
    flat_pair = pltpu.VMEM((8, 2 * PATCHES, HD), jnp.bfloat16)
    turned_pair = pltpu.VMEM((8, HD, 2 * PATCHES), jnp.bfloat16)
    flat = pltpu.VMEM((16, PATCHES, HD), jnp.bfloat16)
    wide = pltpu.VMEM((16, PATCHES, HD), jnp.float32)
    return list(
        pl.pallas_call(
            attend_back_kernel,
            out_shape=tuple(
                jax.ShapeDtypeStruct((192, 4 * PATCHES), jnp.bfloat16) for _ in range(4)
            ),
            in_specs=[pl.BlockSpec(memory_space=pltpu.SMEM)] + [vmem] * 12,
            out_specs=(vmem,) * 4,
            scratch_shapes=[
                turned_pair,
                flat_pair,
                pltpu.VMEM((16, HD, PATCHES), jnp.bfloat16),
                flat,
                flat,
                turned_pair,
                flat_pair,
                wide,
                wide,
                pltpu.VMEM((8, HD, 2 * PATCHES), jnp.float32),
            ],
            compiler_params=pltpu.CompilerParams(vmem_limit_bytes=48 * 2**20),
            cost_estimate=pl.CostEstimate(
                flops=22 * 10**9, bytes_accessed=10**7, transcendentals=10**7
            ),
            name="attend_back",
        )(meta, *blocks, *grads, lse, mixed, cosine, sine)
    )


def assemble_kernel(meta, *refs):
    for place in range(8):
        refs[8][:, pl.ds(pl.multiple_of(meta[place] * 128, 128), 128)] = refs[place][...]


def assemble(meta, shard_list):
    vmem = pl.BlockSpec(memory_space=pltpu.VMEM)
    rows = shard_list[0].shape[0]
    return pl.pallas_call(
        assemble_kernel,
        out_shape=jax.ShapeDtypeStruct((rows, 8 * 128), shard_list[0].dtype),
        in_specs=[pl.BlockSpec(memory_space=pltpu.SMEM)] + [vmem] * 8,
        out_specs=vmem,
        name="assemble",
    )(meta, *shard_list)


def place_frames(lengths, order, levels):
    frames = levels.shape[0]
    ids = jnp.arange(frames, dtype=jnp.int32)
    ends = jnp.cumsum(lengths)
    begins = ends - lengths
    inside = (ids[:, None] >= begins[None, :]) & (ids[:, None] < ends[None, :])
    start = jnp.sum(jnp.where(inside, begins[None, :], 0), axis=1)
    is_long = jnp.sum(jnp.where(inside, lengths[None, :], 0), axis=1) == frames // 2
    before = ids[None, :] < ids[:, None]
    same = is_long[None, :] == is_long[:, None]
    slot = jnp.sum((before & same).astype(jnp.int32), axis=1) + jnp.where(is_long, 0, frames // 2)
    stretches = order.shape[0]
    per_stretch = frames // stretches
    held = order[None, :] == (ids // per_stretch)[:, None]
    stored = (
        jnp.sum(jnp.where(held, jnp.arange(stretches, dtype=jnp.int32)[None, :], 0), axis=1)
        * per_stretch
        + ids % per_stretch
    )
    table = jnp.stack([stored, ids - start, levels])
    hit = slot[None, :] == ids[:, None]
    return jnp.sum(jnp.where(hit[None], table[:, None, :], 0), axis=2)


def shards_halves(
    clean,
    noise,
    levels,
    lengths,
    order,
    step,
    w_attn,
    m_attn,
    v_attn,
    w_mlp,
    m_mlp,
    v_mlp,
    w_mod,
    m_mod,
    v_mod,
    w_io,
    m_io,
    v_io,
    vectors,
    m_vec,
    v_vec,
):
    bfloat = jnp.bfloat16
    single = jnp.float32
    ctx_index = lax.axis_index("ctx")
    tp_index = lax.axis_index("tp")
    member = ctx_index % 4
    feat_dim = clean.shape[1]
    offsets = ring_offsets(ctx_index)
    relative = [tp_index ^ k for k in range(4)]

    both = jnp.stack([clean.reshape(4, 4, 64, feat_dim), noise.reshape(4, 4, 64, feat_dim)], axis=1)
    quarter = lax.dynamic_index_in_dim(both, tp_index, 2, keepdims=False)
    token_ring = ring_gather(quarter.reshape(4 * 128, feat_dim))
    front_shard = jnp.concatenate(
        [
            jnp.transpose(w_attn[:3].reshape(3, 128, 4, HD), (2, 0, 3, 1)).reshape(QKV_ROWS, 128),
            w_io[0],
            vectors,
            jnp.zeros((8, 128), single),
        ],
        axis=0,
    ).astype(bfloat)
    front_ring = ring_gather(front_shard)

    table = place_frames(lengths, order, levels)
    stored, position, slot_levels = table[0], table[1], table[2]
    half_base = (ctx_index // 4) * HALF_SLOTS
    half_position = lax.dynamic_slice_in_dim(position, half_base, HALF_SLOTS, 0)
    own_levels = lax.dynamic_slice_in_dim(slot_levels, 4 * ctx_index, 4, 0)
    own_levels = jnp.stack(
        [lax.dynamic_index_in_dim(own_levels, r, 0, keepdims=False) for r in relative]
    )
    own_stored = lax.dynamic_slice_in_dim(stored, 4 * ctx_index, 4, 0)
    gathered = jnp.stack(token_ring).reshape(8 * 4, 128, feat_dim)
    my_place = ring_position(ctx_index)
    picked = []
    for frame in relative:
        at = lax.dynamic_index_in_dim(own_stored, frame, 0, keepdims=False)
        distance = (ring_position(at // 4) - my_place) % 8
        index = jnp.where(distance <= 4, distance + 3, 8 - distance)
        index = jnp.where(distance == 0, 0, index)
        picked.append(
            lax.dynamic_index_in_dim(gathered, index * 4 + at % 4, 0, keepdims=False)
        )
    quarters = spread_frames(jnp.stack(picked))
    by_source = [
        jnp.stack([quarters[b][k ^ b] for k in range(4)]).reshape(4, 2, 64, feat_dim)
        for b in range(4)
    ]
    pieces = reorder_four(by_source, tp_index)
    tokens = jnp.concatenate(pieces, axis=2)

    rows_of = jnp.concatenate(
        [
            slot_levels,
            jnp.stack(
                [
                    lax.dynamic_index_in_dim(
                        slot_levels, 4 * (ctx_index ^ a) + (tp_index ^ b), 0, keepdims=False
                    )
                    for a in range(8)
                    for b in range(4)
                ]
            ),
        ]
    )
    half_dim = D // 2
    column = ctx_index * 128 + jnp.arange(128, dtype=jnp.int32)
    frequency = jnp.exp(
        -math.log(10000.0) * (column % half_dim).astype(single) / half_dim
    )
    angle = rows_of.astype(single)[:, None] * frequency[None, :]
    cond = jax.nn.silu(jnp.where(column[None, :] < half_dim, jnp.cos(angle), jnp.sin(angle)))
    cond_low = cond.astype(bfloat)
    cond_slots, cond_relative = cond_low[:32], cond_low[32:]
    quarter_cols = 6 * D // 4
    mod_cols = lax.dynamic_slice_in_dim(w_mod, tp_index * quarter_cols, quarter_cols, 1)
    mod_part = jnp.dot(cond_slots, mod_cols.astype(bfloat), preferred_element_type=single)
    mod_own = reduce_blocks(mod_part.reshape(8, 4, quarter_cols), ctx_index, single)
    mod_quarters = reorder_four(spread_frames(mod_own), tp_index)
    mod_all = jnp.concatenate(mod_quarters, axis=1)
    mod_rel = jnp.stack(reorder_four([mod_all[k] for k in range(4)], tp_index))
    mod_rel = mod_rel.reshape(4, 6, D)

    time_pairs = HD // 8
    side_pairs = (HD // 2 - time_pairs) // 2

    def frequencies(count):
        return 10000.0 ** (-jnp.arange(count, dtype=single) / count)

    patch = jnp.arange(PATCHES, dtype=jnp.int32)
    time_angle = half_position.astype(single)[:, None] * frequencies(time_pairs)[None, :]
    height_angle = frequencies(side_pairs)[:, None] * (patch // GRID).astype(single)[None, :]
    width_angle = frequencies(side_pairs)[:, None] * (patch % GRID).astype(single)[None, :]
    side_angle = jnp.concatenate([height_angle, width_angle], axis=0)

    def full_table(time_part, side_part):
        return jnp.concatenate(
            [
                jnp.broadcast_to(time_part[:, :, None], (HALF_SLOTS, time_pairs, PATCHES)),
                jnp.broadcast_to(side_part[None], (HALF_SLOTS, 2 * side_pairs, PATCHES)),
            ],
            axis=1,
        )

    cosine = full_table(jnp.cos(time_angle), jnp.cos(side_angle))
    sine = full_table(jnp.sin(time_angle), jnp.sin(side_angle))

    signal_scale, noise_scale, weight = plan(own_levels)
    clean_full = tokens[:, 0].astype(single)
    noise_full = tokens[:, 1].astype(single)
    noisy_low = (
        signal_scale[:, None, None] * clean_full + noise_scale[:, None, None] * noise_full
    ).astype(bfloat)
    target = signal_scale[0] * noise_full[0] - noise_scale[0] * clean_full[0]
    all_weight = plan(levels)[2]
    weight_sum = PATCHES * jnp.sum(all_weight)

    front_meta = jnp.stack(
        offsets + [4 * member + r for r in relative] + [member ^ k for k in range(4)]
    ).astype(jnp.int32)
    front_all, hidden_frames, resid_in, head_blocks = call_front(
        front_meta, front_ring, noisy_low, mod_rel[:, :2], cosine, sine
    )
    hidden_one = hidden_frames.reshape(4 * PATCHES, D)
    qkv_w = front_all[:QKV_ROWS]
    vec_w = front_all[QKV_ROWS + 128 : QKV_ROWS + 136].astype(single)
    mod_own_frame = mod_rel[0] + vec_w[:6]
    shift_one, scale_one, gate_one, shift_two, scale_two, gate_two = (
        mod_own_frame[k : k + 1] for k in range(6)
    )

    mid_shard = jnp.concatenate([jnp.transpose(w_attn[3]), w_io[1]], axis=0).astype(bfloat)
    mid_shard, front_all = lax.optimization_barrier((mid_shard, front_all))
    mid_all = assemble(jnp.stack(offsets).astype(jnp.int32), ring_gather(mid_shard))
    out_w, head_w = mid_all[:256], mid_all[256:]
    mlp_w = lax.all_gather(w_mlp.astype(bfloat), "ctx", axis=1, tiled=True)
    up_w, down_w = mlp_w[0], mlp_w[1]

    def exchange(blocks):
        return [blocks[0]] + [swap(blocks[k], "ctx", k) for k in (1, 2, 3)]

    attend_meta = jnp.concatenate([jnp.stack([member, tp_index]), half_position]).astype(jnp.int32)
    head_in = exchange([head_blocks[k] for k in range(4)])
    mixed_blocks, lse, mixed = call_attend(attend_meta, head_in)
    mix_low = jnp.concatenate(reorder_four(exchange(mixed_blocks), member), axis=0)

    attn_part = lax.dot_general(mix_low, out_w, TN, preferred_element_type=single)
    attn_out = sum_frames(attn_part.reshape(4, PATCHES, D))
    resid_mid = resid_in + gate_one * attn_out
    normed_two, inv_two = layer_norm(resid_mid)
    hidden_own = (normed_two * (1.0 + scale_two) + shift_two).astype(bfloat)
    hidden_two = jnp.concatenate(spread_frames(hidden_own), axis=0)
    upward = jnp.dot(hidden_two, up_w, preferred_element_type=single)
    activ_low = jax.nn.gelu(upward, approximate=False).astype(bfloat)
    mlp_part = lax.dot_general(activ_low, down_w, NT, preferred_element_type=single)
    mlp_out = sum_frames(mlp_part.reshape(4, PATCHES, D))
    resid_out = resid_mid + gate_two * mlp_out
    normed_three, inv_three = layer_norm(resid_out)
    gain = vec_w[7:8]
    final_low = (normed_three * gain).astype(bfloat)
    pred = lax.dot_general(final_low, head_w, NT, preferred_element_type=single)
    diff = pred - target
    error_part = weight[0] * jnp.sum(jnp.mean(diff * diff, axis=1))
    grad_pred = (2.0 / feat_dim * weight[0] * diff / weight_sum).astype(bfloat)
    grad_head = lax.dot_general(grad_pred, final_low, TN, preferred_element_type=single)
    grad_final = jnp.dot(grad_pred, head_w, preferred_element_type=single)
    grad_gain = jnp.sum(grad_final * normed_three, axis=0)
    grad_three = norm_back(grad_final * gain, normed_three, inv_three)
    grad_gate_two = jnp.sum(grad_three * mlp_out, axis=0)
    grad_mlp_low = jnp.concatenate(spread_frames((gate_two * grad_three).astype(bfloat)), axis=0)

    grad_activ = jnp.dot(grad_mlp_low, down_w, preferred_element_type=single)
    grad_up_low = (grad_activ * gelu_slope(upward)).astype(bfloat)
    hidden_part = lax.dot_general(grad_up_low, up_w, NT, preferred_element_type=single)
    grad_hidden_two = sum_frames(hidden_part.reshape(4, PATCHES, D))
    grad_down = lax.dot_general(grad_mlp_low, activ_low, TN, preferred_element_type=single)
    grad_up = lax.dot_general(hidden_two, grad_up_low, TN, preferred_element_type=single)
    red_mlp = lax.psum_scatter(
        jnp.stack([grad_up, grad_down]).astype(bfloat), "ctx", scatter_dimension=1, tiled=True
    ).astype(single)

    grad_shift_two = jnp.sum(grad_hidden_two, axis=0)
    grad_scale_two = jnp.sum(grad_hidden_two * normed_two, axis=0)
    grad_mid = grad_three + norm_back(grad_hidden_two * (1.0 + scale_two), normed_two, inv_two)
    grad_gate_one = jnp.sum(grad_mid * attn_out, axis=0)
    grad_attn_low = jnp.concatenate(spread_frames((gate_one * grad_mid).astype(bfloat)), axis=0)

    grad_mix = lax.dot_general(out_w, grad_attn_low, NT, preferred_element_type=single).astype(
        bfloat
    )
    grad_blocks = reorder_four([grad_mix[HD * k : HD * k + HD] for k in range(4)], member)
    grad_in_blocks = exchange(grad_blocks)
    grad_outproj = jnp.dot(mix_low, grad_attn_low, preferred_element_type=single)
    back_blocks = call_attend_back(
        attend_meta, head_in, grad_in_blocks, lse, mixed, cosine, sine
    )
    grad_qkv = jnp.concatenate(reorder_four(exchange(back_blocks), member), axis=0)

    hidden_part = lax.dot_general(grad_qkv, qkv_w, TN, preferred_element_type=single)
    grad_hidden_one = sum_frames(hidden_part.reshape(4, PATCHES, D))
    grad_qkv_w = jnp.dot(grad_qkv, hidden_one, preferred_element_type=single)

    def lane_blocks(values):
        return jnp.transpose(values.reshape(values.shape[0], 8, 128), (1, 0, 2))

    red_out = reduce_blocks(lane_blocks(grad_outproj), ctx_index, bfloat)
    red_qkv = reduce_blocks(lane_blocks(grad_qkv_w), ctx_index, bfloat)
    red_attn = jnp.concatenate(
        [
            jnp.transpose(red_qkv.reshape(4, 3, HD, 128), (1, 3, 0, 2)).reshape(3, 128, 256),
            jnp.transpose(red_out)[None],
        ],
        axis=0,
    )

    grad_shift_one = jnp.sum(grad_hidden_one, axis=0)
    normed_one, inv_one = layer_norm(resid_in)
    grad_scale_one = jnp.sum(grad_hidden_one * normed_one, axis=0)
    grad_in = grad_mid + norm_back(grad_hidden_one * (1.0 + scale_one), normed_one, inv_one)
    grad_in_low = grad_in.astype(bfloat)
    grad_embed = lax.dot_general(noisy_low[0], grad_in_low, TN, preferred_element_type=single)
    grad_mod = jnp.stack(
        [
            grad_shift_one,
            grad_scale_one,
            grad_gate_one,
            grad_shift_two,
            grad_scale_two,
            grad_gate_two,
        ]
    ).astype(bfloat)
    mod_rows = jnp.stack(spread_frames(grad_mod))
    for bit in (1, 2, 4):
        mod_rows = jnp.concatenate([mod_rows, swap(mod_rows, "ctx", bit)], axis=0)
    grad_mod_w = lax.dot_general(
        cond_relative, mod_rows.reshape(32, 6 * D), TN, preferred_element_type=single
    )
    mod_cols = lax.dynamic_slice_in_dim(mod_rows, ctx_index * 128, 128, 2)
    grad_mod_vec = jnp.sum(mod_cols.astype(single), axis=0)

    def reduce_io(weight_grad, vector_grad):
        rows = jnp.concatenate([weight_grad, vector_grad[None], jnp.zeros((15, D), single)], axis=0)
        total = reduce_blocks(lane_blocks(rows), ctx_index, bfloat)
        for bit in (1, 2):
            total = total + swap(total, "tp", bit)
        return total[:128], total[128:129]

    red_head, red_gain = reduce_io(grad_head, grad_gain)
    red_embed, red_bias = reduce_io(grad_embed, jnp.sum(grad_in, axis=0))
    red_io = jnp.stack([red_embed, red_head])
    red_vec = jnp.concatenate([grad_mod_vec, red_bias, red_gain], axis=0)

    shared_sq = (
        jnp.sum(grad_mod_w * grad_mod_w) + jnp.sum(red_io * red_io) + jnp.sum(red_vec * red_vec)
    )
    own_sq = (
        jnp.sum(red_attn * red_attn)
        + jnp.sum(red_mlp * red_mlp)
        + jnp.where(tp_index == 0, shared_sq, 0.0)
    )
    sums = sum_all(
        jnp.where(jnp.arange(128) < 64, own_sq, error_part).reshape(1, 128)
    )
    loss_value = sums[0, 64] / weight_sum
    grad_norm = jnp.sqrt(sums[0, 0])
    factor = jnp.minimum(1.0, clip_limit / (grad_norm + 1e-06))
    count = step[0].astype(single)
    attn_new = adam(w_attn, m_attn, v_attn, red_attn, factor, count, rate_matrix, decay_rate)
    mlp_new = adam(w_mlp, m_mlp, v_mlp, red_mlp, factor, count, rate_matrix, decay_rate)
    mod_new = adam(w_mod, m_mod, v_mod, grad_mod_w, factor, count, rate_matrix, decay_rate)
    io_new = adam(w_io, m_io, v_io, red_io, factor, count, rate_matrix, decay_rate)
    vec_new = adam(vectors, m_vec, v_vec, red_vec, factor, count, rate_vector, 0.0)
    return (
        (loss_value, grad_norm)
        + attn_new
        + mlp_new
        + mod_new
        + (io_new[0], io_new[1], io_new[2][0], io_new[2][1], io_new[3])
        + vec_new
    )


def solution(mesh):
    halves = mesh.shape["ctx"] == 8 and mesh.shape["tp"] == 4
    placed = (
        P("ctx", None),
        P("ctx", None),
        P(),
        P(),
        P(),
        P(),
        P(None, "ctx", "tp"),
        P(None, "ctx", "tp"),
        P(None, "ctx", "tp"),
        P(None, "ctx", "tp"),
        P(None, "ctx", "tp"),
        P(None, "ctx", "tp"),
        P("ctx", None),
        P("ctx", None),
        P("ctx", None),
        P(None, None, "ctx"),
        P(None, None, "ctx"),
        P(None, None, "ctx"),
        P(None, "ctx"),
        P(None, "ctx"),
        P(None, "ctx"),
    )
    return jax.shard_map(
        shards_halves if halves else shards,
        mesh=mesh,
        in_specs=placed,
        out_specs=(
            P(),
            P(),
            P(None, "ctx", "tp"),
            P(None, "ctx", "tp"),
            P(None, "ctx", "tp"),
            P(None, "ctx", "tp"),
            P(None, "ctx", "tp"),
            P(None, "ctx", "tp"),
            P(None, "ctx", "tp"),
            P(None, "ctx", "tp"),
            P("ctx", None),
            P("ctx", None),
            P("ctx", None),
            P("ctx", None),
            P(None, None, "ctx"),
            P(None, None, "ctx"),
            P(None, "ctx"),
            P(None, "ctx"),
            P(None, None, "ctx"),
            P(None, "ctx"),
            P(None, "ctx"),
            P(None, "ctx"),
            P(None, "ctx"),
        ),
        check_vma=False,
    )
```

```python
import functools
import math

import jax
import jax.numpy as jnp
from jax import lax
from jax.experimental import pallas as pl
from jax.experimental.pallas import tpu as pltpu
from jax.sharding import PartitionSpec as P

D = 1024
HD = 64
GRID = 16
PATCHES = 256
LEVELS = 1000


ln_eps = 1e-06
snr_limit = 5.0
clip_limit = 0.001
beta_one = 0.9
beta_two = 0.999
adam_eps = 1e-08
rate_matrix = 0.05
rate_vector = 0.3
decay_rate = 0.1
neg_large = -1e30


def clip_starts(frame_ids, lengths):
    clip_ends = jnp.cumsum(lengths)
    before = (clip_ends[None, :] <= frame_ids[:, None]).astype(jnp.int32)
    return jnp.sum(before * lengths[None, :], axis=1)


def plan(levels):
    fraction = (levels.astype(jnp.float32) + 1.0) / (LEVELS + 1.0)
    signal_scale = jnp.cos(0.5 * math.pi * fraction)
    noise_scale = jnp.sin(0.5 * math.pi * fraction)
    snr_value = signal_scale * signal_scale / (noise_scale * noise_scale)
    weight = jnp.minimum(snr_value, snr_limit) / (snr_value + 1.0)
    return (signal_scale, noise_scale, weight)


def condition(levels, width):
    half_dim = width // 2
    frequency = jnp.exp(-math.log(10000.0) * jnp.arange(half_dim, dtype=jnp.float32) / half_dim)
    angle_tab = levels.astype(jnp.float32)[:, None] * frequency[None, :]
    return jax.nn.silu(jnp.concatenate([jnp.cos(angle_tab), jnp.sin(angle_tab)], axis=1))


def rope_tables(time_pos, height_pos, width_pos, head_dim):
    pair_count = head_dim // 2
    time_pairs = head_dim // 8
    height_pairs = (pair_count - time_pairs) // 2
    width_pairs = pair_count - time_pairs - height_pairs

    def angles(position, count):
        frequency = 10000.0 ** (-jnp.arange(count, dtype=jnp.float32) / count)
        return position.astype(jnp.float32)[:, None] * frequency[None, :]

    angle_tab = jnp.concatenate(
        [
            angles(time_pos, time_pairs),
            angles(height_pos, height_pairs),
            angles(width_pos, width_pairs),
        ],
        axis=1,
    )
    return (jnp.cos(angle_tab), jnp.sin(angle_tab))


def rotate(values, cosine, sine):
    half_dim = values.shape[-1] // 2
    first_half = values[..., :half_dim]
    second_half = values[..., half_dim:]
    cosine = cosine[:, None, :]
    sine = sine[:, None, :]
    return jnp.concatenate(
        [first_half * cosine - second_half * sine, second_half * cosine + first_half * sine],
        axis=-1,
    )


def rotate_back(grads, cosine, sine):
    half_dim = grads.shape[-1] // 2
    first_half = grads[..., :half_dim]
    second_half = grads[..., half_dim:]
    cosine = cosine[:, None, :]
    sine = sine[:, None, :]
    return jnp.concatenate(
        [first_half * cosine + second_half * sine, second_half * cosine - first_half * sine],
        axis=-1,
    )


def layer_norm(values):
    centred = values - jnp.mean(values, axis=-1, keepdims=True)
    inv_std = lax.rsqrt(jnp.mean(centred * centred, axis=-1, keepdims=True) + ln_eps)
    return (centred * inv_std, inv_std)


def norm_back(grad_in, normed, inv_std):
    mean_grad = jnp.mean(grad_in, axis=-1, keepdims=True)
    mean_proj = jnp.mean(grad_in * normed, axis=-1, keepdims=True)
    return inv_std * (grad_in - mean_grad - normed * mean_proj)


def gelu_slope(values):
    return 0.5 * (1.0 + lax.erf(values / math.sqrt(2.0))) + values * jnp.exp(
        -0.5 * values * values
    ) / math.sqrt(2.0 * math.pi)


def stretch_mask(query_stretch, key_stretch, stretch_frames, lengths):
    offsets = jnp.arange(stretch_frames, dtype=jnp.int32)
    query_frames = query_stretch * stretch_frames + offsets
    key_frames = key_stretch * stretch_frames + offsets
    starts = clip_starts(query_frames, lengths)
    return (key_frames[None, :] <= query_frames[:, None]) & (key_frames[None, :] >= starts[:, None])


def expand_mask(allowed):
    return jnp.repeat(jnp.repeat(allowed, PATCHES, axis=0), PATCHES, axis=1)


def online_step(current, query_block, key_block, value_block, keep, scale):
    run_max, run_sum, run_acc = current
    scores = (
        jnp.einsum("qhe,khe->hqk", query_block, key_block, preferred_element_type=jnp.float32)
        * scale
    )
    scores = jnp.where(keep[None], scores, neg_large)
    new_max = jnp.maximum(run_max, jnp.max(scores, axis=-1))
    probs = jnp.where(keep[None], jnp.exp(scores - new_max[..., None]), 0.0)
    shrink = jnp.exp(run_max - new_max)
    run_sum = run_sum * shrink + jnp.sum(probs, axis=-1)
    added = jnp.einsum(
        "hqk,khe->qhe", probs.astype(jnp.bfloat16), value_block, preferred_element_type=jnp.float32
    )
    run_acc = run_acc * jnp.transpose(shrink)[:, :, None] + added
    return (new_max, run_sum, run_acc)


def pair_grads(
    query_block, grad_block, lse_block, delta_block, key_block, value_block, keep, scale
):
    scores = (
        jnp.einsum("qhe,khe->hqk", query_block, key_block, preferred_element_type=jnp.float32)
        * scale
    )
    probs = jnp.where(keep[None], jnp.exp(scores - lse_block[..., None]), 0.0)
    grad_probs = jnp.einsum(
        "qhe,khe->hqk", grad_block, value_block, preferred_element_type=jnp.float32
    )
    grad_scores = (probs * (grad_probs - delta_block[..., None])).astype(jnp.bfloat16)
    grad_query = (
        jnp.einsum("hqk,khe->qhe", grad_scores, key_block, preferred_element_type=jnp.float32)
        * scale
    )
    grad_key = (
        jnp.einsum("hqk,qhe->khe", grad_scores, query_block, preferred_element_type=jnp.float32)
        * scale
    )
    grad_value = jnp.einsum(
        "hqk,qhe->khe", probs.astype(jnp.bfloat16), grad_block, preferred_element_type=jnp.float32
    )
    return (grad_query, grad_key, grad_value)


def adam(weight_now, first_mom, second_mom, grad, factor, count, rate, decay):
    grad = grad * factor
    first_mom = beta_one * first_mom + (1.0 - beta_one) * grad
    second_mom = beta_two * second_mom + (1.0 - beta_two) * grad * grad
    first_hat = first_mom / (1.0 - beta_one**count)
    second_hat = second_mom / (1.0 - beta_two**count)
    updated = weight_now - rate * (
        first_hat / (jnp.sqrt(second_hat) + adam_eps) + decay * weight_now
    )
    return (updated, first_mom, second_mom, updated.astype(jnp.bfloat16))


def shards(
    clean,
    noise,
    levels,
    lengths,
    order,
    step,
    w_attn,
    m_attn,
    v_attn,
    w_mlp,
    m_mlp,
    v_mlp,
    w_mod,
    m_mod,
    v_mod,
    w_io,
    m_io,
    v_io,
    vectors,
    m_vec,
    v_vec,
):
    ctx_count = lax.axis_size("ctx")
    ctx_index = lax.axis_index("ctx")
    tp_index = lax.axis_index("tp")
    tok_rows = clean.shape[0]
    feat_dim = clean.shape[1]
    frames_dev = tok_rows // PATCHES
    stretch_frames = frames_dev // 2
    stretch_rows = stretch_frames * PATCHES
    scale = HD ** (-0.5)
    bfloat = jnp.bfloat16
    single = jnp.float32
    attn_w, mlp_w, mod_w, io_w, vec_low = (
        lax.all_gather(w_attn.astype(bfloat), "ctx", axis=1, tiled=True),
        lax.all_gather(w_mlp.astype(bfloat), "ctx", axis=1, tiled=True),
        lax.all_gather(w_mod.astype(bfloat), "ctx", axis=0, tiled=True),
        lax.all_gather(w_io.astype(bfloat), "ctx", axis=2, tiled=True),
        lax.all_gather(vectors.astype(bfloat), "ctx", axis=1, tiled=True),
    )
    vec_w = vec_low.astype(single)
    local_width = attn_w.shape[2]
    heads_dev = local_width // HD
    frame_count = levels.shape[0]
    local_stretches = lax.dynamic_slice_in_dim(order, 2 * ctx_index, 2, 0)
    frame_ids = (
        local_stretches[:, None] * stretch_frames
        + jnp.arange(stretch_frames, dtype=jnp.int32)[None, :]
    ).reshape(frames_dev)
    table_hit = frame_ids[:, None] == jnp.arange(frame_count, dtype=jnp.int32)[None, :]
    frame_levels = jnp.sum(jnp.where(table_hit, levels[None, :], 0), axis=1)
    starts = clip_starts(frame_ids, lengths)
    signal_scale, noise_scale, weight = plan(frame_levels)
    signal_col = signal_scale[:, None, None]
    noise_col = noise_scale[:, None, None]
    clean_full = clean.astype(single).reshape(frames_dev, PATCHES, feat_dim)
    noise_full = noise.astype(single).reshape(frames_dev, PATCHES, feat_dim)
    noisy = signal_col * clean_full + noise_col * noise_full
    target = signal_col * noise_full - noise_col * clean_full
    noisy_low = noisy.reshape(tok_rows, feat_dim).astype(bfloat)
    embedded = jnp.dot(noisy_low, io_w[0], preferred_element_type=single) + vec_w[6]
    cond_low = condition(frame_levels, D).astype(bfloat)
    modulate = (
        jnp.dot(cond_low, mod_w, preferred_element_type=single) + vec_w[:6].reshape(6 * D)
    ).reshape(frames_dev, 6, 1, D)
    patch_ids = jnp.arange(PATCHES, dtype=jnp.int32)
    time_pos = jnp.repeat(frame_ids - starts, PATCHES)
    height_pos = jnp.tile(patch_ids // GRID, frames_dev)
    width_pos = jnp.tile(patch_ids % GRID, frames_dev)
    cosine, sine = rope_tables(time_pos, height_pos, width_pos, HD)
    resid_in = embedded.reshape(frames_dev, PATCHES, D)
    normed_one, inv_one = layer_norm(resid_in)
    hidden_one = (
        (normed_one * (1.0 + modulate[:, 1]) + modulate[:, 0]).reshape(tok_rows, D).astype(bfloat)
    )
    query_pre = jnp.dot(hidden_one, attn_w[0], preferred_element_type=single).reshape(
        tok_rows, heads_dev, HD
    )
    key_pre = jnp.dot(hidden_one, attn_w[1], preferred_element_type=single).reshape(
        tok_rows, heads_dev, HD
    )
    query_low = rotate(query_pre, cosine, sine).astype(bfloat)
    key_low = rotate(key_pre, cosine, sine).astype(bfloat)
    value_low = (
        jnp.dot(hidden_one, attn_w[2], preferred_element_type=single)
        .astype(bfloat)
        .reshape(tok_rows, heads_dev, HD)
    )
    query_stretches = query_low.reshape(2, stretch_rows, heads_dev, HD)
    init_state = (
        jnp.full((2, heads_dev, stretch_rows), neg_large, single),
        jnp.zeros((2, heads_dev, stretch_rows), single),
        jnp.zeros((2, stretch_rows, heads_dev, HD), single),
    )
    key_flat = key_low.reshape(tok_rows, local_width)
    value_flat = value_low.reshape(tok_rows, local_width)
    carry_state = init_state
    key_piece = lax.all_gather(key_flat, "ctx", axis=0, tiled=True)
    value_piece = lax.all_gather(value_flat, "ctx", axis=0, tiled=True)

    def per_stretch(block_num, carry_state):
        key_block = lax.dynamic_slice_in_dim(
            key_piece, block_num * stretch_rows, stretch_rows, 0
        ).reshape(stretch_rows, heads_dev, HD)
        value_block = lax.dynamic_slice_in_dim(
            value_piece, block_num * stretch_rows, stretch_rows, 0
        ).reshape(stretch_rows, heads_dev, HD)
        key_stretch = lax.dynamic_index_in_dim(order, block_num, 0, keepdims=False)
        updated = []
        for half_num in range(2):
            allowed = stretch_mask(local_stretches[half_num], key_stretch, stretch_frames, lengths)
            current = (carry_state[0][half_num], carry_state[1][half_num], carry_state[2][half_num])
            current = lax.cond(
                jnp.any(allowed),
                lambda cur, keep_mask: online_step(
                    cur,
                    query_stretches[half_num],
                    key_block,
                    value_block,
                    expand_mask(keep_mask),
                    scale,
                ),
                lambda cur, keep_mask: cur,
                current,
                allowed,
            )
            updated.append(current)
        return tuple((jnp.stack([updated[0][member], updated[1][member]]) for member in range(3)))

    run_max, run_sum, run_acc = lax.fori_loop(
        0, key_piece.shape[0] // stretch_rows, per_stretch, carry_state
    )
    mix_rows = (run_acc / jnp.transpose(run_sum, (0, 2, 1))[..., None]).reshape(
        tok_rows, heads_dev, HD
    )
    lse_stretches = run_max + jnp.log(run_sum)
    mix_low = mix_rows.reshape(tok_rows, local_width).astype(bfloat)
    attn_out = lax.psum(
        jnp.einsum("rh,dh->rd", mix_low, attn_w[3], preferred_element_type=single).astype(
            jnp.bfloat16
        ),
        "tp",
    ).astype(jnp.float32)
    attn_full = attn_out.reshape(frames_dev, PATCHES, D)
    resid_mid = resid_in + modulate[:, 2] * attn_full
    normed_two, inv_two = layer_norm(resid_mid)
    hidden_two = (
        (normed_two * (1.0 + modulate[:, 4]) + modulate[:, 3]).reshape(tok_rows, D).astype(bfloat)
    )
    upward = jnp.dot(hidden_two, mlp_w[0], preferred_element_type=single)
    activ_low = jax.nn.gelu(upward, approximate=False).astype(bfloat)
    mlp_out = lax.psum(
        jnp.einsum("rf,df->rd", activ_low, mlp_w[1], preferred_element_type=single).astype(
            jnp.bfloat16
        ),
        "tp",
    ).astype(jnp.float32)
    mlp_full = mlp_out.reshape(frames_dev, PATCHES, D)
    resid_out = resid_mid + modulate[:, 5] * mlp_full
    normed_three, inv_three = layer_norm(resid_out)
    final_low = (normed_three * vec_w[7]).reshape(tok_rows, D).astype(bfloat)
    pred = jnp.einsum("rd,pd->rp", final_low, io_w[1], preferred_element_type=single)
    diff = pred.reshape(frames_dev, PATCHES, feat_dim) - target
    error = jnp.mean(diff * diff, axis=2)
    weight_sum, error_sum = lax.psum(
        (PATCHES * jnp.sum(weight), jnp.sum(weight[:, None] * error)), "ctx"
    )
    loss_value = error_sum / weight_sum
    grad_pred = (
        (2.0 / feat_dim * weight[:, None, None] * diff / weight_sum)
        .reshape(tok_rows, feat_dim)
        .astype(bfloat)
    )
    grad_head = jnp.einsum("rp,rd->pd", grad_pred, final_low, preferred_element_type=single)
    grad_final = jnp.einsum("rp,pd->rd", grad_pred, io_w[1], preferred_element_type=single).reshape(
        frames_dev, PATCHES, D
    )
    grad_gain = jnp.sum(grad_final * normed_three, axis=(0, 1))
    grad_three = norm_back(grad_final * vec_w[7], normed_three, inv_three)
    grad_mlp_low = (modulate[:, 5] * grad_three).reshape(tok_rows, D).astype(bfloat)
    grad_gate_two = jnp.sum(grad_three * mlp_full, axis=1)
    grad_activ = jnp.einsum("rd,df->rf", grad_mlp_low, mlp_w[1], preferred_element_type=single)
    grad_down = jnp.einsum("rd,rf->df", grad_mlp_low, activ_low, preferred_element_type=single)
    grad_up_low = (grad_activ * gelu_slope(upward)).astype(bfloat)
    grad_up = jnp.einsum("rd,rf->df", hidden_two, grad_up_low, preferred_element_type=single)
    grad_hidden_two = lax.psum(
        jnp.einsum("rf,df->rd", grad_up_low, mlp_w[0], preferred_element_type=single).astype(
            jnp.bfloat16
        ),
        "tp",
    ).astype(jnp.float32)
    grad_hidden_two = grad_hidden_two.reshape(frames_dev, PATCHES, D)
    grad_shift_two = jnp.sum(grad_hidden_two, axis=1)
    grad_scale_two = jnp.sum(grad_hidden_two * normed_two, axis=1)
    grad_mid = grad_three + norm_back(grad_hidden_two * (1.0 + modulate[:, 4]), normed_two, inv_two)
    grad_attn_low = (modulate[:, 2] * grad_mid).reshape(tok_rows, D).astype(bfloat)
    grad_gate_one = jnp.sum(grad_mid * attn_full, axis=1)
    grad_outproj = jnp.einsum("rd,rh->dh", grad_attn_low, mix_low, preferred_element_type=single)
    grad_mix_low = jnp.einsum(
        "rd,dh->rh", grad_attn_low, attn_w[3], preferred_element_type=single
    ).astype(bfloat)
    delta_rows = jnp.sum(
        grad_mix_low.astype(single).reshape(tok_rows, heads_dev, HD) * mix_rows, axis=2
    )
    grad_stretches = grad_mix_low.reshape(2, stretch_rows, heads_dev, HD)
    delta_stretches = jnp.transpose(delta_rows.reshape(2, stretch_rows, heads_dev), (0, 2, 1))

    def span_back(key_block, value_block, key_stretch, grad_query_acc):
        key_sum = jnp.zeros((stretch_rows, heads_dev, HD), single)
        value_sum = jnp.zeros((stretch_rows, heads_dev, HD), single)
        query_parts = []
        for half_num in range(2):
            allowed = stretch_mask(local_stretches[half_num], key_stretch, stretch_frames, lengths)
            result = lax.cond(
                jnp.any(allowed),
                lambda keep_mask: pair_grads(
                    query_stretches[half_num],
                    grad_stretches[half_num],
                    lse_stretches[half_num],
                    delta_stretches[half_num],
                    key_block,
                    value_block,
                    expand_mask(keep_mask),
                    scale,
                ),
                lambda keep_mask: (jnp.zeros((stretch_rows, heads_dev, HD), single),) * 3,
                allowed,
            )
            query_parts.append(grad_query_acc[half_num] + result[0])
            key_sum = key_sum + result[1]
            value_sum = value_sum + result[2]
        return (
            jnp.stack(query_parts),
            key_sum.reshape(stretch_rows, local_width),
            value_sum.reshape(stretch_rows, local_width),
        )

    init_back = (
        jnp.zeros((2, stretch_rows, heads_dev, HD), single),
        jnp.zeros((ctx_count * tok_rows, local_width), single),
        jnp.zeros((ctx_count * tok_rows, local_width), single),
    )
    carry_state = init_back
    fold_key_piece = lax.all_gather(key_flat, "ctx", axis=0, tiled=True)
    fold_value_piece = lax.all_gather(value_flat, "ctx", axis=0, tiled=True)

    def per_stretch(block_num, carry_state):
        grad_query_acc, grad_keys_all, grad_values_all = carry_state
        key_block = lax.dynamic_slice_in_dim(
            fold_key_piece, block_num * stretch_rows, stretch_rows, 0
        ).reshape(stretch_rows, heads_dev, HD)
        value_block = lax.dynamic_slice_in_dim(
            fold_value_piece, block_num * stretch_rows, stretch_rows, 0
        ).reshape(stretch_rows, heads_dev, HD)
        key_stretch = lax.dynamic_index_in_dim(order, block_num, 0, keepdims=False)
        grad_query_acc, key_sum, value_sum = span_back(
            key_block, value_block, key_stretch, grad_query_acc
        )
        place = block_num * stretch_rows
        grad_keys_all = lax.dynamic_update_slice_in_dim(grad_keys_all, key_sum, place, 0)
        grad_values_all = lax.dynamic_update_slice_in_dim(grad_values_all, value_sum, place, 0)
        return (grad_query_acc, grad_keys_all, grad_values_all)

    grad_query_acc, grad_keys_all, grad_values_all = lax.fori_loop(
        0, fold_key_piece.shape[0] // stretch_rows, per_stretch, carry_state
    )
    grad_keys, grad_values = (
        lax.psum_scatter(
            grad_keys_all.astype(jnp.bfloat16), "ctx", scatter_dimension=0, tiled=True
        ).astype(jnp.float32),
        lax.psum_scatter(
            grad_values_all.astype(jnp.bfloat16), "ctx", scatter_dimension=0, tiled=True
        ).astype(jnp.float32),
    )
    grad_query = grad_query_acc.reshape(tok_rows, local_width)
    query_back = (
        rotate_back(grad_query.reshape(tok_rows, heads_dev, HD), cosine, sine)
        .reshape(tok_rows, local_width)
        .astype(bfloat)
    )
    key_back = (
        rotate_back(grad_keys.reshape(tok_rows, heads_dev, HD), cosine, sine)
        .reshape(tok_rows, local_width)
        .astype(bfloat)
    )
    value_back = grad_values.astype(bfloat)
    grad_wq = jnp.einsum("rd,rh->dh", hidden_one, query_back, preferred_element_type=single)
    grad_wk = jnp.einsum("rd,rh->dh", hidden_one, key_back, preferred_element_type=single)
    grad_wv = jnp.einsum("rd,rh->dh", hidden_one, value_back, preferred_element_type=single)
    partial_one = (
        jnp.einsum("rh,dh->rd", query_back, attn_w[0], preferred_element_type=single)
        + jnp.einsum("rh,dh->rd", key_back, attn_w[1], preferred_element_type=single)
        + jnp.einsum("rh,dh->rd", value_back, attn_w[2], preferred_element_type=single)
    )
    grad_hidden_one = (
        lax.psum(partial_one.astype(jnp.bfloat16), "tp")
        .astype(jnp.float32)
        .reshape(frames_dev, PATCHES, D)
    )
    grad_shift_one = jnp.sum(grad_hidden_one, axis=1)
    grad_scale_one = jnp.sum(grad_hidden_one * normed_one, axis=1)
    grad_in = grad_mid + norm_back(grad_hidden_one * (1.0 + modulate[:, 1]), normed_one, inv_one)
    grad_mod = jnp.stack(
        [
            grad_shift_one,
            grad_scale_one,
            grad_gate_one,
            grad_shift_two,
            grad_scale_two,
            grad_gate_two,
        ],
        axis=1,
    )
    grad_mod_w = jnp.einsum(
        "fd,fc->dc",
        cond_low,
        grad_mod.reshape(frames_dev, 6 * D).astype(bfloat),
        preferred_element_type=single,
    )
    grad_in_low = grad_in.reshape(tok_rows, D).astype(bfloat)
    grad_embed = jnp.einsum("rp,rd->pd", noisy_low, grad_in_low, preferred_element_type=single)
    grad_vec = jnp.concatenate(
        [jnp.sum(grad_mod, axis=0), jnp.sum(grad_in, axis=(0, 1))[None], grad_gain[None]], axis=0
    )
    grad_attn = jnp.stack([grad_wq, grad_wk, grad_wv, grad_outproj])
    grad_mlp = jnp.stack([grad_up, grad_down])
    grad_io = jnp.stack([grad_embed, grad_head])
    red_attn, red_mlp, red_mod, red_io, red_vec = (
        lax.psum_scatter(
            grad_attn.astype(jnp.bfloat16), "ctx", scatter_dimension=1, tiled=True
        ).astype(jnp.float32),
        lax.psum_scatter(
            grad_mlp.astype(jnp.bfloat16), "ctx", scatter_dimension=1, tiled=True
        ).astype(jnp.float32),
        lax.psum_scatter(
            grad_mod_w.astype(jnp.bfloat16), "ctx", scatter_dimension=0, tiled=True
        ).astype(jnp.float32),
        lax.psum_scatter(
            grad_io.astype(jnp.bfloat16), "ctx", scatter_dimension=2, tiled=True
        ).astype(jnp.float32),
        lax.psum_scatter(
            grad_vec.astype(jnp.bfloat16), "ctx", scatter_dimension=1, tiled=True
        ).astype(jnp.float32),
    )
    shared_sq = jnp.sum(red_mod * red_mod) + jnp.sum(red_io * red_io) + jnp.sum(red_vec * red_vec)
    own_sq = (
        jnp.sum(red_attn * red_attn)
        + jnp.sum(red_mlp * red_mlp)
        + jnp.where(tp_index == 0, shared_sq, 0.0)
    )
    grad_norm = jnp.sqrt(lax.psum(own_sq, ("ctx", "tp")))
    factor = jnp.minimum(1.0, clip_limit / (grad_norm + 1e-06))
    count = step[0].astype(single)
    attn_new = adam(w_attn, m_attn, v_attn, red_attn, factor, count, rate_matrix, decay_rate)
    mlp_new = adam(w_mlp, m_mlp, v_mlp, red_mlp, factor, count, rate_matrix, decay_rate)
    mod_new = adam(w_mod, m_mod, v_mod, red_mod, factor, count, rate_matrix, decay_rate)
    io_new = adam(w_io, m_io, v_io, red_io, factor, count, rate_matrix, decay_rate)
    vec_new = adam(vectors, m_vec, v_vec, red_vec, factor, count, rate_vector, 0.0)
    return (
        loss_value,
        grad_norm,
        attn_new[0],
        attn_new[1],
        attn_new[2],
        attn_new[3],
        mlp_new[0],
        mlp_new[1],
        mlp_new[2],
        mlp_new[3],
        mod_new[0],
        mod_new[1],
        mod_new[2],
        mod_new[3],
        io_new[0],
        io_new[1],
        io_new[2][0],
        io_new[2][1],
        io_new[3],
        vec_new[0],
        vec_new[1],
        vec_new[2],
        vec_new[3],
    )


RING = (0, 1, 3, 5, 7, 6, 4, 2)
RING_NEXT = tuple((RING[i], RING[(i + 1) % 8]) for i in range(8))
RING_PREV = tuple((b, a) for a, b in RING_NEXT)
HALF_SLOTS = 16
QKV_ROWS = 768
ATTN_ROWS = 1024
FRONT_ROWS = 912
TOKEN_ROWS = 512
IO_ROWS = 80
MOD_ROWS = 48
RING_ROWS = TOKEN_ROWS + FRONT_ROWS + 384
NT = (((1,), (1,)), ((), ()))
TN = (((0,), (0,)), ((), ()))


def swap(values, axis, bit):
    size = 8 if axis == "ctx" else 4
    return lax.ppermute(values, axis, [(i, i ^ bit) for i in range(size)])


def after(values, *others):
    return lax.optimization_barrier((values,) + others)[0]


def ring_gather(shard):
    half = shard.shape[0] // 2
    ahead = [shard]
    behind = [shard]
    for _ in range(3):
        ahead.append(lax.ppermute(ahead[-1], "ctx", RING_NEXT))
        behind.append(lax.ppermute(behind[-1], "ctx", RING_PREV))
    first = lax.ppermute(ahead[-1][:half], "ctx", RING_NEXT)
    second = lax.ppermute(behind[-1][half:], "ctx", RING_PREV)
    return ahead + behind[1:] + [jnp.concatenate([first, second], axis=0)]


def reduce_blocks(blocks, ctx_index, wire):
    return reduce_along_z(reduce_along_x(blocks, ctx_index, wire), ctx_index, wire)


def reduce_along_x(blocks, ctx_index, wire):
    x = ctx_index % 2
    pairs = blocks.reshape((4, 2) + blocks.shape[1:])
    first, second = pairs[:, 0], pairs[:, 1]
    even = x == 0
    away = jnp.where(even, second, first).astype(wire)
    return jnp.where(even, first, second) + swap(away, "ctx", 1).astype(jnp.float32)


def pieces_along_z(held, ctx_index, wire):
    z = ctx_index // 2
    low = held.astype(wire)
    came = []
    for bit in (1, 2, 3):
        piece = lax.dynamic_index_in_dim(low, z ^ bit, 0, keepdims=False)
        came.append(swap(piece, "ctx", 2 * bit))
    return lax.dynamic_index_in_dim(held, z, 0, keepdims=False), came


def reduce_along_z(held, ctx_index, wire):
    total, came = pieces_along_z(held, ctx_index, wire)
    for piece in came:
        total = total + piece.astype(jnp.float32)
    return total


def spread_frames(own):
    core = swap(own, "tp", 1)
    across = swap(own, "tp", 2)
    return [own, core, across, swap(across, "tp", 1)]


def sum_across(far):
    return (far[0] + swap(far[1], "tp", 1).astype(jnp.float32)).astype(jnp.bfloat16)


def sum_frames(near, across):
    return near[0], swap(near[1], "tp", 1), swap(across, "tp", 2)


def reorder_four(items, index):
    low_bit = (index & 1) == 1
    high_bit = (index & 2) == 2
    once = [jnp.where(low_bit, items[k ^ 1], items[k]) for k in range(4)]
    return [jnp.where(high_bit, once[k ^ 2], once[k]) for k in range(4)]


def sum_all(values):
    for axis, bit in (("tp", 1), ("tp", 2), ("ctx", 1)):
        values = values + swap(values, axis, bit)
    return [values] + [swap(values, "ctx", bit) for bit in (2, 4, 6)]


def prepare_kernel(meta, clean, noise, w_attn, w_io, vectors, ring):
    front = ring.at[TOKEN_ROWS:RING_ROWS]
    for frame in range(4):
        rows = pl.ds(pl.multiple_of(256 * frame + 64 * meta[1], 64), 64)
        ring[128 * frame : 128 * frame + 64, :] = clean[rows, :]
        ring[128 * frame + 64 : 128 * frame + 128, :] = noise[rows, :]
    for part in range(3):
        front[256 * part : 256 * part + 256, :] = w_attn[part].T.astype(jnp.bfloat16)
    base = QKV_ROWS
    front[base : base + 128, :] = w_io[0].astype(jnp.bfloat16)
    front[base + 128 : base + 144, :] = jnp.concatenate(
        [vectors[...], jnp.zeros((8, 128), jnp.float32)], axis=0
    ).astype(jnp.bfloat16)
    for part in range(2):
        base = FRONT_ROWS + 128 * part
        front[base : base + 128, :] = w_attn[3, :, 128 * part : 128 * part + 128].astype(
            jnp.bfloat16
        )
    front[FRONT_ROWS + 256 : FRONT_ROWS + 384, :] = w_io[1].T.astype(jnp.bfloat16)


def vmem_specs(count):
    return [pl.BlockSpec(memory_space=pltpu.VMEM)] * count


def smem_specs(count):
    return [pl.BlockSpec(memory_space=pltpu.SMEM)] * count


def call_prepare(device, clean, noise, w_attn, w_io, vectors):
    return pl.pallas_call(
        prepare_kernel,
        out_shape=jax.ShapeDtypeStruct((RING_ROWS, 128), jnp.bfloat16),
        in_specs=smem_specs(1) + vmem_specs(5),
        out_specs=vmem_specs(1)[0],
        name="prepare",
    )(device, clean, noise, w_attn, w_io, vectors)


def place_kernel(device, lengths, order, levels, front, attend, rows, inverse, stored, position, level):
    ctx, tp = device[0], device[1]
    frames, stretches, clips = levels.shape[0], order.shape[0], lengths.shape[0]
    per_stretch = frames // stretches
    half = frames // 2

    def per_stretch_place(place, carry):
        inverse[order[place]] = place
        return carry

    lax.fori_loop(0, stretches, per_stretch_place, 0)

    def per_frame(frame, counts):
        long_count, short_count = counts
        begin, start, length = jnp.int32(0), jnp.int32(0), jnp.int32(0)
        for clip in range(clips):
            size = lengths[clip]
            inside = (frame >= begin) & (frame < begin + size)
            start = jnp.where(inside, begin, start)
            length = jnp.where(inside, size, length)
            begin = begin + size
        is_long = length == half
        slot = jnp.where(is_long, long_count, half + short_count)
        stored[slot] = inverse[lax.div(frame, jnp.int32(per_stretch))] * per_stretch + lax.rem(
            frame, jnp.int32(per_stretch)
        )
        position[slot] = frame - start
        level[slot] = levels[frame]
        grown = is_long.astype(jnp.int32)
        return (long_count + grown, short_count + 1 - grown)

    lax.fori_loop(0, frames, per_frame, (jnp.int32(0), jnp.int32(0)))

    def where_on_ring(index):
        z, x = index >> 1, index & 1
        return jnp.where(x == 1, z + 1, (8 - z) & 7)

    mine = where_on_ring(ctx)
    member = ctx & 3
    for place, offset in enumerate((0, 7, 6, 5, 1, 2, 3, 4)):
        at = (mine + offset) & 7
        front[place] = jnp.where(
            at == 0, 0, jnp.where(at <= 4, 2 * at - 1, 2 * (8 - at))
        )
    for k in range(4):
        front[8 + k] = 4 * member + (tp ^ k)
        front[12 + k] = member ^ k
        at = stored[4 * ctx + (tp ^ k)]
        distance = (where_on_ring(at >> 2) - mine) & 7
        place = jnp.where(distance == 0, 0, jnp.where(distance <= 4, distance + 3, 8 - distance))
        front[16 + k] = place * 4 + (at & 3)
        front[20 + k] = tp ^ k
    attend[0] = member
    attend[1] = tp
    base = lax.div(ctx, jnp.int32(4)) * half

    def per_slot(slot, carry):
        attend[2 + slot] = position[base + slot]
        return carry

    lax.fori_loop(0, half, per_slot, 0)

    def per_row(row, carry):
        rows[row] = level[row]
        rows[frames + row] = level[4 * (ctx ^ (row & 7)) + (tp ^ (row >> 3))]
        return carry

    lax.fori_loop(0, frames, per_row, 0)


def call_place(device, lengths, order, levels):
    frames = levels.shape[0]
    return pl.pallas_call(
        place_kernel,
        out_shape=(
            jax.ShapeDtypeStruct((24,), jnp.int32),
            jax.ShapeDtypeStruct((2 + frames // 2,), jnp.int32),
            jax.ShapeDtypeStruct((2 * frames,), jnp.int32),
        ),
        in_specs=smem_specs(4),
        out_specs=smem_specs(3),
        scratch_shapes=[pltpu.SMEM((order.shape[0],), jnp.int32)]
        + [pltpu.SMEM((frames,), jnp.int32)] * 3,
        name="place",
    )(device, lengths, order, levels)


def pick_kernel(meta, *refs):
    out, sems = refs[8:]
    for frame in range(4):
        wanted = meta[16 + frame]
        for place in range(8):

            @pl.when((wanted >> 2) == place)
            def _():
                start = pl.multiple_of((wanted & 3) * 128, 128)
                pltpu.make_async_copy(
                    refs[place].at[pl.ds(start, 128), :],
                    out.at[128 * frame : 128 * frame + 128, :],
                    sems.at[frame],
                ).start()

    for frame in range(4):
        pltpu.make_async_copy(
            refs[0].at[0:128, :], out.at[128 * frame : 128 * frame + 128, :], sems.at[frame]
        ).wait()


def hbm_specs(count):
    return [pl.BlockSpec(memory_space=pltpu.HBM)] * count


def call_pick(meta, pieces):
    return pl.pallas_call(
        pick_kernel,
        out_shape=jax.ShapeDtypeStruct((TOKEN_ROWS, 128), jnp.bfloat16),
        in_specs=smem_specs(1) + hbm_specs(8),
        out_specs=vmem_specs(1)[0],
        scratch_shapes=[pltpu.SemaphoreType.DMA((4,))],
        compiler_params=pltpu.CompilerParams(vmem_limit_bytes=56 * 2**20),
        name="pick",
    )(meta, *pieces)


def centred_norm(values):
    centred = values - jnp.mean(values, axis=-1, keepdims=True)
    inv_std = lax.rsqrt(jnp.mean(centred * centred, axis=-1, keepdims=True) + ln_eps)
    return centred * inv_std, inv_std


def front_kernel(meta, scales, *refs):
    pieces, quarters = refs[:8], refs[8:12]
    mod, cosine, sine = refs[12:15]
    weights_out, mid_out, hidden_out, resid_out = refs[15:19]
    head_outs = refs[19:23]
    noisy_out, target_out, mod_out = refs[23:26]
    tokens, heads, weights, mid, hidden, resid, target, mod_own, held, sems, out_sems = refs[26:]
    copies = [
        pltpu.make_async_copy(
            pieces[place].at[TOKEN_ROWS:RING_ROWS, :], held.at[place], sems.at[place]
        )
        for place in range(8)
    ]
    for copy in copies:
        copy.start()
    for source in range(4):
        rows = pl.ds(pl.multiple_of(meta[20 + source] * 64, 64), 64)
        for frame in range(4):
            base = 128 * (frame ^ source)
            clean = quarters[source][base : base + 64, :].astype(jnp.float32)
            noise = quarters[source][base + 64 : base + 128, :].astype(jnp.float32)
            mixed = scales[frame] * clean + scales[4 + frame] * noise
            tokens[frame, rows, :] = mixed.astype(jnp.bfloat16)
            if frame == 0:
                target[rows, :] = scales[0] * noise - scales[4] * clean
    outs = [
        pltpu.make_async_copy(tokens.at[0], noisy_out, out_sems.at[0]),
        pltpu.make_async_copy(target, target_out, out_sems.at[1]),
        pltpu.make_async_copy(weights, weights_out, out_sems.at[2]),
        pltpu.make_async_copy(resid, resid_out, out_sems.at[3]),
    ] + [
        pltpu.make_async_copy(hidden.at[frame], hidden_out.at[frame], out_sems.at[4 + frame])
        for frame in range(4)
    ]
    outs.append(pltpu.make_async_copy(mod_own, mod_out, out_sems.at[8]))
    outs.append(pltpu.make_async_copy(mid, mid_out, out_sems.at[9]))
    for place in range(8):
        copies[place].wait()
        block = pl.ds(pl.multiple_of(meta[place] * 128, 128), 128)
        weights[:, block] = held[place, 0:FRONT_ROWS, :]
        for part in range(3):
            base = FRONT_ROWS + 128 * part
            mid[block, 128 * part : 128 * part + 128] = held[place, base : base + 128, :]
    for index in (0, 1, 2, 9):
        outs[index].start()
    embed = weights[QKV_ROWS : QKV_ROWS + 128, :]
    vec_rows = weights[QKV_ROWS + 128 : FRONT_ROWS, :].astype(jnp.float32)
    mod_own[0:6, :] = mod[0] + vec_rows[0:6]
    mod_own[6:8, :] = vec_rows[6:8]
    outs[8].start()
    for frame in range(4):
        values = jnp.dot(tokens[frame], embed, preferred_element_type=jnp.float32) + vec_rows[6:7]
        if frame == 0:
            resid[...] = values
            outs[3].start()
        normed, _ = centred_norm(values)
        shift = mod[frame, 0:1, :] + vec_rows[0:1]
        scale = mod[frame, 1:2, :] + vec_rows[1:2]
        low = (normed * (1.0 + scale) + shift).astype(jnp.bfloat16)
        hidden[frame] = low
        outs[4 + frame].start()
        mixed = lax.dot_general(
            weights[0:QKV_ROWS, :], low, NT, preferred_element_type=jnp.float32
        )
        cos_now = cosine[meta[8 + frame]]
        sin_now = sine[meta[8 + frame]]
        cols = slice(256 * frame, 256 * frame + 256)
        for head in range(4):
            where_to = head
            for part in range(2):
                base = 256 * part + 64 * head
                upper = mixed[base : base + 32]
                lower = mixed[base + 32 : base + 64]
                heads[where_to, 64 * part : 64 * part + 32, cols] = (
                    upper * cos_now - lower * sin_now
                ).astype(jnp.bfloat16)
                heads[where_to, 64 * part + 32 : 64 * part + 64, cols] = (
                    lower * cos_now + upper * sin_now
                ).astype(jnp.bfloat16)
            base = 512 + 64 * head
            heads[where_to, 128:192, cols] = mixed[base : base + 64].astype(jnp.bfloat16)
    for k in range(4):
        outs.append(pltpu.make_async_copy(heads.at[meta[12 + k]], head_outs[k], out_sems.at[10 + k]))
        outs[10 + k].start()
    for copy in outs:
        copy.wait()


def call_front(meta, scales, pieces, quarters, mod, cosine, sine):
    return pl.pallas_call(
        front_kernel,
        out_shape=(
            jax.ShapeDtypeStruct((FRONT_ROWS, D), jnp.bfloat16),
            jax.ShapeDtypeStruct((D, 384), jnp.bfloat16),
            jax.ShapeDtypeStruct((4, PATCHES, D), jnp.bfloat16),
            jax.ShapeDtypeStruct((PATCHES, D), jnp.float32),
        )
        + (jax.ShapeDtypeStruct((192, 4 * PATCHES), jnp.bfloat16),) * 4
        + (
            jax.ShapeDtypeStruct((PATCHES, 128), jnp.bfloat16),
            jax.ShapeDtypeStruct((PATCHES, 128), jnp.float32),
            jax.ShapeDtypeStruct((8, D), jnp.float32),
        ),
        in_specs=smem_specs(2) + hbm_specs(8) + vmem_specs(7),
        out_specs=hbm_specs(11),
        scratch_shapes=[
            pltpu.VMEM((4, PATCHES, 128), jnp.bfloat16),
            pltpu.VMEM((4, 192, 4 * PATCHES), jnp.bfloat16),
            pltpu.VMEM((FRONT_ROWS, D), jnp.bfloat16),
            pltpu.VMEM((D, 384), jnp.bfloat16),
            pltpu.VMEM((4, PATCHES, D), jnp.bfloat16),
            pltpu.VMEM((PATCHES, D), jnp.float32),
            pltpu.VMEM((PATCHES, 128), jnp.float32),
            pltpu.VMEM((8, D), jnp.float32),
            pltpu.VMEM((8, FRONT_ROWS + 384, 128), jnp.bfloat16),
            pltpu.SemaphoreType.DMA((8,)),
            pltpu.SemaphoreType.DMA((14,)),
        ],
        compiler_params=pltpu.CompilerParams(vmem_limit_bytes=52 * 2**20),
        cost_estimate=pl.CostEstimate(flops=2 * 10**9, bytes_accessed=10**7, transcendentals=0),
        name="front",
    )(meta, scales, *pieces, *quarters, mod, cosine, sine)


def total_own(held, came, across):
    return held[...] + came[...].astype(jnp.float32) + across[...].astype(jnp.float32)


def middle_kernel(held, came, across, resid, mod, attn_out, resid_mid, hidden):
    total = total_own(held, came, across)
    attn_out[...] = total
    values = resid[...] + mod[2:3, :] * total
    resid_mid[...] = values
    normed, _ = centred_norm(values)
    hidden[...] = (normed * (1.0 + mod[4:5, :]) + mod[3:4, :]).astype(jnp.bfloat16)


def row_call(kernel, name, outs, *operands, smem=0):
    return pl.pallas_call(
        kernel,
        out_shape=tuple(outs),
        in_specs=smem_specs(smem) + vmem_specs(len(operands) - smem),
        out_specs=vmem_specs(len(outs)),
        compiler_params=pltpu.CompilerParams(vmem_limit_bytes=16 * 2**20),
        cost_estimate=pl.CostEstimate(flops=10**9, bytes_accessed=4 * 10**6, transcendentals=0),
        name=name,
    )(*operands)


def frame_f32():
    return jax.ShapeDtypeStruct((PATCHES, D), jnp.float32)


def frame_low():
    return jax.ShapeDtypeStruct((PATCHES, D), jnp.bfloat16)


def back_through_norm(grad, normed, inv_std):
    mean_grad = jnp.mean(grad, axis=-1, keepdims=True)
    mean_proj = jnp.mean(grad * normed, axis=-1, keepdims=True)
    return inv_std * (grad - mean_grad - normed * mean_proj)


def column_sum(values):
    return jnp.sum(values, axis=0, keepdims=True)


def loss_kernel(
    scales, held, came, across, resid_mid, mod, mid, target, grad_low, grad_three, io_rows, gate, error
):
    mlp_out = total_own(held, came, across)
    values = resid_mid[...] + mod[5:6, :] * mlp_out
    normed, inv_std = centred_norm(values)
    gain = mod[7:8, :]
    final = (normed * gain).astype(jnp.bfloat16)
    head = mid[:, 256:384]
    pred = jnp.dot(final, head, preferred_element_type=jnp.float32)
    diff = pred - target[...]
    per_token = jnp.sum(diff * diff, axis=1, keepdims=True)
    error[...] = jnp.broadcast_to(
        scales[0] * jnp.sum(per_token, axis=0, keepdims=True) / diff.shape[1], error.shape
    )
    grad_pred = (scales[1] * diff).astype(jnp.bfloat16)
    grad_final = lax.dot_general(grad_pred, head, NT, preferred_element_type=jnp.float32)
    grad_gain = column_sum(grad_final * normed)
    grad = back_through_norm(grad_final * gain, normed, inv_std)
    grad_three[...] = grad
    grad_low[...] = (mod[5:6, :] * grad).astype(jnp.bfloat16)
    gate[...] = column_sum(grad * mlp_out)
    io_rows[0:128, :] = lax.dot_general(grad_pred, final, TN, preferred_element_type=jnp.float32)
    io_rows[128:136, :] = jnp.concatenate([grad_gain, jnp.zeros((7, D), jnp.float32)], axis=0)


def second_kernel(
    held, came, across, resid_mid, mod, grad_three, attn_out, grad_low, grad_mid, rows
):
    grad_hidden = total_own(held, came, across)
    normed, inv_std = centred_norm(resid_mid[...])
    grad = grad_three[...] + back_through_norm(grad_hidden * (1.0 + mod[4:5, :]), normed, inv_std)
    grad_mid[...] = grad
    grad_low[...] = (mod[2:3, :] * grad).astype(jnp.bfloat16)
    rows[0:1, :] = column_sum(grad * attn_out[...])
    rows[1:2, :] = column_sum(grad_hidden)
    rows[2:3, :] = column_sum(grad_hidden * normed)


def first_kernel(
    device,
    held,
    came,
    across,
    resid,
    mod,
    grad_mid,
    noisy,
    rows_two,
    gate_two,
    head_rows,
    mod_rows,
    near_held,
    near_away,
    far_held,
    far_away,
    io_rows,
):
    grad_hidden = total_own(held, came, across)
    normed, inv_std = centred_norm(resid[...])
    grad = grad_mid[...] + back_through_norm(grad_hidden * (1.0 + mod[1:2, :]), normed, inv_std)
    rows = [
        column_sum(grad_hidden),
        column_sum(grad_hidden * normed),
        rows_two[0:1, :],
        rows_two[1:2, :],
        rows_two[2:3, :],
        gate_two[...],
    ]
    blocks = [row[:, 128 * k : 128 * k + 128] for row in rows for k in range(8)]
    mod_rows[...] = jnp.concatenate(blocks, axis=0).astype(jnp.bfloat16)
    io_rows[0:128, :] = lax.dot_general(
        noisy[...], grad.astype(jnp.bfloat16), TN, preferred_element_type=jnp.float32
    )
    io_rows[128:256, :] = head_rows[0:128, :]
    io_rows[256:264, :] = jnp.concatenate(
        [column_sum(grad), head_rows[128:129, :], jnp.zeros((6, D), jnp.float32)], axis=0
    )
    io_rows[264:320, :] = jnp.zeros((56, D), jnp.float32)
    for k, out in enumerate((near_held, near_away, far_held, far_away)):
        group = pl.ds(pl.multiple_of(IO_ROWS * (device[1] ^ k), 16), IO_ROWS)
        out[...] = io_rows[group, :].astype(out.dtype)


def side_kernel(device, held, came, across, mod_rows, keep, away):
    total = total_own(held, came, across)
    side = device[0] & 1
    for block in range(8):
        piece = total[:, 128 * block : 128 * block + 128]

        @pl.when(side == block % 2)
        def _():
            keep[block // 2] = piece

        @pl.when(side != block % 2)
        def _():
            away[IO_ROWS * (block // 2) : IO_ROWS * (block // 2) + IO_ROWS, :] = piece.astype(
                jnp.bfloat16
            )

    away[4 * IO_ROWS :, :] = mod_rows[...]


def merge_kernel(
    device, held, came, out_held, out_came, io_held, io_came, mod_rows, own, io_own, *outs
):
    z = device[0] >> 1
    for bit in range(4):
        total = jnp.concatenate(
            [
                held[z ^ bit] + came[z ^ bit].astype(jnp.float32),
                out_held[z ^ bit] + out_came[z ^ bit].astype(jnp.float32),
            ],
            axis=0,
        )
        rows = pl.ds(pl.multiple_of(IO_ROWS * (z ^ bit), 16), IO_ROWS)
        io_total = io_held[z ^ bit] + io_came[rows, :].astype(jnp.float32)
        if bit == 0:
            own[...] = total
            io_own[...] = io_total
        else:
            out = outs[bit]
            out[0:ATTN_ROWS, :] = total.astype(jnp.bfloat16)
            out[ATTN_ROWS : ATTN_ROWS + IO_ROWS, :] = io_total.astype(jnp.bfloat16)
            base = ATTN_ROWS + IO_ROWS
            out[base : base + MOD_ROWS, :] = mod_rows[...]
            out[base + MOD_ROWS : base + 2 * MOD_ROWS, :] = io_came[4 * IO_ROWS :, :]
    outs[0][0:MOD_ROWS, :] = mod_rows[...]
    outs[0][MOD_ROWS : 2 * MOD_ROWS, :] = io_came[4 * IO_ROWS :, :]


def mod_grad_kernel(device, cond, *refs):
    parts = refs[:4]
    grad, vector, io_grad, square, rows = refs[4:]
    for index in range(4):
        for frame in range(8):
            block = parts[index][MOD_ROWS * frame : MOD_ROWS * frame + MOD_ROWS, :].astype(
                jnp.float32
            )
            at = 8 * index + frame
            for k in range(MOD_ROWS):
                rows[at : at + 1, 128 * k : 128 * k + 128] = block[k : k + 1, :]
        base = 8 * MOD_ROWS
        group = pl.ds(pl.multiple_of(IO_ROWS * (device[1] ^ index), 16), IO_ROWS)
        io_grad[group, :] = parts[index][base : base + IO_ROWS, :].astype(jnp.float32) + parts[
            index
        ][base + IO_ROWS : base + 2 * IO_ROWS, :].astype(jnp.float32)
    total = jnp.zeros((1, 1), jnp.float32)
    for index in range(6):
        cols = slice(D * index, D * index + D)
        part = lax.dot_general(
            cond[...], rows[:, cols].astype(jnp.bfloat16), TN, preferred_element_type=jnp.float32
        )
        grad[:, cols] = part
        total = total + jnp.sum(column_sum(part * part), axis=1, keepdims=True)
        own = pl.ds(pl.multiple_of(D * index + 128 * device[0], 128), 128)
        vector[index : index + 1, :] = column_sum(rows[:, own])
    vector[6:8, :] = io_grad[256:258, :]
    mixed = vector[0:6, :]
    total = total + jnp.sum(column_sum(mixed * mixed), axis=1, keepdims=True)
    square[...] = jnp.broadcast_to(total, square.shape)


def call_mod_grad(device, cond, parts):
    return pl.pallas_call(
        mod_grad_kernel,
        out_shape=(
            jax.ShapeDtypeStruct((128, 6 * D), jnp.float32),
            jax.ShapeDtypeStruct((8, 128), jnp.float32),
            jax.ShapeDtypeStruct((4 * IO_ROWS, 128), jnp.float32),
            jax.ShapeDtypeStruct((1, 128), jnp.float32),
        ),
        in_specs=smem_specs(1) + vmem_specs(5),
        out_specs=vmem_specs(4),
        scratch_shapes=[pltpu.VMEM((32, 6 * D), jnp.float32)],
        compiler_params=pltpu.CompilerParams(vmem_limit_bytes=12 * 2**20),
        cost_estimate=pl.CostEstimate(flops=10**8, bytes_accessed=4 * 10**6, transcendentals=0),
        name="mod_grad",
    )(device, cond, *parts)


def mlp_kernel(first, second, weights, held, away, active, slope):
    for frame, source in enumerate((first, second)):
        rows = slice(256 * frame, 256 * frame + 256)
        upward = jnp.dot(source[...], weights[0], preferred_element_type=jnp.float32)
        inner = 0.5 * (1.0 + lax.erf(upward * (1.0 / math.sqrt(2.0))))
        low = (upward * inner).astype(jnp.bfloat16)
        active[rows, :] = low
        change = inner + upward * jnp.exp(-0.5 * upward * upward) * (
            1.0 / math.sqrt(2.0 * math.pi)
        )
        slope[rows, :] = change.astype(jnp.bfloat16)
        part = lax.dot_general(low, weights[1], NT, preferred_element_type=jnp.float32)
        if frame:
            away[...] = part.astype(jnp.bfloat16)
        else:
            held[...] = part


def mlp_back_kernel(first, second, weights, slope, held, away, grad_up):
    for frame, source in enumerate((first, second)):
        rows = slice(256 * frame, 256 * frame + 256)
        grad = jnp.dot(source[...], weights[1], preferred_element_type=jnp.float32)
        low = (grad * slope[rows, :].astype(jnp.float32)).astype(jnp.bfloat16)
        grad_up[rows, :] = low
        part = lax.dot_general(low, weights[0], NT, preferred_element_type=jnp.float32)
        if frame:
            away[...] = part.astype(jnp.bfloat16)
        else:
            held[...] = part


def call_mlp(kernel, name, outs, *operands):
    return pl.pallas_call(
        kernel,
        out_shape=(frame_f32(), frame_low()) + outs,
        in_specs=vmem_specs(len(operands)),
        out_specs=vmem_specs(2 + len(outs)),
        compiler_params=pltpu.CompilerParams(vmem_limit_bytes=16 * 2**20),
        cost_estimate=pl.CostEstimate(
            flops=4 * 10**9, bytes_accessed=2 * 10**7, transcendentals=10**6
        ),
        name=name,
    )(*operands)


def weight_grad_kernel(*refs):
    hidden, grads = refs[:4], refs[4:8]
    grad_up, active = refs[8:10], refs[10:12]
    result, out, sems = refs[12:]
    width = active[0].shape[1]
    copies = []
    for index, (left, right) in enumerate(((hidden, grad_up), (grads, active))):
        total = jnp.zeros((D, width), jnp.float32)
        for frame in range(4):
            rows = slice(256 * (frame % 2), 256 * (frame % 2) + 256)
            total = total + lax.dot_general(
                left[frame][...],
                right[frame // 2][rows, :],
                TN,
                preferred_element_type=jnp.float32,
            )
        out[index] = total.astype(jnp.bfloat16)
        copies.append(
            pltpu.make_async_copy(
                out.at[index], result.at[:, width * index : width * index + width], sems.at[index]
            )
        )
        copies[index].start()
    for copy in copies:
        copy.wait()


def call_weight_grad(hidden, grads, grad_up, active):
    operands = (*hidden, *grads, *grad_up, *active)
    return pl.pallas_call(
        weight_grad_kernel,
        out_shape=jax.ShapeDtypeStruct((D, 2 * active[0].shape[1]), jnp.bfloat16),
        in_specs=vmem_specs(len(operands)),
        out_specs=hbm_specs(1)[0],
        scratch_shapes=[
            pltpu.VMEM((2, D, active[0].shape[1]), jnp.bfloat16),
            pltpu.SemaphoreType.DMA((2,)),
        ],
        compiler_params=pltpu.CompilerParams(vmem_limit_bytes=20 * 2**20),
        cost_estimate=pl.CostEstimate(flops=5 * 10**9, bytes_accessed=2 * 10**7, transcendentals=0),
        name="weight_grad",
    )(*operands)


def side_blocks(device, total, held, away):
    side = device[0] & 1
    for z in range(4):
        held[z] = total[:, pl.ds(pl.multiple_of(256 * z + 128 * side, 128), 128)]
        away[z] = total[:, pl.ds(pl.multiple_of(256 * z + 128 * (1 - side), 128), 128)].astype(
            jnp.bfloat16
        )


def head_grad_kernel(device, left, right, held, away, total):
    total[...] = jnp.dot(left[...], right[...], preferred_element_type=jnp.float32)
    side_blocks(device, total, held, away)


def call_head_grad(device, left, right):
    rows = left.shape[0]
    return pl.pallas_call(
        head_grad_kernel,
        out_shape=(
            jax.ShapeDtypeStruct((4, rows, 128), jnp.float32),
            jax.ShapeDtypeStruct((4, rows, 128), jnp.bfloat16),
        ),
        in_specs=smem_specs(1) + vmem_specs(2),
        out_specs=vmem_specs(2),
        scratch_shapes=[pltpu.VMEM((rows, D), jnp.float32)],
        compiler_params=pltpu.CompilerParams(vmem_limit_bytes=12 * 2**20),
        cost_estimate=pl.CostEstimate(flops=2 * 10**9, bytes_accessed=10**7, transcendentals=0),
        name="head_grad",
    )(device, left, right)


def qkv_back_kernel(meta, *refs):
    blocks, weights = refs[:4], refs[4]
    grads, near_held, near_away, far_held, far_away = refs[5:]
    for k in range(4):
        head = meta[0] ^ k
        for part in range(3):
            rows = pl.ds(pl.multiple_of(256 * part + 64 * head, 64), 64)
            grads[rows, :] = blocks[k][64 * part : 64 * part + 64, :]
    for frame, out in ((2, far_held), (3, far_away), (0, near_held), (1, near_away)):
        part = lax.dot_general(
            grads[:, 256 * frame : 256 * frame + 256],
            weights[0:QKV_ROWS, :],
            TN,
            preferred_element_type=jnp.float32,
        )
        out[...] = part.astype(out.dtype)


def call_qkv_back(meta, blocks, weights):
    return row_call(
        qkv_back_kernel,
        "qkv_back",
        (
            jax.ShapeDtypeStruct((QKV_ROWS, 4 * PATCHES), jnp.bfloat16),
            frame_f32(),
            frame_low(),
            frame_f32(),
            frame_low(),
        ),
        meta,
        *blocks,
        weights,
        smem=1,
    )


def adam_step(weight_now, first_mom, second_mom, grad, scale, rate, decay):
    factor, first_fix, second_fix = scale
    grad = grad * factor
    first_mom = beta_one * first_mom + (1.0 - beta_one) * grad
    second_mom = beta_two * second_mom + (1.0 - beta_two) * grad * grad
    updated = weight_now - rate * (
        first_mom * first_fix / (jnp.sqrt(second_mom * second_fix) + adam_eps) + decay * weight_now
    )
    return updated, first_mom, second_mom, updated.astype(jnp.bfloat16)


def adam_kernel(*refs):
    fixes, sums = refs[0], refs[1:5]
    groups = [refs[5 + 4 * k : 9 + 4 * k] for k in range(3)]
    io_in, vec_in = refs[17:21], refs[21:25]
    outs = [refs[25 + 4 * k : 29 + 4 * k] for k in range(3)]
    io_out, vec_out, norm_out = refs[37:42], refs[42:46], refs[46]
    slots, low_slots, sems = refs[47:]
    total = (sums[0][...] + sums[1][...]) + (sums[2][...] + sums[3][...])
    norm = jnp.sqrt(total)
    norm_out[0:1, :] = norm
    norm_out[1:2, :] = total
    factor = jnp.minimum(1.0, clip_limit / (norm[:, 0:1] + 1e-06))
    scale = (factor, fixes[0], fixes[1])
    tasks = []
    for k, group in enumerate(groups):
        rows, width = group[0].shape[-2:]
        for lead in range(group[0].shape[0] if len(group[0].shape) == 3 else 1):
            for col in range(0, width, 1024):
                span = min(1024, width - col)
                tasks.append((k, lead, col, span))
    running = {}
    for number, (k, lead, col, span) in enumerate(tasks):
        slot = number % 4
        if number >= 4:
            for copy in running.pop(number - 4):
                copy.wait()
        cut = (slice(None), slice(col, col + span))
        if len(groups[k][0].shape) == 3:
            cut = (lead,) + cut
        values = [ref[cut].astype(jnp.float32) for ref in groups[k]]
        results = adam_step(*values, scale, rate_matrix, decay_rate)
        copies = []
        for index, result in enumerate(results):
            source = low_slots.at[slot] if index == 3 else slots.at[slot, index]
            source = source.at[:, 0:span]
            source[...] = result
            copies.append(
                pltpu.make_async_copy(source, outs[k][index].at[cut], sems.at[slot, index])
            )
            copies[index].start()
        running[number] = copies
    results = adam_step(*(ref[...] for ref in io_in), scale, rate_matrix, decay_rate)
    io_out[0][...] = results[0]
    io_out[1][...] = results[1]
    io_out[2][...] = results[2][0]
    io_out[3][...] = results[2][1]
    io_out[4][...] = results[3]
    results = adam_step(*(ref[...] for ref in vec_in), scale, rate_vector, 0.0)
    for out, result in zip(vec_out, results):
        out[...] = result
    for copies in running.values():
        for copy in copies:
            copy.wait()


def call_adam(fixes, sums, groups, io_group, vec_group):
    operands = [*sums, *(array for group in groups for array in group), *io_group, *vec_group]

    def results(group):
        low = jax.ShapeDtypeStruct(group[0].shape, jnp.bfloat16)
        return (jax.ShapeDtypeStruct(group[0].shape, jnp.float32),) * 3 + (low,)

    io_like = results(io_group)
    half = jax.ShapeDtypeStruct(io_group[0].shape[1:], jnp.float32)
    out_shape = sum((results(group) for group in groups), ())
    out_shape = out_shape + io_like[:2] + (half, half) + io_like[3:] + results(vec_group)
    out_shape = out_shape + (jax.ShapeDtypeStruct((2, 128), jnp.float32),)
    return pl.pallas_call(
        adam_kernel,
        out_shape=out_shape,
        in_specs=smem_specs(1) + vmem_specs(len(operands)),
        out_specs=hbm_specs(12) + vmem_specs(10),
        scratch_shapes=[
            pltpu.VMEM((4, 3, 128, 1024), jnp.float32),
            pltpu.VMEM((4, 128, 1024), jnp.bfloat16),
            pltpu.SemaphoreType.DMA((4, 4)),
        ],
        compiler_params=pltpu.CompilerParams(vmem_limit_bytes=20 * 2**20),
        cost_estimate=pl.CostEstimate(flops=10**7, bytes_accessed=2 * 10**7, transcendentals=0),
        name="adam",
    )(fixes, *operands)


def finish_kernel(*refs):
    own, io_own, mod_own, pieces = refs[0], refs[1], refs[2], refs[3:6]
    scattered, grad, spread, square = refs[6:]
    total = own[...]
    io_total = io_own[...]
    spread[0 : 2 * MOD_ROWS, :] = mod_own[...]
    for index, piece in enumerate(pieces):
        total = total + piece[0:ATTN_ROWS, :].astype(jnp.float32)
        base = ATTN_ROWS + IO_ROWS
        io_total = io_total + piece[ATTN_ROWS:base, :].astype(jnp.float32)
        spread[2 * MOD_ROWS * (index + 1) : 2 * MOD_ROWS * (index + 2), :] = piece[base:, :]
    high = io_total.astype(jnp.bfloat16)
    base = 8 * MOD_ROWS
    spread[base : base + IO_ROWS, :] = high
    spread[base + IO_ROWS :, :] = (io_total - high.astype(jnp.float32)).astype(jnp.bfloat16)
    for part in range(4):
        grad[part] = total[256 * part : 256 * part + 256].T
    rest = scattered[...].astype(jnp.float32)
    squares = jnp.zeros((1, 1), jnp.float32)
    for values in (total, rest, io_total):
        squares = squares + jnp.sum(column_sum(values * values), axis=1, keepdims=True)
    square[...] = jnp.broadcast_to(squares, square.shape)


def turn(block):
    return block.astype(jnp.float32).T.astype(jnp.bfloat16)


def query_rows(meta, pair):
    first = 2 * pair
    start_first = first - meta[2 + first]
    start_second = first + 1 - meta[3 + first]
    left = lax.broadcasted_iota(jnp.int32, (1, 2 * PATCHES), 1) < PATCHES
    upto = jnp.where(left, first, first + 1)
    since = jnp.where(left, start_first, start_second)
    return jnp.minimum(start_first, start_second), since, upto


def attend_kernel(meta, *refs):
    blocks = refs[:4]
    outs = refs[4:8]
    lse, mixed, query, key, value = refs[8:]
    for member in range(4):
        for frame in range(4):
            slot = 4 * (meta[0] ^ member) + (meta[1] ^ frame)
            cols = slice(256 * frame, 256 * frame + 256)
            lanes = pl.ds(pl.multiple_of((slot % 2) * 256, 256), 256)
            query[slot // 2, :, lanes] = blocks[member][0:64, cols] * 0.125
            key[slot // 2, lanes, :] = turn(blocks[member][64:128, cols])
            value[slot // 2, :, lanes] = blocks[member][128:192, cols]

    def per_pair(pair, carry):
        low, since, upto = query_rows(meta, pair)
        wanted = query[pair]

        def per_keys(keys, state):
            top, total, acc = state
            both = jnp.dot(key[keys], wanted, preferred_element_type=jnp.float32)
            scores = []
            new_top = top
            for side in range(2):
                slot = 2 * keys + side
                bias = jnp.where((slot >= since) & (slot <= upto), 0.0, neg_large)
                scores.append(both[256 * side : 256 * side + 256] + bias)
                new_top = jnp.maximum(new_top, jnp.max(scores[side], axis=0, keepdims=True))
            probs = [jnp.exp(values - new_top) for values in scores]
            shrink = jnp.exp(top - new_top)
            total = total * shrink + jnp.sum(probs[0] + probs[1], axis=0, keepdims=True)
            low_probs = jnp.concatenate([values.astype(jnp.bfloat16) for values in probs], axis=0)
            acc = acc * shrink + jnp.dot(
                value[keys], low_probs, preferred_element_type=jnp.float32
            )
            return (new_top, total, acc)

        top, total, acc = lax.fori_loop(
            low // 2,
            pair + 1,
            per_keys,
            (
                jnp.full((1, 2 * PATCHES), neg_large, jnp.float32),
                jnp.zeros((1, 2 * PATCHES), jnp.float32),
                jnp.zeros((HD, 2 * PATCHES), jnp.float32),
            ),
        )
        lse[pair] = top + jnp.log(total)
        mixed[pair] = acc / total
        return carry

    lax.fori_loop(0, 8, per_pair, 0)
    for member in range(4):
        for frame in range(4):
            slot = 4 * (meta[0] ^ member) + (meta[1] ^ frame)
            lanes = pl.ds(pl.multiple_of((slot % 2) * 256, 256), 256)
            outs[member][:, 256 * frame : 256 * frame + 256] = mixed[slot // 2, :, lanes].astype(
                jnp.bfloat16
            )


def call_attend(meta, blocks):
    vmem = pl.BlockSpec(memory_space=pltpu.VMEM)
    result = pl.pallas_call(
        attend_kernel,
        out_shape=tuple(jax.ShapeDtypeStruct((HD, 4 * PATCHES), jnp.bfloat16) for _ in range(4))
        + (
            jax.ShapeDtypeStruct((8, 1, 2 * PATCHES), jnp.float32),
            jax.ShapeDtypeStruct((8, HD, 2 * PATCHES), jnp.float32),
        ),
        in_specs=[pl.BlockSpec(memory_space=pltpu.SMEM)] + [vmem] * 4,
        out_specs=(vmem,) * 6,
        scratch_shapes=[
            pltpu.VMEM((8, HD, 2 * PATCHES), jnp.bfloat16),
            pltpu.VMEM((8, 2 * PATCHES, HD), jnp.bfloat16),
            pltpu.VMEM((8, HD, 2 * PATCHES), jnp.bfloat16),
        ],
        compiler_params=pltpu.CompilerParams(vmem_limit_bytes=16 * 2**20),
        cost_estimate=pl.CostEstimate(flops=9 * 10**9, bytes_accessed=5 * 10**6, transcendentals=10**7),
        name="attend",
    )(meta, *blocks)
    return list(result[:4]), result[4], result[5]


def attend_back_kernel(meta, *refs):
    blocks = refs[:4]
    grads = refs[4:8]
    lse, mixed, cosine, sine = refs[8:12]
    outs = refs[12:16]
    query, query_flat, key, key_flat, value_flat, grad, grad_flat, sum_key, sum_value, sum_query = (
        refs[16:]
    )
    for member in range(4):
        for frame in range(4):
            slot = 4 * (meta[0] ^ member) + (meta[1] ^ frame)
            cols = slice(256 * frame, 256 * frame + 256)
            place = pl.ds(pl.multiple_of((slot % 2) * 256, 256), 256)
            part = blocks[member][0:64, cols] * 0.125
            query[slot // 2, :, place] = part
            query_flat[slot // 2, place, :] = turn(part)
            part = blocks[member][64:128, cols]
            key[slot // 2, :, place] = part
            key_flat[slot // 2, place, :] = turn(part)
            value_flat[slot // 2, place, :] = turn(blocks[member][128:192, cols])
            part = grads[member][:, cols]
            grad[slot // 2, :, place] = part
            grad_flat[slot // 2, place, :] = turn(part)
    sum_key[...] = jnp.zeros_like(sum_key)
    sum_value[...] = jnp.zeros_like(sum_value)

    def per_pair(pair, carry):
        low, since, upto = query_rows(meta, pair)
        wanted = query[pair]
        wanted_grad = grad[pair]
        delta = jnp.sum(wanted_grad.astype(jnp.float32) * mixed[pair], axis=0, keepdims=True)
        level = lse[pair]

        def per_keys(keys, acc):
            scores = jnp.dot(key_flat[keys], wanted, preferred_element_type=jnp.float32)
            grad_probs = jnp.dot(
                value_flat[keys], wanted_grad, preferred_element_type=jnp.float32
            )
            low_probs, low_scores = [], []
            for side in range(2):
                rows = slice(256 * side, 256 * side + 256)
                slot = 2 * keys + side
                bias = jnp.where((slot >= since) & (slot <= upto), -level, neg_large)
                probs = jnp.exp(scores[rows] + bias)
                low_probs.append(probs.astype(jnp.bfloat16))
                low_scores.append((probs * (grad_probs[rows] - delta)).astype(jnp.bfloat16))
            all_probs = jnp.concatenate(low_probs, axis=0)
            all_scores = jnp.concatenate(low_scores, axis=0)
            sum_value[keys] += jnp.dot(
                all_probs, grad_flat[pair], preferred_element_type=jnp.float32
            )
            sum_key[keys] += jnp.dot(
                all_scores, query_flat[pair], preferred_element_type=jnp.float32
            )
            return acc + jnp.dot(key[keys], all_scores, preferred_element_type=jnp.float32)

        sum_query[pair] = lax.fori_loop(
            low // 2, pair + 1, per_keys, jnp.zeros((HD, 2 * PATCHES), jnp.float32)
        )
        return carry

    lax.fori_loop(0, 8, per_pair, 0)
    for member in range(4):
        for frame in range(4):
            slot = 4 * (meta[0] ^ member) + (meta[1] ^ frame)
            cols = slice(256 * frame, 256 * frame + 256)
            place = pl.ds(pl.multiple_of((slot % 2) * 256, 256), 256)
            cos_now = cosine[slot]
            sin_now = sine[slot]
            for base, part in (
                (0, sum_query[slot // 2, :, place] * 0.125),
                (64, sum_key[slot // 2, place, :].T),
            ):
                upper = part[0:32]
                lower = part[32:64]
                outs[member][base : base + 32, cols] = (
                    upper * cos_now + lower * sin_now
                ).astype(jnp.bfloat16)
                outs[member][base + 32 : base + 64, cols] = (
                    lower * cos_now - upper * sin_now
                ).astype(jnp.bfloat16)
            outs[member][128:192, cols] = sum_value[slot // 2, place, :].T.astype(jnp.bfloat16)


def call_attend_back(meta, blocks, grads, lse, mixed, cosine, sine):
    vmem = pl.BlockSpec(memory_space=pltpu.VMEM)
    flat_pair = pltpu.VMEM((8, 2 * PATCHES, HD), jnp.bfloat16)
    turned_pair = pltpu.VMEM((8, HD, 2 * PATCHES), jnp.bfloat16)
    wide = pltpu.VMEM((8, 2 * PATCHES, HD), jnp.float32)
    return list(
        pl.pallas_call(
            attend_back_kernel,
            out_shape=tuple(
                jax.ShapeDtypeStruct((192, 4 * PATCHES), jnp.bfloat16) for _ in range(4)
            ),
            in_specs=[pl.BlockSpec(memory_space=pltpu.SMEM)] + [vmem] * 12,
            out_specs=(vmem,) * 4,
            scratch_shapes=[
                turned_pair,
                flat_pair,
                turned_pair,
                flat_pair,
                flat_pair,
                turned_pair,
                flat_pair,
                wide,
                wide,
                pltpu.VMEM((8, HD, 2 * PATCHES), jnp.float32),
            ],
            compiler_params=pltpu.CompilerParams(vmem_limit_bytes=20 * 2**20),
            cost_estimate=pl.CostEstimate(
                flops=22 * 10**9, bytes_accessed=10**7, transcendentals=10**7
            ),
            name="attend_back",
        )(meta, *blocks, *grads, lse, mixed, cosine, sine)
    )


def shards_halves(
    clean,
    noise,
    levels,
    lengths,
    order,
    step,
    w_attn,
    m_attn,
    v_attn,
    w_mlp,
    m_mlp,
    v_mlp,
    w_mod,
    m_mod,
    v_mod,
    w_io,
    m_io,
    v_io,
    vectors,
    m_vec,
    v_vec,
):
    bfloat = jnp.bfloat16
    single = jnp.float32
    ctx_index = lax.axis_index("ctx")
    tp_index = lax.axis_index("tp")
    member = ctx_index % 4
    device = jnp.stack([ctx_index, tp_index]).astype(jnp.int32)

    pieces = ring_gather(call_prepare(device, clean, noise, w_attn, w_io, vectors))
    front_meta, attend_meta, row_levels = call_place(device, lengths, order, levels)

    half_dim = D // 2
    column = ctx_index * 128 + jnp.arange(128, dtype=jnp.int32)
    frequency = jnp.exp(-math.log(10000.0) * (column % half_dim).astype(single) / half_dim)
    angle = row_levels.astype(single)[:, None] * frequency[None, :]
    cond = jax.nn.silu(jnp.where(column[None, :] < half_dim, jnp.cos(angle), jnp.sin(angle)))
    cond_low = cond.astype(bfloat)
    cond_slots, cond_relative = cond_low[:32], cond_low[32:]
    quarter_cols = 6 * D // 4
    mod_cols = lax.dynamic_slice_in_dim(w_mod, tp_index * quarter_cols, quarter_cols, 1)
    mod_part = jnp.dot(cond_slots, mod_cols.astype(bfloat), preferred_element_type=single)
    mod_held = reduce_along_x(mod_part.reshape(8, 4, quarter_cols), ctx_index, single)
    mod_held = after(mod_held, pieces[2], pieces[5])
    mod_own = after(reduce_along_z(mod_held, ctx_index, single), pieces[3], pieces[6])
    mod_quarters = reorder_four(spread_frames(mod_own), tp_index)
    mod_all = jnp.concatenate(mod_quarters, axis=1)
    mod_rel = jnp.stack(reorder_four([mod_all[k] for k in range(4)], tp_index))
    mod_rel = mod_rel.reshape(4, 6, D)

    time_pairs = HD // 8
    side_pairs = (HD // 2 - time_pairs) // 2

    def frequencies(count):
        return 10000.0 ** (-jnp.arange(count, dtype=single) / count)

    patch = jnp.arange(PATCHES, dtype=jnp.int32)
    half_position = attend_meta[2:].astype(single)
    time_angle = half_position[:, None] * frequencies(time_pairs)[None, :]
    height_angle = frequencies(side_pairs)[:, None] * (patch // GRID).astype(single)[None, :]
    width_angle = frequencies(side_pairs)[:, None] * (patch % GRID).astype(single)[None, :]
    side_angle = jnp.concatenate([height_angle, width_angle], axis=0)

    def full_table(time_part, side_part):
        return jnp.concatenate(
            [
                jnp.broadcast_to(time_part[:, :, None], (HALF_SLOTS, time_pairs, PATCHES)),
                jnp.broadcast_to(side_part[None], (HALF_SLOTS, 2 * side_pairs, PATCHES)),
            ],
            axis=1,
        )

    cosine = full_table(jnp.cos(time_angle), jnp.cos(side_angle))
    sine = full_table(jnp.sin(time_angle), jnp.sin(side_angle))
    signal_scale, noise_scale, weight = plan(row_levels)
    weight_sum = PATCHES * jnp.sum(weight[:32])
    token_scales = jnp.concatenate([signal_scale[32::8], noise_scale[32::8]])
    loss_scales = jnp.stack([weight[32], 2.0 / clean.shape[1] * weight[32] / weight_sum])

    front_meta = after(front_meta, mod_rel, cosine, sine, token_scales)
    quarters = spread_frames(call_pick(front_meta, pieces))
    front_all, mid_all, hidden_frames, resid_in, *head_blocks, noisy_low, target, mod_own = (
        call_front(front_meta, token_scales, pieces, quarters, mod_rel, cosine, sine)
    )
    hidden_one = hidden_frames.reshape(4 * PATCHES, D)

    out_w = mid_all[:, :256]

    def exchange(blocks):
        return [blocks[0]] + [swap(blocks[k], "ctx", k) for k in (1, 2, 3)]

    head_in = exchange(head_blocks)
    mlp_shard = after(w_mlp.astype(bfloat), *head_in)
    mlp_w = lax.all_gather(mlp_shard, "ctx", axis=1, tiled=True)
    mixed_blocks, lse, mixed = call_attend(attend_meta, head_in)
    mix_low = jnp.concatenate(reorder_four(exchange(mixed_blocks), member), axis=0)

    def project(left, right, dims):
        pairs = []
        for base in (2 * PATCHES, 0):
            part = lax.dot_general(
                left[:, base : base + 2 * PATCHES], right, dims, preferred_element_type=single
            )
            pairs.append((part[:PATCHES], part[PATCHES:].astype(bfloat)))
        return pairs[1], pairs[0]

    near, far = project(mix_low, out_w, (((0,), (1,)), ((), ())))
    attn_out, resid_mid, hidden_own = row_call(
        middle_kernel,
        "middle",
        (frame_f32(), frame_f32(), frame_low()),
        *sum_frames(near, sum_across(far)),
        resid_in,
        mod_own,
    )
    hidden_list = spread_frames(hidden_own)
    wide = (2 * PATCHES, w_mlp.shape[2])
    wide_low = jax.ShapeDtypeStruct(wide, bfloat)
    near = call_mlp(mlp_kernel, "mlp", (wide_low, wide_low), *hidden_list[:2], mlp_w)
    far = call_mlp(mlp_kernel, "mlp", (wide_low, wide_low), *hidden_list[2:], mlp_w)
    active, slope = (near[2], far[2]), (near[3], far[3])
    grad_own, grad_three, head_rows, grad_gate_two, error_part = row_call(
        loss_kernel,
        "loss",
        (
            frame_low(),
            frame_f32(),
            jax.ShapeDtypeStruct((136, D), single),
            jax.ShapeDtypeStruct((1, D), single),
            jax.ShapeDtypeStruct((1, 128), single),
        ),
        loss_scales,
        *sum_frames(near[:2], sum_across(far)),
        resid_mid,
        mod_own,
        mid_all,
        target,
        smem=1,
    )
    grad_list = spread_frames(grad_own)
    near = call_mlp(mlp_back_kernel, "mlp_back", (wide_low,), *grad_list[:2], mlp_w, slope[0])
    far = call_mlp(mlp_back_kernel, "mlp_back", (wide_low,), *grad_list[2:], mlp_w, slope[1])
    across = sum_across(far)
    weight_grad = call_weight_grad(
        hidden_list, grad_list, (near[2], after(far[2], across)), active
    )
    scattered = lax.psum_scatter(weight_grad, "ctx", scatter_dimension=0, tiled=True)
    grad_low, grad_mid, rows_two = row_call(
        second_kernel,
        "second",
        (frame_low(), frame_f32(), jax.ShapeDtypeStruct((3, D), single)),
        *sum_frames(near[:2], across),
        after(resid_mid, weight_grad),
        mod_own,
        grad_three,
        attn_out,
    )
    back_list = spread_frames(grad_low)
    grad_attn_low = jnp.concatenate(back_list, axis=0)
    grad_mix = lax.dot_general(
        out_w, grad_attn_low, (((0,), (1,)), ((), ())), preferred_element_type=single
    ).astype(bfloat)
    grad_blocks = reorder_four([grad_mix[HD * k : HD * k + HD] for k in range(4)], member)
    grad_in_blocks = exchange(grad_blocks)
    out_held, out_away = call_head_grad(device, mix_low, after(grad_attn_low, grad_mix))
    out_came = swap(out_away, "ctx", 1)
    grad_in_blocks[0] = after(grad_in_blocks[0], out_held)
    back_blocks = call_attend_back(attend_meta, head_in, grad_in_blocks, lse, mixed, cosine, sine)
    grad_qkv, *parts = call_qkv_back(
        attend_meta, exchange(back_blocks), after(front_all, out_came)
    )
    near, far = parts[:2], parts[2:]
    across = sum_across(far)
    first_terms = sum_frames(near, across)
    qkv_held, qkv_away = call_head_grad(device, after(grad_qkv, across), hidden_one)
    qkv_came = swap(qkv_away, "ctx", 1)
    group_f32 = jax.ShapeDtypeStruct((IO_ROWS, D), single)
    group_low = jax.ShapeDtypeStruct((IO_ROWS, D), bfloat)
    mod_rows, *io_parts, _ = row_call(
        first_kernel,
        "first",
        (
            jax.ShapeDtypeStruct((MOD_ROWS, 128), bfloat),
            group_f32,
            group_low,
            group_f32,
            group_low,
            jax.ShapeDtypeStruct((4 * IO_ROWS, D), single),
        ),
        device,
        *first_terms,
        after(resid_in, qkv_held),
        mod_own,
        grad_mid,
        noisy_low,
        rows_two,
        grad_gate_two,
        head_rows,
        smem=1,
    )
    io_held, io_away = row_call(
        side_kernel,
        "side",
        (
            jax.ShapeDtypeStruct((4, IO_ROWS, 128), single),
            jax.ShapeDtypeStruct((4 * IO_ROWS + MOD_ROWS, 128), bfloat),
        ),
        device,
        *sum_frames(io_parts[:2], sum_across(io_parts[2:])),
        mod_rows,
        smem=1,
    )
    z_rows = jax.ShapeDtypeStruct((ATTN_ROWS + IO_ROWS + 2 * MOD_ROWS, 128), bfloat)
    qkv_own, io_own, *z_pieces = row_call(
        merge_kernel,
        "merge",
        (
            jax.ShapeDtypeStruct((ATTN_ROWS, 128), single),
            jax.ShapeDtypeStruct((IO_ROWS, 128), single),
            jax.ShapeDtypeStruct((2 * MOD_ROWS, 128), bfloat),
            z_rows,
            z_rows,
            z_rows,
        ),
        device,
        qkv_held,
        qkv_came,
        out_held,
        out_came,
        io_held,
        swap(io_away, "ctx", 1),
        mod_rows,
        smem=1,
    )
    red_attn, spread, matrix_sq = row_call(
        finish_kernel,
        "finish",
        (
            jax.ShapeDtypeStruct((4, 128, 256), single),
            jax.ShapeDtypeStruct((8 * MOD_ROWS + 2 * IO_ROWS, 128), bfloat),
            jax.ShapeDtypeStruct((1, 128), single),
        ),
        qkv_own,
        io_own,
        z_pieces[0],
        *(swap(piece, "ctx", 2 * bit) for bit, piece in zip((1, 2, 3), z_pieces[1:])),
        scattered,
    )
    grad_mod_w, red_vec, io_grad, mod_sq = call_mod_grad(
        device, cond_relative, spread_frames(spread)
    )
    red_io = io_grad[: 2 * 128].reshape(2, 128, 128)
    own_sq = matrix_sq + jnp.where(tp_index == 0, mod_sq, 0.0)
    sums = sum_all(jnp.where(jnp.arange(128)[None, :] < 64, own_sq, error_part))
    count = step[0].astype(single)
    fixes = jnp.stack([1.0 / (1.0 - beta_one**count), 1.0 / (1.0 - beta_two**count)])
    hidden_width = w_mlp.shape[2]
    red_mlp = jnp.stack(
        [scattered[:, :hidden_width], scattered[:, hidden_width : 2 * hidden_width]]
    )
    updated = call_adam(
        fixes,
        sums,
        (
            (w_attn, m_attn, v_attn, red_attn),
            (w_mlp, m_mlp, v_mlp, red_mlp),
            (w_mod, m_mod, v_mod, grad_mod_w),
        ),
        (w_io, m_io, v_io, red_io),
        (vectors, m_vec, v_vec, red_vec),
    )
    return (updated[21][1, 64] / weight_sum, updated[21][0, 0], *updated[:21])


def solution(mesh):
    halves = mesh.shape["ctx"] == 8 and mesh.shape["tp"] == 4
    placed = (
        P("ctx", None),
        P("ctx", None),
        P(),
        P(),
        P(),
        P(),
        P(None, "ctx", "tp"),
        P(None, "ctx", "tp"),
        P(None, "ctx", "tp"),
        P(None, "ctx", "tp"),
        P(None, "ctx", "tp"),
        P(None, "ctx", "tp"),
        P("ctx", None),
        P("ctx", None),
        P("ctx", None),
        P(None, None, "ctx"),
        P(None, None, "ctx"),
        P(None, None, "ctx"),
        P(None, "ctx"),
        P(None, "ctx"),
        P(None, "ctx"),
    )
    return jax.shard_map(
        shards_halves if halves else shards,
        mesh=mesh,
        in_specs=placed,
        out_specs=(
            P(),
            P(),
            P(None, "ctx", "tp"),
            P(None, "ctx", "tp"),
            P(None, "ctx", "tp"),
            P(None, "ctx", "tp"),
            P(None, "ctx", "tp"),
            P(None, "ctx", "tp"),
            P(None, "ctx", "tp"),
            P(None, "ctx", "tp"),
            P("ctx", None),
            P("ctx", None),
            P("ctx", None),
            P("ctx", None),
            P(None, None, "ctx"),
            P(None, None, "ctx"),
            P(None, "ctx"),
            P(None, "ctx"),
            P(None, None, "ctx"),
            P(None, "ctx"),
            P(None, "ctx"),
            P(None, "ctx"),
            P(None, "ctx"),
        ),
        check_vma=False,
    )
```

```python
import functools
import math

import jax
import jax.numpy as jnp
from jax import lax
from jax.experimental import pallas as pl
from jax.experimental.pallas import tpu as pltpu
from jax.sharding import PartitionSpec as P

D = 1024
HD = 64
GRID = 16
PATCHES = 256
LEVELS = 1000


ln_eps = 1e-06
snr_limit = 5.0
clip_limit = 0.001
beta_one = 0.9
beta_two = 0.999
adam_eps = 1e-08
rate_matrix = 0.05
rate_vector = 0.3
decay_rate = 0.1
neg_large = -1e30


def clip_starts(frame_ids, lengths):
    clip_ends = jnp.cumsum(lengths)
    before = (clip_ends[None, :] <= frame_ids[:, None]).astype(jnp.int32)
    return jnp.sum(before * lengths[None, :], axis=1)


def plan(levels):
    fraction = (levels.astype(jnp.float32) + 1.0) / (LEVELS + 1.0)
    signal_scale = jnp.cos(0.5 * math.pi * fraction)
    noise_scale = jnp.sin(0.5 * math.pi * fraction)
    snr_value = signal_scale * signal_scale / (noise_scale * noise_scale)
    weight = jnp.minimum(snr_value, snr_limit) / (snr_value + 1.0)
    return (signal_scale, noise_scale, weight)


def condition(levels, width):
    half_dim = width // 2
    frequency = jnp.exp(-math.log(10000.0) * jnp.arange(half_dim, dtype=jnp.float32) / half_dim)
    angle_tab = levels.astype(jnp.float32)[:, None] * frequency[None, :]
    return jax.nn.silu(jnp.concatenate([jnp.cos(angle_tab), jnp.sin(angle_tab)], axis=1))


def rope_tables(time_pos, height_pos, width_pos, head_dim):
    pair_count = head_dim // 2
    time_pairs = head_dim // 8
    height_pairs = (pair_count - time_pairs) // 2
    width_pairs = pair_count - time_pairs - height_pairs

    def angles(position, count):
        frequency = 10000.0 ** (-jnp.arange(count, dtype=jnp.float32) / count)
        return position.astype(jnp.float32)[:, None] * frequency[None, :]

    angle_tab = jnp.concatenate(
        [
            angles(time_pos, time_pairs),
            angles(height_pos, height_pairs),
            angles(width_pos, width_pairs),
        ],
        axis=1,
    )
    return (jnp.cos(angle_tab), jnp.sin(angle_tab))


def rotate(values, cosine, sine):
    half_dim = values.shape[-1] // 2
    first_half = values[..., :half_dim]
    second_half = values[..., half_dim:]
    cosine = cosine[:, None, :]
    sine = sine[:, None, :]
    return jnp.concatenate(
        [first_half * cosine - second_half * sine, second_half * cosine + first_half * sine],
        axis=-1,
    )


def rotate_back(grads, cosine, sine):
    half_dim = grads.shape[-1] // 2
    first_half = grads[..., :half_dim]
    second_half = grads[..., half_dim:]
    cosine = cosine[:, None, :]
    sine = sine[:, None, :]
    return jnp.concatenate(
        [first_half * cosine + second_half * sine, second_half * cosine - first_half * sine],
        axis=-1,
    )


def layer_norm(values):
    centred = values - jnp.mean(values, axis=-1, keepdims=True)
    inv_std = lax.rsqrt(jnp.mean(centred * centred, axis=-1, keepdims=True) + ln_eps)
    return (centred * inv_std, inv_std)


def norm_back(grad_in, normed, inv_std):
    mean_grad = jnp.mean(grad_in, axis=-1, keepdims=True)
    mean_proj = jnp.mean(grad_in * normed, axis=-1, keepdims=True)
    return inv_std * (grad_in - mean_grad - normed * mean_proj)


def gelu_slope(values):
    return 0.5 * (1.0 + lax.erf(values / math.sqrt(2.0))) + values * jnp.exp(
        -0.5 * values * values
    ) / math.sqrt(2.0 * math.pi)


def stretch_mask(query_stretch, key_stretch, stretch_frames, lengths):
    offsets = jnp.arange(stretch_frames, dtype=jnp.int32)
    query_frames = query_stretch * stretch_frames + offsets
    key_frames = key_stretch * stretch_frames + offsets
    starts = clip_starts(query_frames, lengths)
    return (key_frames[None, :] <= query_frames[:, None]) & (key_frames[None, :] >= starts[:, None])


def expand_mask(allowed):
    return jnp.repeat(jnp.repeat(allowed, PATCHES, axis=0), PATCHES, axis=1)


def online_step(current, query_block, key_block, value_block, keep, scale):
    run_max, run_sum, run_acc = current
    scores = (
        jnp.einsum("qhe,khe->hqk", query_block, key_block, preferred_element_type=jnp.float32)
        * scale
    )
    scores = jnp.where(keep[None], scores, neg_large)
    new_max = jnp.maximum(run_max, jnp.max(scores, axis=-1))
    probs = jnp.where(keep[None], jnp.exp(scores - new_max[..., None]), 0.0)
    shrink = jnp.exp(run_max - new_max)
    run_sum = run_sum * shrink + jnp.sum(probs, axis=-1)
    added = jnp.einsum(
        "hqk,khe->qhe", probs.astype(jnp.bfloat16), value_block, preferred_element_type=jnp.float32
    )
    run_acc = run_acc * jnp.transpose(shrink)[:, :, None] + added
    return (new_max, run_sum, run_acc)


def pair_grads(
    query_block, grad_block, lse_block, delta_block, key_block, value_block, keep, scale
):
    scores = (
        jnp.einsum("qhe,khe->hqk", query_block, key_block, preferred_element_type=jnp.float32)
        * scale
    )
    probs = jnp.where(keep[None], jnp.exp(scores - lse_block[..., None]), 0.0)
    grad_probs = jnp.einsum(
        "qhe,khe->hqk", grad_block, value_block, preferred_element_type=jnp.float32
    )
    grad_scores = (probs * (grad_probs - delta_block[..., None])).astype(jnp.bfloat16)
    grad_query = (
        jnp.einsum("hqk,khe->qhe", grad_scores, key_block, preferred_element_type=jnp.float32)
        * scale
    )
    grad_key = (
        jnp.einsum("hqk,qhe->khe", grad_scores, query_block, preferred_element_type=jnp.float32)
        * scale
    )
    grad_value = jnp.einsum(
        "hqk,qhe->khe", probs.astype(jnp.bfloat16), grad_block, preferred_element_type=jnp.float32
    )
    return (grad_query, grad_key, grad_value)


def adam(weight_now, first_mom, second_mom, grad, factor, count, rate, decay):
    grad = grad * factor
    first_mom = beta_one * first_mom + (1.0 - beta_one) * grad
    second_mom = beta_two * second_mom + (1.0 - beta_two) * grad * grad
    first_hat = first_mom / (1.0 - beta_one**count)
    second_hat = second_mom / (1.0 - beta_two**count)
    updated = weight_now - rate * (
        first_hat / (jnp.sqrt(second_hat) + adam_eps) + decay * weight_now
    )
    return (updated, first_mom, second_mom, updated.astype(jnp.bfloat16))


def shards(
    clean,
    noise,
    levels,
    lengths,
    order,
    step,
    w_attn,
    m_attn,
    v_attn,
    w_mlp,
    m_mlp,
    v_mlp,
    w_mod,
    m_mod,
    v_mod,
    w_io,
    m_io,
    v_io,
    vectors,
    m_vec,
    v_vec,
):
    ctx_count = lax.axis_size("ctx")
    ctx_index = lax.axis_index("ctx")
    tp_index = lax.axis_index("tp")
    tok_rows = clean.shape[0]
    feat_dim = clean.shape[1]
    frames_dev = tok_rows // PATCHES
    stretch_frames = frames_dev // 2
    stretch_rows = stretch_frames * PATCHES
    scale = HD ** (-0.5)
    bfloat = jnp.bfloat16
    single = jnp.float32
    attn_w, mlp_w, mod_w, io_w, vec_low = (
        lax.all_gather(w_attn.astype(bfloat), "ctx", axis=1, tiled=True),
        lax.all_gather(w_mlp.astype(bfloat), "ctx", axis=1, tiled=True),
        lax.all_gather(w_mod.astype(bfloat), "ctx", axis=0, tiled=True),
        lax.all_gather(w_io.astype(bfloat), "ctx", axis=2, tiled=True),
        lax.all_gather(vectors.astype(bfloat), "ctx", axis=1, tiled=True),
    )
    vec_w = vec_low.astype(single)
    local_width = attn_w.shape[2]
    heads_dev = local_width // HD
    frame_count = levels.shape[0]
    local_stretches = lax.dynamic_slice_in_dim(order, 2 * ctx_index, 2, 0)
    frame_ids = (
        local_stretches[:, None] * stretch_frames
        + jnp.arange(stretch_frames, dtype=jnp.int32)[None, :]
    ).reshape(frames_dev)
    table_hit = frame_ids[:, None] == jnp.arange(frame_count, dtype=jnp.int32)[None, :]
    frame_levels = jnp.sum(jnp.where(table_hit, levels[None, :], 0), axis=1)
    starts = clip_starts(frame_ids, lengths)
    signal_scale, noise_scale, weight = plan(frame_levels)
    signal_col = signal_scale[:, None, None]
    noise_col = noise_scale[:, None, None]
    clean_full = clean.astype(single).reshape(frames_dev, PATCHES, feat_dim)
    noise_full = noise.astype(single).reshape(frames_dev, PATCHES, feat_dim)
    noisy = signal_col * clean_full + noise_col * noise_full
    target = signal_col * noise_full - noise_col * clean_full
    noisy_low = noisy.reshape(tok_rows, feat_dim).astype(bfloat)
    embedded = jnp.dot(noisy_low, io_w[0], preferred_element_type=single) + vec_w[6]
    cond_low = condition(frame_levels, D).astype(bfloat)
    modulate = (
        jnp.dot(cond_low, mod_w, preferred_element_type=single) + vec_w[:6].reshape(6 * D)
    ).reshape(frames_dev, 6, 1, D)
    patch_ids = jnp.arange(PATCHES, dtype=jnp.int32)
    time_pos = jnp.repeat(frame_ids - starts, PATCHES)
    height_pos = jnp.tile(patch_ids // GRID, frames_dev)
    width_pos = jnp.tile(patch_ids % GRID, frames_dev)
    cosine, sine = rope_tables(time_pos, height_pos, width_pos, HD)
    resid_in = embedded.reshape(frames_dev, PATCHES, D)
    normed_one, inv_one = layer_norm(resid_in)
    hidden_one = (
        (normed_one * (1.0 + modulate[:, 1]) + modulate[:, 0]).reshape(tok_rows, D).astype(bfloat)
    )
    query_pre = jnp.dot(hidden_one, attn_w[0], preferred_element_type=single).reshape(
        tok_rows, heads_dev, HD
    )
    key_pre = jnp.dot(hidden_one, attn_w[1], preferred_element_type=single).reshape(
        tok_rows, heads_dev, HD
    )
    query_low = rotate(query_pre, cosine, sine).astype(bfloat)
    key_low = rotate(key_pre, cosine, sine).astype(bfloat)
    value_low = (
        jnp.dot(hidden_one, attn_w[2], preferred_element_type=single)
        .astype(bfloat)
        .reshape(tok_rows, heads_dev, HD)
    )
    query_stretches = query_low.reshape(2, stretch_rows, heads_dev, HD)
    init_state = (
        jnp.full((2, heads_dev, stretch_rows), neg_large, single),
        jnp.zeros((2, heads_dev, stretch_rows), single),
        jnp.zeros((2, stretch_rows, heads_dev, HD), single),
    )
    key_flat = key_low.reshape(tok_rows, local_width)
    value_flat = value_low.reshape(tok_rows, local_width)
    carry_state = init_state
    key_piece = lax.all_gather(key_flat, "ctx", axis=0, tiled=True)
    value_piece = lax.all_gather(value_flat, "ctx", axis=0, tiled=True)

    def per_stretch(block_num, carry_state):
        key_block = lax.dynamic_slice_in_dim(
            key_piece, block_num * stretch_rows, stretch_rows, 0
        ).reshape(stretch_rows, heads_dev, HD)
        value_block = lax.dynamic_slice_in_dim(
            value_piece, block_num * stretch_rows, stretch_rows, 0
        ).reshape(stretch_rows, heads_dev, HD)
        key_stretch = lax.dynamic_index_in_dim(order, block_num, 0, keepdims=False)
        updated = []
        for half_num in range(2):
            allowed = stretch_mask(local_stretches[half_num], key_stretch, stretch_frames, lengths)
            current = (carry_state[0][half_num], carry_state[1][half_num], carry_state[2][half_num])
            current = lax.cond(
                jnp.any(allowed),
                lambda cur, keep_mask: online_step(
                    cur,
                    query_stretches[half_num],
                    key_block,
                    value_block,
                    expand_mask(keep_mask),
                    scale,
                ),
                lambda cur, keep_mask: cur,
                current,
                allowed,
            )
            updated.append(current)
        return tuple((jnp.stack([updated[0][member], updated[1][member]]) for member in range(3)))

    run_max, run_sum, run_acc = lax.fori_loop(
        0, key_piece.shape[0] // stretch_rows, per_stretch, carry_state
    )
    mix_rows = (run_acc / jnp.transpose(run_sum, (0, 2, 1))[..., None]).reshape(
        tok_rows, heads_dev, HD
    )
    lse_stretches = run_max + jnp.log(run_sum)
    mix_low = mix_rows.reshape(tok_rows, local_width).astype(bfloat)
    attn_out = lax.psum(
        jnp.einsum("rh,dh->rd", mix_low, attn_w[3], preferred_element_type=single).astype(
            jnp.bfloat16
        ),
        "tp",
    ).astype(jnp.float32)
    attn_full = attn_out.reshape(frames_dev, PATCHES, D)
    resid_mid = resid_in + modulate[:, 2] * attn_full
    normed_two, inv_two = layer_norm(resid_mid)
    hidden_two = (
        (normed_two * (1.0 + modulate[:, 4]) + modulate[:, 3]).reshape(tok_rows, D).astype(bfloat)
    )
    upward = jnp.dot(hidden_two, mlp_w[0], preferred_element_type=single)
    activ_low = jax.nn.gelu(upward, approximate=False).astype(bfloat)
    mlp_out = lax.psum(
        jnp.einsum("rf,df->rd", activ_low, mlp_w[1], preferred_element_type=single).astype(
            jnp.bfloat16
        ),
        "tp",
    ).astype(jnp.float32)
    mlp_full = mlp_out.reshape(frames_dev, PATCHES, D)
    resid_out = resid_mid + modulate[:, 5] * mlp_full
    normed_three, inv_three = layer_norm(resid_out)
    final_low = (normed_three * vec_w[7]).reshape(tok_rows, D).astype(bfloat)
    pred = jnp.einsum("rd,pd->rp", final_low, io_w[1], preferred_element_type=single)
    diff = pred.reshape(frames_dev, PATCHES, feat_dim) - target
    error = jnp.mean(diff * diff, axis=2)
    weight_sum, error_sum = lax.psum(
        (PATCHES * jnp.sum(weight), jnp.sum(weight[:, None] * error)), "ctx"
    )
    loss_value = error_sum / weight_sum
    grad_pred = (
        (2.0 / feat_dim * weight[:, None, None] * diff / weight_sum)
        .reshape(tok_rows, feat_dim)
        .astype(bfloat)
    )
    grad_head = jnp.einsum("rp,rd->pd", grad_pred, final_low, preferred_element_type=single)
    grad_final = jnp.einsum("rp,pd->rd", grad_pred, io_w[1], preferred_element_type=single).reshape(
        frames_dev, PATCHES, D
    )
    grad_gain = jnp.sum(grad_final * normed_three, axis=(0, 1))
    grad_three = norm_back(grad_final * vec_w[7], normed_three, inv_three)
    grad_mlp_low = (modulate[:, 5] * grad_three).reshape(tok_rows, D).astype(bfloat)
    grad_gate_two = jnp.sum(grad_three * mlp_full, axis=1)
    grad_activ = jnp.einsum("rd,df->rf", grad_mlp_low, mlp_w[1], preferred_element_type=single)
    grad_down = jnp.einsum("rd,rf->df", grad_mlp_low, activ_low, preferred_element_type=single)
    grad_up_low = (grad_activ * gelu_slope(upward)).astype(bfloat)
    grad_up = jnp.einsum("rd,rf->df", hidden_two, grad_up_low, preferred_element_type=single)
    grad_hidden_two = lax.psum(
        jnp.einsum("rf,df->rd", grad_up_low, mlp_w[0], preferred_element_type=single).astype(
            jnp.bfloat16
        ),
        "tp",
    ).astype(jnp.float32)
    grad_hidden_two = grad_hidden_two.reshape(frames_dev, PATCHES, D)
    grad_shift_two = jnp.sum(grad_hidden_two, axis=1)
    grad_scale_two = jnp.sum(grad_hidden_two * normed_two, axis=1)
    grad_mid = grad_three + norm_back(grad_hidden_two * (1.0 + modulate[:, 4]), normed_two, inv_two)
    grad_attn_low = (modulate[:, 2] * grad_mid).reshape(tok_rows, D).astype(bfloat)
    grad_gate_one = jnp.sum(grad_mid * attn_full, axis=1)
    grad_outproj = jnp.einsum("rd,rh->dh", grad_attn_low, mix_low, preferred_element_type=single)
    grad_mix_low = jnp.einsum(
        "rd,dh->rh", grad_attn_low, attn_w[3], preferred_element_type=single
    ).astype(bfloat)
    delta_rows = jnp.sum(
        grad_mix_low.astype(single).reshape(tok_rows, heads_dev, HD) * mix_rows, axis=2
    )
    grad_stretches = grad_mix_low.reshape(2, stretch_rows, heads_dev, HD)
    delta_stretches = jnp.transpose(delta_rows.reshape(2, stretch_rows, heads_dev), (0, 2, 1))

    def span_back(key_block, value_block, key_stretch, grad_query_acc):
        key_sum = jnp.zeros((stretch_rows, heads_dev, HD), single)
        value_sum = jnp.zeros((stretch_rows, heads_dev, HD), single)
        query_parts = []
        for half_num in range(2):
            allowed = stretch_mask(local_stretches[half_num], key_stretch, stretch_frames, lengths)
            result = lax.cond(
                jnp.any(allowed),
                lambda keep_mask: pair_grads(
                    query_stretches[half_num],
                    grad_stretches[half_num],
                    lse_stretches[half_num],
                    delta_stretches[half_num],
                    key_block,
                    value_block,
                    expand_mask(keep_mask),
                    scale,
                ),
                lambda keep_mask: (jnp.zeros((stretch_rows, heads_dev, HD), single),) * 3,
                allowed,
            )
            query_parts.append(grad_query_acc[half_num] + result[0])
            key_sum = key_sum + result[1]
            value_sum = value_sum + result[2]
        return (
            jnp.stack(query_parts),
            key_sum.reshape(stretch_rows, local_width),
            value_sum.reshape(stretch_rows, local_width),
        )

    init_back = (
        jnp.zeros((2, stretch_rows, heads_dev, HD), single),
        jnp.zeros((ctx_count * tok_rows, local_width), single),
        jnp.zeros((ctx_count * tok_rows, local_width), single),
    )
    carry_state = init_back
    fold_key_piece = lax.all_gather(key_flat, "ctx", axis=0, tiled=True)
    fold_value_piece = lax.all_gather(value_flat, "ctx", axis=0, tiled=True)

    def per_stretch(block_num, carry_state):
        grad_query_acc, grad_keys_all, grad_values_all = carry_state
        key_block = lax.dynamic_slice_in_dim(
            fold_key_piece, block_num * stretch_rows, stretch_rows, 0
        ).reshape(stretch_rows, heads_dev, HD)
        value_block = lax.dynamic_slice_in_dim(
            fold_value_piece, block_num * stretch_rows, stretch_rows, 0
        ).reshape(stretch_rows, heads_dev, HD)
        key_stretch = lax.dynamic_index_in_dim(order, block_num, 0, keepdims=False)
        grad_query_acc, key_sum, value_sum = span_back(
            key_block, value_block, key_stretch, grad_query_acc
        )
        place = block_num * stretch_rows
        grad_keys_all = lax.dynamic_update_slice_in_dim(grad_keys_all, key_sum, place, 0)
        grad_values_all = lax.dynamic_update_slice_in_dim(grad_values_all, value_sum, place, 0)
        return (grad_query_acc, grad_keys_all, grad_values_all)

    grad_query_acc, grad_keys_all, grad_values_all = lax.fori_loop(
        0, fold_key_piece.shape[0] // stretch_rows, per_stretch, carry_state
    )
    grad_keys, grad_values = (
        lax.psum_scatter(
            grad_keys_all.astype(jnp.bfloat16), "ctx", scatter_dimension=0, tiled=True
        ).astype(jnp.float32),
        lax.psum_scatter(
            grad_values_all.astype(jnp.bfloat16), "ctx", scatter_dimension=0, tiled=True
        ).astype(jnp.float32),
    )
    grad_query = grad_query_acc.reshape(tok_rows, local_width)
    query_back = (
        rotate_back(grad_query.reshape(tok_rows, heads_dev, HD), cosine, sine)
        .reshape(tok_rows, local_width)
        .astype(bfloat)
    )
    key_back = (
        rotate_back(grad_keys.reshape(tok_rows, heads_dev, HD), cosine, sine)
        .reshape(tok_rows, local_width)
        .astype(bfloat)
    )
    value_back = grad_values.astype(bfloat)
    grad_wq = jnp.einsum("rd,rh->dh", hidden_one, query_back, preferred_element_type=single)
    grad_wk = jnp.einsum("rd,rh->dh", hidden_one, key_back, preferred_element_type=single)
    grad_wv = jnp.einsum("rd,rh->dh", hidden_one, value_back, preferred_element_type=single)
    partial_one = (
        jnp.einsum("rh,dh->rd", query_back, attn_w[0], preferred_element_type=single)
        + jnp.einsum("rh,dh->rd", key_back, attn_w[1], preferred_element_type=single)
        + jnp.einsum("rh,dh->rd", value_back, attn_w[2], preferred_element_type=single)
    )
    grad_hidden_one = (
        lax.psum(partial_one.astype(jnp.bfloat16), "tp")
        .astype(jnp.float32)
        .reshape(frames_dev, PATCHES, D)
    )
    grad_shift_one = jnp.sum(grad_hidden_one, axis=1)
    grad_scale_one = jnp.sum(grad_hidden_one * normed_one, axis=1)
    grad_in = grad_mid + norm_back(grad_hidden_one * (1.0 + modulate[:, 1]), normed_one, inv_one)
    grad_mod = jnp.stack(
        [
            grad_shift_one,
            grad_scale_one,
            grad_gate_one,
            grad_shift_two,
            grad_scale_two,
            grad_gate_two,
        ],
        axis=1,
    )
    grad_mod_w = jnp.einsum(
        "fd,fc->dc",
        cond_low,
        grad_mod.reshape(frames_dev, 6 * D).astype(bfloat),
        preferred_element_type=single,
    )
    grad_in_low = grad_in.reshape(tok_rows, D).astype(bfloat)
    grad_embed = jnp.einsum("rp,rd->pd", noisy_low, grad_in_low, preferred_element_type=single)
    grad_vec = jnp.concatenate(
        [jnp.sum(grad_mod, axis=0), jnp.sum(grad_in, axis=(0, 1))[None], grad_gain[None]], axis=0
    )
    grad_attn = jnp.stack([grad_wq, grad_wk, grad_wv, grad_outproj])
    grad_mlp = jnp.stack([grad_up, grad_down])
    grad_io = jnp.stack([grad_embed, grad_head])
    red_attn, red_mlp, red_mod, red_io, red_vec = (
        lax.psum_scatter(
            grad_attn.astype(jnp.bfloat16), "ctx", scatter_dimension=1, tiled=True
        ).astype(jnp.float32),
        lax.psum_scatter(
            grad_mlp.astype(jnp.bfloat16), "ctx", scatter_dimension=1, tiled=True
        ).astype(jnp.float32),
        lax.psum_scatter(
            grad_mod_w.astype(jnp.bfloat16), "ctx", scatter_dimension=0, tiled=True
        ).astype(jnp.float32),
        lax.psum_scatter(
            grad_io.astype(jnp.bfloat16), "ctx", scatter_dimension=2, tiled=True
        ).astype(jnp.float32),
        lax.psum_scatter(
            grad_vec.astype(jnp.bfloat16), "ctx", scatter_dimension=1, tiled=True
        ).astype(jnp.float32),
    )
    shared_sq = jnp.sum(red_mod * red_mod) + jnp.sum(red_io * red_io) + jnp.sum(red_vec * red_vec)
    own_sq = (
        jnp.sum(red_attn * red_attn)
        + jnp.sum(red_mlp * red_mlp)
        + jnp.where(tp_index == 0, shared_sq, 0.0)
    )
    grad_norm = jnp.sqrt(lax.psum(own_sq, ("ctx", "tp")))
    factor = jnp.minimum(1.0, clip_limit / (grad_norm + 1e-06))
    count = step[0].astype(single)
    attn_new = adam(w_attn, m_attn, v_attn, red_attn, factor, count, rate_matrix, decay_rate)
    mlp_new = adam(w_mlp, m_mlp, v_mlp, red_mlp, factor, count, rate_matrix, decay_rate)
    mod_new = adam(w_mod, m_mod, v_mod, red_mod, factor, count, rate_matrix, decay_rate)
    io_new = adam(w_io, m_io, v_io, red_io, factor, count, rate_matrix, decay_rate)
    vec_new = adam(vectors, m_vec, v_vec, red_vec, factor, count, rate_vector, 0.0)
    return (
        loss_value,
        grad_norm,
        attn_new[0],
        attn_new[1],
        attn_new[2],
        attn_new[3],
        mlp_new[0],
        mlp_new[1],
        mlp_new[2],
        mlp_new[3],
        mod_new[0],
        mod_new[1],
        mod_new[2],
        mod_new[3],
        io_new[0],
        io_new[1],
        io_new[2][0],
        io_new[2][1],
        io_new[3],
        vec_new[0],
        vec_new[1],
        vec_new[2],
        vec_new[3],
    )


RING = (0, 1, 3, 5, 7, 6, 4, 2)
RING_NEXT = tuple((RING[i], RING[(i + 1) % 8]) for i in range(8))
RING_PREV = tuple((b, a) for a, b in RING_NEXT)
HALF_SLOTS = 16
QKV_ROWS = 768
ATTN_ROWS = 1024
FRONT_ROWS = 912
TOKEN_ROWS = 512
IO_ROWS = 80
MOD_ROWS = 48
RING_ROWS = TOKEN_ROWS + FRONT_ROWS + 384
NT = (((1,), (1,)), ((), ()))
TN = (((0,), (0,)), ((), ()))


def swap(values, axis, bit):
    size = 8 if axis == "ctx" else 4
    return lax.ppermute(values, axis, [(i, i ^ bit) for i in range(size)])


def after(values, *others):
    return lax.optimization_barrier((values,) + others)[0]


def ring_gather(shard):
    half = shard.shape[0] // 2
    ahead = [shard]
    behind = [shard]
    for _ in range(3):
        ahead.append(lax.ppermute(ahead[-1], "ctx", RING_NEXT))
        behind.append(lax.ppermute(behind[-1], "ctx", RING_PREV))
    first = lax.ppermute(ahead[-1][:half], "ctx", RING_NEXT)
    second = lax.ppermute(behind[-1][half:], "ctx", RING_PREV)
    return ahead + behind[1:] + [jnp.concatenate([first, second], axis=0)]


def reduce_blocks(blocks, ctx_index, wire):
    return reduce_along_z(reduce_along_x(blocks, ctx_index, wire), ctx_index, wire)


def reduce_along_x(blocks, ctx_index, wire):
    x = ctx_index % 2
    pairs = blocks.reshape((4, 2) + blocks.shape[1:])
    first, second = pairs[:, 0], pairs[:, 1]
    even = x == 0
    away = jnp.where(even, second, first).astype(wire)
    return jnp.where(even, first, second) + swap(away, "ctx", 1).astype(jnp.float32)


def pieces_along_z(held, ctx_index, wire):
    z = ctx_index // 2
    low = held.astype(wire)
    came = []
    for bit in (1, 2, 3):
        piece = lax.dynamic_index_in_dim(low, z ^ bit, 0, keepdims=False)
        came.append(swap(piece, "ctx", 2 * bit))
    return lax.dynamic_index_in_dim(held, z, 0, keepdims=False), came


def reduce_along_z(held, ctx_index, wire):
    total, came = pieces_along_z(held, ctx_index, wire)
    for piece in came:
        total = total + piece.astype(jnp.float32)
    return total


def spread_frames(own):
    core = swap(own, "tp", 1)
    across = swap(own, "tp", 2)
    return [own, core, across, swap(across, "tp", 1)]


def sum_across(far):
    return (far[0] + swap(far[1], "tp", 1).astype(jnp.float32)).astype(jnp.bfloat16)


def sum_frames(near, across):
    return near[0], swap(near[1], "tp", 1), swap(across, "tp", 2)


def reorder_four(items, index):
    low_bit = (index & 1) == 1
    high_bit = (index & 2) == 2
    once = [jnp.where(low_bit, items[k ^ 1], items[k]) for k in range(4)]
    return [jnp.where(high_bit, once[k ^ 2], once[k]) for k in range(4)]


def sum_terms(values):
    values = values + swap(values, "ctx", 1)
    return [values] + [swap(values, "ctx", bit) for bit in (2, 4, 6)]


def prepare_kernel(meta, clean, noise, w_attn, w_io, vectors, ring):
    front = ring.at[TOKEN_ROWS:RING_ROWS]
    for frame in range(4):
        rows = pl.ds(pl.multiple_of(256 * frame + 64 * meta[1], 64), 64)
        ring[128 * frame : 128 * frame + 64, :] = clean[rows, :]
        ring[128 * frame + 64 : 128 * frame + 128, :] = noise[rows, :]
    for part in range(3):
        front[256 * part : 256 * part + 256, :] = w_attn[part].T.astype(jnp.bfloat16)
    base = QKV_ROWS
    front[base : base + 128, :] = w_io[0].astype(jnp.bfloat16)
    front[base + 128 : base + 144, :] = jnp.concatenate(
        [vectors[...], jnp.zeros((8, 128), jnp.float32)], axis=0
    ).astype(jnp.bfloat16)
    for part in range(2):
        base = FRONT_ROWS + 128 * part
        front[base : base + 128, :] = w_attn[3, :, 128 * part : 128 * part + 128].astype(
            jnp.bfloat16
        )
    front[FRONT_ROWS + 256 : FRONT_ROWS + 384, :] = w_io[1].T.astype(jnp.bfloat16)


def vmem_specs(count):
    return [pl.BlockSpec(memory_space=pltpu.VMEM)] * count


def smem_specs(count):
    return [pl.BlockSpec(memory_space=pltpu.SMEM)] * count


def call_prepare(device, clean, noise, w_attn, w_io, vectors):
    return pl.pallas_call(
        prepare_kernel,
        out_shape=jax.ShapeDtypeStruct((RING_ROWS, 128), jnp.bfloat16),
        in_specs=smem_specs(1) + vmem_specs(5),
        out_specs=vmem_specs(1)[0],
        name="prepare",
    )(device, clean, noise, w_attn, w_io, vectors)


def place_kernel(device, lengths, order, levels, front, attend, rows, inverse, stored, position, level):
    ctx, tp = device[0], device[1]
    frames, stretches, clips = levels.shape[0], order.shape[0], lengths.shape[0]
    per_stretch = frames // stretches
    half = frames // 2

    def per_stretch_place(place, carry):
        inverse[order[place]] = place
        return carry

    lax.fori_loop(0, stretches, per_stretch_place, 0)

    def per_frame(frame, counts):
        long_count, short_count = counts
        begin, start, length = jnp.int32(0), jnp.int32(0), jnp.int32(0)
        for clip in range(clips):
            size = lengths[clip]
            inside = (frame >= begin) & (frame < begin + size)
            start = jnp.where(inside, begin, start)
            length = jnp.where(inside, size, length)
            begin = begin + size
        is_long = length == half
        slot = jnp.where(is_long, long_count, half + short_count)
        stored[slot] = inverse[lax.div(frame, jnp.int32(per_stretch))] * per_stretch + lax.rem(
            frame, jnp.int32(per_stretch)
        )
        position[slot] = frame - start
        level[slot] = levels[frame]
        grown = is_long.astype(jnp.int32)
        return (long_count + grown, short_count + 1 - grown)

    lax.fori_loop(0, frames, per_frame, (jnp.int32(0), jnp.int32(0)))

    def where_on_ring(index):
        z, x = index >> 1, index & 1
        return jnp.where(x == 1, z + 1, (8 - z) & 7)

    mine = where_on_ring(ctx)
    member = ctx & 3
    for place, offset in enumerate((0, 7, 6, 5, 1, 2, 3, 4)):
        at = (mine + offset) & 7
        front[place] = jnp.where(
            at == 0, 0, jnp.where(at <= 4, 2 * at - 1, 2 * (8 - at))
        )
    for k in range(4):
        front[8 + k] = 4 * member + (tp ^ k)
        front[12 + k] = member ^ k
        at = stored[4 * ctx + (tp ^ k)]
        distance = (where_on_ring(at >> 2) - mine) & 7
        place = jnp.where(distance == 0, 0, jnp.where(distance <= 4, distance + 3, 8 - distance))
        front[16 + k] = place * 4 + (at & 3)
        front[20 + k] = tp ^ k
    attend[0] = member
    attend[1] = tp
    base = lax.div(ctx, jnp.int32(4)) * half

    def per_slot(slot, carry):
        attend[2 + slot] = position[base + slot]
        return carry

    lax.fori_loop(0, half, per_slot, 0)

    def per_row(row, carry):
        rows[row] = level[row]
        rows[frames + row] = level[4 * (ctx ^ (row & 7)) + (row >> 3)]
        return carry

    lax.fori_loop(0, frames, per_row, 0)
    for k in range(8):
        rows[2 * frames + k] = level[4 * ctx + (tp ^ (k & 3))]


def call_place(device, lengths, order, levels):
    frames = levels.shape[0]
    return pl.pallas_call(
        place_kernel,
        out_shape=(
            jax.ShapeDtypeStruct((24,), jnp.int32),
            jax.ShapeDtypeStruct((2 + frames // 2,), jnp.int32),
            jax.ShapeDtypeStruct((2 * frames + 8,), jnp.int32),
        ),
        in_specs=smem_specs(4),
        out_specs=smem_specs(3),
        scratch_shapes=[pltpu.SMEM((order.shape[0],), jnp.int32)]
        + [pltpu.SMEM((frames,), jnp.int32)] * 3,
        name="place",
    )(device, lengths, order, levels)


def pick_kernel(meta, *refs):
    out, sems = refs[8:]
    for frame in range(4):
        wanted = meta[16 + frame]
        for place in range(8):

            @pl.when((wanted >> 2) == place)
            def _():
                start = pl.multiple_of((wanted & 3) * 128, 128)
                pltpu.make_async_copy(
                    refs[place].at[pl.ds(start, 128), :],
                    out.at[128 * frame : 128 * frame + 128, :],
                    sems.at[frame],
                ).start()

    for frame in range(4):
        pltpu.make_async_copy(
            refs[0].at[0:128, :], out.at[128 * frame : 128 * frame + 128, :], sems.at[frame]
        ).wait()


def hbm_specs(count):
    return [pl.BlockSpec(memory_space=pltpu.HBM)] * count


def call_pick(meta, pieces):
    return pl.pallas_call(
        pick_kernel,
        out_shape=jax.ShapeDtypeStruct((TOKEN_ROWS, 128), jnp.bfloat16),
        in_specs=smem_specs(1) + hbm_specs(8),
        out_specs=vmem_specs(1)[0],
        scratch_shapes=[pltpu.SemaphoreType.DMA((4,))],
        compiler_params=pltpu.CompilerParams(vmem_limit_bytes=56 * 2**20),
        name="pick",
    )(meta, *pieces)


def centred_norm(values):
    centred = values - jnp.mean(values, axis=-1, keepdims=True)
    inv_std = lax.rsqrt(jnp.mean(centred * centred, axis=-1, keepdims=True) + ln_eps)
    return centred * inv_std, inv_std


def front_kernel(meta, scales, *refs):
    pieces, quarters = refs[:8], refs[8:12]
    mod, cosine, sine = refs[12:15]
    weights_out, mid_out, hidden_out, resid_out = refs[15:19]
    head_outs = refs[19:23]
    noisy_out, target_out, mod_out = refs[23:26]
    tokens, heads, weights, mid, hidden, resid, target, mod_own, held, sems, out_sems = refs[26:]
    copies = [
        pltpu.make_async_copy(
            pieces[place].at[TOKEN_ROWS:RING_ROWS, :], held.at[place], sems.at[place]
        )
        for place in range(8)
    ]
    for copy in copies:
        copy.start()
    for source in range(4):
        rows = pl.ds(pl.multiple_of(meta[20 + source] * 64, 64), 64)
        for frame in range(4):
            base = 128 * (frame ^ source)
            clean = quarters[source][base : base + 64, :].astype(jnp.float32)
            noise = quarters[source][base + 64 : base + 128, :].astype(jnp.float32)
            mixed = scales[frame] * clean + scales[4 + frame] * noise
            tokens[frame, rows, :] = mixed.astype(jnp.bfloat16)
            if frame == 0:
                target[rows, :] = scales[0] * noise - scales[4] * clean
    outs = [
        pltpu.make_async_copy(tokens.at[0], noisy_out, out_sems.at[0]),
        pltpu.make_async_copy(target, target_out, out_sems.at[1]),
        pltpu.make_async_copy(weights, weights_out, out_sems.at[2]),
        pltpu.make_async_copy(resid, resid_out, out_sems.at[3]),
    ] + [
        pltpu.make_async_copy(hidden.at[frame], hidden_out.at[frame], out_sems.at[4 + frame])
        for frame in range(4)
    ]
    outs.append(pltpu.make_async_copy(mod_own, mod_out, out_sems.at[8]))
    outs.append(pltpu.make_async_copy(mid, mid_out, out_sems.at[9]))
    for place in range(8):
        copies[place].wait()
        block = pl.ds(pl.multiple_of(meta[place] * 128, 128), 128)
        weights[:, block] = held[place, 0:FRONT_ROWS, :]
        for part in range(3):
            base = FRONT_ROWS + 128 * part
            mid[block, 128 * part : 128 * part + 128] = held[place, base : base + 128, :]
    for index in (0, 1, 2, 9):
        outs[index].start()
    embed = weights[QKV_ROWS : QKV_ROWS + 128, :]
    vec_rows = weights[QKV_ROWS + 128 : FRONT_ROWS, :].astype(jnp.float32)
    mod_own[0:6, :] = mod[0] + vec_rows[0:6]
    mod_own[6:8, :] = vec_rows[6:8]
    outs[8].start()
    for frame in range(4):
        values = jnp.dot(tokens[frame], embed, preferred_element_type=jnp.float32) + vec_rows[6:7]
        if frame == 0:
            resid[...] = values
            outs[3].start()
        normed, _ = centred_norm(values)
        shift = mod[frame, 0:1, :] + vec_rows[0:1]
        scale = mod[frame, 1:2, :] + vec_rows[1:2]
        low = (normed * (1.0 + scale) + shift).astype(jnp.bfloat16)
        hidden[frame] = low
        outs[4 + frame].start()
        mixed = lax.dot_general(
            weights[0:QKV_ROWS, :], low, NT, preferred_element_type=jnp.float32
        )
        cos_now = cosine[meta[8 + frame]]
        sin_now = sine[meta[8 + frame]]
        cols = slice(256 * frame, 256 * frame + 256)
        for head in range(4):
            where_to = head
            for part in range(2):
                base = 256 * part + 64 * head
                upper = mixed[base : base + 32]
                lower = mixed[base + 32 : base + 64]
                heads[where_to, 64 * part : 64 * part + 32, cols] = (
                    upper * cos_now - lower * sin_now
                ).astype(jnp.bfloat16)
                heads[where_to, 64 * part + 32 : 64 * part + 64, cols] = (
                    lower * cos_now + upper * sin_now
                ).astype(jnp.bfloat16)
            base = 512 + 64 * head
            heads[where_to, 128:192, cols] = mixed[base : base + 64].astype(jnp.bfloat16)
    for k in range(4):
        outs.append(pltpu.make_async_copy(heads.at[meta[12 + k]], head_outs[k], out_sems.at[10 + k]))
        outs[10 + k].start()
    for copy in outs:
        copy.wait()


def call_front(meta, scales, pieces, quarters, mod, cosine, sine):
    return pl.pallas_call(
        front_kernel,
        out_shape=(
            jax.ShapeDtypeStruct((FRONT_ROWS, D), jnp.bfloat16),
            jax.ShapeDtypeStruct((D, 384), jnp.bfloat16),
            jax.ShapeDtypeStruct((4, PATCHES, D), jnp.bfloat16),
            jax.ShapeDtypeStruct((PATCHES, D), jnp.float32),
        )
        + (jax.ShapeDtypeStruct((192, 4 * PATCHES), jnp.bfloat16),) * 4
        + (
            jax.ShapeDtypeStruct((PATCHES, 128), jnp.bfloat16),
            jax.ShapeDtypeStruct((PATCHES, 128), jnp.float32),
            jax.ShapeDtypeStruct((8, D), jnp.float32),
        ),
        in_specs=smem_specs(2) + hbm_specs(8) + vmem_specs(7),
        out_specs=hbm_specs(11),
        scratch_shapes=[
            pltpu.VMEM((4, PATCHES, 128), jnp.bfloat16),
            pltpu.VMEM((4, 192, 4 * PATCHES), jnp.bfloat16),
            pltpu.VMEM((FRONT_ROWS, D), jnp.bfloat16),
            pltpu.VMEM((D, 384), jnp.bfloat16),
            pltpu.VMEM((4, PATCHES, D), jnp.bfloat16),
            pltpu.VMEM((PATCHES, D), jnp.float32),
            pltpu.VMEM((PATCHES, 128), jnp.float32),
            pltpu.VMEM((8, D), jnp.float32),
            pltpu.VMEM((8, FRONT_ROWS + 384, 128), jnp.bfloat16),
            pltpu.SemaphoreType.DMA((8,)),
            pltpu.SemaphoreType.DMA((14,)),
        ],
        compiler_params=pltpu.CompilerParams(vmem_limit_bytes=52 * 2**20),
        cost_estimate=pl.CostEstimate(flops=2 * 10**9, bytes_accessed=10**7, transcendentals=0),
        name="front",
    )(meta, scales, *pieces, *quarters, mod, cosine, sine)


def total_own(held, came, across):
    return held[...] + came[...].astype(jnp.float32) + across[...].astype(jnp.float32)


def middle_kernel(held, came, across, resid, mod, attn_out, resid_mid, hidden):
    total = total_own(held, came, across)
    attn_out[...] = total
    values = resid[...] + mod[2:3, :] * total
    resid_mid[...] = values
    normed, _ = centred_norm(values)
    hidden[...] = (normed * (1.0 + mod[4:5, :]) + mod[3:4, :]).astype(jnp.bfloat16)


def row_call(kernel, name, outs, *operands, smem=0):
    return pl.pallas_call(
        kernel,
        out_shape=tuple(outs),
        in_specs=smem_specs(smem) + vmem_specs(len(operands) - smem),
        out_specs=vmem_specs(len(outs)),
        compiler_params=pltpu.CompilerParams(vmem_limit_bytes=16 * 2**20),
        cost_estimate=pl.CostEstimate(flops=10**9, bytes_accessed=4 * 10**6, transcendentals=0),
        name=name,
    )(*operands)


def frame_f32():
    return jax.ShapeDtypeStruct((PATCHES, D), jnp.float32)


def frame_low():
    return jax.ShapeDtypeStruct((PATCHES, D), jnp.bfloat16)


def back_through_norm(grad, normed, inv_std):
    mean_grad = jnp.mean(grad, axis=-1, keepdims=True)
    mean_proj = jnp.mean(grad * normed, axis=-1, keepdims=True)
    return inv_std * (grad - mean_grad - normed * mean_proj)


def column_sum(values):
    return jnp.sum(values, axis=0, keepdims=True)


def loss_kernel(
    scales, held, came, across, resid_mid, mod, mid, target, grad_low, grad_three, io_rows, gate, error
):
    mlp_out = total_own(held, came, across)
    values = resid_mid[...] + mod[5:6, :] * mlp_out
    normed, inv_std = centred_norm(values)
    gain = mod[7:8, :]
    final = (normed * gain).astype(jnp.bfloat16)
    head = mid[:, 256:384]
    pred = jnp.dot(final, head, preferred_element_type=jnp.float32)
    diff = pred - target[...]
    per_token = jnp.sum(diff * diff, axis=1, keepdims=True)
    error[...] = jnp.broadcast_to(
        scales[0] * jnp.sum(per_token, axis=0, keepdims=True) / diff.shape[1], error.shape
    )
    grad_pred = (scales[1] * diff).astype(jnp.bfloat16)
    grad_final = lax.dot_general(grad_pred, head, NT, preferred_element_type=jnp.float32)
    grad_gain = column_sum(grad_final * normed)
    grad = back_through_norm(grad_final * gain, normed, inv_std)
    grad_three[...] = grad
    grad_low[...] = (mod[5:6, :] * grad).astype(jnp.bfloat16)
    gate[...] = column_sum(grad * mlp_out)
    io_rows[0:128, :] = lax.dot_general(grad_pred, final, TN, preferred_element_type=jnp.float32)
    io_rows[128:136, :] = jnp.concatenate([grad_gain, jnp.zeros((7, D), jnp.float32)], axis=0)


def second_kernel(
    held, came, across, resid_mid, mod, grad_three, attn_out, grad_low, grad_mid, rows
):
    grad_hidden = total_own(held, came, across)
    normed, inv_std = centred_norm(resid_mid[...])
    grad = grad_three[...] + back_through_norm(grad_hidden * (1.0 + mod[4:5, :]), normed, inv_std)
    grad_mid[...] = grad
    grad_low[...] = (mod[2:3, :] * grad).astype(jnp.bfloat16)
    rows[0:1, :] = column_sum(grad * attn_out[...])
    rows[1:2, :] = column_sum(grad_hidden)
    rows[2:3, :] = column_sum(grad_hidden * normed)


def first_kernel(
    device,
    held,
    came,
    across,
    resid,
    mod,
    grad_mid,
    noisy,
    rows_two,
    gate_two,
    head_rows,
    mod_rows,
    near_held,
    near_away,
    far_held,
    far_away,
    io_rows,
):
    grad_hidden = total_own(held, came, across)
    normed, inv_std = centred_norm(resid[...])
    grad = grad_mid[...] + back_through_norm(grad_hidden * (1.0 + mod[1:2, :]), normed, inv_std)
    rows = [
        column_sum(grad_hidden),
        column_sum(grad_hidden * normed),
        rows_two[0:1, :],
        rows_two[1:2, :],
        rows_two[2:3, :],
        gate_two[...],
    ]
    blocks = [row[:, 128 * k : 128 * k + 128] for row in rows for k in range(8)]
    mod_rows[...] = jnp.concatenate(blocks, axis=0).astype(jnp.bfloat16)
    io_rows[0:128, :] = lax.dot_general(
        noisy[...], grad.astype(jnp.bfloat16), TN, preferred_element_type=jnp.float32
    )
    io_rows[128:256, :] = head_rows[0:128, :]
    io_rows[256:264, :] = jnp.concatenate(
        [column_sum(grad), head_rows[128:129, :], jnp.zeros((6, D), jnp.float32)], axis=0
    )
    io_rows[264:320, :] = jnp.zeros((56, D), jnp.float32)
    for k, out in enumerate((near_held, near_away, far_held, far_away)):
        group = pl.ds(pl.multiple_of(IO_ROWS * (device[1] ^ k), 16), IO_ROWS)
        out[...] = io_rows[group, :].astype(out.dtype)


def side_kernel(device, held, came, across, mod_rows, keep, away):
    total = total_own(held, came, across)
    side = device[0] & 1
    for block in range(8):
        piece = total[:, 128 * block : 128 * block + 128]

        @pl.when(side == block % 2)
        def _():
            keep[block // 2] = piece

        @pl.when(side != block % 2)
        def _():
            away[IO_ROWS * (block // 2) : IO_ROWS * (block // 2) + IO_ROWS, :] = piece.astype(
                jnp.bfloat16
            )

    away[4 * IO_ROWS :, :] = mod_rows[...]


def merge_kernel(
    device, held, came, out_held, out_came, io_held, io_came, mod_rows, own, io_own, *outs
):
    z = device[0] >> 1
    for bit in range(4):
        total = jnp.concatenate(
            [
                held[z ^ bit] + came[z ^ bit].astype(jnp.float32),
                out_held[z ^ bit] + out_came[z ^ bit].astype(jnp.float32),
            ],
            axis=0,
        )
        rows = pl.ds(pl.multiple_of(IO_ROWS * (z ^ bit), 16), IO_ROWS)
        io_total = io_held[z ^ bit] + io_came[rows, :].astype(jnp.float32)
        if bit == 0:
            own[...] = total
            io_own[...] = io_total
        else:
            out = outs[bit]
            out[0:ATTN_ROWS, :] = total.astype(jnp.bfloat16)
            out[ATTN_ROWS : ATTN_ROWS + IO_ROWS, :] = io_total.astype(jnp.bfloat16)
            base = ATTN_ROWS + IO_ROWS
            out[base : base + MOD_ROWS, :] = mod_rows[...]
            out[base + MOD_ROWS : base + 2 * MOD_ROWS, :] = io_came[4 * IO_ROWS :, :]
    outs[0][0:MOD_ROWS, :] = mod_rows[...]
    outs[0][MOD_ROWS : 2 * MOD_ROWS, :] = io_came[4 * IO_ROWS :, :]


def mod_grad_kernel(device, cond, *refs):
    parts = refs[:4]
    rows_out, vector, io_grad, square, rows = refs[4:]
    base = 8 * MOD_ROWS + 2 * IO_ROWS
    terms = []
    for index in range(4):
        owner = device[1] ^ index
        block = parts[index][0 : 8 * MOD_ROWS, :].astype(jnp.float32)
        for frame in range(8):
            for k in range(MOD_ROWS):
                at = MOD_ROWS * frame + k
                rows[owner, frame : frame + 1, 128 * k : 128 * k + 128] = block[at : at + 1, :]
        group = pl.ds(pl.multiple_of(IO_ROWS * owner, 16), IO_ROWS)
        high = parts[index][8 * MOD_ROWS : 8 * MOD_ROWS + IO_ROWS, :].astype(jnp.float32)
        rest = parts[index][8 * MOD_ROWS + IO_ROWS : base, :].astype(jnp.float32)
        io_grad[group, :] = high + rest
        terms.append(column_sum(parts[index][base : base + 16, :].astype(jnp.float32)))
    total = jnp.zeros((1, 1), jnp.float32)
    for index in range(6):
        cols = slice(D * index, D * index + D)
        low = rows[:, :, cols].reshape(32, D)
        rows_out[:, cols] = low.astype(jnp.bfloat16)
        part = lax.dot_general(
            cond[32:64, :], low.astype(jnp.bfloat16), TN, preferred_element_type=jnp.float32
        )
        total = total + jnp.sum(column_sum(part * part), axis=1, keepdims=True)
        own = pl.ds(pl.multiple_of(D * index + 128 * device[0], 128), 128)
        vector[index : index + 1, :] = column_sum(rows[:, :, own].reshape(32, 128))
    vector[6:8, :] = io_grad[256:258, :]
    mixed = vector[0:6, :]
    total = total + jnp.sum(column_sum(mixed * mixed), axis=1, keepdims=True)
    left = lax.broadcasted_iota(jnp.int32, (1, 128), 1) < 64
    square[...] = ((terms[0] + terms[1]) + (terms[2] + terms[3])) + jnp.where(left, total, 0.0)


def call_mod_grad(device, cond, parts):
    return pl.pallas_call(
        mod_grad_kernel,
        out_shape=(
            jax.ShapeDtypeStruct((32, 6 * D), jnp.bfloat16),
            jax.ShapeDtypeStruct((8, 128), jnp.float32),
            jax.ShapeDtypeStruct((4 * IO_ROWS, 128), jnp.float32),
            jax.ShapeDtypeStruct((1, 128), jnp.float32),
        ),
        in_specs=smem_specs(1) + vmem_specs(5),
        out_specs=vmem_specs(4),
        scratch_shapes=[pltpu.VMEM((4, 8, 6 * D), jnp.float32)],
        compiler_params=pltpu.CompilerParams(vmem_limit_bytes=12 * 2**20),
        cost_estimate=pl.CostEstimate(flops=10**8, bytes_accessed=4 * 10**6, transcendentals=0),
        name="mod_grad",
    )(device, cond, *parts)


def mlp_kernel(first, second, weights, held, away, active, slope):
    for frame, source in enumerate((first, second)):
        rows = slice(256 * frame, 256 * frame + 256)
        upward = jnp.dot(source[...], weights[0], preferred_element_type=jnp.float32)
        inner = 0.5 * (1.0 + lax.erf(upward * (1.0 / math.sqrt(2.0))))
        low = (upward * inner).astype(jnp.bfloat16)
        active[rows, :] = low
        change = inner + upward * jnp.exp(-0.5 * upward * upward) * (
            1.0 / math.sqrt(2.0 * math.pi)
        )
        slope[rows, :] = change.astype(jnp.bfloat16)
        part = lax.dot_general(low, weights[1], NT, preferred_element_type=jnp.float32)
        if frame:
            away[...] = part.astype(jnp.bfloat16)
        else:
            held[...] = part


def mlp_back_kernel(first, second, weights, slope, held, away, grad_up):
    for frame, source in enumerate((first, second)):
        rows = slice(256 * frame, 256 * frame + 256)
        grad = jnp.dot(source[...], weights[1], preferred_element_type=jnp.float32)
        low = (grad * slope[rows, :].astype(jnp.float32)).astype(jnp.bfloat16)
        grad_up[rows, :] = low
        part = lax.dot_general(low, weights[0], NT, preferred_element_type=jnp.float32)
        if frame:
            away[...] = part.astype(jnp.bfloat16)
        else:
            held[...] = part


def call_mlp(kernel, name, outs, *operands):
    return pl.pallas_call(
        kernel,
        out_shape=(frame_f32(), frame_low()) + outs,
        in_specs=vmem_specs(len(operands)),
        out_specs=vmem_specs(2 + len(outs)),
        compiler_params=pltpu.CompilerParams(vmem_limit_bytes=16 * 2**20),
        cost_estimate=pl.CostEstimate(
            flops=4 * 10**9, bytes_accessed=2 * 10**7, transcendentals=10**6
        ),
        name=name,
    )(*operands)


def weight_grad_kernel(*refs):
    hidden, grads = refs[:4], refs[4:8]
    grad_up, active = refs[8:10], refs[10:12]
    result, out, sems = refs[12:]
    width = active[0].shape[1]
    copies = []
    for index, (left, right) in enumerate(((hidden, grad_up), (grads, active))):
        total = jnp.zeros((D, width), jnp.float32)
        for frame in range(4):
            rows = slice(256 * (frame % 2), 256 * (frame % 2) + 256)
            total = total + lax.dot_general(
                left[frame][...],
                right[frame // 2][rows, :],
                TN,
                preferred_element_type=jnp.float32,
            )
        out[index] = total.astype(jnp.bfloat16)
        copies.append(
            pltpu.make_async_copy(
                out.at[index], result.at[:, width * index : width * index + width], sems.at[index]
            )
        )
        copies[index].start()
    for copy in copies:
        copy.wait()


def call_weight_grad(hidden, grads, grad_up, active):
    operands = (*hidden, *grads, *grad_up, *active)
    return pl.pallas_call(
        weight_grad_kernel,
        out_shape=jax.ShapeDtypeStruct((D, 2 * active[0].shape[1]), jnp.bfloat16),
        in_specs=vmem_specs(len(operands)),
        out_specs=hbm_specs(1)[0],
        scratch_shapes=[
            pltpu.VMEM((2, D, active[0].shape[1]), jnp.bfloat16),
            pltpu.SemaphoreType.DMA((2,)),
        ],
        compiler_params=pltpu.CompilerParams(vmem_limit_bytes=20 * 2**20),
        cost_estimate=pl.CostEstimate(flops=5 * 10**9, bytes_accessed=2 * 10**7, transcendentals=0),
        name="weight_grad",
    )(*operands)


def side_blocks(device, total, held, away):
    side = device[0] & 1
    for z in range(4):
        held[z] = total[:, pl.ds(pl.multiple_of(256 * z + 128 * side, 128), 128)]
        away[z] = total[:, pl.ds(pl.multiple_of(256 * z + 128 * (1 - side), 128), 128)].astype(
            jnp.bfloat16
        )


def head_grad_kernel(device, left, right, held, away, total):
    total[...] = jnp.dot(left[...], right[...], preferred_element_type=jnp.float32)
    side_blocks(device, total, held, away)


def call_head_grad(device, left, right):
    rows = left.shape[0]
    return pl.pallas_call(
        head_grad_kernel,
        out_shape=(
            jax.ShapeDtypeStruct((4, rows, 128), jnp.float32),
            jax.ShapeDtypeStruct((4, rows, 128), jnp.bfloat16),
        ),
        in_specs=smem_specs(1) + vmem_specs(2),
        out_specs=vmem_specs(2),
        scratch_shapes=[pltpu.VMEM((rows, D), jnp.float32)],
        compiler_params=pltpu.CompilerParams(vmem_limit_bytes=12 * 2**20),
        cost_estimate=pl.CostEstimate(flops=2 * 10**9, bytes_accessed=10**7, transcendentals=0),
        name="head_grad",
    )(device, left, right)


def qkv_back_kernel(meta, *refs):
    blocks, weights = refs[:4], refs[4]
    grads, near_held, near_away, far_held, far_away = refs[5:]
    for k in range(4):
        head = meta[0] ^ k
        for part in range(3):
            rows = pl.ds(pl.multiple_of(256 * part + 64 * head, 64), 64)
            grads[rows, :] = blocks[k][64 * part : 64 * part + 64, :]
    for frame, out in ((2, far_held), (3, far_away), (0, near_held), (1, near_away)):
        part = lax.dot_general(
            grads[:, 256 * frame : 256 * frame + 256],
            weights[0:QKV_ROWS, :],
            TN,
            preferred_element_type=jnp.float32,
        )
        out[...] = part.astype(out.dtype)


def call_qkv_back(meta, blocks, weights):
    return row_call(
        qkv_back_kernel,
        "qkv_back",
        (
            jax.ShapeDtypeStruct((QKV_ROWS, 4 * PATCHES), jnp.bfloat16),
            frame_f32(),
            frame_low(),
            frame_f32(),
            frame_low(),
        ),
        meta,
        *blocks,
        weights,
        smem=1,
    )


def adam_step(weight_now, first_mom, second_mom, grad, scale, rate, decay):
    factor, first_fix, second_fix = scale
    grad = grad * factor
    first_mom = beta_one * first_mom + (1.0 - beta_one) * grad
    second_mom = beta_two * second_mom + (1.0 - beta_two) * grad * grad
    updated = weight_now - rate * (
        first_mom * first_fix / (jnp.sqrt(second_mom * second_fix) + adam_eps) + decay * weight_now
    )
    return updated, first_mom, second_mom, updated.astype(jnp.bfloat16)


def adam_kernel(*refs):
    fixes, sums = refs[0], refs[1:5]
    attn_grad, mlp_grad, cond, mod_rows = refs[5:9]
    io_in, vec_in = refs[9:13], refs[13:17]
    groups = [refs[17 + 3 * k : 20 + 3 * k] for k in range(3)]
    outs = [refs[26 + 4 * k : 30 + 4 * k] for k in range(3)]
    io_out, vec_out, norm_out = refs[38:43], refs[43:47], refs[47]
    held, slots, low_slots, in_sems, sems = refs[48:]
    depth = held.shape[0]
    tasks = []
    for k in (2, 1, 0):
        width = groups[k][0].shape[-1]
        for lead in range(groups[k][0].shape[0] if k < 2 else 1):
            for col in range(0, width, 1024):
                tasks.append((k, lead, col, min(1024, width - col)))

    def fetches(number):
        k, lead, col, span = tasks[number]
        cut = ((lead,) if k < 2 else ()) + (slice(None), slice(col, col + span))
        slot = number % depth
        return [
            pltpu.make_async_copy(
                groups[k][index].at[cut], held.at[slot, index, :, 0:span], in_sems.at[slot, index]
            )
            for index in range(3)
        ]

    for number in range(min(depth, len(tasks))):
        for copy in fetches(number):
            copy.start()
    total = (sums[0][...] + sums[1][...]) + (sums[2][...] + sums[3][...])
    norm = jnp.sqrt(total)
    norm_out[0:1, :] = norm
    norm_out[1:2, :] = total
    factor = jnp.minimum(1.0, clip_limit / (norm[:, 0:1] + 1e-06))
    scale = (factor, fixes[0], fixes[1])
    results = adam_step(*(ref[...] for ref in io_in), scale, rate_matrix, decay_rate)
    io_out[0][...] = results[0]
    io_out[1][...] = results[1]
    io_out[2][...] = results[2][0]
    io_out[3][...] = results[2][1]
    io_out[4][...] = results[3]
    results = adam_step(*(ref[...] for ref in vec_in), scale, rate_vector, 0.0)
    for out, result in zip(vec_out, results):
        out[...] = result
    running = {}
    for number, (k, lead, col, span) in enumerate(tasks):
        slot = number % depth
        for copy in fetches(number):
            copy.wait()
        for copy in running.pop(number - depth, ()):
            copy.wait()
        cut = ((lead,) if k < 2 else ()) + (slice(None), slice(col, col + span))
        if k == 0:
            grad = attn_grad[lead]
        elif k == 1:
            base = groups[1][0].shape[-1] * lead + col
            grad = mlp_grad[:, base : base + span].astype(jnp.float32)
        else:
            grad = lax.dot_general(
                cond[32:64, :],
                mod_rows[:, col : col + span],
                TN,
                preferred_element_type=jnp.float32,
            )
        values = [held[slot, index, :, 0:span] for index in range(3)]
        results = adam_step(*values, grad, scale, rate_matrix, decay_rate)
        copies = []
        for index, result in enumerate(results):
            source = low_slots.at[slot] if index == 3 else slots.at[slot, index]
            source = source.at[:, 0:span]
            source[...] = result
            copies.append(
                pltpu.make_async_copy(source, outs[k][index].at[cut], sems.at[slot, index])
            )
            copies[index].start()
        running[number] = copies
        if number + depth < len(tasks):
            for copy in fetches(number + depth):
                copy.start()
    for copies in running.values():
        for copy in copies:
            copy.wait()


def call_adam(fixes, sums, grads, io_group, vec_group, groups):
    held = [array for group in groups for array in group]
    inside = [*sums, *grads, *io_group, *vec_group]

    def results(group):
        low = jax.ShapeDtypeStruct(group[0].shape, jnp.bfloat16)
        return (jax.ShapeDtypeStruct(group[0].shape, jnp.float32),) * 3 + (low,)

    io_like = results(io_group)
    half = jax.ShapeDtypeStruct(io_group[0].shape[1:], jnp.float32)
    out_shape = sum((results(group) for group in groups), ())
    out_shape = out_shape + io_like[:2] + (half, half) + io_like[3:] + results(vec_group)
    out_shape = out_shape + (jax.ShapeDtypeStruct((2, 128), jnp.float32),)
    return pl.pallas_call(
        adam_kernel,
        out_shape=out_shape,
        in_specs=smem_specs(1) + vmem_specs(len(inside)) + hbm_specs(9),
        out_specs=hbm_specs(12) + vmem_specs(10),
        scratch_shapes=[
            pltpu.VMEM((6, 3, 128, 1024), jnp.float32),
            pltpu.VMEM((6, 3, 128, 1024), jnp.float32),
            pltpu.VMEM((6, 128, 1024), jnp.bfloat16),
            pltpu.SemaphoreType.DMA((6, 3)),
            pltpu.SemaphoreType.DMA((6, 4)),
        ],
        compiler_params=pltpu.CompilerParams(vmem_limit_bytes=52 * 2**20),
        cost_estimate=pl.CostEstimate(flops=10**7, bytes_accessed=2 * 10**7, transcendentals=0),
        name="adam",
    )(fixes, *inside, *held)


def finish_kernel(*refs):
    own, io_own, mod_own, pieces = refs[0], refs[1], refs[2], refs[3:6]
    scattered, error, grad, spread = refs[6:]
    total = own[...]
    io_total = io_own[...]
    spread[0 : 2 * MOD_ROWS, :] = mod_own[...]
    for index, piece in enumerate(pieces):
        total = total + piece[0:ATTN_ROWS, :].astype(jnp.float32)
        base = ATTN_ROWS + IO_ROWS
        io_total = io_total + piece[ATTN_ROWS:base, :].astype(jnp.float32)
        spread[2 * MOD_ROWS * (index + 1) : 2 * MOD_ROWS * (index + 2), :] = piece[base:, :]
    high = io_total.astype(jnp.bfloat16)
    base = 8 * MOD_ROWS
    spread[base : base + IO_ROWS, :] = high
    base = base + IO_ROWS
    spread[base : base + IO_ROWS, :] = (io_total - high.astype(jnp.float32)).astype(jnp.bfloat16)
    for part in range(4):
        grad[part] = total[256 * part : 256 * part + 256].T
    rest = scattered[...].astype(jnp.float32)
    squares = jnp.zeros((1, 1), jnp.float32)
    for values in (total, rest, io_total):
        squares = squares + jnp.sum(column_sum(values * values), axis=1, keepdims=True)
    left = lax.broadcasted_iota(jnp.int32, (1, 128), 1) < 64
    value = jnp.where(left, squares, error[...])
    terms = []
    for _ in range(3):
        terms.append(value.astype(jnp.bfloat16).astype(jnp.float32))
        value = value - terms[-1]
    spread[base + IO_ROWS :, :] = jnp.concatenate(
        terms + [jnp.zeros((13, 128), jnp.float32)], axis=0
    ).astype(jnp.bfloat16)


def turn(block):
    return block.astype(jnp.float32).T.astype(jnp.bfloat16)


def query_rows(meta, pair):
    first = 2 * pair
    start_first = first - meta[2 + first]
    start_second = first + 1 - meta[3 + first]
    left = lax.broadcasted_iota(jnp.int32, (1, 2 * PATCHES), 1) < PATCHES
    upto = jnp.where(left, first, first + 1)
    since = jnp.where(left, start_first, start_second)
    return jnp.minimum(start_first, start_second), since, upto


def attend_kernel(meta, *refs):
    blocks = refs[:4]
    outs = refs[4:8]
    lse, mixed, query, key, value, scores = refs[8:]
    for member in range(4):
        for frame in range(4):
            slot = 4 * (meta[0] ^ member) + (meta[1] ^ frame)
            cols = slice(256 * frame, 256 * frame + 256)
            lanes = pl.ds(pl.multiple_of((slot % 2) * 256, 256), 256)
            query[slot // 2, :, lanes] = blocks[member][0:64, cols] * 0.125
            key[slot // 2, lanes, :] = turn(blocks[member][64:128, cols])
            value[slot // 2, :, lanes] = blocks[member][128:192, cols]

    def per_pair(pair, carry):
        low, since, upto = query_rows(meta, pair)
        wanted = query[pair]

        def first_pass(keys, top):
            both = jnp.dot(key[keys], wanted, preferred_element_type=jnp.float32)
            for side in range(2):
                slot = 2 * keys + side
                bias = jnp.where((slot >= since) & (slot <= upto), 0.0, neg_large)
                part = both[256 * side : 256 * side + 256] + bias
                scores[keys, 256 * side : 256 * side + 256, :] = part
                top = jnp.maximum(top, jnp.max(part.reshape(32, 8, 2 * PATCHES), axis=0))
            return top

        tops = lax.fori_loop(
            low // 2, pair + 1, first_pass, jnp.full((8, 2 * PATCHES), neg_large, jnp.float32)
        )
        top = jnp.max(tops, axis=0, keepdims=True)

        def second_pass(keys, state):
            total, acc = state
            probs = jnp.exp(scores[keys] - top)
            total = total + jnp.sum(probs.reshape(64, 8, 2 * PATCHES), axis=0)
            acc = acc + jnp.dot(
                value[keys], probs.astype(jnp.bfloat16), preferred_element_type=jnp.float32
            )
            return (total, acc)

        totals, acc = lax.fori_loop(
            low // 2,
            pair + 1,
            second_pass,
            (
                jnp.zeros((8, 2 * PATCHES), jnp.float32),
                jnp.zeros((HD, 2 * PATCHES), jnp.float32),
            ),
        )
        total = jnp.sum(totals, axis=0, keepdims=True)
        lse[pair] = top + jnp.log(total)
        mixed[pair] = acc / total
        return carry

    lax.fori_loop(0, 8, per_pair, 0)
    for member in range(4):
        for frame in range(4):
            slot = 4 * (meta[0] ^ member) + (meta[1] ^ frame)
            lanes = pl.ds(pl.multiple_of((slot % 2) * 256, 256), 256)
            outs[member][:, 256 * frame : 256 * frame + 256] = mixed[slot // 2, :, lanes].astype(
                jnp.bfloat16
            )


def call_attend(meta, blocks):
    vmem = pl.BlockSpec()
    result = pl.pallas_call(
        attend_kernel,
        out_shape=tuple(jax.ShapeDtypeStruct((HD, 4 * PATCHES), jnp.bfloat16) for _ in range(4))
        + (
            jax.ShapeDtypeStruct((8, 1, 2 * PATCHES), jnp.float32),
            jax.ShapeDtypeStruct((8, HD, 2 * PATCHES), jnp.float32),
        ),
        in_specs=[pl.BlockSpec(memory_space=pltpu.SMEM)] + [vmem] * 4,
        out_specs=(vmem,) * 6,
        scratch_shapes=[
            pltpu.VMEM((8, HD, 2 * PATCHES), jnp.bfloat16),
            pltpu.VMEM((8, 2 * PATCHES, HD), jnp.bfloat16),
            pltpu.VMEM((8, HD, 2 * PATCHES), jnp.bfloat16),
            pltpu.VMEM((8, 2 * PATCHES, 2 * PATCHES), jnp.float32),
        ],
        compiler_params=pltpu.CompilerParams(vmem_limit_bytes=48 * 2**20),
        cost_estimate=pl.CostEstimate(flops=9 * 10**9, bytes_accessed=5 * 10**6, transcendentals=10**7),
        name="attend",
    )(meta, *blocks)
    return list(result[:4]), result[4], result[5]


def attend_back_kernel(meta, *refs):
    blocks = refs[:4]
    grads = refs[4:8]
    lse, mixed, cosine, sine = refs[8:12]
    outs = refs[12:16]
    query, key, key_flat, value_flat, grad, sum_key, sum_value, sum_query = refs[16:]
    for member in range(4):
        for frame in range(4):
            slot = 4 * (meta[0] ^ member) + (meta[1] ^ frame)
            cols = slice(256 * frame, 256 * frame + 256)
            place = pl.ds(pl.multiple_of((slot % 2) * 256, 256), 256)
            part = blocks[member][0:64, cols] * 0.125
            query[slot // 2, :, place] = part
            part = blocks[member][64:128, cols]
            key[slot // 2, :, place] = part
            key_flat[slot // 2, place, :] = turn(part)
            value_flat[slot // 2, place, :] = turn(blocks[member][128:192, cols])
            part = grads[member][:, cols]
            grad[slot // 2, :, place] = part
    sum_key[...] = jnp.zeros_like(sum_key)
    sum_value[...] = jnp.zeros_like(sum_value)

    def per_pair(pair, carry):
        low, since, upto = query_rows(meta, pair)
        wanted = query[pair]
        wanted_grad = grad[pair]
        delta = jnp.sum(wanted_grad.astype(jnp.float32) * mixed[pair], axis=0, keepdims=True)
        level = lse[pair]

        def per_keys(keys, acc):
            scores = jnp.dot(key_flat[keys], wanted, preferred_element_type=jnp.float32)
            grad_probs = jnp.dot(
                value_flat[keys], wanted_grad, preferred_element_type=jnp.float32
            )
            low_probs, low_scores = [], []
            for side in range(2):
                rows = slice(256 * side, 256 * side + 256)
                slot = 2 * keys + side
                bias = jnp.where((slot >= since) & (slot <= upto), -level, neg_large)
                probs = jnp.exp(scores[rows] + bias)
                low_probs.append(probs.astype(jnp.bfloat16))
                low_scores.append((probs * (grad_probs[rows] - delta)).astype(jnp.bfloat16))
            all_probs = jnp.concatenate(low_probs, axis=0)
            all_scores = jnp.concatenate(low_scores, axis=0)
            sum_value[keys] += lax.dot_general(
                wanted_grad, all_probs, NT, preferred_element_type=jnp.float32
            )
            sum_key[keys] += lax.dot_general(
                wanted, all_scores, NT, preferred_element_type=jnp.float32
            )
            return acc + jnp.dot(key[keys], all_scores, preferred_element_type=jnp.float32)

        sum_query[pair] = lax.fori_loop(
            low // 2, pair + 1, per_keys, jnp.zeros((HD, 2 * PATCHES), jnp.float32)
        )
        return carry

    lax.fori_loop(0, 8, per_pair, 0)
    for member in range(4):
        for frame in range(4):
            slot = 4 * (meta[0] ^ member) + (meta[1] ^ frame)
            cols = slice(256 * frame, 256 * frame + 256)
            place = pl.ds(pl.multiple_of((slot % 2) * 256, 256), 256)
            cos_now = cosine[slot]
            sin_now = sine[slot]
            for base, part in (
                (0, sum_query[slot // 2, :, place] * 0.125),
                (64, sum_key[slot // 2, :, place]),
            ):
                upper = part[0:32]
                lower = part[32:64]
                outs[member][base : base + 32, cols] = (
                    upper * cos_now + lower * sin_now
                ).astype(jnp.bfloat16)
                outs[member][base + 32 : base + 64, cols] = (
                    lower * cos_now - upper * sin_now
                ).astype(jnp.bfloat16)
            outs[member][128:192, cols] = sum_value[slot // 2, :, place].astype(jnp.bfloat16)


def call_attend_back(meta, blocks, grads, lse, mixed, cosine, sine):
    vmem = pl.BlockSpec()
    flat_pair = pltpu.VMEM((8, 2 * PATCHES, HD), jnp.bfloat16)
    turned_pair = pltpu.VMEM((8, HD, 2 * PATCHES), jnp.bfloat16)
    wide = pltpu.VMEM((8, HD, 2 * PATCHES), jnp.float32)
    return list(
        pl.pallas_call(
            attend_back_kernel,
            out_shape=tuple(
                jax.ShapeDtypeStruct((192, 4 * PATCHES), jnp.bfloat16) for _ in range(4)
            ),
            in_specs=[pl.BlockSpec(memory_space=pltpu.SMEM)] + [vmem] * 12,
            out_specs=(vmem,) * 4,
            scratch_shapes=[
                turned_pair,
                turned_pair,
                flat_pair,
                flat_pair,
                turned_pair,
                wide,
                wide,
                pltpu.VMEM((8, HD, 2 * PATCHES), jnp.float32),
            ],
            compiler_params=pltpu.CompilerParams(vmem_limit_bytes=48 * 2**20),
            cost_estimate=pl.CostEstimate(
                flops=30 * 10**9, bytes_accessed=10**7, transcendentals=10**7
            ),
            name="attend_back",
        )(meta, *blocks, *grads, lse, mixed, cosine, sine)
    )


def shards_halves(
    clean,
    noise,
    levels,
    lengths,
    order,
    step,
    w_attn,
    m_attn,
    v_attn,
    w_mlp,
    m_mlp,
    v_mlp,
    w_mod,
    m_mod,
    v_mod,
    w_io,
    m_io,
    v_io,
    vectors,
    m_vec,
    v_vec,
):
    bfloat = jnp.bfloat16
    single = jnp.float32
    ctx_index = lax.axis_index("ctx")
    tp_index = lax.axis_index("tp")
    member = ctx_index % 4
    device = jnp.stack([ctx_index, tp_index]).astype(jnp.int32)

    pieces = ring_gather(call_prepare(device, clean, noise, w_attn, w_io, vectors))
    front_meta, attend_meta, row_levels = call_place(device, lengths, order, levels)

    count = step[0].astype(single)
    fixes = jnp.stack([1.0 / (1.0 - beta_one**count), 1.0 / (1.0 - beta_two**count)])

    half_dim = D // 2
    column = ctx_index * 128 + jnp.arange(128, dtype=jnp.int32)
    frequency = jnp.exp(-math.log(10000.0) * (column % half_dim).astype(single) / half_dim)
    angle = row_levels.astype(single)[:, None] * frequency[None, :]
    cond = jax.nn.silu(jnp.where(column[None, :] < half_dim, jnp.cos(angle), jnp.sin(angle)))
    cond_low = cond.astype(bfloat)
    cond_slots = cond_low[:32]
    quarter_cols = 6 * D // 4
    mod_cols = lax.dynamic_slice_in_dim(w_mod, tp_index * quarter_cols, quarter_cols, 1)
    mod_part = jnp.dot(cond_slots, mod_cols.astype(bfloat), preferred_element_type=single)
    mod_held = reduce_along_x(mod_part.reshape(8, 4, quarter_cols), ctx_index, single)
    mod_held = after(mod_held, pieces[2], pieces[5])
    mod_own = after(reduce_along_z(mod_held, ctx_index, single), pieces[3], pieces[6])
    mod_quarters = reorder_four(spread_frames(mod_own), tp_index)
    mod_all = jnp.concatenate(mod_quarters, axis=1)
    mod_rel = jnp.stack(reorder_four([mod_all[k] for k in range(4)], tp_index))
    mod_rel = mod_rel.reshape(4, 6, D)

    time_pairs = HD // 8
    side_pairs = (HD // 2 - time_pairs) // 2

    def frequencies(count):
        return 10000.0 ** (-jnp.arange(count, dtype=single) / count)

    patch = jnp.arange(PATCHES, dtype=jnp.int32)
    half_position = attend_meta[2:].astype(single)
    time_angle = half_position[:, None] * frequencies(time_pairs)[None, :]
    height_angle = frequencies(side_pairs)[:, None] * (patch // GRID).astype(single)[None, :]
    width_angle = frequencies(side_pairs)[:, None] * (patch % GRID).astype(single)[None, :]
    side_angle = jnp.concatenate([height_angle, width_angle], axis=0)

    def full_table(time_part, side_part):
        return jnp.concatenate(
            [
                jnp.broadcast_to(time_part[:, :, None], (HALF_SLOTS, time_pairs, PATCHES)),
                jnp.broadcast_to(side_part[None], (HALF_SLOTS, 2 * side_pairs, PATCHES)),
            ],
            axis=1,
        )

    cosine = full_table(jnp.cos(time_angle), jnp.cos(side_angle))
    sine = full_table(jnp.sin(time_angle), jnp.sin(side_angle))
    signal_scale, noise_scale, weight = plan(row_levels)
    weight_sum = PATCHES * jnp.sum(weight[:32])
    token_scales = jnp.concatenate([signal_scale[64:68], noise_scale[64:68]])
    loss_scales = jnp.stack([weight[64], 2.0 / clean.shape[1] * weight[64] / weight_sum])

    front_meta = after(front_meta, mod_rel, cosine, sine, token_scales, loss_scales, fixes)
    quarters = spread_frames(call_pick(front_meta, pieces))
    front_all, mid_all, hidden_frames, resid_in, *head_blocks, noisy_low, target, mod_own = (
        call_front(front_meta, token_scales, pieces, quarters, mod_rel, cosine, sine)
    )
    hidden_one = hidden_frames.reshape(4 * PATCHES, D)

    out_w = mid_all[:, :256]

    def exchange(blocks):
        return [blocks[0]] + [swap(blocks[k], "ctx", k) for k in (1, 2, 3)]

    head_in = exchange(head_blocks)
    mlp_shard = after(w_mlp.astype(bfloat), *head_in)
    mlp_w = lax.all_gather(mlp_shard, "ctx", axis=1, tiled=True)
    mixed_blocks, lse, mixed = call_attend(attend_meta, head_in)
    mix_low = jnp.concatenate(reorder_four(exchange(mixed_blocks), member), axis=0)

    def project(left, right, dims):
        pairs = []
        for base in (2 * PATCHES, 0):
            part = lax.dot_general(
                left[:, base : base + 2 * PATCHES], right, dims, preferred_element_type=single
            )
            pairs.append((part[:PATCHES], part[PATCHES:].astype(bfloat)))
        return pairs[1], pairs[0]

    near, far = project(mix_low, out_w, (((0,), (1,)), ((), ())))
    attn_out, resid_mid, hidden_own = row_call(
        middle_kernel,
        "middle",
        (frame_f32(), frame_f32(), frame_low()),
        *sum_frames(near, sum_across(far)),
        resid_in,
        mod_own,
    )
    hidden_list = spread_frames(hidden_own)
    wide = (2 * PATCHES, w_mlp.shape[2])
    wide_low = jax.ShapeDtypeStruct(wide, bfloat)
    far = call_mlp(mlp_kernel, "mlp", (wide_low, wide_low), *hidden_list[2:], mlp_w)
    across = sum_across(far)
    near = call_mlp(
        mlp_kernel,
        "mlp",
        (wide_low, wide_low),
        after(hidden_list[0], across),
        hidden_list[1],
        mlp_w,
    )
    active, slope = (near[2], far[2]), (near[3], far[3])
    grad_own, grad_three, head_rows, grad_gate_two, error_part = row_call(
        loss_kernel,
        "loss",
        (
            frame_low(),
            frame_f32(),
            jax.ShapeDtypeStruct((136, D), single),
            jax.ShapeDtypeStruct((1, D), single),
            jax.ShapeDtypeStruct((1, 128), single),
        ),
        loss_scales,
        *sum_frames(near[:2], across),
        resid_mid,
        mod_own,
        mid_all,
        target,
        smem=1,
    )
    grad_list = spread_frames(grad_own)
    near = call_mlp(mlp_back_kernel, "mlp_back", (wide_low,), *grad_list[:2], mlp_w, slope[0])
    far = call_mlp(
        mlp_back_kernel,
        "mlp_back",
        (wide_low,),
        after(grad_list[2], near[0]),
        grad_list[3],
        mlp_w,
        slope[1],
    )
    across = sum_across(far)
    weight_grad = call_weight_grad(
        hidden_list, grad_list, (near[2], after(far[2], across)), active
    )
    scattered = lax.psum_scatter(weight_grad, "ctx", scatter_dimension=0, tiled=True)
    grad_low, grad_mid, rows_two = row_call(
        second_kernel,
        "second",
        (frame_low(), frame_f32(), jax.ShapeDtypeStruct((3, D), single)),
        *sum_frames(near[:2], across),
        after(resid_mid, weight_grad),
        mod_own,
        grad_three,
        attn_out,
    )
    back_list = spread_frames(grad_low)
    grad_attn_low = jnp.concatenate(back_list, axis=0)
    grad_mix = lax.dot_general(
        out_w, grad_attn_low, (((0,), (1,)), ((), ())), preferred_element_type=single
    ).astype(bfloat)
    grad_blocks = reorder_four([grad_mix[HD * k : HD * k + HD] for k in range(4)], member)
    grad_in_blocks = exchange(grad_blocks)
    out_held, out_away = call_head_grad(device, mix_low, after(grad_attn_low, grad_mix))
    out_came = swap(out_away, "ctx", 1)
    grad_in_blocks[0] = after(grad_in_blocks[0], out_held)
    back_blocks = call_attend_back(attend_meta, head_in, grad_in_blocks, lse, mixed, cosine, sine)
    grad_qkv, *parts = call_qkv_back(
        attend_meta, exchange(back_blocks), after(front_all, out_came)
    )
    near, far = parts[:2], parts[2:]
    across = sum_across(far)
    first_terms = sum_frames(near, across)
    qkv_held, qkv_away = call_head_grad(device, after(grad_qkv, across), hidden_one)
    qkv_came = swap(qkv_away, "ctx", 1)
    group_f32 = jax.ShapeDtypeStruct((IO_ROWS, D), single)
    group_low = jax.ShapeDtypeStruct((IO_ROWS, D), bfloat)
    mod_rows, *io_parts, _ = row_call(
        first_kernel,
        "first",
        (
            jax.ShapeDtypeStruct((MOD_ROWS, 128), bfloat),
            group_f32,
            group_low,
            group_f32,
            group_low,
            jax.ShapeDtypeStruct((4 * IO_ROWS, D), single),
        ),
        device,
        *first_terms,
        after(resid_in, qkv_held),
        mod_own,
        grad_mid,
        noisy_low,
        rows_two,
        grad_gate_two,
        head_rows,
        smem=1,
    )
    io_held, io_away = row_call(
        side_kernel,
        "side",
        (
            jax.ShapeDtypeStruct((4, IO_ROWS, 128), single),
            jax.ShapeDtypeStruct((4 * IO_ROWS + MOD_ROWS, 128), bfloat),
        ),
        device,
        *sum_frames(io_parts[:2], sum_across(io_parts[2:])),
        mod_rows,
        smem=1,
    )
    z_rows = jax.ShapeDtypeStruct((ATTN_ROWS + IO_ROWS + 2 * MOD_ROWS, 128), bfloat)
    qkv_own, io_own, *z_pieces = row_call(
        merge_kernel,
        "merge",
        (
            jax.ShapeDtypeStruct((ATTN_ROWS, 128), single),
            jax.ShapeDtypeStruct((IO_ROWS, 128), single),
            jax.ShapeDtypeStruct((2 * MOD_ROWS, 128), bfloat),
            z_rows,
            z_rows,
            z_rows,
        ),
        device,
        qkv_held,
        qkv_came,
        out_held,
        out_came,
        io_held,
        swap(io_away, "ctx", 1),
        mod_rows,
        smem=1,
    )
    red_attn, spread = row_call(
        finish_kernel,
        "finish",
        (
            jax.ShapeDtypeStruct((4, 128, 256), single),
            jax.ShapeDtypeStruct((8 * MOD_ROWS + 2 * IO_ROWS + 16, 128), bfloat),
        ),
        qkv_own,
        io_own,
        z_pieces[0],
        *(swap(piece, "ctx", 2 * bit) for bit, piece in zip((1, 2, 3), z_pieces[1:])),
        scattered,
        error_part,
    )
    all_rows, red_vec, io_grad, square = call_mod_grad(device, cond_low, spread_frames(spread))
    updated = call_adam(
        fixes,
        sum_terms(square),
        (red_attn, scattered, cond_low, all_rows),
        (w_io, m_io, v_io, io_grad[: 2 * 128].reshape(2, 128, 128)),
        (vectors, m_vec, v_vec, red_vec),
        ((w_attn, m_attn, v_attn), (w_mlp, m_mlp, v_mlp), (w_mod, m_mod, v_mod)),
    )
    return (updated[21][1, 64] / weight_sum, updated[21][0, 0], *updated[:21])


def solution(mesh):
    halves = mesh.shape["ctx"] == 8 and mesh.shape["tp"] == 4
    placed = (
        P("ctx", None),
        P("ctx", None),
        P(),
        P(),
        P(),
        P(),
        P(None, "ctx", "tp"),
        P(None, "ctx", "tp"),
        P(None, "ctx", "tp"),
        P(None, "ctx", "tp"),
        P(None, "ctx", "tp"),
        P(None, "ctx", "tp"),
        P("ctx", None),
        P("ctx", None),
        P("ctx", None),
        P(None, None, "ctx"),
        P(None, None, "ctx"),
        P(None, None, "ctx"),
        P(None, "ctx"),
        P(None, "ctx"),
        P(None, "ctx"),
    )
    return jax.shard_map(
        shards_halves if halves else shards,
        mesh=mesh,
        in_specs=placed,
        out_specs=(
            P(),
            P(),
            P(None, "ctx", "tp"),
            P(None, "ctx", "tp"),
            P(None, "ctx", "tp"),
            P(None, "ctx", "tp"),
            P(None, "ctx", "tp"),
            P(None, "ctx", "tp"),
            P(None, "ctx", "tp"),
            P(None, "ctx", "tp"),
            P("ctx", None),
            P("ctx", None),
            P("ctx", None),
            P("ctx", None),
            P(None, None, "ctx"),
            P(None, None, "ctx"),
            P(None, "ctx"),
            P(None, "ctx"),
            P(None, None, "ctx"),
            P(None, "ctx"),
            P(None, "ctx"),
            P(None, "ctx"),
            P(None, "ctx"),
        ),
        check_vma=False,
    )
```

```python
import functools
import math

import jax
import jax.numpy as jnp
from jax import lax
from jax.experimental import pallas as pl
from jax.experimental.pallas import tpu as pltpu
from jax.sharding import PartitionSpec as P

D = 1024
HD = 64
GRID = 16
PATCHES = 256
LEVELS = 1000


ln_eps = 1e-06
snr_limit = 5.0
clip_limit = 0.001
beta_one = 0.9
beta_two = 0.999
adam_eps = 1e-08
rate_matrix = 0.05
rate_vector = 0.3
decay_rate = 0.1
neg_large = -1e30


def clip_starts(frame_ids, lengths):
    clip_ends = jnp.cumsum(lengths)
    before = (clip_ends[None, :] <= frame_ids[:, None]).astype(jnp.int32)
    return jnp.sum(before * lengths[None, :], axis=1)


def plan(levels):
    fraction = (levels.astype(jnp.float32) + 1.0) / (LEVELS + 1.0)
    signal_scale = jnp.cos(0.5 * math.pi * fraction)
    noise_scale = jnp.sin(0.5 * math.pi * fraction)
    snr_value = signal_scale * signal_scale / (noise_scale * noise_scale)
    weight = jnp.minimum(snr_value, snr_limit) / (snr_value + 1.0)
    return (signal_scale, noise_scale, weight)


def condition(levels, width):
    half_dim = width // 2
    frequency = jnp.exp(-math.log(10000.0) * jnp.arange(half_dim, dtype=jnp.float32) / half_dim)
    angle_tab = levels.astype(jnp.float32)[:, None] * frequency[None, :]
    return jax.nn.silu(jnp.concatenate([jnp.cos(angle_tab), jnp.sin(angle_tab)], axis=1))


def rope_tables(time_pos, height_pos, width_pos, head_dim):
    pair_count = head_dim // 2
    time_pairs = head_dim // 8
    height_pairs = (pair_count - time_pairs) // 2
    width_pairs = pair_count - time_pairs - height_pairs

    def angles(position, count):
        frequency = 10000.0 ** (-jnp.arange(count, dtype=jnp.float32) / count)
        return position.astype(jnp.float32)[:, None] * frequency[None, :]

    angle_tab = jnp.concatenate(
        [
            angles(time_pos, time_pairs),
            angles(height_pos, height_pairs),
            angles(width_pos, width_pairs),
        ],
        axis=1,
    )
    return (jnp.cos(angle_tab), jnp.sin(angle_tab))


def rotate(values, cosine, sine):
    half_dim = values.shape[-1] // 2
    first_half = values[..., :half_dim]
    second_half = values[..., half_dim:]
    cosine = cosine[:, None, :]
    sine = sine[:, None, :]
    return jnp.concatenate(
        [first_half * cosine - second_half * sine, second_half * cosine + first_half * sine],
        axis=-1,
    )


def rotate_back(grads, cosine, sine):
    half_dim = grads.shape[-1] // 2
    first_half = grads[..., :half_dim]
    second_half = grads[..., half_dim:]
    cosine = cosine[:, None, :]
    sine = sine[:, None, :]
    return jnp.concatenate(
        [first_half * cosine + second_half * sine, second_half * cosine - first_half * sine],
        axis=-1,
    )


def layer_norm(values):
    centred = values - jnp.mean(values, axis=-1, keepdims=True)
    inv_std = lax.rsqrt(jnp.mean(centred * centred, axis=-1, keepdims=True) + ln_eps)
    return (centred * inv_std, inv_std)


def norm_back(grad_in, normed, inv_std):
    mean_grad = jnp.mean(grad_in, axis=-1, keepdims=True)
    mean_proj = jnp.mean(grad_in * normed, axis=-1, keepdims=True)
    return inv_std * (grad_in - mean_grad - normed * mean_proj)


def gelu_slope(values):
    return 0.5 * (1.0 + lax.erf(values / math.sqrt(2.0))) + values * jnp.exp(
        -0.5 * values * values
    ) / math.sqrt(2.0 * math.pi)


def stretch_mask(query_stretch, key_stretch, stretch_frames, lengths):
    offsets = jnp.arange(stretch_frames, dtype=jnp.int32)
    query_frames = query_stretch * stretch_frames + offsets
    key_frames = key_stretch * stretch_frames + offsets
    starts = clip_starts(query_frames, lengths)
    return (key_frames[None, :] <= query_frames[:, None]) & (key_frames[None, :] >= starts[:, None])


def expand_mask(allowed):
    return jnp.repeat(jnp.repeat(allowed, PATCHES, axis=0), PATCHES, axis=1)


def online_step(current, query_block, key_block, value_block, keep, scale):
    run_max, run_sum, run_acc = current
    scores = (
        jnp.einsum("qhe,khe->hqk", query_block, key_block, preferred_element_type=jnp.float32)
        * scale
    )
    scores = jnp.where(keep[None], scores, neg_large)
    new_max = jnp.maximum(run_max, jnp.max(scores, axis=-1))
    probs = jnp.where(keep[None], jnp.exp(scores - new_max[..., None]), 0.0)
    shrink = jnp.exp(run_max - new_max)
    run_sum = run_sum * shrink + jnp.sum(probs, axis=-1)
    added = jnp.einsum(
        "hqk,khe->qhe", probs.astype(jnp.bfloat16), value_block, preferred_element_type=jnp.float32
    )
    run_acc = run_acc * jnp.transpose(shrink)[:, :, None] + added
    return (new_max, run_sum, run_acc)


def pair_grads(
    query_block, grad_block, lse_block, delta_block, key_block, value_block, keep, scale
):
    scores = (
        jnp.einsum("qhe,khe->hqk", query_block, key_block, preferred_element_type=jnp.float32)
        * scale
    )
    probs = jnp.where(keep[None], jnp.exp(scores - lse_block[..., None]), 0.0)
    grad_probs = jnp.einsum(
        "qhe,khe->hqk", grad_block, value_block, preferred_element_type=jnp.float32
    )
    grad_scores = (probs * (grad_probs - delta_block[..., None])).astype(jnp.bfloat16)
    grad_query = (
        jnp.einsum("hqk,khe->qhe", grad_scores, key_block, preferred_element_type=jnp.float32)
        * scale
    )
    grad_key = (
        jnp.einsum("hqk,qhe->khe", grad_scores, query_block, preferred_element_type=jnp.float32)
        * scale
    )
    grad_value = jnp.einsum(
        "hqk,qhe->khe", probs.astype(jnp.bfloat16), grad_block, preferred_element_type=jnp.float32
    )
    return (grad_query, grad_key, grad_value)


def adam(weight_now, first_mom, second_mom, grad, factor, count, rate, decay):
    grad = grad * factor
    first_mom = beta_one * first_mom + (1.0 - beta_one) * grad
    second_mom = beta_two * second_mom + (1.0 - beta_two) * grad * grad
    first_hat = first_mom / (1.0 - beta_one**count)
    second_hat = second_mom / (1.0 - beta_two**count)
    updated = weight_now - rate * (
        first_hat / (jnp.sqrt(second_hat) + adam_eps) + decay * weight_now
    )
    return (updated, first_mom, second_mom, updated.astype(jnp.bfloat16))


def shards(
    clean,
    noise,
    levels,
    lengths,
    order,
    step,
    w_attn,
    m_attn,
    v_attn,
    w_mlp,
    m_mlp,
    v_mlp,
    w_mod,
    m_mod,
    v_mod,
    w_io,
    m_io,
    v_io,
    vectors,
    m_vec,
    v_vec,
):
    ctx_count = lax.axis_size("ctx")
    ctx_index = lax.axis_index("ctx")
    tp_index = lax.axis_index("tp")
    tok_rows = clean.shape[0]
    feat_dim = clean.shape[1]
    frames_dev = tok_rows // PATCHES
    stretch_frames = frames_dev // 2
    stretch_rows = stretch_frames * PATCHES
    scale = HD ** (-0.5)
    bfloat = jnp.bfloat16
    single = jnp.float32
    attn_w, mlp_w, mod_w, io_w, vec_low = (
        lax.all_gather(w_attn.astype(bfloat), "ctx", axis=1, tiled=True),
        lax.all_gather(w_mlp.astype(bfloat), "ctx", axis=1, tiled=True),
        lax.all_gather(w_mod.astype(bfloat), "ctx", axis=0, tiled=True),
        lax.all_gather(w_io.astype(bfloat), "ctx", axis=2, tiled=True),
        lax.all_gather(vectors.astype(bfloat), "ctx", axis=1, tiled=True),
    )
    vec_w = vec_low.astype(single)
    local_width = attn_w.shape[2]
    heads_dev = local_width // HD
    frame_count = levels.shape[0]
    local_stretches = lax.dynamic_slice_in_dim(order, 2 * ctx_index, 2, 0)
    frame_ids = (
        local_stretches[:, None] * stretch_frames
        + jnp.arange(stretch_frames, dtype=jnp.int32)[None, :]
    ).reshape(frames_dev)
    table_hit = frame_ids[:, None] == jnp.arange(frame_count, dtype=jnp.int32)[None, :]
    frame_levels = jnp.sum(jnp.where(table_hit, levels[None, :], 0), axis=1)
    starts = clip_starts(frame_ids, lengths)
    signal_scale, noise_scale, weight = plan(frame_levels)
    signal_col = signal_scale[:, None, None]
    noise_col = noise_scale[:, None, None]
    clean_full = clean.astype(single).reshape(frames_dev, PATCHES, feat_dim)
    noise_full = noise.astype(single).reshape(frames_dev, PATCHES, feat_dim)
    noisy = signal_col * clean_full + noise_col * noise_full
    target = signal_col * noise_full - noise_col * clean_full
    noisy_low = noisy.reshape(tok_rows, feat_dim).astype(bfloat)
    embedded = jnp.dot(noisy_low, io_w[0], preferred_element_type=single) + vec_w[6]
    cond_low = condition(frame_levels, D).astype(bfloat)
    modulate = (
        jnp.dot(cond_low, mod_w, preferred_element_type=single) + vec_w[:6].reshape(6 * D)
    ).reshape(frames_dev, 6, 1, D)
    patch_ids = jnp.arange(PATCHES, dtype=jnp.int32)
    time_pos = jnp.repeat(frame_ids - starts, PATCHES)
    height_pos = jnp.tile(patch_ids // GRID, frames_dev)
    width_pos = jnp.tile(patch_ids % GRID, frames_dev)
    cosine, sine = rope_tables(time_pos, height_pos, width_pos, HD)
    resid_in = embedded.reshape(frames_dev, PATCHES, D)
    normed_one, inv_one = layer_norm(resid_in)
    hidden_one = (
        (normed_one * (1.0 + modulate[:, 1]) + modulate[:, 0]).reshape(tok_rows, D).astype(bfloat)
    )
    query_pre = jnp.dot(hidden_one, attn_w[0], preferred_element_type=single).reshape(
        tok_rows, heads_dev, HD
    )
    key_pre = jnp.dot(hidden_one, attn_w[1], preferred_element_type=single).reshape(
        tok_rows, heads_dev, HD
    )
    query_low = rotate(query_pre, cosine, sine).astype(bfloat)
    key_low = rotate(key_pre, cosine, sine).astype(bfloat)
    value_low = (
        jnp.dot(hidden_one, attn_w[2], preferred_element_type=single)
        .astype(bfloat)
        .reshape(tok_rows, heads_dev, HD)
    )
    query_stretches = query_low.reshape(2, stretch_rows, heads_dev, HD)
    init_state = (
        jnp.full((2, heads_dev, stretch_rows), neg_large, single),
        jnp.zeros((2, heads_dev, stretch_rows), single),
        jnp.zeros((2, stretch_rows, heads_dev, HD), single),
    )
    key_flat = key_low.reshape(tok_rows, local_width)
    value_flat = value_low.reshape(tok_rows, local_width)
    carry_state = init_state
    key_piece = lax.all_gather(key_flat, "ctx", axis=0, tiled=True)
    value_piece = lax.all_gather(value_flat, "ctx", axis=0, tiled=True)

    def per_stretch(block_num, carry_state):
        key_block = lax.dynamic_slice_in_dim(
            key_piece, block_num * stretch_rows, stretch_rows, 0
        ).reshape(stretch_rows, heads_dev, HD)
        value_block = lax.dynamic_slice_in_dim(
            value_piece, block_num * stretch_rows, stretch_rows, 0
        ).reshape(stretch_rows, heads_dev, HD)
        key_stretch = lax.dynamic_index_in_dim(order, block_num, 0, keepdims=False)
        updated = []
        for half_num in range(2):
            allowed = stretch_mask(local_stretches[half_num], key_stretch, stretch_frames, lengths)
            current = (carry_state[0][half_num], carry_state[1][half_num], carry_state[2][half_num])
            current = lax.cond(
                jnp.any(allowed),
                lambda cur, keep_mask: online_step(
                    cur,
                    query_stretches[half_num],
                    key_block,
                    value_block,
                    expand_mask(keep_mask),
                    scale,
                ),
                lambda cur, keep_mask: cur,
                current,
                allowed,
            )
            updated.append(current)
        return tuple((jnp.stack([updated[0][member], updated[1][member]]) for member in range(3)))

    run_max, run_sum, run_acc = lax.fori_loop(
        0, key_piece.shape[0] // stretch_rows, per_stretch, carry_state
    )
    mix_rows = (run_acc / jnp.transpose(run_sum, (0, 2, 1))[..., None]).reshape(
        tok_rows, heads_dev, HD
    )
    lse_stretches = run_max + jnp.log(run_sum)
    mix_low = mix_rows.reshape(tok_rows, local_width).astype(bfloat)
    attn_out = lax.psum(
        jnp.einsum("rh,dh->rd", mix_low, attn_w[3], preferred_element_type=single).astype(
            jnp.bfloat16
        ),
        "tp",
    ).astype(jnp.float32)
    attn_full = attn_out.reshape(frames_dev, PATCHES, D)
    resid_mid = resid_in + modulate[:, 2] * attn_full
    normed_two, inv_two = layer_norm(resid_mid)
    hidden_two = (
        (normed_two * (1.0 + modulate[:, 4]) + modulate[:, 3]).reshape(tok_rows, D).astype(bfloat)
    )
    upward = jnp.dot(hidden_two, mlp_w[0], preferred_element_type=single)
    activ_low = jax.nn.gelu(upward, approximate=False).astype(bfloat)
    mlp_out = lax.psum(
        jnp.einsum("rf,df->rd", activ_low, mlp_w[1], preferred_element_type=single).astype(
            jnp.bfloat16
        ),
        "tp",
    ).astype(jnp.float32)
    mlp_full = mlp_out.reshape(frames_dev, PATCHES, D)
    resid_out = resid_mid + modulate[:, 5] * mlp_full
    normed_three, inv_three = layer_norm(resid_out)
    final_low = (normed_three * vec_w[7]).reshape(tok_rows, D).astype(bfloat)
    pred = jnp.einsum("rd,pd->rp", final_low, io_w[1], preferred_element_type=single)
    diff = pred.reshape(frames_dev, PATCHES, feat_dim) - target
    error = jnp.mean(diff * diff, axis=2)
    weight_sum, error_sum = lax.psum(
        (PATCHES * jnp.sum(weight), jnp.sum(weight[:, None] * error)), "ctx"
    )
    loss_value = error_sum / weight_sum
    grad_pred = (
        (2.0 / feat_dim * weight[:, None, None] * diff / weight_sum)
        .reshape(tok_rows, feat_dim)
        .astype(bfloat)
    )
    grad_head = jnp.einsum("rp,rd->pd", grad_pred, final_low, preferred_element_type=single)
    grad_final = jnp.einsum("rp,pd->rd", grad_pred, io_w[1], preferred_element_type=single).reshape(
        frames_dev, PATCHES, D
    )
    grad_gain = jnp.sum(grad_final * normed_three, axis=(0, 1))
    grad_three = norm_back(grad_final * vec_w[7], normed_three, inv_three)
    grad_mlp_low = (modulate[:, 5] * grad_three).reshape(tok_rows, D).astype(bfloat)
    grad_gate_two = jnp.sum(grad_three * mlp_full, axis=1)
    grad_activ = jnp.einsum("rd,df->rf", grad_mlp_low, mlp_w[1], preferred_element_type=single)
    grad_down = jnp.einsum("rd,rf->df", grad_mlp_low, activ_low, preferred_element_type=single)
    grad_up_low = (grad_activ * gelu_slope(upward)).astype(bfloat)
    grad_up = jnp.einsum("rd,rf->df", hidden_two, grad_up_low, preferred_element_type=single)
    grad_hidden_two = lax.psum(
        jnp.einsum("rf,df->rd", grad_up_low, mlp_w[0], preferred_element_type=single).astype(
            jnp.bfloat16
        ),
        "tp",
    ).astype(jnp.float32)
    grad_hidden_two = grad_hidden_two.reshape(frames_dev, PATCHES, D)
    grad_shift_two = jnp.sum(grad_hidden_two, axis=1)
    grad_scale_two = jnp.sum(grad_hidden_two * normed_two, axis=1)
    grad_mid = grad_three + norm_back(grad_hidden_two * (1.0 + modulate[:, 4]), normed_two, inv_two)
    grad_attn_low = (modulate[:, 2] * grad_mid).reshape(tok_rows, D).astype(bfloat)
    grad_gate_one = jnp.sum(grad_mid * attn_full, axis=1)
    grad_outproj = jnp.einsum("rd,rh->dh", grad_attn_low, mix_low, preferred_element_type=single)
    grad_mix_low = jnp.einsum(
        "rd,dh->rh", grad_attn_low, attn_w[3], preferred_element_type=single
    ).astype(bfloat)
    delta_rows = jnp.sum(
        grad_mix_low.astype(single).reshape(tok_rows, heads_dev, HD) * mix_rows, axis=2
    )
    grad_stretches = grad_mix_low.reshape(2, stretch_rows, heads_dev, HD)
    delta_stretches = jnp.transpose(delta_rows.reshape(2, stretch_rows, heads_dev), (0, 2, 1))

    def span_back(key_block, value_block, key_stretch, grad_query_acc):
        key_sum = jnp.zeros((stretch_rows, heads_dev, HD), single)
        value_sum = jnp.zeros((stretch_rows, heads_dev, HD), single)
        query_parts = []
        for half_num in range(2):
            allowed = stretch_mask(local_stretches[half_num], key_stretch, stretch_frames, lengths)
            result = lax.cond(
                jnp.any(allowed),
                lambda keep_mask: pair_grads(
                    query_stretches[half_num],
                    grad_stretches[half_num],
                    lse_stretches[half_num],
                    delta_stretches[half_num],
                    key_block,
                    value_block,
                    expand_mask(keep_mask),
                    scale,
                ),
                lambda keep_mask: (jnp.zeros((stretch_rows, heads_dev, HD), single),) * 3,
                allowed,
            )
            query_parts.append(grad_query_acc[half_num] + result[0])
            key_sum = key_sum + result[1]
            value_sum = value_sum + result[2]
        return (
            jnp.stack(query_parts),
            key_sum.reshape(stretch_rows, local_width),
            value_sum.reshape(stretch_rows, local_width),
        )

    init_back = (
        jnp.zeros((2, stretch_rows, heads_dev, HD), single),
        jnp.zeros((ctx_count * tok_rows, local_width), single),
        jnp.zeros((ctx_count * tok_rows, local_width), single),
    )
    carry_state = init_back
    fold_key_piece = lax.all_gather(key_flat, "ctx", axis=0, tiled=True)
    fold_value_piece = lax.all_gather(value_flat, "ctx", axis=0, tiled=True)

    def per_stretch(block_num, carry_state):
        grad_query_acc, grad_keys_all, grad_values_all = carry_state
        key_block = lax.dynamic_slice_in_dim(
            fold_key_piece, block_num * stretch_rows, stretch_rows, 0
        ).reshape(stretch_rows, heads_dev, HD)
        value_block = lax.dynamic_slice_in_dim(
            fold_value_piece, block_num * stretch_rows, stretch_rows, 0
        ).reshape(stretch_rows, heads_dev, HD)
        key_stretch = lax.dynamic_index_in_dim(order, block_num, 0, keepdims=False)
        grad_query_acc, key_sum, value_sum = span_back(
            key_block, value_block, key_stretch, grad_query_acc
        )
        place = block_num * stretch_rows
        grad_keys_all = lax.dynamic_update_slice_in_dim(grad_keys_all, key_sum, place, 0)
        grad_values_all = lax.dynamic_update_slice_in_dim(grad_values_all, value_sum, place, 0)
        return (grad_query_acc, grad_keys_all, grad_values_all)

    grad_query_acc, grad_keys_all, grad_values_all = lax.fori_loop(
        0, fold_key_piece.shape[0] // stretch_rows, per_stretch, carry_state
    )
    grad_keys, grad_values = (
        lax.psum_scatter(
            grad_keys_all.astype(jnp.bfloat16), "ctx", scatter_dimension=0, tiled=True
        ).astype(jnp.float32),
        lax.psum_scatter(
            grad_values_all.astype(jnp.bfloat16), "ctx", scatter_dimension=0, tiled=True
        ).astype(jnp.float32),
    )
    grad_query = grad_query_acc.reshape(tok_rows, local_width)
    query_back = (
        rotate_back(grad_query.reshape(tok_rows, heads_dev, HD), cosine, sine)
        .reshape(tok_rows, local_width)
        .astype(bfloat)
    )
    key_back = (
        rotate_back(grad_keys.reshape(tok_rows, heads_dev, HD), cosine, sine)
        .reshape(tok_rows, local_width)
        .astype(bfloat)
    )
    value_back = grad_values.astype(bfloat)
    grad_wq = jnp.einsum("rd,rh->dh", hidden_one, query_back, preferred_element_type=single)
    grad_wk = jnp.einsum("rd,rh->dh", hidden_one, key_back, preferred_element_type=single)
    grad_wv = jnp.einsum("rd,rh->dh", hidden_one, value_back, preferred_element_type=single)
    partial_one = (
        jnp.einsum("rh,dh->rd", query_back, attn_w[0], preferred_element_type=single)
        + jnp.einsum("rh,dh->rd", key_back, attn_w[1], preferred_element_type=single)
        + jnp.einsum("rh,dh->rd", value_back, attn_w[2], preferred_element_type=single)
    )
    grad_hidden_one = (
        lax.psum(partial_one.astype(jnp.bfloat16), "tp")
        .astype(jnp.float32)
        .reshape(frames_dev, PATCHES, D)
    )
    grad_shift_one = jnp.sum(grad_hidden_one, axis=1)
    grad_scale_one = jnp.sum(grad_hidden_one * normed_one, axis=1)
    grad_in = grad_mid + norm_back(grad_hidden_one * (1.0 + modulate[:, 1]), normed_one, inv_one)
    grad_mod = jnp.stack(
        [
            grad_shift_one,
            grad_scale_one,
            grad_gate_one,
            grad_shift_two,
            grad_scale_two,
            grad_gate_two,
        ],
        axis=1,
    )
    grad_mod_w = jnp.einsum(
        "fd,fc->dc",
        cond_low,
        grad_mod.reshape(frames_dev, 6 * D).astype(bfloat),
        preferred_element_type=single,
    )
    grad_in_low = grad_in.reshape(tok_rows, D).astype(bfloat)
    grad_embed = jnp.einsum("rp,rd->pd", noisy_low, grad_in_low, preferred_element_type=single)
    grad_vec = jnp.concatenate(
        [jnp.sum(grad_mod, axis=0), jnp.sum(grad_in, axis=(0, 1))[None], grad_gain[None]], axis=0
    )
    grad_attn = jnp.stack([grad_wq, grad_wk, grad_wv, grad_outproj])
    grad_mlp = jnp.stack([grad_up, grad_down])
    grad_io = jnp.stack([grad_embed, grad_head])
    red_attn, red_mlp, red_mod, red_io, red_vec = (
        lax.psum_scatter(
            grad_attn.astype(jnp.bfloat16), "ctx", scatter_dimension=1, tiled=True
        ).astype(jnp.float32),
        lax.psum_scatter(
            grad_mlp.astype(jnp.bfloat16), "ctx", scatter_dimension=1, tiled=True
        ).astype(jnp.float32),
        lax.psum_scatter(
            grad_mod_w.astype(jnp.bfloat16), "ctx", scatter_dimension=0, tiled=True
        ).astype(jnp.float32),
        lax.psum_scatter(
            grad_io.astype(jnp.bfloat16), "ctx", scatter_dimension=2, tiled=True
        ).astype(jnp.float32),
        lax.psum_scatter(
            grad_vec.astype(jnp.bfloat16), "ctx", scatter_dimension=1, tiled=True
        ).astype(jnp.float32),
    )
    shared_sq = jnp.sum(red_mod * red_mod) + jnp.sum(red_io * red_io) + jnp.sum(red_vec * red_vec)
    own_sq = (
        jnp.sum(red_attn * red_attn)
        + jnp.sum(red_mlp * red_mlp)
        + jnp.where(tp_index == 0, shared_sq, 0.0)
    )
    grad_norm = jnp.sqrt(lax.psum(own_sq, ("ctx", "tp")))
    factor = jnp.minimum(1.0, clip_limit / (grad_norm + 1e-06))
    count = step[0].astype(single)
    attn_new = adam(w_attn, m_attn, v_attn, red_attn, factor, count, rate_matrix, decay_rate)
    mlp_new = adam(w_mlp, m_mlp, v_mlp, red_mlp, factor, count, rate_matrix, decay_rate)
    mod_new = adam(w_mod, m_mod, v_mod, red_mod, factor, count, rate_matrix, decay_rate)
    io_new = adam(w_io, m_io, v_io, red_io, factor, count, rate_matrix, decay_rate)
    vec_new = adam(vectors, m_vec, v_vec, red_vec, factor, count, rate_vector, 0.0)
    return (
        loss_value,
        grad_norm,
        attn_new[0],
        attn_new[1],
        attn_new[2],
        attn_new[3],
        mlp_new[0],
        mlp_new[1],
        mlp_new[2],
        mlp_new[3],
        mod_new[0],
        mod_new[1],
        mod_new[2],
        mod_new[3],
        io_new[0],
        io_new[1],
        io_new[2][0],
        io_new[2][1],
        io_new[3],
        vec_new[0],
        vec_new[1],
        vec_new[2],
        vec_new[3],
    )


HALF_SLOTS = 16
QKV_ROWS = 768
ATTN_ROWS = 1024
FRONT_ROWS = 912
TOKEN_ROWS = 512
IO_ROWS = 80
MOD_ROWS = 48
NT = (((1,), (1,)), ((), ()))
TN = (((0,), (0,)), ((), ()))


def swap(values, axis, bit):
    size = 8 if axis == "ctx" else 4
    return lax.ppermute(values, axis, [(i, i ^ bit) for i in range(size)])


def after(values, *others):
    return lax.optimization_barrier((values,) + others)[0]


def gather_swaps(shard):
    along_x = swap(shard, "ctx", 1)
    along_z = [swap(shard, "ctx", bit) for bit in (2, 4, 6)]
    return [shard, along_x, *along_z, swap(jnp.concatenate(along_z, axis=0), "ctx", 1)]


def reduce_blocks(blocks, ctx_index, wire):
    return reduce_along_z(reduce_along_x(blocks, ctx_index, wire), ctx_index, wire)


def reduce_along_x(blocks, ctx_index, wire):
    x = ctx_index % 2
    pairs = blocks.reshape((4, 2) + blocks.shape[1:])
    first, second = pairs[:, 0], pairs[:, 1]
    even = x == 0
    away = jnp.where(even, second, first).astype(wire)
    return jnp.where(even, first, second) + swap(away, "ctx", 1).astype(jnp.float32)


def pieces_along_z(held, ctx_index, wire):
    z = ctx_index // 2
    low = held.astype(wire)
    came = []
    for bit in (1, 2, 3):
        piece = lax.dynamic_index_in_dim(low, z ^ bit, 0, keepdims=False)
        came.append(swap(piece, "ctx", 2 * bit))
    return lax.dynamic_index_in_dim(held, z, 0, keepdims=False), came


def reduce_along_z(held, ctx_index, wire):
    total, came = pieces_along_z(held, ctx_index, wire)
    for piece in came:
        total = total + piece.astype(jnp.float32)
    return total


def spread_frames(own):
    core = swap(own, "tp", 1)
    across = swap(own, "tp", 2)
    return [own, core, across, swap(across, "tp", 1)]


def sum_across(far):
    return (far[0] + swap(far[1], "tp", 1).astype(jnp.float32)).astype(jnp.bfloat16)


def sum_frames(near, across):
    return near[0], swap(near[1], "tp", 1), swap(across, "tp", 2)


def reorder_four(items, index):
    low_bit = (index & 1) == 1
    high_bit = (index & 2) == 2
    once = [jnp.where(low_bit, items[k ^ 1], items[k]) for k in range(4)]
    return [jnp.where(high_bit, once[k ^ 2], once[k]) for k in range(4)]


def sum_terms(values):
    values = values + swap(values, "ctx", 1)
    return [values] + [swap(values, "ctx", bit) for bit in (2, 4, 6)]


def token_kernel(meta, clean, noise, ring):
    for frame in range(4):
        rows = pl.ds(pl.multiple_of(256 * frame + 64 * meta[1], 64), 64)
        ring[128 * frame : 128 * frame + 64, :] = clean[rows, :]
        ring[128 * frame + 64 : 128 * frame + 128, :] = noise[rows, :]


def prepare_kernel(w_attn, w_io, vectors, front):
    for part in range(3):
        front[256 * part : 256 * part + 256, :] = w_attn[part].T.astype(jnp.bfloat16)
    base = QKV_ROWS
    front[base : base + 128, :] = w_io[0].astype(jnp.bfloat16)
    front[base + 128 : base + 144, :] = jnp.concatenate(
        [vectors[...], jnp.zeros((8, 128), jnp.float32)], axis=0
    ).astype(jnp.bfloat16)
    for part in range(2):
        base = FRONT_ROWS + 128 * part
        front[base : base + 128, :] = w_attn[3, :, 128 * part : 128 * part + 128].astype(
            jnp.bfloat16
        )
    front[FRONT_ROWS + 256 : FRONT_ROWS + 384, :] = w_io[1].T.astype(jnp.bfloat16)


def vmem_specs(count):
    return [pl.BlockSpec(memory_space=pltpu.VMEM)] * count


def smem_specs(count):
    return [pl.BlockSpec(memory_space=pltpu.SMEM)] * count


def call_tokens(device, clean, noise):
    return pl.pallas_call(
        token_kernel,
        out_shape=jax.ShapeDtypeStruct((TOKEN_ROWS, 128), jnp.bfloat16),
        in_specs=smem_specs(1) + vmem_specs(2),
        out_specs=vmem_specs(1)[0],
        name="tokens",
    )(device, clean, noise)


def call_prepare(w_attn, w_io, vectors):
    return pl.pallas_call(
        prepare_kernel,
        out_shape=jax.ShapeDtypeStruct((FRONT_ROWS + 384, 128), jnp.bfloat16),
        in_specs=vmem_specs(3),
        out_specs=vmem_specs(1)[0],
        name="prepare",
    )(w_attn, w_io, vectors)


def place_kernel(device, lengths, order, levels, front, attend, rows, inverse, stored, position, level):
    ctx, tp = device[0], device[1]
    frames, stretches, clips = levels.shape[0], order.shape[0], lengths.shape[0]
    per_stretch = frames // stretches
    half = frames // 2

    def per_stretch_place(place, carry):
        inverse[order[place]] = place
        return carry

    lax.fori_loop(0, stretches, per_stretch_place, 0)

    def per_frame(frame, counts):
        long_count, short_count = counts
        begin, start, length = jnp.int32(0), jnp.int32(0), jnp.int32(0)
        for clip in range(clips):
            size = lengths[clip]
            inside = (frame >= begin) & (frame < begin + size)
            start = jnp.where(inside, begin, start)
            length = jnp.where(inside, size, length)
            begin = begin + size
        is_long = length == half
        slot = jnp.where(is_long, long_count, half + short_count)
        stored[slot] = inverse[lax.div(frame, jnp.int32(per_stretch))] * per_stretch + lax.rem(
            frame, jnp.int32(per_stretch)
        )
        position[slot] = frame - start
        level[slot] = levels[frame]
        grown = is_long.astype(jnp.int32)
        return (long_count + grown, short_count + 1 - grown)

    lax.fori_loop(0, frames, per_frame, (jnp.int32(0), jnp.int32(0)))

    member = ctx & 3
    for k in range(4):
        front[8 + k] = 4 * member + (tp ^ k)
        front[12 + k] = member ^ k
        at = stored[4 * ctx + (tp ^ k)]
        front[16 + k] = ((at >> 2) ^ ctx) * 4 + (at & 3)
        front[20 + k] = tp ^ k
    for k in range(8):
        front[k] = 0
    attend[0] = member
    attend[1] = tp
    base = lax.div(ctx, jnp.int32(4)) * half

    def per_slot(slot, carry):
        attend[2 + slot] = position[base + slot]
        return carry

    lax.fori_loop(0, half, per_slot, 0)

    def per_row(row, carry):
        rows[row] = level[row]
        rows[frames + row] = level[4 * (ctx ^ (row & 7)) + (row >> 3)]
        return carry

    lax.fori_loop(0, frames, per_row, 0)
    for k in range(8):
        rows[2 * frames + k] = level[4 * ctx + (tp ^ (k & 3))]


def call_place(device, lengths, order, levels):
    frames = levels.shape[0]
    return pl.pallas_call(
        place_kernel,
        out_shape=(
            jax.ShapeDtypeStruct((24,), jnp.int32),
            jax.ShapeDtypeStruct((2 + frames // 2,), jnp.int32),
            jax.ShapeDtypeStruct((2 * frames + 8,), jnp.int32),
        ),
        in_specs=smem_specs(4),
        out_specs=smem_specs(3),
        scratch_shapes=[pltpu.SMEM((order.shape[0],), jnp.int32)]
        + [pltpu.SMEM((frames,), jnp.int32)] * 3,
        name="place",
    )(device, lengths, order, levels)


def pick_kernel(meta, *refs):
    out, sems = refs[6:]
    places = [(refs[0], 0), (refs[1], 0)]
    for bit in range(3):
        places += [(refs[2 + bit], 0), (refs[5], TOKEN_ROWS * bit)]
    for frame in range(4):
        wanted = meta[16 + frame]
        for place, (source, base) in enumerate(places):

            @pl.when((wanted >> 2) == place)
            def _():
                start = pl.multiple_of(base + (wanted & 3) * 128, 128)
                pltpu.make_async_copy(
                    source.at[pl.ds(start, 128), :],
                    out.at[128 * frame : 128 * frame + 128, :],
                    sems.at[frame],
                ).start()

    for frame in range(4):
        pltpu.make_async_copy(
            refs[0].at[0:128, :], out.at[128 * frame : 128 * frame + 128, :], sems.at[frame]
        ).wait()


def hbm_specs(count):
    return [pl.BlockSpec(memory_space=pltpu.HBM)] * count


def call_pick(meta, pieces):
    return pl.pallas_call(
        pick_kernel,
        out_shape=jax.ShapeDtypeStruct((TOKEN_ROWS, 128), jnp.bfloat16),
        in_specs=smem_specs(1) + hbm_specs(6),
        out_specs=vmem_specs(1)[0],
        scratch_shapes=[pltpu.SemaphoreType.DMA((4,))],
        compiler_params=pltpu.CompilerParams(vmem_limit_bytes=56 * 2**20),
        name="pick",
    )(meta, *pieces)


def centred_norm(values):
    centred = values - jnp.mean(values, axis=-1, keepdims=True)
    inv_std = lax.rsqrt(jnp.mean(centred * centred, axis=-1, keepdims=True) + ln_eps)
    return centred * inv_std, inv_std


def front_kernel(meta, scales, *refs):
    pieces, quarters = refs[0], refs[1:5]
    mod, cosine, sine = refs[5:8]
    weights_out, mid_out, hidden_out, resid_out = refs[8:12]
    head_outs = refs[12:16]
    noisy_out, target_out, mod_out = refs[16:19]
    tokens, heads, weights, mid, hidden, resid, target, mod_own, held, sems, out_sems = refs[19:]
    copies = [
        pltpu.make_async_copy(pieces.at[place], held.at[place], sems.at[place])
        for place in range(8)
    ]
    for copy in copies:
        copy.start()
    for source in range(4):
        rows = pl.ds(pl.multiple_of(meta[20 + source] * 64, 64), 64)
        for frame in range(4):
            base = 128 * (frame ^ source)
            clean = quarters[source][base : base + 64, :].astype(jnp.float32)
            noise = quarters[source][base + 64 : base + 128, :].astype(jnp.float32)
            mixed = scales[frame] * clean + scales[4 + frame] * noise
            tokens[frame, rows, :] = mixed.astype(jnp.bfloat16)
            if frame == 0:
                target[rows, :] = scales[0] * noise - scales[4] * clean
    outs = [
        pltpu.make_async_copy(tokens.at[0], noisy_out, out_sems.at[0]),
        pltpu.make_async_copy(target, target_out, out_sems.at[1]),
        pltpu.make_async_copy(weights, weights_out, out_sems.at[2]),
        pltpu.make_async_copy(resid, resid_out, out_sems.at[3]),
    ] + [
        pltpu.make_async_copy(hidden.at[frame], hidden_out.at[frame], out_sems.at[4 + frame])
        for frame in range(4)
    ]
    outs.append(pltpu.make_async_copy(mod_own, mod_out, out_sems.at[8]))
    outs.append(pltpu.make_async_copy(mid, mid_out, out_sems.at[9]))
    for place in range(8):
        copies[place].wait()
        block = slice(128 * place, 128 * place + 128)
        weights[:, block] = held[place, 0:FRONT_ROWS, :]
        for part in range(3):
            base = FRONT_ROWS + 128 * part
            mid[block, 128 * part : 128 * part + 128] = held[place, base : base + 128, :]
    for index in (0, 1, 2, 9):
        outs[index].start()
    embed = weights[QKV_ROWS : QKV_ROWS + 128, :]
    vec_rows = weights[QKV_ROWS + 128 : FRONT_ROWS, :].astype(jnp.float32)
    mod_own[0:6, :] = mod[0] + vec_rows[0:6]
    mod_own[6:8, :] = vec_rows[6:8]
    outs[8].start()
    for frame in range(4):
        values = jnp.dot(tokens[frame], embed, preferred_element_type=jnp.float32) + vec_rows[6:7]
        if frame == 0:
            resid[...] = values
            outs[3].start()
        normed, _ = centred_norm(values)
        shift = mod[frame, 0:1, :] + vec_rows[0:1]
        scale = mod[frame, 1:2, :] + vec_rows[1:2]
        low = (normed * (1.0 + scale) + shift).astype(jnp.bfloat16)
        hidden[frame] = low
        outs[4 + frame].start()
        mixed = lax.dot_general(
            weights[0:QKV_ROWS, :], low, NT, preferred_element_type=jnp.float32
        )
        cos_now = cosine[meta[8 + frame]]
        sin_now = sine[meta[8 + frame]]
        cols = slice(256 * frame, 256 * frame + 256)
        for head in range(4):
            where_to = head
            for part in range(2):
                base = 256 * part + 64 * head
                upper = mixed[base : base + 32]
                lower = mixed[base + 32 : base + 64]
                heads[where_to, 64 * part : 64 * part + 32, cols] = (
                    upper * cos_now - lower * sin_now
                ).astype(jnp.bfloat16)
                heads[where_to, 64 * part + 32 : 64 * part + 64, cols] = (
                    lower * cos_now + upper * sin_now
                ).astype(jnp.bfloat16)
            base = 512 + 64 * head
            heads[where_to, 128:192, cols] = mixed[base : base + 64].astype(jnp.bfloat16)
    for k in range(4):
        outs.append(pltpu.make_async_copy(heads.at[meta[12 + k]], head_outs[k], out_sems.at[10 + k]))
        outs[10 + k].start()
    for copy in outs:
        copy.wait()


def call_front(meta, scales, pieces, quarters, mod, cosine, sine):
    return pl.pallas_call(
        front_kernel,
        out_shape=(
            jax.ShapeDtypeStruct((FRONT_ROWS, D), jnp.bfloat16),
            jax.ShapeDtypeStruct((D, 384), jnp.bfloat16),
            jax.ShapeDtypeStruct((4, PATCHES, D), jnp.bfloat16),
            jax.ShapeDtypeStruct((PATCHES, D), jnp.float32),
        )
        + (jax.ShapeDtypeStruct((192, 4 * PATCHES), jnp.bfloat16),) * 4
        + (
            jax.ShapeDtypeStruct((PATCHES, 128), jnp.bfloat16),
            jax.ShapeDtypeStruct((PATCHES, 128), jnp.float32),
            jax.ShapeDtypeStruct((8, D), jnp.float32),
        ),
        in_specs=smem_specs(2) + hbm_specs(1) + vmem_specs(7),
        out_specs=hbm_specs(11),
        scratch_shapes=[
            pltpu.VMEM((4, PATCHES, 128), jnp.bfloat16),
            pltpu.VMEM((4, 192, 4 * PATCHES), jnp.bfloat16),
            pltpu.VMEM((FRONT_ROWS, D), jnp.bfloat16),
            pltpu.VMEM((D, 384), jnp.bfloat16),
            pltpu.VMEM((4, PATCHES, D), jnp.bfloat16),
            pltpu.VMEM((PATCHES, D), jnp.float32),
            pltpu.VMEM((PATCHES, 128), jnp.float32),
            pltpu.VMEM((8, D), jnp.float32),
            pltpu.VMEM((8, FRONT_ROWS + 384, 128), jnp.bfloat16),
            pltpu.SemaphoreType.DMA((8,)),
            pltpu.SemaphoreType.DMA((14,)),
        ],
        compiler_params=pltpu.CompilerParams(vmem_limit_bytes=52 * 2**20),
        cost_estimate=pl.CostEstimate(flops=2 * 10**9, bytes_accessed=10**7, transcendentals=0),
        name="front",
    )(meta, scales, pieces, *quarters, mod, cosine, sine)


def total_own(held, came, across):
    return held[...] + came[...].astype(jnp.float32) + across[...].astype(jnp.float32)


def middle_kernel(held, came, across, resid, mod, attn_out, resid_mid, hidden):
    total = total_own(held, came, across)
    attn_out[...] = total
    values = resid[...] + mod[2:3, :] * total
    resid_mid[...] = values
    normed, _ = centred_norm(values)
    hidden[...] = (normed * (1.0 + mod[4:5, :]) + mod[3:4, :]).astype(jnp.bfloat16)


def row_call(kernel, name, outs, *operands, smem=0):
    return pl.pallas_call(
        kernel,
        out_shape=tuple(outs),
        in_specs=smem_specs(smem) + vmem_specs(len(operands) - smem),
        out_specs=vmem_specs(len(outs)),
        compiler_params=pltpu.CompilerParams(vmem_limit_bytes=16 * 2**20),
        cost_estimate=pl.CostEstimate(flops=10**9, bytes_accessed=4 * 10**6, transcendentals=0),
        name=name,
    )(*operands)


def frame_f32():
    return jax.ShapeDtypeStruct((PATCHES, D), jnp.float32)


def frame_low():
    return jax.ShapeDtypeStruct((PATCHES, D), jnp.bfloat16)


def back_through_norm(grad, normed, inv_std):
    mean_grad = jnp.mean(grad, axis=-1, keepdims=True)
    mean_proj = jnp.mean(grad * normed, axis=-1, keepdims=True)
    return inv_std * (grad - mean_grad - normed * mean_proj)


def column_sum(values):
    return jnp.sum(values, axis=0, keepdims=True)


def loss_kernel(
    scales, held, came, across, resid_mid, mod, mid, target, grad_low, grad_three, io_rows, gate, error
):
    mlp_out = total_own(held, came, across)
    values = resid_mid[...] + mod[5:6, :] * mlp_out
    normed, inv_std = centred_norm(values)
    gain = mod[7:8, :]
    final = (normed * gain).astype(jnp.bfloat16)
    head = mid[:, 256:384]
    pred = jnp.dot(final, head, preferred_element_type=jnp.float32)
    diff = pred - target[...]
    per_token = jnp.sum(diff * diff, axis=1, keepdims=True)
    error[...] = jnp.broadcast_to(
        scales[0] * jnp.sum(per_token, axis=0, keepdims=True) / diff.shape[1], error.shape
    )
    grad_pred = (scales[1] * diff).astype(jnp.bfloat16)
    grad_final = lax.dot_general(grad_pred, head, NT, preferred_element_type=jnp.float32)
    grad_gain = column_sum(grad_final * normed)
    grad = back_through_norm(grad_final * gain, normed, inv_std)
    grad_three[...] = grad
    grad_low[...] = (mod[5:6, :] * grad).astype(jnp.bfloat16)
    gate[...] = column_sum(grad * mlp_out)
    io_rows[0:128, :] = lax.dot_general(grad_pred, final, TN, preferred_element_type=jnp.float32)
    io_rows[128:136, :] = jnp.concatenate([grad_gain, jnp.zeros((7, D), jnp.float32)], axis=0)


def second_kernel(
    held, came, across, resid_mid, mod, grad_three, attn_out, grad_low, grad_mid, rows
):
    grad_hidden = total_own(held, came, across)
    normed, inv_std = centred_norm(resid_mid[...])
    grad = grad_three[...] + back_through_norm(grad_hidden * (1.0 + mod[4:5, :]), normed, inv_std)
    grad_mid[...] = grad
    grad_low[...] = (mod[2:3, :] * grad).astype(jnp.bfloat16)
    rows[0:1, :] = column_sum(grad * attn_out[...])
    rows[1:2, :] = column_sum(grad_hidden)
    rows[2:3, :] = column_sum(grad_hidden * normed)


def first_kernel(
    device,
    held,
    came,
    across,
    resid,
    mod,
    grad_mid,
    noisy,
    rows_two,
    gate_two,
    head_rows,
    mod_rows,
    near_held,
    near_away,
    far_held,
    far_away,
    io_rows,
):
    grad_hidden = total_own(held, came, across)
    normed, inv_std = centred_norm(resid[...])
    grad = grad_mid[...] + back_through_norm(grad_hidden * (1.0 + mod[1:2, :]), normed, inv_std)
    rows = [
        column_sum(grad_hidden),
        column_sum(grad_hidden * normed),
        rows_two[0:1, :],
        rows_two[1:2, :],
        rows_two[2:3, :],
        gate_two[...],
    ]
    blocks = [row[:, 128 * k : 128 * k + 128] for row in rows for k in range(8)]
    mod_rows[...] = jnp.concatenate(blocks, axis=0).astype(jnp.bfloat16)
    io_rows[0:128, :] = lax.dot_general(
        noisy[...], grad.astype(jnp.bfloat16), TN, preferred_element_type=jnp.float32
    )
    io_rows[128:256, :] = head_rows[0:128, :]
    io_rows[256:264, :] = jnp.concatenate(
        [column_sum(grad), head_rows[128:129, :], jnp.zeros((6, D), jnp.float32)], axis=0
    )
    io_rows[264:320, :] = jnp.zeros((56, D), jnp.float32)
    for k, out in enumerate((near_held, near_away, far_held, far_away)):
        group = pl.ds(pl.multiple_of(IO_ROWS * (device[1] ^ k), 16), IO_ROWS)
        out[...] = io_rows[group, :].astype(out.dtype)


def side_kernel(device, held, came, across, mod_rows, keep, away):
    total = total_own(held, came, across)
    side = device[0] & 1
    for block in range(8):
        piece = total[:, 128 * block : 128 * block + 128]

        @pl.when(side == block % 2)
        def _():
            keep[block // 2] = piece

        @pl.when(side != block % 2)
        def _():
            away[IO_ROWS * (block // 2) : IO_ROWS * (block // 2) + IO_ROWS, :] = piece.astype(
                jnp.bfloat16
            )

    away[4 * IO_ROWS :, :] = mod_rows[...]


def merge_kernel(
    device, held, came, out_held, out_came, io_held, io_came, mod_rows, own, io_own, *outs
):
    z = device[0] >> 1
    for bit in range(4):
        total = jnp.concatenate(
            [
                held[z ^ bit] + came[z ^ bit].astype(jnp.float32),
                out_held[z ^ bit] + out_came[z ^ bit].astype(jnp.float32),
            ],
            axis=0,
        )
        rows = pl.ds(pl.multiple_of(IO_ROWS * (z ^ bit), 16), IO_ROWS)
        io_total = io_held[z ^ bit] + io_came[rows, :].astype(jnp.float32)
        if bit == 0:
            own[...] = total
            io_own[...] = io_total
        else:
            out = outs[bit]
            out[0:ATTN_ROWS, :] = total.astype(jnp.bfloat16)
            out[ATTN_ROWS : ATTN_ROWS + IO_ROWS, :] = io_total.astype(jnp.bfloat16)
            base = ATTN_ROWS + IO_ROWS
            out[base : base + MOD_ROWS, :] = mod_rows[...]
            out[base + MOD_ROWS : base + 2 * MOD_ROWS, :] = io_came[4 * IO_ROWS :, :]
    outs[0][0:MOD_ROWS, :] = mod_rows[...]
    outs[0][MOD_ROWS : 2 * MOD_ROWS, :] = io_came[4 * IO_ROWS :, :]


def mod_grad_kernel(device, cond, *refs):
    parts = refs[:4]
    rows_out, vector, io_grad, square, rows = refs[4:]
    base = 8 * MOD_ROWS + 2 * IO_ROWS
    terms = []
    for index in range(4):
        owner = device[1] ^ index
        block = parts[index][0 : 8 * MOD_ROWS, :].astype(jnp.float32)
        for frame in range(8):
            for k in range(MOD_ROWS):
                at = MOD_ROWS * frame + k
                rows[owner, frame : frame + 1, 128 * k : 128 * k + 128] = block[at : at + 1, :]
        group = pl.ds(pl.multiple_of(IO_ROWS * owner, 16), IO_ROWS)
        high = parts[index][8 * MOD_ROWS : 8 * MOD_ROWS + IO_ROWS, :].astype(jnp.float32)
        rest = parts[index][8 * MOD_ROWS + IO_ROWS : base, :].astype(jnp.float32)
        io_grad[group, :] = high + rest
        terms.append(column_sum(parts[index][base : base + 16, :].astype(jnp.float32)))
    total = jnp.zeros((1, 1), jnp.float32)
    for index in range(6):
        cols = slice(D * index, D * index + D)
        low = rows[:, :, cols].reshape(32, D)
        rows_out[:, cols] = low.astype(jnp.bfloat16)
        part = lax.dot_general(
            cond[32:64, :], low.astype(jnp.bfloat16), TN, preferred_element_type=jnp.float32
        )
        total = total + jnp.sum(column_sum(part * part), axis=1, keepdims=True)
        own = pl.ds(pl.multiple_of(D * index + 128 * device[0], 128), 128)
        vector[index : index + 1, :] = column_sum(rows[:, :, own].reshape(32, 128))
    vector[6:8, :] = io_grad[256:258, :]
    mixed = vector[0:6, :]
    total = total + jnp.sum(column_sum(mixed * mixed), axis=1, keepdims=True)
    left = lax.broadcasted_iota(jnp.int32, (1, 128), 1) < 64
    square[...] = ((terms[0] + terms[1]) + (terms[2] + terms[3])) + jnp.where(left, total, 0.0)


def call_mod_grad(device, cond, parts):
    return pl.pallas_call(
        mod_grad_kernel,
        out_shape=(
            jax.ShapeDtypeStruct((32, 6 * D), jnp.bfloat16),
            jax.ShapeDtypeStruct((8, 128), jnp.float32),
            jax.ShapeDtypeStruct((4 * IO_ROWS, 128), jnp.float32),
            jax.ShapeDtypeStruct((1, 128), jnp.float32),
        ),
        in_specs=smem_specs(1) + vmem_specs(5),
        out_specs=vmem_specs(4),
        scratch_shapes=[pltpu.VMEM((4, 8, 6 * D), jnp.float32)],
        compiler_params=pltpu.CompilerParams(vmem_limit_bytes=12 * 2**20),
        cost_estimate=pl.CostEstimate(flops=10**8, bytes_accessed=4 * 10**6, transcendentals=0),
        name="mod_grad",
    )(device, cond, *parts)


def mlp_kernel(first, second, weights, held, away, active, slope):
    for frame, source in enumerate((first, second)):
        rows = slice(256 * frame, 256 * frame + 256)
        upward = jnp.dot(source[...], weights[0], preferred_element_type=jnp.float32)
        inner = 0.5 * (1.0 + lax.erf(upward * (1.0 / math.sqrt(2.0))))
        low = (upward * inner).astype(jnp.bfloat16)
        active[rows, :] = low
        change = inner + upward * jnp.exp(-0.5 * upward * upward) * (
            1.0 / math.sqrt(2.0 * math.pi)
        )
        slope[rows, :] = change.astype(jnp.bfloat16)
        part = lax.dot_general(low, weights[1], NT, preferred_element_type=jnp.float32)
        if frame:
            away[...] = part.astype(jnp.bfloat16)
        else:
            held[...] = part


def mlp_back_kernel(first, second, weights, slope, held, away, grad_up):
    for frame, source in enumerate((first, second)):
        rows = slice(256 * frame, 256 * frame + 256)
        grad = jnp.dot(source[...], weights[1], preferred_element_type=jnp.float32)
        low = (grad * slope[rows, :].astype(jnp.float32)).astype(jnp.bfloat16)
        grad_up[rows, :] = low
        part = lax.dot_general(low, weights[0], NT, preferred_element_type=jnp.float32)
        if frame:
            away[...] = part.astype(jnp.bfloat16)
        else:
            held[...] = part


def call_mlp(kernel, name, outs, *operands):
    return pl.pallas_call(
        kernel,
        out_shape=(frame_f32(), frame_low()) + outs,
        in_specs=vmem_specs(len(operands)),
        out_specs=vmem_specs(2 + len(outs)),
        compiler_params=pltpu.CompilerParams(vmem_limit_bytes=16 * 2**20),
        cost_estimate=pl.CostEstimate(
            flops=4 * 10**9, bytes_accessed=2 * 10**7, transcendentals=10**6
        ),
        name=name,
    )(*operands)


def weight_grad_kernel(*refs):
    hidden, grads = refs[:4], refs[4:8]
    grad_up, active = refs[8:10], refs[10:12]
    result, out, sems = refs[12:]
    width = active[0].shape[1]
    copies = []
    for index, (left, right) in enumerate(((hidden, grad_up), (grads, active))):
        total = jnp.zeros((D, width), jnp.float32)
        for frame in range(4):
            rows = slice(256 * (frame % 2), 256 * (frame % 2) + 256)
            total = total + lax.dot_general(
                left[frame][...],
                right[frame // 2][rows, :],
                TN,
                preferred_element_type=jnp.float32,
            )
        out[index] = total.astype(jnp.bfloat16)
        copies.append(
            pltpu.make_async_copy(
                out.at[index], result.at[:, width * index : width * index + width], sems.at[index]
            )
        )
        copies[index].start()
    for copy in copies:
        copy.wait()


def call_weight_grad(hidden, grads, grad_up, active):
    operands = (*hidden, *grads, *grad_up, *active)
    return pl.pallas_call(
        weight_grad_kernel,
        out_shape=jax.ShapeDtypeStruct((D, 2 * active[0].shape[1]), jnp.bfloat16),
        in_specs=vmem_specs(len(operands)),
        out_specs=hbm_specs(1)[0],
        scratch_shapes=[
            pltpu.VMEM((2, D, active[0].shape[1]), jnp.bfloat16),
            pltpu.SemaphoreType.DMA((2,)),
        ],
        compiler_params=pltpu.CompilerParams(vmem_limit_bytes=20 * 2**20),
        cost_estimate=pl.CostEstimate(flops=5 * 10**9, bytes_accessed=2 * 10**7, transcendentals=0),
        name="weight_grad",
    )(*operands)


def side_blocks(device, total, held, away):
    side = device[0] & 1
    for z in range(4):
        held[z] = total[:, pl.ds(pl.multiple_of(256 * z + 128 * side, 128), 128)]
        away[z] = total[:, pl.ds(pl.multiple_of(256 * z + 128 * (1 - side), 128), 128)].astype(
            jnp.bfloat16
        )


def head_grad_kernel(device, left, right, held, away, total):
    total[...] = jnp.dot(left[...], right[...], preferred_element_type=jnp.float32)
    side_blocks(device, total, held, away)


def call_head_grad(device, left, right):
    rows = left.shape[0]
    return pl.pallas_call(
        head_grad_kernel,
        out_shape=(
            jax.ShapeDtypeStruct((4, rows, 128), jnp.float32),
            jax.ShapeDtypeStruct((4, rows, 128), jnp.bfloat16),
        ),
        in_specs=smem_specs(1) + vmem_specs(2),
        out_specs=vmem_specs(2),
        scratch_shapes=[pltpu.VMEM((rows, D), jnp.float32)],
        compiler_params=pltpu.CompilerParams(vmem_limit_bytes=12 * 2**20),
        cost_estimate=pl.CostEstimate(flops=2 * 10**9, bytes_accessed=10**7, transcendentals=0),
        name="head_grad",
    )(device, left, right)


def qkv_back_kernel(meta, *refs):
    blocks, weights = refs[:4], refs[4]
    grads, near_held, near_away, far_held, far_away = refs[5:]
    for k in range(4):
        head = meta[0] ^ k
        for part in range(3):
            rows = pl.ds(pl.multiple_of(256 * part + 64 * head, 64), 64)
            grads[rows, :] = blocks[k][64 * part : 64 * part + 64, :]
    for frame, out in ((2, far_held), (3, far_away), (0, near_held), (1, near_away)):
        part = lax.dot_general(
            grads[:, 256 * frame : 256 * frame + 256],
            weights[0:QKV_ROWS, :],
            TN,
            preferred_element_type=jnp.float32,
        )
        out[...] = part.astype(out.dtype)


def call_qkv_back(meta, blocks, weights):
    return row_call(
        qkv_back_kernel,
        "qkv_back",
        (
            jax.ShapeDtypeStruct((QKV_ROWS, 4 * PATCHES), jnp.bfloat16),
            frame_f32(),
            frame_low(),
            frame_f32(),
            frame_low(),
        ),
        meta,
        *blocks,
        weights,
        smem=1,
    )


def adam_step(weight_now, first_mom, second_mom, grad, scale, rate, decay):
    factor, first_fix, second_fix = scale
    grad = grad * factor
    first_mom = beta_one * first_mom + (1.0 - beta_one) * grad
    second_mom = beta_two * second_mom + (1.0 - beta_two) * grad * grad
    updated = weight_now - rate * (
        first_mom * first_fix / (jnp.sqrt(second_mom * second_fix) + adam_eps) + decay * weight_now
    )
    return updated, first_mom, second_mom, updated.astype(jnp.bfloat16)


def preload_kernel(*refs):
    sources, targets, sems = refs[:3], refs[4:7], refs[7]
    copies = [
        pltpu.make_async_copy(sources[k], targets[k], sems.at[k]) for k in range(3)
    ]
    for copy in copies:
        copy.start()
    for copy in copies:
        copy.wait()


def call_preload(arrays, values):
    return pl.pallas_call(
        preload_kernel,
        out_shape=tuple(jax.ShapeDtypeStruct(a.shape, a.dtype) for a in arrays),
        in_specs=hbm_specs(3) + vmem_specs(1),
        out_specs=vmem_specs(3),
        scratch_shapes=[pltpu.SemaphoreType.DMA((3,))],
        compiler_params=pltpu.CompilerParams(vmem_limit_bytes=4 * 2**20),
        cost_estimate=pl.CostEstimate(flops=10**6, bytes_accessed=10**7, transcendentals=0),
        name="preload",
    )(*arrays, values)


def adam_kernel(*refs):
    fixes, sums = refs[0], refs[1:5]
    attn_grad, mlp_grad, cond, mod_rows = refs[5:9]
    io_in, vec_in = refs[9:13], refs[13:17]
    groups = [refs[17 + 3 * k : 20 + 3 * k] for k in range(3)]
    outs = [refs[26 + 4 * k : 30 + 4 * k] for k in range(3)]
    io_out, vec_out, norm_out = refs[38:43], refs[43:47], refs[47]
    held, slots, low_slots, in_sems, sems = refs[48:]
    depth = held.shape[0]
    tasks = []
    for k in (1, 0, 2):
        width = groups[k][0].shape[-1]
        for lead in range(groups[k][0].shape[0] if k < 2 else 1):
            for col in range(0, width, 1024):
                tasks.append((k, lead, col, min(1024, width - col)))

    def fetches(number):
        k, lead, col, span = tasks[number]
        cut = ((lead,) if k < 2 else ()) + (slice(None), slice(col, col + span))
        slot = number % depth
        if k == 2:
            return []
        return [
            pltpu.make_async_copy(
                groups[k][index].at[cut], held.at[slot, index, :, 0:span], in_sems.at[slot, index]
            )
            for index in range(3)
        ]

    for number in range(min(depth, len(tasks))):
        for copy in fetches(number):
            copy.start()
    total = (sums[0][...] + sums[1][...]) + (sums[2][...] + sums[3][...])
    norm = jnp.sqrt(total)
    norm_out[0:1, :] = norm
    norm_out[1:2, :] = total
    factor = jnp.minimum(1.0, clip_limit / (norm[:, 0:1] + 1e-06))
    scale = (factor, fixes[0], fixes[1])
    results = adam_step(*(ref[...] for ref in io_in), scale, rate_matrix, decay_rate)
    io_out[0][...] = results[0]
    io_out[1][...] = results[1]
    io_out[2][...] = results[2][0]
    io_out[3][...] = results[2][1]
    io_out[4][...] = results[3]
    results = adam_step(*(ref[...] for ref in vec_in), scale, rate_vector, 0.0)
    for out, result in zip(vec_out, results):
        out[...] = result
    running = {}
    for number, (k, lead, col, span) in enumerate(tasks):
        slot = number % depth
        for copy in fetches(number):
            copy.wait()
        for copy in running.pop(number - depth, ()):
            copy.wait()
        cut = ((lead,) if k < 2 else ()) + (slice(None), slice(col, col + span))
        if k == 0:
            grad = attn_grad[lead]
        elif k == 1:
            base = groups[1][0].shape[-1] * lead + col
            grad = mlp_grad[:, base : base + span].astype(jnp.float32)
        else:
            grad = lax.dot_general(
                cond[32:64, :],
                mod_rows[:, col : col + span],
                TN,
                preferred_element_type=jnp.float32,
            )
        if k == 2:
            values = [ref[:, col : col + span] for ref in groups[2]]
        else:
            values = [held[slot, index, :, 0:span] for index in range(3)]
        results = adam_step(*values, grad, scale, rate_matrix, decay_rate)
        copies = []
        for index, result in enumerate(results):
            source = low_slots.at[slot] if index == 3 else slots.at[slot, index]
            source = source.at[:, 0:span]
            source[...] = result
            copies.append(
                pltpu.make_async_copy(source, outs[k][index].at[cut], sems.at[slot, index])
            )
            copies[index].start()
        running[number] = copies
        if number + depth < len(tasks):
            for copy in fetches(number + depth):
                copy.start()
    for copies in running.values():
        for copy in copies:
            copy.wait()


def call_adam(fixes, sums, grads, io_group, vec_group, groups):
    held = [array for group in groups for array in group]
    inside = [*sums, *grads, *io_group, *vec_group]

    def results(group):
        low = jax.ShapeDtypeStruct(group[0].shape, jnp.bfloat16)
        return (jax.ShapeDtypeStruct(group[0].shape, jnp.float32),) * 3 + (low,)

    io_like = results(io_group)
    half = jax.ShapeDtypeStruct(io_group[0].shape[1:], jnp.float32)
    out_shape = sum((results(group) for group in groups), ())
    out_shape = out_shape + io_like[:2] + (half, half) + io_like[3:] + results(vec_group)
    out_shape = out_shape + (jax.ShapeDtypeStruct((2, 128), jnp.float32),)
    return pl.pallas_call(
        adam_kernel,
        out_shape=out_shape,
        in_specs=smem_specs(1) + vmem_specs(len(inside)) + hbm_specs(6) + vmem_specs(3),
        out_specs=hbm_specs(12) + vmem_specs(10),
        scratch_shapes=[
            pltpu.VMEM((6, 3, 128, 1024), jnp.float32),
            pltpu.VMEM((6, 3, 128, 1024), jnp.float32),
            pltpu.VMEM((6, 128, 1024), jnp.bfloat16),
            pltpu.SemaphoreType.DMA((6, 3)),
            pltpu.SemaphoreType.DMA((6, 4)),
        ],
        compiler_params=pltpu.CompilerParams(vmem_limit_bytes=28 * 2**20),
        cost_estimate=pl.CostEstimate(flops=10**7, bytes_accessed=2 * 10**7, transcendentals=0),
        name="adam",
    )(fixes, *inside, *held)


def square_kernel(scattered, square):
    rest = scattered[...].astype(jnp.float32)
    square[...] = jnp.broadcast_to(
        jnp.sum(column_sum(rest * rest), axis=1, keepdims=True), square.shape
    )


def finish_kernel(*refs):
    own, io_own, mod_own, pieces = refs[0], refs[1], refs[2], refs[3:6]
    rest, error, grad, spread = refs[6:]
    total = own[...]
    io_total = io_own[...]
    spread[0 : 2 * MOD_ROWS, :] = mod_own[...]
    for index, piece in enumerate(pieces):
        total = total + piece[0:ATTN_ROWS, :].astype(jnp.float32)
        base = ATTN_ROWS + IO_ROWS
        io_total = io_total + piece[ATTN_ROWS:base, :].astype(jnp.float32)
        spread[2 * MOD_ROWS * (index + 1) : 2 * MOD_ROWS * (index + 2), :] = piece[base:, :]
    high = io_total.astype(jnp.bfloat16)
    base = 8 * MOD_ROWS
    spread[base : base + IO_ROWS, :] = high
    base = base + IO_ROWS
    spread[base : base + IO_ROWS, :] = (io_total - high.astype(jnp.float32)).astype(jnp.bfloat16)
    for part in range(4):
        grad[part] = total[256 * part : 256 * part + 256].T
    squares = rest[:, 0:1]
    for values in (total, io_total):
        squares = squares + jnp.sum(column_sum(values * values), axis=1, keepdims=True)
    left = lax.broadcasted_iota(jnp.int32, (1, 128), 1) < 64
    value = jnp.where(left, squares, error[...])
    terms = []
    for _ in range(3):
        terms.append(value.astype(jnp.bfloat16).astype(jnp.float32))
        value = value - terms[-1]
    spread[base + IO_ROWS :, :] = jnp.concatenate(
        terms + [jnp.zeros((13, 128), jnp.float32)], axis=0
    ).astype(jnp.bfloat16)


def turn(block):
    return block.astype(jnp.float32).T.astype(jnp.bfloat16)


def query_rows(meta, pair):
    first = 2 * pair
    start_first = first - meta[2 + first]
    start_second = first + 1 - meta[3 + first]
    left = lax.broadcasted_iota(jnp.int32, (1, 2 * PATCHES), 1) < PATCHES
    upto = jnp.where(left, first, first + 1)
    since = jnp.where(left, start_first, start_second)
    return jnp.minimum(start_first, start_second), since, upto


def attend_kernel(meta, *refs):
    blocks = refs[:4]
    outs = refs[4:8]
    lse, mixed, query, key, value, scores = refs[8:]
    for member in range(4):
        for frame in range(4):
            slot = 4 * (meta[0] ^ member) + (meta[1] ^ frame)
            cols = slice(256 * frame, 256 * frame + 256)
            lanes = pl.ds(pl.multiple_of((slot % 2) * 256, 256), 256)
            query[slot // 2, :, lanes] = blocks[member][0:64, cols] * 0.125
            key[slot // 2, lanes, :] = turn(blocks[member][64:128, cols])
            value[slot // 2, :, lanes] = blocks[member][128:192, cols]

    def per_pair(pair, carry):
        low, since, upto = query_rows(meta, pair)
        wanted = query[pair]

        def first_pass(keys, top):
            both = jnp.dot(key[keys], wanted, preferred_element_type=jnp.float32)
            for side in range(2):
                slot = 2 * keys + side
                bias = jnp.where((slot >= since) & (slot <= upto), 0.0, neg_large)
                part = both[256 * side : 256 * side + 256] + bias
                scores[keys, 256 * side : 256 * side + 256, :] = part
                top = jnp.maximum(top, jnp.max(part.reshape(32, 8, 2 * PATCHES), axis=0))
            return top

        tops = lax.fori_loop(
            low // 2, pair + 1, first_pass, jnp.full((8, 2 * PATCHES), neg_large, jnp.float32)
        )
        top = jnp.max(tops, axis=0, keepdims=True)

        def second_pass(keys, state):
            total, acc = state
            probs = jnp.exp(scores[keys] - top)
            total = total + jnp.sum(probs.reshape(64, 8, 2 * PATCHES), axis=0)
            acc = acc + jnp.dot(
                value[keys], probs.astype(jnp.bfloat16), preferred_element_type=jnp.float32
            )
            return (total, acc)

        totals, acc = lax.fori_loop(
            low // 2,
            pair + 1,
            second_pass,
            (
                jnp.zeros((8, 2 * PATCHES), jnp.float32),
                jnp.zeros((HD, 2 * PATCHES), jnp.float32),
            ),
        )
        total = jnp.sum(totals, axis=0, keepdims=True)
        lse[pair] = top + jnp.log(total)
        mixed[pair] = acc / total
        return carry

    lax.fori_loop(0, 8, per_pair, 0)
    for member in range(4):
        for frame in range(4):
            slot = 4 * (meta[0] ^ member) + (meta[1] ^ frame)
            lanes = pl.ds(pl.multiple_of((slot % 2) * 256, 256), 256)
            outs[member][:, 256 * frame : 256 * frame + 256] = mixed[slot // 2, :, lanes].astype(
                jnp.bfloat16
            )


def call_attend(meta, blocks):
    vmem = pl.BlockSpec()
    result = pl.pallas_call(
        attend_kernel,
        out_shape=tuple(jax.ShapeDtypeStruct((HD, 4 * PATCHES), jnp.bfloat16) for _ in range(4))
        + (
            jax.ShapeDtypeStruct((8, 1, 2 * PATCHES), jnp.float32),
            jax.ShapeDtypeStruct((8, HD, 2 * PATCHES), jnp.float32),
        ),
        in_specs=[pl.BlockSpec(memory_space=pltpu.SMEM)] + [vmem] * 4,
        out_specs=(vmem,) * 6,
        scratch_shapes=[
            pltpu.VMEM((8, HD, 2 * PATCHES), jnp.bfloat16),
            pltpu.VMEM((8, 2 * PATCHES, HD), jnp.bfloat16),
            pltpu.VMEM((8, HD, 2 * PATCHES), jnp.bfloat16),
            pltpu.VMEM((8, 2 * PATCHES, 2 * PATCHES), jnp.float32),
        ],
        compiler_params=pltpu.CompilerParams(vmem_limit_bytes=48 * 2**20),
        cost_estimate=pl.CostEstimate(flops=9 * 10**9, bytes_accessed=5 * 10**6, transcendentals=10**7),
        name="attend",
    )(meta, *blocks)
    return list(result[:4]), result[4], result[5]


def attend_back_kernel(meta, *refs):
    blocks = refs[:4]
    grads = refs[4:8]
    lse, mixed, cosine, sine = refs[8:12]
    outs = refs[12:16]
    query, key, key_flat, value_flat, grad, sum_key, sum_value, sum_query = refs[16:]
    for member in range(4):
        for frame in range(4):
            slot = 4 * (meta[0] ^ member) + (meta[1] ^ frame)
            cols = slice(256 * frame, 256 * frame + 256)
            place = pl.ds(pl.multiple_of((slot % 2) * 256, 256), 256)
            part = blocks[member][0:64, cols] * 0.125
            query[slot // 2, :, place] = part
            part = blocks[member][64:128, cols]
            key[slot // 2, :, place] = part
            key_flat[slot // 2, place, :] = turn(part)
            value_flat[slot // 2, place, :] = turn(blocks[member][128:192, cols])
            part = grads[member][:, cols]
            grad[slot // 2, :, place] = part
    sum_key[...] = jnp.zeros_like(sum_key)
    sum_value[...] = jnp.zeros_like(sum_value)

    def per_pair(pair, carry):
        low, since, upto = query_rows(meta, pair)
        wanted = query[pair]
        wanted_grad = grad[pair]
        delta = jnp.sum(wanted_grad.astype(jnp.float32) * mixed[pair], axis=0, keepdims=True)
        level = lse[pair]

        def per_keys(keys, acc):
            scores = jnp.dot(key_flat[keys], wanted, preferred_element_type=jnp.float32)
            grad_probs = jnp.dot(
                value_flat[keys], wanted_grad, preferred_element_type=jnp.float32
            )
            low_probs, low_scores = [], []
            for side in range(2):
                rows = slice(256 * side, 256 * side + 256)
                slot = 2 * keys + side
                bias = jnp.where((slot >= since) & (slot <= upto), -level, neg_large)
                probs = jnp.exp(scores[rows] + bias)
                low_probs.append(probs.astype(jnp.bfloat16))
                low_scores.append((probs * (grad_probs[rows] - delta)).astype(jnp.bfloat16))
            all_probs = jnp.concatenate(low_probs, axis=0)
            all_scores = jnp.concatenate(low_scores, axis=0)
            sum_value[keys] += lax.dot_general(
                wanted_grad, all_probs, NT, preferred_element_type=jnp.float32
            )
            sum_key[keys] += lax.dot_general(
                wanted, all_scores, NT, preferred_element_type=jnp.float32
            )
            return acc + jnp.dot(key[keys], all_scores, preferred_element_type=jnp.float32)

        sum_query[pair] = lax.fori_loop(
            low // 2, pair + 1, per_keys, jnp.zeros((HD, 2 * PATCHES), jnp.float32)
        )
        return carry

    lax.fori_loop(0, 8, per_pair, 0)
    for member in range(4):
        for frame in range(4):
            slot = 4 * (meta[0] ^ member) + (meta[1] ^ frame)
            cols = slice(256 * frame, 256 * frame + 256)
            place = pl.ds(pl.multiple_of((slot % 2) * 256, 256), 256)
            cos_now = cosine[slot]
            sin_now = sine[slot]
            for base, part in (
                (0, sum_query[slot // 2, :, place] * 0.125),
                (64, sum_key[slot // 2, :, place]),
            ):
                upper = part[0:32]
                lower = part[32:64]
                outs[member][base : base + 32, cols] = (
                    upper * cos_now + lower * sin_now
                ).astype(jnp.bfloat16)
                outs[member][base + 32 : base + 64, cols] = (
                    lower * cos_now - upper * sin_now
                ).astype(jnp.bfloat16)
            outs[member][128:192, cols] = sum_value[slot // 2, :, place].astype(jnp.bfloat16)


def call_attend_back(meta, blocks, grads, lse, mixed, cosine, sine):
    vmem = pl.BlockSpec()
    flat_pair = pltpu.VMEM((8, 2 * PATCHES, HD), jnp.bfloat16)
    turned_pair = pltpu.VMEM((8, HD, 2 * PATCHES), jnp.bfloat16)
    wide = pltpu.VMEM((8, HD, 2 * PATCHES), jnp.float32)
    return list(
        pl.pallas_call(
            attend_back_kernel,
            out_shape=tuple(
                jax.ShapeDtypeStruct((192, 4 * PATCHES), jnp.bfloat16) for _ in range(4)
            ),
            in_specs=[pl.BlockSpec(memory_space=pltpu.SMEM)] + [vmem] * 12,
            out_specs=(vmem,) * 4,
            scratch_shapes=[
                turned_pair,
                turned_pair,
                flat_pair,
                flat_pair,
                turned_pair,
                wide,
                wide,
                pltpu.VMEM((8, HD, 2 * PATCHES), jnp.float32),
            ],
            compiler_params=pltpu.CompilerParams(vmem_limit_bytes=48 * 2**20),
            cost_estimate=pl.CostEstimate(
                flops=30 * 10**9, bytes_accessed=10**7, transcendentals=10**7
            ),
            name="attend_back",
        )(meta, *blocks, *grads, lse, mixed, cosine, sine)
    )


def shards_halves(
    clean,
    noise,
    levels,
    lengths,
    order,
    step,
    w_attn,
    m_attn,
    v_attn,
    w_mlp,
    m_mlp,
    v_mlp,
    w_mod,
    m_mod,
    v_mod,
    w_io,
    m_io,
    v_io,
    vectors,
    m_vec,
    v_vec,
):
    bfloat = jnp.bfloat16
    single = jnp.float32
    ctx_index = lax.axis_index("ctx")
    tp_index = lax.axis_index("tp")
    member = ctx_index % 4
    device = jnp.stack([ctx_index, tp_index]).astype(jnp.int32)

    front_shard = call_prepare(w_attn, w_io, vectors)
    token_shard = call_tokens(after(device, front_shard), clean, noise)
    pieces = gather_swaps(token_shard)
    front_pieces = lax.all_gather(front_shard, "ctx", axis=0)
    front_meta, attend_meta, row_levels = call_place(
        after(device, pieces[1]), lengths, order, levels
    )

    count = step[0].astype(single)
    fixes = jnp.stack([1.0 / (1.0 - beta_one**count), 1.0 / (1.0 - beta_two**count)])

    half_dim = D // 2
    column = ctx_index * 128 + jnp.arange(128, dtype=jnp.int32)
    frequency = jnp.exp(-math.log(10000.0) * (column % half_dim).astype(single) / half_dim)
    angle = row_levels.astype(single)[:, None] * frequency[None, :]
    cond = jax.nn.silu(jnp.where(column[None, :] < half_dim, jnp.cos(angle), jnp.sin(angle)))
    cond_low = cond.astype(bfloat)
    cond_slots = cond_low[:32]
    quarter_cols = 6 * D // 4
    mod_cols = lax.dynamic_slice_in_dim(w_mod, tp_index * quarter_cols, quarter_cols, 1)
    mod_part = jnp.dot(cond_slots, mod_cols.astype(bfloat), preferred_element_type=single)
    mod_held = reduce_along_x(mod_part.reshape(8, 4, quarter_cols), ctx_index, single)
    mod_own = reduce_along_z(mod_held, ctx_index, single)
    mod_quarters = reorder_four(spread_frames(mod_own), tp_index)
    mod_all = jnp.concatenate(mod_quarters, axis=1)
    mod_rel = jnp.stack(reorder_four([mod_all[k] for k in range(4)], tp_index))
    mod_rel = mod_rel.reshape(4, 6, D)

    time_pairs = HD // 8
    side_pairs = (HD // 2 - time_pairs) // 2

    def frequencies(count):
        return 10000.0 ** (-jnp.arange(count, dtype=single) / count)

    patch = jnp.arange(PATCHES, dtype=jnp.int32)
    half_position = attend_meta[2:].astype(single)
    time_angle = half_position[:, None] * frequencies(time_pairs)[None, :]
    height_angle = frequencies(side_pairs)[:, None] * (patch // GRID).astype(single)[None, :]
    width_angle = frequencies(side_pairs)[:, None] * (patch % GRID).astype(single)[None, :]
    side_angle = jnp.concatenate([height_angle, width_angle], axis=0)

    def full_table(time_part, side_part):
        return jnp.concatenate(
            [
                jnp.broadcast_to(time_part[:, :, None], (HALF_SLOTS, time_pairs, PATCHES)),
                jnp.broadcast_to(side_part[None], (HALF_SLOTS, 2 * side_pairs, PATCHES)),
            ],
            axis=1,
        )

    cosine = full_table(jnp.cos(time_angle), jnp.cos(side_angle))
    sine = full_table(jnp.sin(time_angle), jnp.sin(side_angle))
    signal_scale, noise_scale, weight = plan(row_levels)
    weight_sum = PATCHES * jnp.sum(weight[:32])
    token_scales = jnp.concatenate([signal_scale[64:68], noise_scale[64:68]])
    loss_scales = jnp.stack([weight[64], 2.0 / clean.shape[1] * weight[64] / weight_sum])

    front_meta = after(front_meta, mod_rel, cosine, sine, token_scales, loss_scales, fixes)
    quarters = spread_frames(call_pick(front_meta, pieces))
    front_all, mid_all, hidden_frames, resid_in, *head_blocks, noisy_low, target, mod_own = (
        call_front(front_meta, token_scales, front_pieces, quarters, mod_rel, cosine, sine)
    )
    hidden_one = hidden_frames.reshape(4 * PATCHES, D)

    out_w = mid_all[:, :256]

    def exchange(blocks):
        return [blocks[0]] + [swap(blocks[k], "ctx", k) for k in (1, 2, 3)]

    head_in = exchange(head_blocks)
    mlp_shard = after(w_mlp.astype(bfloat), *head_in)
    mlp_w = lax.all_gather(mlp_shard, "ctx", axis=1, tiled=True)
    mixed_blocks, lse, mixed = call_attend(attend_meta, head_in)
    mix_low = jnp.concatenate(reorder_four(exchange(mixed_blocks), member), axis=0)

    def project(left, right, dims):
        pairs = []
        for base in (2 * PATCHES, 0):
            part = lax.dot_general(
                left[:, base : base + 2 * PATCHES], right, dims, preferred_element_type=single
            )
            pairs.append((part[:PATCHES], part[PATCHES:].astype(bfloat)))
        return pairs[1], pairs[0]

    near, far = project(mix_low, out_w, (((0,), (1,)), ((), ())))
    attn_out, resid_mid, hidden_own = row_call(
        middle_kernel,
        "middle",
        (frame_f32(), frame_f32(), frame_low()),
        *sum_frames(near, sum_across(far)),
        resid_in,
        mod_own,
    )
    hidden_list = spread_frames(hidden_own)
    wide = (2 * PATCHES, w_mlp.shape[2])
    wide_low = jax.ShapeDtypeStruct(wide, bfloat)
    far = call_mlp(mlp_kernel, "mlp", (wide_low, wide_low), *hidden_list[2:], mlp_w)
    across = sum_across(far)
    near = call_mlp(
        mlp_kernel,
        "mlp",
        (wide_low, wide_low),
        after(hidden_list[0], across),
        hidden_list[1],
        mlp_w,
    )
    active, slope = (near[2], far[2]), (near[3], far[3])
    grad_own, grad_three, head_rows, grad_gate_two, error_part = row_call(
        loss_kernel,
        "loss",
        (
            frame_low(),
            frame_f32(),
            jax.ShapeDtypeStruct((136, D), single),
            jax.ShapeDtypeStruct((1, D), single),
            jax.ShapeDtypeStruct((1, 128), single),
        ),
        loss_scales,
        *sum_frames(near[:2], across),
        resid_mid,
        mod_own,
        mid_all,
        target,
        smem=1,
    )
    grad_list = spread_frames(grad_own)
    near = call_mlp(mlp_back_kernel, "mlp_back", (wide_low,), *grad_list[:2], mlp_w, slope[0])
    far = call_mlp(
        mlp_back_kernel,
        "mlp_back",
        (wide_low,),
        after(grad_list[2], near[0]),
        grad_list[3],
        mlp_w,
        slope[1],
    )
    across = sum_across(far)
    weight_grad = call_weight_grad(
        hidden_list, grad_list, (near[2], after(far[2], across)), active
    )
    scattered = lax.psum_scatter(weight_grad, "ctx", scatter_dimension=0, tiled=True)
    grad_low, grad_mid, rows_two = row_call(
        second_kernel,
        "second",
        (frame_low(), frame_f32(), jax.ShapeDtypeStruct((3, D), single)),
        *sum_frames(near[:2], across),
        after(resid_mid, weight_grad),
        mod_own,
        grad_three,
        attn_out,
    )
    back_list = spread_frames(grad_low)
    grad_attn_low = jnp.concatenate(back_list, axis=0)
    grad_mix = lax.dot_general(
        out_w, grad_attn_low, (((0,), (1,)), ((), ())), preferred_element_type=single
    ).astype(bfloat)
    grad_blocks = reorder_four([grad_mix[HD * k : HD * k + HD] for k in range(4)], member)
    grad_in_blocks = exchange(grad_blocks)
    out_held, out_away = call_head_grad(device, mix_low, after(grad_attn_low, grad_mix))
    out_came = swap(out_away, "ctx", 1)
    grad_in_blocks[0] = after(grad_in_blocks[0], out_held)
    back_blocks = call_attend_back(attend_meta, head_in, grad_in_blocks, lse, mixed, cosine, sine)
    grad_qkv, *parts = call_qkv_back(
        attend_meta, exchange(back_blocks), after(front_all, out_came)
    )
    near, far = parts[:2], parts[2:]
    across = sum_across(far)
    first_terms = sum_frames(near, across)
    qkv_held, qkv_away = call_head_grad(device, after(grad_qkv, across), hidden_one)
    qkv_came = swap(qkv_away, "ctx", 1)
    group_f32 = jax.ShapeDtypeStruct((IO_ROWS, D), single)
    group_low = jax.ShapeDtypeStruct((IO_ROWS, D), bfloat)
    mod_rows, *io_parts, _ = row_call(
        first_kernel,
        "first",
        (
            jax.ShapeDtypeStruct((MOD_ROWS, 128), bfloat),
            group_f32,
            group_low,
            group_f32,
            group_low,
            jax.ShapeDtypeStruct((4 * IO_ROWS, D), single),
        ),
        device,
        *first_terms,
        after(resid_in, qkv_held),
        mod_own,
        grad_mid,
        noisy_low,
        rows_two,
        grad_gate_two,
        head_rows,
        smem=1,
    )
    io_held, io_away = row_call(
        side_kernel,
        "side",
        (
            jax.ShapeDtypeStruct((4, IO_ROWS, 128), single),
            jax.ShapeDtypeStruct((4 * IO_ROWS + MOD_ROWS, 128), bfloat),
        ),
        device,
        *sum_frames(io_parts[:2], sum_across(io_parts[2:])),
        mod_rows,
        smem=1,
    )
    z_rows = jax.ShapeDtypeStruct((ATTN_ROWS + IO_ROWS + 2 * MOD_ROWS, 128), bfloat)
    qkv_own, io_own, *z_pieces = row_call(
        merge_kernel,
        "merge",
        (
            jax.ShapeDtypeStruct((ATTN_ROWS, 128), single),
            jax.ShapeDtypeStruct((IO_ROWS, 128), single),
            jax.ShapeDtypeStruct((2 * MOD_ROWS, 128), bfloat),
            z_rows,
            z_rows,
            z_rows,
        ),
        device,
        qkv_held,
        qkv_came,
        out_held,
        out_came,
        io_held,
        swap(io_away, "ctx", 1),
        mod_rows,
        smem=1,
    )
    red_attn, spread = row_call(
        finish_kernel,
        "finish",
        (
            jax.ShapeDtypeStruct((4, 128, 256), single),
            jax.ShapeDtypeStruct((8 * MOD_ROWS + 2 * IO_ROWS + 16, 128), bfloat),
        ),
        qkv_own,
        io_own,
        z_pieces[0],
        *(swap(piece, "ctx", 2 * bit) for bit, piece in zip((1, 2, 3), z_pieces[1:])),
        row_call(square_kernel, "square", (jax.ShapeDtypeStruct((1, 128), single),), scattered)[0],
        error_part,
    )
    all_rows, red_vec, io_grad, square = call_mod_grad(device, cond_low, spread_frames(spread))
    terms = sum_terms(square)
    loaded = call_preload((w_mod, m_mod, v_mod), terms[0])
    updated = call_adam(
        fixes,
        terms,
        (red_attn, scattered, cond_low, all_rows),
        (w_io, m_io, v_io, io_grad[: 2 * 128].reshape(2, 128, 128)),
        (vectors, m_vec, v_vec, red_vec),
        ((w_attn, m_attn, v_attn), (w_mlp, m_mlp, v_mlp), loaded),
    )
    return (updated[21][1, 64] / weight_sum, updated[21][0, 0], *updated[:21])


def solution(mesh):
    halves = mesh.shape["ctx"] == 8 and mesh.shape["tp"] == 4
    placed = (
        P("ctx", None),
        P("ctx", None),
        P(),
        P(),
        P(),
        P(),
        P(None, "ctx", "tp"),
        P(None, "ctx", "tp"),
        P(None, "ctx", "tp"),
        P(None, "ctx", "tp"),
        P(None, "ctx", "tp"),
        P(None, "ctx", "tp"),
        P("ctx", None),
        P("ctx", None),
        P("ctx", None),
        P(None, None, "ctx"),
        P(None, None, "ctx"),
        P(None, None, "ctx"),
        P(None, "ctx"),
        P(None, "ctx"),
        P(None, "ctx"),
    )
    return jax.shard_map(
        shards_halves if halves else shards,
        mesh=mesh,
        in_specs=placed,
        out_specs=(
            P(),
            P(),
            P(None, "ctx", "tp"),
            P(None, "ctx", "tp"),
            P(None, "ctx", "tp"),
            P(None, "ctx", "tp"),
            P(None, "ctx", "tp"),
            P(None, "ctx", "tp"),
            P(None, "ctx", "tp"),
            P(None, "ctx", "tp"),
            P("ctx", None),
            P("ctx", None),
            P("ctx", None),
            P("ctx", None),
            P(None, None, "ctx"),
            P(None, None, "ctx"),
            P(None, "ctx"),
            P(None, "ctx"),
            P(None, None, "ctx"),
            P(None, "ctx"),
            P(None, "ctx"),
            P(None, "ctx"),
            P(None, "ctx"),
        ),
        check_vma=False,
    )
```

```python
import functools
import math

import jax
import jax.numpy as jnp
from jax import lax
from jax.experimental import pallas as pl
from jax.experimental.pallas import tpu as pltpu
from jax.sharding import PartitionSpec as P

D = 1024
HD = 64
GRID = 16
PATCHES = 256
LEVELS = 1000


ln_eps = 1e-06
snr_limit = 5.0
clip_limit = 0.001
beta_one = 0.9
beta_two = 0.999
adam_eps = 1e-08
rate_matrix = 0.05
rate_vector = 0.3
decay_rate = 0.1
neg_large = -1e30


def clip_starts(frame_ids, lengths):
    clip_ends = jnp.cumsum(lengths)
    before = (clip_ends[None, :] <= frame_ids[:, None]).astype(jnp.int32)
    return jnp.sum(before * lengths[None, :], axis=1)


def plan(levels):
    fraction = (levels.astype(jnp.float32) + 1.0) / (LEVELS + 1.0)
    signal_scale = jnp.cos(0.5 * math.pi * fraction)
    noise_scale = jnp.sin(0.5 * math.pi * fraction)
    snr_value = signal_scale * signal_scale / (noise_scale * noise_scale)
    weight = jnp.minimum(snr_value, snr_limit) / (snr_value + 1.0)
    return (signal_scale, noise_scale, weight)


def condition(levels, width):
    half_dim = width // 2
    frequency = jnp.exp(-math.log(10000.0) * jnp.arange(half_dim, dtype=jnp.float32) / half_dim)
    angle_tab = levels.astype(jnp.float32)[:, None] * frequency[None, :]
    return jax.nn.silu(jnp.concatenate([jnp.cos(angle_tab), jnp.sin(angle_tab)], axis=1))


def rope_tables(time_pos, height_pos, width_pos, head_dim):
    pair_count = head_dim // 2
    time_pairs = head_dim // 8
    height_pairs = (pair_count - time_pairs) // 2
    width_pairs = pair_count - time_pairs - height_pairs

    def angles(position, count):
        frequency = 10000.0 ** (-jnp.arange(count, dtype=jnp.float32) / count)
        return position.astype(jnp.float32)[:, None] * frequency[None, :]

    angle_tab = jnp.concatenate(
        [
            angles(time_pos, time_pairs),
            angles(height_pos, height_pairs),
            angles(width_pos, width_pairs),
        ],
        axis=1,
    )
    return (jnp.cos(angle_tab), jnp.sin(angle_tab))


def rotate(values, cosine, sine):
    half_dim = values.shape[-1] // 2
    first_half = values[..., :half_dim]
    second_half = values[..., half_dim:]
    cosine = cosine[:, None, :]
    sine = sine[:, None, :]
    return jnp.concatenate(
        [first_half * cosine - second_half * sine, second_half * cosine + first_half * sine],
        axis=-1,
    )


def rotate_back(grads, cosine, sine):
    half_dim = grads.shape[-1] // 2
    first_half = grads[..., :half_dim]
    second_half = grads[..., half_dim:]
    cosine = cosine[:, None, :]
    sine = sine[:, None, :]
    return jnp.concatenate(
        [first_half * cosine + second_half * sine, second_half * cosine - first_half * sine],
        axis=-1,
    )


def layer_norm(values):
    centred = values - jnp.mean(values, axis=-1, keepdims=True)
    inv_std = lax.rsqrt(jnp.mean(centred * centred, axis=-1, keepdims=True) + ln_eps)
    return (centred * inv_std, inv_std)


def norm_back(grad_in, normed, inv_std):
    mean_grad = jnp.mean(grad_in, axis=-1, keepdims=True)
    mean_proj = jnp.mean(grad_in * normed, axis=-1, keepdims=True)
    return inv_std * (grad_in - mean_grad - normed * mean_proj)


def gelu_slope(values):
    return 0.5 * (1.0 + lax.erf(values / math.sqrt(2.0))) + values * jnp.exp(
        -0.5 * values * values
    ) / math.sqrt(2.0 * math.pi)


def stretch_mask(query_stretch, key_stretch, stretch_frames, lengths):
    offsets = jnp.arange(stretch_frames, dtype=jnp.int32)
    query_frames = query_stretch * stretch_frames + offsets
    key_frames = key_stretch * stretch_frames + offsets
    starts = clip_starts(query_frames, lengths)
    return (key_frames[None, :] <= query_frames[:, None]) & (key_frames[None, :] >= starts[:, None])


def expand_mask(allowed):
    return jnp.repeat(jnp.repeat(allowed, PATCHES, axis=0), PATCHES, axis=1)


def online_step(current, query_block, key_block, value_block, keep, scale):
    run_max, run_sum, run_acc = current
    scores = (
        jnp.einsum("qhe,khe->hqk", query_block, key_block, preferred_element_type=jnp.float32)
        * scale
    )
    scores = jnp.where(keep[None], scores, neg_large)
    new_max = jnp.maximum(run_max, jnp.max(scores, axis=-1))
    probs = jnp.where(keep[None], jnp.exp(scores - new_max[..., None]), 0.0)
    shrink = jnp.exp(run_max - new_max)
    run_sum = run_sum * shrink + jnp.sum(probs, axis=-1)
    added = jnp.einsum(
        "hqk,khe->qhe", probs.astype(jnp.bfloat16), value_block, preferred_element_type=jnp.float32
    )
    run_acc = run_acc * jnp.transpose(shrink)[:, :, None] + added
    return (new_max, run_sum, run_acc)


def pair_grads(
    query_block, grad_block, lse_block, delta_block, key_block, value_block, keep, scale
):
    scores = (
        jnp.einsum("qhe,khe->hqk", query_block, key_block, preferred_element_type=jnp.float32)
        * scale
    )
    probs = jnp.where(keep[None], jnp.exp(scores - lse_block[..., None]), 0.0)
    grad_probs = jnp.einsum(
        "qhe,khe->hqk", grad_block, value_block, preferred_element_type=jnp.float32
    )
    grad_scores = (probs * (grad_probs - delta_block[..., None])).astype(jnp.bfloat16)
    grad_query = (
        jnp.einsum("hqk,khe->qhe", grad_scores, key_block, preferred_element_type=jnp.float32)
        * scale
    )
    grad_key = (
        jnp.einsum("hqk,qhe->khe", grad_scores, query_block, preferred_element_type=jnp.float32)
        * scale
    )
    grad_value = jnp.einsum(
        "hqk,qhe->khe", probs.astype(jnp.bfloat16), grad_block, preferred_element_type=jnp.float32
    )
    return (grad_query, grad_key, grad_value)


def adam(weight_now, first_mom, second_mom, grad, factor, count, rate, decay):
    grad = grad * factor
    first_mom = beta_one * first_mom + (1.0 - beta_one) * grad
    second_mom = beta_two * second_mom + (1.0 - beta_two) * grad * grad
    first_hat = first_mom / (1.0 - beta_one**count)
    second_hat = second_mom / (1.0 - beta_two**count)
    updated = weight_now - rate * (
        first_hat / (jnp.sqrt(second_hat) + adam_eps) + decay * weight_now
    )
    return (updated, first_mom, second_mom, updated.astype(jnp.bfloat16))


def shards(
    clean,
    noise,
    levels,
    lengths,
    order,
    step,
    w_attn,
    m_attn,
    v_attn,
    w_mlp,
    m_mlp,
    v_mlp,
    w_mod,
    m_mod,
    v_mod,
    w_io,
    m_io,
    v_io,
    vectors,
    m_vec,
    v_vec,
):
    ctx_count = lax.axis_size("ctx")
    ctx_index = lax.axis_index("ctx")
    tp_index = lax.axis_index("tp")
    tok_rows = clean.shape[0]
    feat_dim = clean.shape[1]
    frames_dev = tok_rows // PATCHES
    stretch_frames = frames_dev // 2
    stretch_rows = stretch_frames * PATCHES
    scale = HD ** (-0.5)
    bfloat = jnp.bfloat16
    single = jnp.float32
    attn_w, mlp_w, mod_w, io_w, vec_low = (
        lax.all_gather(w_attn.astype(bfloat), "ctx", axis=1, tiled=True),
        lax.all_gather(w_mlp.astype(bfloat), "ctx", axis=1, tiled=True),
        lax.all_gather(w_mod.astype(bfloat), "ctx", axis=0, tiled=True),
        lax.all_gather(w_io.astype(bfloat), "ctx", axis=2, tiled=True),
        lax.all_gather(vectors.astype(bfloat), "ctx", axis=1, tiled=True),
    )
    vec_w = vec_low.astype(single)
    local_width = attn_w.shape[2]
    heads_dev = local_width // HD
    frame_count = levels.shape[0]
    local_stretches = lax.dynamic_slice_in_dim(order, 2 * ctx_index, 2, 0)
    frame_ids = (
        local_stretches[:, None] * stretch_frames
        + jnp.arange(stretch_frames, dtype=jnp.int32)[None, :]
    ).reshape(frames_dev)
    table_hit = frame_ids[:, None] == jnp.arange(frame_count, dtype=jnp.int32)[None, :]
    frame_levels = jnp.sum(jnp.where(table_hit, levels[None, :], 0), axis=1)
    starts = clip_starts(frame_ids, lengths)
    signal_scale, noise_scale, weight = plan(frame_levels)
    signal_col = signal_scale[:, None, None]
    noise_col = noise_scale[:, None, None]
    clean_full = clean.astype(single).reshape(frames_dev, PATCHES, feat_dim)
    noise_full = noise.astype(single).reshape(frames_dev, PATCHES, feat_dim)
    noisy = signal_col * clean_full + noise_col * noise_full
    target = signal_col * noise_full - noise_col * clean_full
    noisy_low = noisy.reshape(tok_rows, feat_dim).astype(bfloat)
    embedded = jnp.dot(noisy_low, io_w[0], preferred_element_type=single) + vec_w[6]
    cond_low = condition(frame_levels, D).astype(bfloat)
    modulate = (
        jnp.dot(cond_low, mod_w, preferred_element_type=single) + vec_w[:6].reshape(6 * D)
    ).reshape(frames_dev, 6, 1, D)
    patch_ids = jnp.arange(PATCHES, dtype=jnp.int32)
    time_pos = jnp.repeat(frame_ids - starts, PATCHES)
    height_pos = jnp.tile(patch_ids // GRID, frames_dev)
    width_pos = jnp.tile(patch_ids % GRID, frames_dev)
    cosine, sine = rope_tables(time_pos, height_pos, width_pos, HD)
    resid_in = embedded.reshape(frames_dev, PATCHES, D)
    normed_one, inv_one = layer_norm(resid_in)
    hidden_one = (
        (normed_one * (1.0 + modulate[:, 1]) + modulate[:, 0]).reshape(tok_rows, D).astype(bfloat)
    )
    query_pre = jnp.dot(hidden_one, attn_w[0], preferred_element_type=single).reshape(
        tok_rows, heads_dev, HD
    )
    key_pre = jnp.dot(hidden_one, attn_w[1], preferred_element_type=single).reshape(
        tok_rows, heads_dev, HD
    )
    query_low = rotate(query_pre, cosine, sine).astype(bfloat)
    key_low = rotate(key_pre, cosine, sine).astype(bfloat)
    value_low = (
        jnp.dot(hidden_one, attn_w[2], preferred_element_type=single)
        .astype(bfloat)
        .reshape(tok_rows, heads_dev, HD)
    )
    query_stretches = query_low.reshape(2, stretch_rows, heads_dev, HD)
    init_state = (
        jnp.full((2, heads_dev, stretch_rows), neg_large, single),
        jnp.zeros((2, heads_dev, stretch_rows), single),
        jnp.zeros((2, stretch_rows, heads_dev, HD), single),
    )
    key_flat = key_low.reshape(tok_rows, local_width)
    value_flat = value_low.reshape(tok_rows, local_width)
    carry_state = init_state
    key_piece = lax.all_gather(key_flat, "ctx", axis=0, tiled=True)
    value_piece = lax.all_gather(value_flat, "ctx", axis=0, tiled=True)

    def per_stretch(block_num, carry_state):
        key_block = lax.dynamic_slice_in_dim(
            key_piece, block_num * stretch_rows, stretch_rows, 0
        ).reshape(stretch_rows, heads_dev, HD)
        value_block = lax.dynamic_slice_in_dim(
            value_piece, block_num * stretch_rows, stretch_rows, 0
        ).reshape(stretch_rows, heads_dev, HD)
        key_stretch = lax.dynamic_index_in_dim(order, block_num, 0, keepdims=False)
        updated = []
        for half_num in range(2):
            allowed = stretch_mask(local_stretches[half_num], key_stretch, stretch_frames, lengths)
            current = (carry_state[0][half_num], carry_state[1][half_num], carry_state[2][half_num])
            current = lax.cond(
                jnp.any(allowed),
                lambda cur, keep_mask: online_step(
                    cur,
                    query_stretches[half_num],
                    key_block,
                    value_block,
                    expand_mask(keep_mask),
                    scale,
                ),
                lambda cur, keep_mask: cur,
                current,
                allowed,
            )
            updated.append(current)
        return tuple((jnp.stack([updated[0][member], updated[1][member]]) for member in range(3)))

    run_max, run_sum, run_acc = lax.fori_loop(
        0, key_piece.shape[0] // stretch_rows, per_stretch, carry_state
    )
    mix_rows = (run_acc / jnp.transpose(run_sum, (0, 2, 1))[..., None]).reshape(
        tok_rows, heads_dev, HD
    )
    lse_stretches = run_max + jnp.log(run_sum)
    mix_low = mix_rows.reshape(tok_rows, local_width).astype(bfloat)
    attn_out = lax.psum(
        jnp.einsum("rh,dh->rd", mix_low, attn_w[3], preferred_element_type=single).astype(
            jnp.bfloat16
        ),
        "tp",
    ).astype(jnp.float32)
    attn_full = attn_out.reshape(frames_dev, PATCHES, D)
    resid_mid = resid_in + modulate[:, 2] * attn_full
    normed_two, inv_two = layer_norm(resid_mid)
    hidden_two = (
        (normed_two * (1.0 + modulate[:, 4]) + modulate[:, 3]).reshape(tok_rows, D).astype(bfloat)
    )
    upward = jnp.dot(hidden_two, mlp_w[0], preferred_element_type=single)
    activ_low = jax.nn.gelu(upward, approximate=False).astype(bfloat)
    mlp_out = lax.psum(
        jnp.einsum("rf,df->rd", activ_low, mlp_w[1], preferred_element_type=single).astype(
            jnp.bfloat16
        ),
        "tp",
    ).astype(jnp.float32)
    mlp_full = mlp_out.reshape(frames_dev, PATCHES, D)
    resid_out = resid_mid + modulate[:, 5] * mlp_full
    normed_three, inv_three = layer_norm(resid_out)
    final_low = (normed_three * vec_w[7]).reshape(tok_rows, D).astype(bfloat)
    pred = jnp.einsum("rd,pd->rp", final_low, io_w[1], preferred_element_type=single)
    diff = pred.reshape(frames_dev, PATCHES, feat_dim) - target
    error = jnp.mean(diff * diff, axis=2)
    weight_sum, error_sum = lax.psum(
        (PATCHES * jnp.sum(weight), jnp.sum(weight[:, None] * error)), "ctx"
    )
    loss_value = error_sum / weight_sum
    grad_pred = (
        (2.0 / feat_dim * weight[:, None, None] * diff / weight_sum)
        .reshape(tok_rows, feat_dim)
        .astype(bfloat)
    )
    grad_head = jnp.einsum("rp,rd->pd", grad_pred, final_low, preferred_element_type=single)
    grad_final = jnp.einsum("rp,pd->rd", grad_pred, io_w[1], preferred_element_type=single).reshape(
        frames_dev, PATCHES, D
    )
    grad_gain = jnp.sum(grad_final * normed_three, axis=(0, 1))
    grad_three = norm_back(grad_final * vec_w[7], normed_three, inv_three)
    grad_mlp_low = (modulate[:, 5] * grad_three).reshape(tok_rows, D).astype(bfloat)
    grad_gate_two = jnp.sum(grad_three * mlp_full, axis=1)
    grad_activ = jnp.einsum("rd,df->rf", grad_mlp_low, mlp_w[1], preferred_element_type=single)
    grad_down = jnp.einsum("rd,rf->df", grad_mlp_low, activ_low, preferred_element_type=single)
    grad_up_low = (grad_activ * gelu_slope(upward)).astype(bfloat)
    grad_up = jnp.einsum("rd,rf->df", hidden_two, grad_up_low, preferred_element_type=single)
    grad_hidden_two = lax.psum(
        jnp.einsum("rf,df->rd", grad_up_low, mlp_w[0], preferred_element_type=single).astype(
            jnp.bfloat16
        ),
        "tp",
    ).astype(jnp.float32)
    grad_hidden_two = grad_hidden_two.reshape(frames_dev, PATCHES, D)
    grad_shift_two = jnp.sum(grad_hidden_two, axis=1)
    grad_scale_two = jnp.sum(grad_hidden_two * normed_two, axis=1)
    grad_mid = grad_three + norm_back(grad_hidden_two * (1.0 + modulate[:, 4]), normed_two, inv_two)
    grad_attn_low = (modulate[:, 2] * grad_mid).reshape(tok_rows, D).astype(bfloat)
    grad_gate_one = jnp.sum(grad_mid * attn_full, axis=1)
    grad_outproj = jnp.einsum("rd,rh->dh", grad_attn_low, mix_low, preferred_element_type=single)
    grad_mix_low = jnp.einsum(
        "rd,dh->rh", grad_attn_low, attn_w[3], preferred_element_type=single
    ).astype(bfloat)
    delta_rows = jnp.sum(
        grad_mix_low.astype(single).reshape(tok_rows, heads_dev, HD) * mix_rows, axis=2
    )
    grad_stretches = grad_mix_low.reshape(2, stretch_rows, heads_dev, HD)
    delta_stretches = jnp.transpose(delta_rows.reshape(2, stretch_rows, heads_dev), (0, 2, 1))

    def span_back(key_block, value_block, key_stretch, grad_query_acc):
        key_sum = jnp.zeros((stretch_rows, heads_dev, HD), single)
        value_sum = jnp.zeros((stretch_rows, heads_dev, HD), single)
        query_parts = []
        for half_num in range(2):
            allowed = stretch_mask(local_stretches[half_num], key_stretch, stretch_frames, lengths)
            result = lax.cond(
                jnp.any(allowed),
                lambda keep_mask: pair_grads(
                    query_stretches[half_num],
                    grad_stretches[half_num],
                    lse_stretches[half_num],
                    delta_stretches[half_num],
                    key_block,
                    value_block,
                    expand_mask(keep_mask),
                    scale,
                ),
                lambda keep_mask: (jnp.zeros((stretch_rows, heads_dev, HD), single),) * 3,
                allowed,
            )
            query_parts.append(grad_query_acc[half_num] + result[0])
            key_sum = key_sum + result[1]
            value_sum = value_sum + result[2]
        return (
            jnp.stack(query_parts),
            key_sum.reshape(stretch_rows, local_width),
            value_sum.reshape(stretch_rows, local_width),
        )

    init_back = (
        jnp.zeros((2, stretch_rows, heads_dev, HD), single),
        jnp.zeros((ctx_count * tok_rows, local_width), single),
        jnp.zeros((ctx_count * tok_rows, local_width), single),
    )
    carry_state = init_back
    fold_key_piece = lax.all_gather(key_flat, "ctx", axis=0, tiled=True)
    fold_value_piece = lax.all_gather(value_flat, "ctx", axis=0, tiled=True)

    def per_stretch(block_num, carry_state):
        grad_query_acc, grad_keys_all, grad_values_all = carry_state
        key_block = lax.dynamic_slice_in_dim(
            fold_key_piece, block_num * stretch_rows, stretch_rows, 0
        ).reshape(stretch_rows, heads_dev, HD)
        value_block = lax.dynamic_slice_in_dim(
            fold_value_piece, block_num * stretch_rows, stretch_rows, 0
        ).reshape(stretch_rows, heads_dev, HD)
        key_stretch = lax.dynamic_index_in_dim(order, block_num, 0, keepdims=False)
        grad_query_acc, key_sum, value_sum = span_back(
            key_block, value_block, key_stretch, grad_query_acc
        )
        place = block_num * stretch_rows
        grad_keys_all = lax.dynamic_update_slice_in_dim(grad_keys_all, key_sum, place, 0)
        grad_values_all = lax.dynamic_update_slice_in_dim(grad_values_all, value_sum, place, 0)
        return (grad_query_acc, grad_keys_all, grad_values_all)

    grad_query_acc, grad_keys_all, grad_values_all = lax.fori_loop(
        0, fold_key_piece.shape[0] // stretch_rows, per_stretch, carry_state
    )
    grad_keys, grad_values = (
        lax.psum_scatter(
            grad_keys_all.astype(jnp.bfloat16), "ctx", scatter_dimension=0, tiled=True
        ).astype(jnp.float32),
        lax.psum_scatter(
            grad_values_all.astype(jnp.bfloat16), "ctx", scatter_dimension=0, tiled=True
        ).astype(jnp.float32),
    )
    grad_query = grad_query_acc.reshape(tok_rows, local_width)
    query_back = (
        rotate_back(grad_query.reshape(tok_rows, heads_dev, HD), cosine, sine)
        .reshape(tok_rows, local_width)
        .astype(bfloat)
    )
    key_back = (
        rotate_back(grad_keys.reshape(tok_rows, heads_dev, HD), cosine, sine)
        .reshape(tok_rows, local_width)
        .astype(bfloat)
    )
    value_back = grad_values.astype(bfloat)
    grad_wq = jnp.einsum("rd,rh->dh", hidden_one, query_back, preferred_element_type=single)
    grad_wk = jnp.einsum("rd,rh->dh", hidden_one, key_back, preferred_element_type=single)
    grad_wv = jnp.einsum("rd,rh->dh", hidden_one, value_back, preferred_element_type=single)
    partial_one = (
        jnp.einsum("rh,dh->rd", query_back, attn_w[0], preferred_element_type=single)
        + jnp.einsum("rh,dh->rd", key_back, attn_w[1], preferred_element_type=single)
        + jnp.einsum("rh,dh->rd", value_back, attn_w[2], preferred_element_type=single)
    )
    grad_hidden_one = (
        lax.psum(partial_one.astype(jnp.bfloat16), "tp")
        .astype(jnp.float32)
        .reshape(frames_dev, PATCHES, D)
    )
    grad_shift_one = jnp.sum(grad_hidden_one, axis=1)
    grad_scale_one = jnp.sum(grad_hidden_one * normed_one, axis=1)
    grad_in = grad_mid + norm_back(grad_hidden_one * (1.0 + modulate[:, 1]), normed_one, inv_one)
    grad_mod = jnp.stack(
        [
            grad_shift_one,
            grad_scale_one,
            grad_gate_one,
            grad_shift_two,
            grad_scale_two,
            grad_gate_two,
        ],
        axis=1,
    )
    grad_mod_w = jnp.einsum(
        "fd,fc->dc",
        cond_low,
        grad_mod.reshape(frames_dev, 6 * D).astype(bfloat),
        preferred_element_type=single,
    )
    grad_in_low = grad_in.reshape(tok_rows, D).astype(bfloat)
    grad_embed = jnp.einsum("rp,rd->pd", noisy_low, grad_in_low, preferred_element_type=single)
    grad_vec = jnp.concatenate(
        [jnp.sum(grad_mod, axis=0), jnp.sum(grad_in, axis=(0, 1))[None], grad_gain[None]], axis=0
    )
    grad_attn = jnp.stack([grad_wq, grad_wk, grad_wv, grad_outproj])
    grad_mlp = jnp.stack([grad_up, grad_down])
    grad_io = jnp.stack([grad_embed, grad_head])
    red_attn, red_mlp, red_mod, red_io, red_vec = (
        lax.psum_scatter(
            grad_attn.astype(jnp.bfloat16), "ctx", scatter_dimension=1, tiled=True
        ).astype(jnp.float32),
        lax.psum_scatter(
            grad_mlp.astype(jnp.bfloat16), "ctx", scatter_dimension=1, tiled=True
        ).astype(jnp.float32),
        lax.psum_scatter(
            grad_mod_w.astype(jnp.bfloat16), "ctx", scatter_dimension=0, tiled=True
        ).astype(jnp.float32),
        lax.psum_scatter(
            grad_io.astype(jnp.bfloat16), "ctx", scatter_dimension=2, tiled=True
        ).astype(jnp.float32),
        lax.psum_scatter(
            grad_vec.astype(jnp.bfloat16), "ctx", scatter_dimension=1, tiled=True
        ).astype(jnp.float32),
    )
    shared_sq = jnp.sum(red_mod * red_mod) + jnp.sum(red_io * red_io) + jnp.sum(red_vec * red_vec)
    own_sq = (
        jnp.sum(red_attn * red_attn)
        + jnp.sum(red_mlp * red_mlp)
        + jnp.where(tp_index == 0, shared_sq, 0.0)
    )
    grad_norm = jnp.sqrt(lax.psum(own_sq, ("ctx", "tp")))
    factor = jnp.minimum(1.0, clip_limit / (grad_norm + 1e-06))
    count = step[0].astype(single)
    attn_new = adam(w_attn, m_attn, v_attn, red_attn, factor, count, rate_matrix, decay_rate)
    mlp_new = adam(w_mlp, m_mlp, v_mlp, red_mlp, factor, count, rate_matrix, decay_rate)
    mod_new = adam(w_mod, m_mod, v_mod, red_mod, factor, count, rate_matrix, decay_rate)
    io_new = adam(w_io, m_io, v_io, red_io, factor, count, rate_matrix, decay_rate)
    vec_new = adam(vectors, m_vec, v_vec, red_vec, factor, count, rate_vector, 0.0)
    return (
        loss_value,
        grad_norm,
        attn_new[0],
        attn_new[1],
        attn_new[2],
        attn_new[3],
        mlp_new[0],
        mlp_new[1],
        mlp_new[2],
        mlp_new[3],
        mod_new[0],
        mod_new[1],
        mod_new[2],
        mod_new[3],
        io_new[0],
        io_new[1],
        io_new[2][0],
        io_new[2][1],
        io_new[3],
        vec_new[0],
        vec_new[1],
        vec_new[2],
        vec_new[3],
    )


HALF_SLOTS = 16
QKV_ROWS = 768
ATTN_ROWS = 1024
FRONT_ROWS = 912
TOKEN_ROWS = 512
IO_ROWS = 80
MOD_ROWS = 48
NT = (((1,), (1,)), ((), ()))
TN = (((0,), (0,)), ((), ()))


def swap(values, axis, bit):
    size = 8 if axis == "ctx" else 4
    return lax.ppermute(values, axis, [(i, i ^ bit) for i in range(size)])


def after(values, *others):
    return lax.optimization_barrier((values,) + others)[0]


def gather_swaps(shard):
    along_x = swap(shard, "ctx", 1)
    along_z = [swap(shard, "ctx", bit) for bit in (2, 4, 6)]
    return [shard, along_x, *along_z, swap(jnp.concatenate(along_z, axis=0), "ctx", 1)]


def reduce_blocks(blocks, ctx_index, wire):
    return reduce_along_z(reduce_along_x(blocks, ctx_index, wire), ctx_index, wire)


def reduce_along_x(blocks, ctx_index, wire):
    x = ctx_index % 2
    pairs = blocks.reshape((4, 2) + blocks.shape[1:])
    first, second = pairs[:, 0], pairs[:, 1]
    even = x == 0
    away = jnp.where(even, second, first).astype(wire)
    return jnp.where(even, first, second) + swap(away, "ctx", 1).astype(jnp.float32)


def pieces_along_z(held, ctx_index, wire):
    z = ctx_index // 2
    low = held.astype(wire)
    came = []
    for bit in (1, 2, 3):
        piece = lax.dynamic_index_in_dim(low, z ^ bit, 0, keepdims=False)
        came.append(swap(piece, "ctx", 2 * bit))
    return lax.dynamic_index_in_dim(held, z, 0, keepdims=False), came


def reduce_along_z(held, ctx_index, wire):
    total, came = pieces_along_z(held, ctx_index, wire)
    for piece in came:
        total = total + piece.astype(jnp.float32)
    return total


def spread_frames(own):
    core = swap(own, "tp", 1)
    across = swap(own, "tp", 2)
    return [own, core, across, swap(across, "tp", 1)]


def sum_across(far):
    return (far[0] + swap(far[1], "tp", 1).astype(jnp.float32)).astype(jnp.bfloat16)


def sum_frames(near, across):
    return near[0], swap(near[1], "tp", 1), swap(across, "tp", 2)


def reorder_four(items, index):
    low_bit = (index & 1) == 1
    high_bit = (index & 2) == 2
    once = [jnp.where(low_bit, items[k ^ 1], items[k]) for k in range(4)]
    return [jnp.where(high_bit, once[k ^ 2], once[k]) for k in range(4)]


def sum_terms(values):
    values = values + swap(values, "ctx", 1)
    return [values] + [swap(values, "ctx", bit) for bit in (2, 4, 6)]


def token_kernel(meta, clean, noise, ring):
    for frame in range(4):
        rows = pl.ds(pl.multiple_of(256 * frame + 64 * meta[1], 64), 64)
        ring[128 * frame : 128 * frame + 64, :] = clean[rows, :]
        ring[128 * frame + 64 : 128 * frame + 128, :] = noise[rows, :]


def prepare_kernel(w_attn, w_io, vectors, front):
    for part in range(3):
        front[256 * part : 256 * part + 256, :] = w_attn[part].T.astype(jnp.bfloat16)
    base = QKV_ROWS
    front[base : base + 128, :] = w_io[0].astype(jnp.bfloat16)
    front[base + 128 : base + 144, :] = jnp.concatenate(
        [vectors[...], jnp.zeros((8, 128), jnp.float32)], axis=0
    ).astype(jnp.bfloat16)
    for part in range(2):
        base = FRONT_ROWS + 128 * part
        front[base : base + 128, :] = w_attn[3, :, 128 * part : 128 * part + 128].astype(
            jnp.bfloat16
        )
    front[FRONT_ROWS + 256 : FRONT_ROWS + 384, :] = w_io[1].T.astype(jnp.bfloat16)


def vmem_specs(count):
    return [pl.BlockSpec(memory_space=pltpu.VMEM)] * count


def smem_specs(count):
    return [pl.BlockSpec(memory_space=pltpu.SMEM)] * count


def call_tokens(device, clean, noise):
    return pl.pallas_call(
        token_kernel,
        out_shape=jax.ShapeDtypeStruct((TOKEN_ROWS, 128), jnp.bfloat16),
        in_specs=smem_specs(1) + vmem_specs(2),
        out_specs=vmem_specs(1)[0],
        name="tokens",
    )(device, clean, noise)


def call_prepare(w_attn, w_io, vectors):
    return pl.pallas_call(
        prepare_kernel,
        out_shape=jax.ShapeDtypeStruct((FRONT_ROWS + 384, 128), jnp.bfloat16),
        in_specs=vmem_specs(3),
        out_specs=vmem_specs(1)[0],
        name="prepare",
    )(w_attn, w_io, vectors)


def place_kernel(device, lengths, order, levels, front, attend, rows, inverse, stored, position, level):
    ctx, tp = device[0], device[1]
    frames, stretches, clips = levels.shape[0], order.shape[0], lengths.shape[0]
    per_stretch = frames // stretches
    half = frames // 2

    def per_stretch_place(place, carry):
        inverse[order[place]] = place
        return carry

    lax.fori_loop(0, stretches, per_stretch_place, 0)

    def per_frame(frame, counts):
        long_count, short_count = counts
        begin, start, length = jnp.int32(0), jnp.int32(0), jnp.int32(0)
        for clip in range(clips):
            size = lengths[clip]
            inside = (frame >= begin) & (frame < begin + size)
            start = jnp.where(inside, begin, start)
            length = jnp.where(inside, size, length)
            begin = begin + size
        is_long = length == half
        slot = jnp.where(is_long, long_count, half + short_count)
        stored[slot] = inverse[lax.div(frame, jnp.int32(per_stretch))] * per_stretch + lax.rem(
            frame, jnp.int32(per_stretch)
        )
        position[slot] = frame - start
        level[slot] = levels[frame]
        grown = is_long.astype(jnp.int32)
        return (long_count + grown, short_count + 1 - grown)

    lax.fori_loop(0, frames, per_frame, (jnp.int32(0), jnp.int32(0)))

    member = ctx & 3
    for k in range(4):
        front[8 + k] = 4 * member + (tp ^ k)
        front[12 + k] = member ^ k
        at = stored[4 * ctx + (tp ^ k)]
        front[16 + k] = ((at >> 2) ^ ctx) * 4 + (at & 3)
        front[20 + k] = tp ^ k
    for k in range(8):
        front[k] = 0
    attend[0] = member
    attend[1] = tp
    base = lax.div(ctx, jnp.int32(4)) * half

    def per_slot(slot, carry):
        attend[2 + slot] = position[base + slot]
        return carry

    lax.fori_loop(0, half, per_slot, 0)

    def per_row(row, carry):
        rows[row] = level[row]
        rows[frames + row] = level[4 * (ctx ^ (row & 7)) + (row >> 3)]
        return carry

    lax.fori_loop(0, frames, per_row, 0)
    for k in range(8):
        rows[2 * frames + k] = level[4 * ctx + (tp ^ (k & 3))]


def call_place(device, lengths, order, levels):
    frames = levels.shape[0]
    return pl.pallas_call(
        place_kernel,
        out_shape=(
            jax.ShapeDtypeStruct((24,), jnp.int32),
            jax.ShapeDtypeStruct((2 + frames // 2,), jnp.int32),
            jax.ShapeDtypeStruct((2 * frames + 8,), jnp.int32),
        ),
        in_specs=smem_specs(4),
        out_specs=smem_specs(3),
        scratch_shapes=[pltpu.SMEM((order.shape[0],), jnp.int32)]
        + [pltpu.SMEM((frames,), jnp.int32)] * 3,
        name="place",
    )(device, lengths, order, levels)


def pick_kernel(meta, *refs):
    out, sems = refs[6:]
    places = [(refs[0], 0), (refs[1], 0)]
    for bit in range(3):
        places += [(refs[2 + bit], 0), (refs[5], TOKEN_ROWS * bit)]
    for frame in range(4):
        wanted = meta[16 + frame]
        for place, (source, base) in enumerate(places):

            @pl.when((wanted >> 2) == place)
            def _():
                start = pl.multiple_of(base + (wanted & 3) * 128, 128)
                pltpu.make_async_copy(
                    source.at[pl.ds(start, 128), :],
                    out.at[128 * frame : 128 * frame + 128, :],
                    sems.at[frame],
                ).start()

    for frame in range(4):
        pltpu.make_async_copy(
            refs[0].at[0:128, :], out.at[128 * frame : 128 * frame + 128, :], sems.at[frame]
        ).wait()


def hbm_specs(count):
    return [pl.BlockSpec(memory_space=pltpu.HBM)] * count


def call_pick(meta, pieces):
    return pl.pallas_call(
        pick_kernel,
        out_shape=jax.ShapeDtypeStruct((TOKEN_ROWS, 128), jnp.bfloat16),
        in_specs=smem_specs(1) + hbm_specs(6),
        out_specs=vmem_specs(1)[0],
        scratch_shapes=[pltpu.SemaphoreType.DMA((4,))],
        compiler_params=pltpu.CompilerParams(vmem_limit_bytes=56 * 2**20),
        name="pick",
    )(meta, *pieces)


def centred_norm(values):
    centred = values - jnp.mean(values, axis=-1, keepdims=True)
    inv_std = lax.rsqrt(jnp.mean(centred * centred, axis=-1, keepdims=True) + ln_eps)
    return centred * inv_std, inv_std


def front_kernel(meta, scales, *refs):
    pieces, quarters = refs[0], refs[1:5]
    mod, cosine, sine = refs[5:8]
    weights_out, mid_out, hidden_out, resid_out = refs[8:12]
    head_outs = refs[12:16]
    noisy_out, target_out, mod_out = refs[16:19]
    tokens, heads, weights, mid, hidden, resid, target, mod_own, held, sems, out_sems = refs[19:]
    copies = [
        pltpu.make_async_copy(pieces.at[place], held.at[place], sems.at[place])
        for place in range(8)
    ]
    for copy in copies:
        copy.start()
    for source in range(4):
        rows = pl.ds(pl.multiple_of(meta[20 + source] * 64, 64), 64)
        for frame in range(4):
            base = 128 * (frame ^ source)
            clean = quarters[source][base : base + 64, :].astype(jnp.float32)
            noise = quarters[source][base + 64 : base + 128, :].astype(jnp.float32)
            mixed = scales[frame] * clean + scales[4 + frame] * noise
            tokens[frame, rows, :] = mixed.astype(jnp.bfloat16)
            if frame == 0:
                target[rows, :] = scales[0] * noise - scales[4] * clean
    outs = [
        pltpu.make_async_copy(tokens.at[0], noisy_out, out_sems.at[0]),
        pltpu.make_async_copy(target, target_out, out_sems.at[1]),
        pltpu.make_async_copy(weights, weights_out, out_sems.at[2]),
        pltpu.make_async_copy(resid, resid_out, out_sems.at[3]),
    ] + [
        pltpu.make_async_copy(hidden.at[frame], hidden_out.at[frame], out_sems.at[4 + frame])
        for frame in range(4)
    ]
    outs.append(pltpu.make_async_copy(mod_own, mod_out, out_sems.at[8]))
    outs.append(pltpu.make_async_copy(mid, mid_out, out_sems.at[9]))
    for place in range(8):
        copies[place].wait()
        block = slice(128 * place, 128 * place + 128)
        weights[:, block] = held[place, 0:FRONT_ROWS, :]
        for part in range(3):
            base = FRONT_ROWS + 128 * part
            mid[block, 128 * part : 128 * part + 128] = held[place, base : base + 128, :]
    for index in (0, 1, 2, 9):
        outs[index].start()
    embed = weights[QKV_ROWS : QKV_ROWS + 128, :]
    vec_rows = weights[QKV_ROWS + 128 : FRONT_ROWS, :].astype(jnp.float32)
    mod_own[0:6, :] = mod[0] + vec_rows[0:6]
    mod_own[6:8, :] = vec_rows[6:8]
    outs[8].start()
    for frame in range(4):
        values = jnp.dot(tokens[frame], embed, preferred_element_type=jnp.float32) + vec_rows[6:7]
        if frame == 0:
            resid[...] = values
            outs[3].start()
        normed, _ = centred_norm(values)
        shift = mod[frame, 0:1, :] + vec_rows[0:1]
        scale = mod[frame, 1:2, :] + vec_rows[1:2]
        low = (normed * (1.0 + scale) + shift).astype(jnp.bfloat16)
        hidden[frame] = low
        outs[4 + frame].start()
        mixed = lax.dot_general(
            weights[0:QKV_ROWS, :], low, NT, preferred_element_type=jnp.float32
        )
        cos_now = cosine[meta[8 + frame]]
        sin_now = sine[meta[8 + frame]]
        cols = slice(256 * frame, 256 * frame + 256)
        for head in range(4):
            where_to = head
            for part in range(2):
                base = 256 * part + 64 * head
                upper = mixed[base : base + 32]
                lower = mixed[base + 32 : base + 64]
                heads[where_to, 64 * part : 64 * part + 32, cols] = (
                    upper * cos_now - lower * sin_now
                ).astype(jnp.bfloat16)
                heads[where_to, 64 * part + 32 : 64 * part + 64, cols] = (
                    lower * cos_now + upper * sin_now
                ).astype(jnp.bfloat16)
            base = 512 + 64 * head
            heads[where_to, 128:192, cols] = mixed[base : base + 64].astype(jnp.bfloat16)
    for k in range(4):
        outs.append(pltpu.make_async_copy(heads.at[meta[12 + k]], head_outs[k], out_sems.at[10 + k]))
        outs[10 + k].start()
    for copy in outs:
        copy.wait()


def call_front(meta, scales, pieces, quarters, mod, cosine, sine):
    return pl.pallas_call(
        front_kernel,
        out_shape=(
            jax.ShapeDtypeStruct((FRONT_ROWS, D), jnp.bfloat16),
            jax.ShapeDtypeStruct((D, 384), jnp.bfloat16),
            jax.ShapeDtypeStruct((4, PATCHES, D), jnp.bfloat16),
            jax.ShapeDtypeStruct((PATCHES, D), jnp.float32),
        )
        + (jax.ShapeDtypeStruct((192, 4 * PATCHES), jnp.bfloat16),) * 4
        + (
            jax.ShapeDtypeStruct((PATCHES, 128), jnp.bfloat16),
            jax.ShapeDtypeStruct((PATCHES, 128), jnp.float32),
            jax.ShapeDtypeStruct((8, D), jnp.float32),
        ),
        in_specs=smem_specs(2) + hbm_specs(1) + vmem_specs(7),
        out_specs=hbm_specs(11),
        scratch_shapes=[
            pltpu.VMEM((4, PATCHES, 128), jnp.bfloat16),
            pltpu.VMEM((4, 192, 4 * PATCHES), jnp.bfloat16),
            pltpu.VMEM((FRONT_ROWS, D), jnp.bfloat16),
            pltpu.VMEM((D, 384), jnp.bfloat16),
            pltpu.VMEM((4, PATCHES, D), jnp.bfloat16),
            pltpu.VMEM((PATCHES, D), jnp.float32),
            pltpu.VMEM((PATCHES, 128), jnp.float32),
            pltpu.VMEM((8, D), jnp.float32),
            pltpu.VMEM((8, FRONT_ROWS + 384, 128), jnp.bfloat16),
            pltpu.SemaphoreType.DMA((8,)),
            pltpu.SemaphoreType.DMA((14,)),
        ],
        compiler_params=pltpu.CompilerParams(vmem_limit_bytes=52 * 2**20),
        cost_estimate=pl.CostEstimate(flops=2 * 10**9, bytes_accessed=10**7, transcendentals=0),
        name="front",
    )(meta, scales, pieces, *quarters, mod, cosine, sine)


def total_own(held, came, across):
    return held[...] + came[...].astype(jnp.float32) + across[...].astype(jnp.float32)


def middle_kernel(held, came, across, resid, mod, attn_out, resid_mid, hidden):
    total = total_own(held, came, across)
    attn_out[...] = total
    values = resid[...] + mod[2:3, :] * total
    resid_mid[...] = values
    normed, _ = centred_norm(values)
    hidden[...] = (normed * (1.0 + mod[4:5, :]) + mod[3:4, :]).astype(jnp.bfloat16)


def row_call(kernel, name, outs, *operands, smem=0):
    return pl.pallas_call(
        kernel,
        out_shape=tuple(outs),
        in_specs=smem_specs(smem) + vmem_specs(len(operands) - smem),
        out_specs=vmem_specs(len(outs)),
        compiler_params=pltpu.CompilerParams(vmem_limit_bytes=16 * 2**20),
        cost_estimate=pl.CostEstimate(flops=10**9, bytes_accessed=4 * 10**6, transcendentals=0),
        name=name,
    )(*operands)


def frame_f32():
    return jax.ShapeDtypeStruct((PATCHES, D), jnp.float32)


def frame_low():
    return jax.ShapeDtypeStruct((PATCHES, D), jnp.bfloat16)


def back_through_norm(grad, normed, inv_std):
    mean_grad = jnp.mean(grad, axis=-1, keepdims=True)
    mean_proj = jnp.mean(grad * normed, axis=-1, keepdims=True)
    return inv_std * (grad - mean_grad - normed * mean_proj)


def column_sum(values):
    return jnp.sum(values, axis=0, keepdims=True)


def loss_kernel(
    scales, held, came, across, resid_mid, mod, mid, target, grad_low, grad_three, io_rows, gate, error
):
    mlp_out = total_own(held, came, across)
    values = resid_mid[...] + mod[5:6, :] * mlp_out
    normed, inv_std = centred_norm(values)
    gain = mod[7:8, :]
    final = (normed * gain).astype(jnp.bfloat16)
    head = mid[:, 256:384]
    pred = jnp.dot(final, head, preferred_element_type=jnp.float32)
    diff = pred - target[...]
    per_token = jnp.sum(diff * diff, axis=1, keepdims=True)
    error[...] = jnp.broadcast_to(
        scales[0] * jnp.sum(per_token, axis=0, keepdims=True) / diff.shape[1], error.shape
    )
    grad_pred = (scales[1] * diff).astype(jnp.bfloat16)
    grad_final = lax.dot_general(grad_pred, head, NT, preferred_element_type=jnp.float32)
    grad_gain = column_sum(grad_final * normed)
    grad = back_through_norm(grad_final * gain, normed, inv_std)
    grad_three[...] = grad
    grad_low[...] = (mod[5:6, :] * grad).astype(jnp.bfloat16)
    gate[...] = column_sum(grad * mlp_out)
    io_rows[0:128, :] = lax.dot_general(grad_pred, final, TN, preferred_element_type=jnp.float32)
    io_rows[128:136, :] = jnp.concatenate([grad_gain, jnp.zeros((7, D), jnp.float32)], axis=0)


def second_kernel(
    held, came, across, resid_mid, mod, grad_three, attn_out, grad_low, grad_mid, rows
):
    grad_hidden = total_own(held, came, across)
    normed, inv_std = centred_norm(resid_mid[...])
    grad = grad_three[...] + back_through_norm(grad_hidden * (1.0 + mod[4:5, :]), normed, inv_std)
    grad_mid[...] = grad
    grad_low[...] = (mod[2:3, :] * grad).astype(jnp.bfloat16)
    rows[0:1, :] = column_sum(grad * attn_out[...])
    rows[1:2, :] = column_sum(grad_hidden)
    rows[2:3, :] = column_sum(grad_hidden * normed)


def first_kernel(
    device,
    held,
    came,
    across,
    resid,
    mod,
    grad_mid,
    noisy,
    rows_two,
    gate_two,
    head_rows,
    mod_rows,
    near_held,
    near_away,
    far_held,
    far_away,
    io_rows,
):
    grad_hidden = total_own(held, came, across)
    normed, inv_std = centred_norm(resid[...])
    grad = grad_mid[...] + back_through_norm(grad_hidden * (1.0 + mod[1:2, :]), normed, inv_std)
    rows = [
        column_sum(grad_hidden),
        column_sum(grad_hidden * normed),
        rows_two[0:1, :],
        rows_two[1:2, :],
        rows_two[2:3, :],
        gate_two[...],
    ]
    blocks = [row[:, 128 * k : 128 * k + 128] for row in rows for k in range(8)]
    mod_rows[...] = jnp.concatenate(blocks, axis=0).astype(jnp.bfloat16)
    io_rows[0:128, :] = lax.dot_general(
        noisy[...], grad.astype(jnp.bfloat16), TN, preferred_element_type=jnp.float32
    )
    io_rows[128:256, :] = head_rows[0:128, :]
    io_rows[256:264, :] = jnp.concatenate(
        [column_sum(grad), head_rows[128:129, :], jnp.zeros((6, D), jnp.float32)], axis=0
    )
    io_rows[264:320, :] = jnp.zeros((56, D), jnp.float32)
    for k, out in enumerate((near_held, near_away, far_held, far_away)):
        group = pl.ds(pl.multiple_of(IO_ROWS * (device[1] ^ k), 16), IO_ROWS)
        out[...] = io_rows[group, :].astype(out.dtype)


def side_kernel(device, held, came, across, mod_rows, keep, away):
    total = total_own(held, came, across)
    side = device[0] & 1
    for block in range(8):
        piece = total[:, 128 * block : 128 * block + 128]

        @pl.when(side == block % 2)
        def _():
            keep[block // 2] = piece

        @pl.when(side != block % 2)
        def _():
            away[IO_ROWS * (block // 2) : IO_ROWS * (block // 2) + IO_ROWS, :] = piece.astype(
                jnp.bfloat16
            )

    away[4 * IO_ROWS :, :] = mod_rows[...]


def merge_kernel(
    device, held, came, out_held, out_came, io_held, io_came, mod_rows, own, io_own, *outs
):
    z = device[0] >> 1
    for bit in range(4):
        total = jnp.concatenate(
            [
                held[z ^ bit] + came[z ^ bit].astype(jnp.float32),
                out_held[z ^ bit] + out_came[z ^ bit].astype(jnp.float32),
            ],
            axis=0,
        )
        rows = pl.ds(pl.multiple_of(IO_ROWS * (z ^ bit), 16), IO_ROWS)
        io_total = io_held[z ^ bit] + io_came[rows, :].astype(jnp.float32)
        if bit == 0:
            own[...] = total
            io_own[...] = io_total
        else:
            out = outs[bit]
            out[0:ATTN_ROWS, :] = total.astype(jnp.bfloat16)
            out[ATTN_ROWS : ATTN_ROWS + IO_ROWS, :] = io_total.astype(jnp.bfloat16)
            base = ATTN_ROWS + IO_ROWS
            out[base : base + MOD_ROWS, :] = mod_rows[...]
            out[base + MOD_ROWS : base + 2 * MOD_ROWS, :] = io_came[4 * IO_ROWS :, :]
    outs[0][0:MOD_ROWS, :] = mod_rows[...]
    outs[0][MOD_ROWS : 2 * MOD_ROWS, :] = io_came[4 * IO_ROWS :, :]


def mod_grad_kernel(device, cond, *refs):
    parts = refs[:4]
    rows_out, vector, io_grad, square, rows = refs[4:]
    base = 8 * MOD_ROWS + 2 * IO_ROWS
    terms = []
    for index in range(4):
        owner = device[1] ^ index
        block = parts[index][0 : 8 * MOD_ROWS, :].astype(jnp.float32)
        for frame in range(8):
            for k in range(MOD_ROWS):
                at = MOD_ROWS * frame + k
                rows[owner, frame : frame + 1, 128 * k : 128 * k + 128] = block[at : at + 1, :]
        group = pl.ds(pl.multiple_of(IO_ROWS * owner, 16), IO_ROWS)
        high = parts[index][8 * MOD_ROWS : 8 * MOD_ROWS + IO_ROWS, :].astype(jnp.float32)
        rest = parts[index][8 * MOD_ROWS + IO_ROWS : base, :].astype(jnp.float32)
        io_grad[group, :] = high + rest
        terms.append(column_sum(parts[index][base : base + 16, :].astype(jnp.float32)))
    total = jnp.zeros((1, 1), jnp.float32)
    for index in range(6):
        cols = slice(D * index, D * index + D)
        low = rows[:, :, cols].reshape(32, D)
        rows_out[:, cols] = low.astype(jnp.bfloat16)
        part = lax.dot_general(
            cond[32:64, :], low.astype(jnp.bfloat16), TN, preferred_element_type=jnp.float32
        )
        total = total + jnp.sum(column_sum(part * part), axis=1, keepdims=True)
        own = pl.ds(pl.multiple_of(D * index + 128 * device[0], 128), 128)
        vector[index : index + 1, :] = column_sum(rows[:, :, own].reshape(32, 128))
    vector[6:8, :] = io_grad[256:258, :]
    mixed = vector[0:6, :]
    total = total + jnp.sum(column_sum(mixed * mixed), axis=1, keepdims=True)
    left = lax.broadcasted_iota(jnp.int32, (1, 128), 1) < 64
    square[...] = ((terms[0] + terms[1]) + (terms[2] + terms[3])) + jnp.where(left, total, 0.0)


def call_mod_grad(device, cond, parts):
    return pl.pallas_call(
        mod_grad_kernel,
        out_shape=(
            jax.ShapeDtypeStruct((32, 6 * D), jnp.bfloat16),
            jax.ShapeDtypeStruct((8, 128), jnp.float32),
            jax.ShapeDtypeStruct((4 * IO_ROWS, 128), jnp.float32),
            jax.ShapeDtypeStruct((1, 128), jnp.float32),
        ),
        in_specs=smem_specs(1) + vmem_specs(5),
        out_specs=vmem_specs(4),
        scratch_shapes=[pltpu.VMEM((4, 8, 6 * D), jnp.float32)],
        compiler_params=pltpu.CompilerParams(vmem_limit_bytes=12 * 2**20),
        cost_estimate=pl.CostEstimate(flops=10**8, bytes_accessed=4 * 10**6, transcendentals=0),
        name="mod_grad",
    )(device, cond, *parts)


def mlp_kernel(first, second, weights, held, away, active, slope):
    for frame, source in enumerate((first, second)):
        rows = slice(256 * frame, 256 * frame + 256)
        upward = jnp.dot(source[...], weights[0], preferred_element_type=jnp.float32)
        inner = 0.5 * (1.0 + lax.erf(upward * (1.0 / math.sqrt(2.0))))
        low = (upward * inner).astype(jnp.bfloat16)
        active[rows, :] = low
        change = inner + upward * jnp.exp(-0.5 * upward * upward) * (
            1.0 / math.sqrt(2.0 * math.pi)
        )
        slope[rows, :] = change.astype(jnp.bfloat16)
        part = lax.dot_general(low, weights[1], NT, preferred_element_type=jnp.float32)
        if frame:
            away[...] = part.astype(jnp.bfloat16)
        else:
            held[...] = part


def mlp_back_kernel(first, second, weights, slope, held, away, grad_up):
    for frame, source in enumerate((first, second)):
        rows = slice(256 * frame, 256 * frame + 256)
        grad = jnp.dot(source[...], weights[1], preferred_element_type=jnp.float32)
        low = (grad * slope[rows, :].astype(jnp.float32)).astype(jnp.bfloat16)
        grad_up[rows, :] = low
        part = lax.dot_general(low, weights[0], NT, preferred_element_type=jnp.float32)
        if frame:
            away[...] = part.astype(jnp.bfloat16)
        else:
            held[...] = part


def call_mlp(kernel, name, outs, *operands):
    return pl.pallas_call(
        kernel,
        out_shape=(frame_f32(), frame_low()) + outs,
        in_specs=vmem_specs(len(operands)),
        out_specs=vmem_specs(2 + len(outs)),
        compiler_params=pltpu.CompilerParams(vmem_limit_bytes=16 * 2**20),
        cost_estimate=pl.CostEstimate(
            flops=4 * 10**9, bytes_accessed=2 * 10**7, transcendentals=10**6
        ),
        name=name,
    )(*operands)


def weight_grad_kernel(*refs):
    hidden, grads = refs[:4], refs[4:8]
    grad_up, active = refs[8:10], refs[10:12]
    result, out, sems = refs[12:]
    width = active[0].shape[1]
    copies = []
    for index, (left, right) in enumerate(((hidden, grad_up), (grads, active))):
        total = jnp.zeros((D, width), jnp.float32)
        for frame in range(4):
            rows = slice(256 * (frame % 2), 256 * (frame % 2) + 256)
            total = total + lax.dot_general(
                left[frame][...],
                right[frame // 2][rows, :],
                TN,
                preferred_element_type=jnp.float32,
            )
        out[index] = total.astype(jnp.bfloat16)
        copies.append(
            pltpu.make_async_copy(
                out.at[index], result.at[:, width * index : width * index + width], sems.at[index]
            )
        )
        copies[index].start()
    for copy in copies:
        copy.wait()


def call_weight_grad(hidden, grads, grad_up, active):
    operands = (*hidden, *grads, *grad_up, *active)
    return pl.pallas_call(
        weight_grad_kernel,
        out_shape=jax.ShapeDtypeStruct((D, 2 * active[0].shape[1]), jnp.bfloat16),
        in_specs=vmem_specs(len(operands)),
        out_specs=hbm_specs(1)[0],
        scratch_shapes=[
            pltpu.VMEM((2, D, active[0].shape[1]), jnp.bfloat16),
            pltpu.SemaphoreType.DMA((2,)),
        ],
        compiler_params=pltpu.CompilerParams(vmem_limit_bytes=20 * 2**20),
        cost_estimate=pl.CostEstimate(flops=5 * 10**9, bytes_accessed=2 * 10**7, transcendentals=0),
        name="weight_grad",
    )(*operands)


def side_blocks(device, total, held, away):
    side = device[0] & 1
    for z in range(4):
        held[z] = total[:, pl.ds(pl.multiple_of(256 * z + 128 * side, 128), 128)]
        away[z] = total[:, pl.ds(pl.multiple_of(256 * z + 128 * (1 - side), 128), 128)].astype(
            jnp.bfloat16
        )


def head_grad_kernel(device, left, right, held, away, total):
    total[...] = jnp.dot(left[...], right[...], preferred_element_type=jnp.float32)
    side_blocks(device, total, held, away)


def call_head_grad(device, left, right):
    rows = left.shape[0]
    return pl.pallas_call(
        head_grad_kernel,
        out_shape=(
            jax.ShapeDtypeStruct((4, rows, 128), jnp.float32),
            jax.ShapeDtypeStruct((4, rows, 128), jnp.bfloat16),
        ),
        in_specs=smem_specs(1) + vmem_specs(2),
        out_specs=vmem_specs(2),
        scratch_shapes=[pltpu.VMEM((rows, D), jnp.float32)],
        compiler_params=pltpu.CompilerParams(vmem_limit_bytes=12 * 2**20),
        cost_estimate=pl.CostEstimate(flops=2 * 10**9, bytes_accessed=10**7, transcendentals=0),
        name="head_grad",
    )(device, left, right)


def qkv_back_kernel(meta, *refs):
    blocks, weights = refs[:4], refs[4]
    grads, near_held, near_away, far_held, far_away = refs[5:]
    for k in range(4):
        head = meta[0] ^ k
        for part in range(3):
            rows = pl.ds(pl.multiple_of(256 * part + 64 * head, 64), 64)
            grads[rows, :] = blocks[k][64 * part : 64 * part + 64, :]
    for frame, out in ((2, far_held), (3, far_away), (0, near_held), (1, near_away)):
        part = lax.dot_general(
            grads[:, 256 * frame : 256 * frame + 256],
            weights[0:QKV_ROWS, :],
            TN,
            preferred_element_type=jnp.float32,
        )
        out[...] = part.astype(out.dtype)


def call_qkv_back(meta, blocks, weights):
    return row_call(
        qkv_back_kernel,
        "qkv_back",
        (
            jax.ShapeDtypeStruct((QKV_ROWS, 4 * PATCHES), jnp.bfloat16),
            frame_f32(),
            frame_low(),
            frame_f32(),
            frame_low(),
        ),
        meta,
        *blocks,
        weights,
        smem=1,
    )


def adam_step(weight_now, first_mom, second_mom, grad, scale, rate, decay):
    factor, first_fix, second_fix = scale
    grad = grad * factor
    first_mom = beta_one * first_mom + (1.0 - beta_one) * grad
    second_mom = beta_two * second_mom + (1.0 - beta_two) * grad * grad
    updated = weight_now - rate * (
        first_mom * first_fix / (jnp.sqrt(second_mom * second_fix) + adam_eps) + decay * weight_now
    )
    return updated, first_mom, second_mom, updated.astype(jnp.bfloat16)


def preload_kernel(*refs):
    sources, targets, sems = refs[:3], refs[4:7], refs[7]
    copies = [
        pltpu.make_async_copy(sources[k], targets[k], sems.at[k]) for k in range(3)
    ]
    for copy in copies:
        copy.start()
    for copy in copies:
        copy.wait()


def call_preload(arrays, values):
    return pl.pallas_call(
        preload_kernel,
        out_shape=tuple(jax.ShapeDtypeStruct(a.shape, a.dtype) for a in arrays),
        in_specs=hbm_specs(3) + vmem_specs(1),
        out_specs=vmem_specs(3),
        scratch_shapes=[pltpu.SemaphoreType.DMA((3,))],
        compiler_params=pltpu.CompilerParams(vmem_limit_bytes=4 * 2**20),
        cost_estimate=pl.CostEstimate(flops=10**6, bytes_accessed=10**7, transcendentals=0),
        name="preload",
    )(*arrays, values)


def adam_kernel(*refs):
    fixes, sums = refs[0], refs[1:5]
    attn_grad, mlp_grad, cond, mod_rows = refs[5:9]
    io_in, vec_in = refs[9:13], refs[13:17]
    groups = [refs[17 + 3 * k : 20 + 3 * k] for k in range(3)]
    outs = [refs[26 + 4 * k : 30 + 4 * k] for k in range(3)]
    io_out, vec_out, norm_out = refs[38:43], refs[43:47], refs[47]
    held, slots, low_slots, in_sems, sems = refs[48:]
    depth = held.shape[0]
    tasks = []
    for k in (1, 0, 2):
        width = groups[k][0].shape[-1]
        for lead in range(groups[k][0].shape[0] if k < 2 else 1):
            for col in range(0, width, 1024):
                tasks.append((k, lead, col, min(1024, width - col)))

    def fetches(number):
        k, lead, col, span = tasks[number]
        cut = ((lead,) if k < 2 else ()) + (slice(None), slice(col, col + span))
        slot = number % depth
        if k == 2:
            return []
        return [
            pltpu.make_async_copy(
                groups[k][index].at[cut], held.at[slot, index, :, 0:span], in_sems.at[slot, index]
            )
            for index in range(3)
        ]

    for number in range(min(depth, len(tasks))):
        for copy in fetches(number):
            copy.start()
    total = (sums[0][...] + sums[1][...]) + (sums[2][...] + sums[3][...])
    norm = jnp.sqrt(total)
    norm_out[0:1, :] = norm
    norm_out[1:2, :] = total
    factor = jnp.minimum(1.0, clip_limit / (norm[:, 0:1] + 1e-06))
    scale = (factor, fixes[0], fixes[1])
    results = adam_step(*(ref[...] for ref in io_in), scale, rate_matrix, decay_rate)
    io_out[0][...] = results[0]
    io_out[1][...] = results[1]
    io_out[2][...] = results[2][0]
    io_out[3][...] = results[2][1]
    io_out[4][...] = results[3]
    results = adam_step(*(ref[...] for ref in vec_in), scale, rate_vector, 0.0)
    for out, result in zip(vec_out, results):
        out[...] = result
    running = {}
    for number, (k, lead, col, span) in enumerate(tasks):
        slot = number % depth
        for copy in fetches(number):
            copy.wait()
        for copy in running.pop(number - depth, ()):
            copy.wait()
        cut = ((lead,) if k < 2 else ()) + (slice(None), slice(col, col + span))
        if k == 0:
            grad = attn_grad[lead]
        elif k == 1:
            base = groups[1][0].shape[-1] * lead + col
            grad = mlp_grad[:, base : base + span].astype(jnp.float32)
        else:
            grad = lax.dot_general(
                cond[32:64, :],
                mod_rows[:, col : col + span],
                TN,
                preferred_element_type=jnp.float32,
            )
        if k == 2:
            values = [ref[:, col : col + span] for ref in groups[2]]
        else:
            values = [held[slot, index, :, 0:span] for index in range(3)]
        results = adam_step(*values, grad, scale, rate_matrix, decay_rate)
        copies = []
        for index, result in enumerate(results):
            source = low_slots.at[slot] if index == 3 else slots.at[slot, index]
            source = source.at[:, 0:span]
            source[...] = result
            copies.append(
                pltpu.make_async_copy(source, outs[k][index].at[cut], sems.at[slot, index])
            )
            copies[index].start()
        running[number] = copies
        if number + depth < len(tasks):
            for copy in fetches(number + depth):
                copy.start()
    for copies in running.values():
        for copy in copies:
            copy.wait()


def call_adam(fixes, sums, grads, io_group, vec_group, groups):
    held = [array for group in groups for array in group]
    inside = [*sums, *grads, *io_group, *vec_group]

    def results(group):
        low = jax.ShapeDtypeStruct(group[0].shape, jnp.bfloat16)
        return (jax.ShapeDtypeStruct(group[0].shape, jnp.float32),) * 3 + (low,)

    io_like = results(io_group)
    half = jax.ShapeDtypeStruct(io_group[0].shape[1:], jnp.float32)
    out_shape = sum((results(group) for group in groups), ())
    out_shape = out_shape + io_like[:2] + (half, half) + io_like[3:] + results(vec_group)
    out_shape = out_shape + (jax.ShapeDtypeStruct((2, 128), jnp.float32),)
    return pl.pallas_call(
        adam_kernel,
        out_shape=out_shape,
        in_specs=smem_specs(1) + vmem_specs(len(inside)) + hbm_specs(6) + vmem_specs(3),
        out_specs=hbm_specs(12) + vmem_specs(10),
        scratch_shapes=[
            pltpu.VMEM((6, 3, 128, 1024), jnp.float32),
            pltpu.VMEM((6, 3, 128, 1024), jnp.float32),
            pltpu.VMEM((6, 128, 1024), jnp.bfloat16),
            pltpu.SemaphoreType.DMA((6, 3)),
            pltpu.SemaphoreType.DMA((6, 4)),
        ],
        compiler_params=pltpu.CompilerParams(vmem_limit_bytes=28 * 2**20),
        cost_estimate=pl.CostEstimate(flops=10**7, bytes_accessed=2 * 10**7, transcendentals=0),
        name="adam",
    )(fixes, *inside, *held)


def square_kernel(scattered, square):
    rest = scattered[...].astype(jnp.float32)
    square[...] = jnp.broadcast_to(
        jnp.sum(column_sum(rest * rest), axis=1, keepdims=True), square.shape
    )


def finish_kernel(*refs):
    own, io_own, mod_own, pieces = refs[0], refs[1], refs[2], refs[3:6]
    rest, error, grad, spread = refs[6:]
    total = own[...]
    io_total = io_own[...]
    spread[0 : 2 * MOD_ROWS, :] = mod_own[...]
    for index, piece in enumerate(pieces):
        total = total + piece[0:ATTN_ROWS, :].astype(jnp.float32)
        base = ATTN_ROWS + IO_ROWS
        io_total = io_total + piece[ATTN_ROWS:base, :].astype(jnp.float32)
        spread[2 * MOD_ROWS * (index + 1) : 2 * MOD_ROWS * (index + 2), :] = piece[base:, :]
    high = io_total.astype(jnp.bfloat16)
    base = 8 * MOD_ROWS
    spread[base : base + IO_ROWS, :] = high
    base = base + IO_ROWS
    spread[base : base + IO_ROWS, :] = (io_total - high.astype(jnp.float32)).astype(jnp.bfloat16)
    for part in range(4):
        grad[part] = total[256 * part : 256 * part + 256].T
    squares = rest[:, 0:1]
    for values in (total, io_total):
        squares = squares + jnp.sum(column_sum(values * values), axis=1, keepdims=True)
    left = lax.broadcasted_iota(jnp.int32, (1, 128), 1) < 64
    value = jnp.where(left, squares, error[...])
    terms = []
    for _ in range(3):
        terms.append(value.astype(jnp.bfloat16).astype(jnp.float32))
        value = value - terms[-1]
    spread[base + IO_ROWS :, :] = jnp.concatenate(
        terms + [jnp.zeros((13, 128), jnp.float32)], axis=0
    ).astype(jnp.bfloat16)


def turn(block):
    return block.astype(jnp.float32).T.astype(jnp.bfloat16)


def query_rows(meta, pair):
    first = 2 * pair
    start_first = first - meta[2 + first]
    start_second = first + 1 - meta[3 + first]
    left = lax.broadcasted_iota(jnp.int32, (1, 2 * PATCHES), 1) < PATCHES
    upto = jnp.where(left, first, first + 1)
    since = jnp.where(left, start_first, start_second)
    return jnp.minimum(start_first, start_second), since, upto


def attend_kernel(meta, *refs):
    blocks = refs[:4]
    outs = refs[4:8]
    lse, mixed, query, key, value, scores = refs[8:]
    for member in range(4):
        for frame in range(4):
            slot = 4 * (meta[0] ^ member) + (meta[1] ^ frame)
            cols = slice(256 * frame, 256 * frame + 256)
            lanes = pl.ds(pl.multiple_of((slot % 2) * 256, 256), 256)
            query[slot // 2, :, lanes] = blocks[member][0:64, cols] * 0.125
            key[slot // 2, lanes, :] = turn(blocks[member][64:128, cols])
            value[slot // 2, :, lanes] = blocks[member][128:192, cols]

    def per_pair(pair, carry):
        low, since, upto = query_rows(meta, pair)
        wanted = query[pair]

        def first_pass(keys, top):
            both = jnp.dot(key[keys], wanted, preferred_element_type=jnp.float32)
            for side in range(2):
                slot = 2 * keys + side
                bias = jnp.where((slot >= since) & (slot <= upto), 0.0, neg_large)
                part = both[256 * side : 256 * side + 256] + bias
                scores[keys, 256 * side : 256 * side + 256, :] = part
                top = jnp.maximum(top, jnp.max(part.reshape(32, 8, 2 * PATCHES), axis=0))
            return top

        tops = lax.fori_loop(
            low // 2, pair + 1, first_pass, jnp.full((8, 2 * PATCHES), neg_large, jnp.float32)
        )
        top = jnp.max(tops, axis=0, keepdims=True)

        def second_pass(keys, state):
            total, acc = state
            probs = jnp.exp(scores[keys] - top)
            total = total + jnp.sum(probs.reshape(64, 8, 2 * PATCHES), axis=0)
            acc = acc + jnp.dot(
                value[keys], probs.astype(jnp.bfloat16), preferred_element_type=jnp.float32
            )
            return (total, acc)

        totals, acc = lax.fori_loop(
            low // 2,
            pair + 1,
            second_pass,
            (
                jnp.zeros((8, 2 * PATCHES), jnp.float32),
                jnp.zeros((HD, 2 * PATCHES), jnp.float32),
            ),
        )
        total = jnp.sum(totals, axis=0, keepdims=True)
        lse[pair] = top + jnp.log(total)
        mixed[pair] = acc / total
        return carry

    lax.fori_loop(0, 8, per_pair, 0)
    for member in range(4):
        for frame in range(4):
            slot = 4 * (meta[0] ^ member) + (meta[1] ^ frame)
            lanes = pl.ds(pl.multiple_of((slot % 2) * 256, 256), 256)
            outs[member][:, 256 * frame : 256 * frame + 256] = mixed[slot // 2, :, lanes].astype(
                jnp.bfloat16
            )


def call_attend(meta, blocks):
    vmem = pl.BlockSpec()
    result = pl.pallas_call(
        attend_kernel,
        out_shape=tuple(jax.ShapeDtypeStruct((HD, 4 * PATCHES), jnp.bfloat16) for _ in range(4))
        + (
            jax.ShapeDtypeStruct((8, 1, 2 * PATCHES), jnp.float32),
            jax.ShapeDtypeStruct((8, HD, 2 * PATCHES), jnp.float32),
        ),
        in_specs=[pl.BlockSpec(memory_space=pltpu.SMEM)] + [vmem] * 4,
        out_specs=(vmem,) * 6,
        scratch_shapes=[
            pltpu.VMEM((8, HD, 2 * PATCHES), jnp.bfloat16),
            pltpu.VMEM((8, 2 * PATCHES, HD), jnp.bfloat16),
            pltpu.VMEM((8, HD, 2 * PATCHES), jnp.bfloat16),
            pltpu.VMEM((8, 2 * PATCHES, 2 * PATCHES), jnp.float32),
        ],
        compiler_params=pltpu.CompilerParams(vmem_limit_bytes=48 * 2**20),
        cost_estimate=pl.CostEstimate(flops=9 * 10**9, bytes_accessed=5 * 10**6, transcendentals=10**7),
        name="attend",
    )(meta, *blocks)
    return list(result[:4]), result[4], result[5]


def attend_back_kernel(meta, *refs):
    blocks = refs[:4]
    grads = refs[4:8]
    lse, mixed, cosine, sine = refs[8:12]
    outs = refs[12:16]
    query, key, key_flat, value_flat, grad, sum_key, sum_value, sum_query = refs[16:]
    for member in range(4):
        for frame in range(4):
            slot = 4 * (meta[0] ^ member) + (meta[1] ^ frame)
            cols = slice(256 * frame, 256 * frame + 256)
            place = pl.ds(pl.multiple_of((slot % 2) * 256, 256), 256)
            part = blocks[member][0:64, cols] * 0.125
            query[slot // 2, :, place] = part
            part = blocks[member][64:128, cols]
            key[slot // 2, :, place] = part
            key_flat[slot // 2, place, :] = turn(part)
            value_flat[slot // 2, place, :] = turn(blocks[member][128:192, cols])
            part = grads[member][:, cols]
            grad[slot // 2, :, place] = part
    sum_key[...] = jnp.zeros_like(sum_key)
    sum_value[...] = jnp.zeros_like(sum_value)

    def per_pair(pair, carry):
        low, since, upto = query_rows(meta, pair)
        wanted = query[pair]
        wanted_grad = grad[pair]
        delta = jnp.sum(wanted_grad.astype(jnp.float32) * mixed[pair], axis=0, keepdims=True)
        level = lse[pair]

        def per_keys(keys, acc):
            scores = jnp.dot(key_flat[keys], wanted, preferred_element_type=jnp.float32)
            grad_probs = jnp.dot(
                value_flat[keys], wanted_grad, preferred_element_type=jnp.float32
            )
            low_probs, low_scores = [], []
            for side in range(2):
                rows = slice(256 * side, 256 * side + 256)
                slot = 2 * keys + side
                bias = jnp.where((slot >= since) & (slot <= upto), -level, neg_large)
                probs = jnp.exp(scores[rows] + bias)
                low_probs.append(probs.astype(jnp.bfloat16))
                low_scores.append((probs * (grad_probs[rows] - delta)).astype(jnp.bfloat16))
            all_probs = jnp.concatenate(low_probs, axis=0)
            all_scores = jnp.concatenate(low_scores, axis=0)
            sum_value[keys] += lax.dot_general(
                wanted_grad, all_probs, NT, preferred_element_type=jnp.float32
            )
            sum_key[keys] += lax.dot_general(
                wanted, all_scores, NT, preferred_element_type=jnp.float32
            )
            return acc + jnp.dot(key[keys], all_scores, preferred_element_type=jnp.float32)

        sum_query[pair] = lax.fori_loop(
            low // 2, pair + 1, per_keys, jnp.zeros((HD, 2 * PATCHES), jnp.float32)
        )
        return carry

    lax.fori_loop(0, 8, per_pair, 0)
    for member in range(4):
        for frame in range(4):
            slot = 4 * (meta[0] ^ member) + (meta[1] ^ frame)
            cols = slice(256 * frame, 256 * frame + 256)
            place = pl.ds(pl.multiple_of((slot % 2) * 256, 256), 256)
            cos_now = cosine[slot]
            sin_now = sine[slot]
            for base, part in (
                (0, sum_query[slot // 2, :, place] * 0.125),
                (64, sum_key[slot // 2, :, place]),
            ):
                upper = part[0:32]
                lower = part[32:64]
                outs[member][base : base + 32, cols] = (
                    upper * cos_now + lower * sin_now
                ).astype(jnp.bfloat16)
                outs[member][base + 32 : base + 64, cols] = (
                    lower * cos_now - upper * sin_now
                ).astype(jnp.bfloat16)
            outs[member][128:192, cols] = sum_value[slot // 2, :, place].astype(jnp.bfloat16)


def call_attend_back(meta, blocks, grads, lse, mixed, cosine, sine):
    vmem = pl.BlockSpec()
    flat_pair = pltpu.VMEM((8, 2 * PATCHES, HD), jnp.bfloat16)
    turned_pair = pltpu.VMEM((8, HD, 2 * PATCHES), jnp.bfloat16)
    wide = pltpu.VMEM((8, HD, 2 * PATCHES), jnp.float32)
    return list(
        pl.pallas_call(
            attend_back_kernel,
            out_shape=tuple(
                jax.ShapeDtypeStruct((192, 4 * PATCHES), jnp.bfloat16) for _ in range(4)
            ),
            in_specs=[pl.BlockSpec(memory_space=pltpu.SMEM)] + [vmem] * 12,
            out_specs=(vmem,) * 4,
            scratch_shapes=[
                turned_pair,
                turned_pair,
                flat_pair,
                flat_pair,
                turned_pair,
                wide,
                wide,
                pltpu.VMEM((8, HD, 2 * PATCHES), jnp.float32),
            ],
            compiler_params=pltpu.CompilerParams(vmem_limit_bytes=48 * 2**20),
            cost_estimate=pl.CostEstimate(
                flops=30 * 10**9, bytes_accessed=10**7, transcendentals=10**7
            ),
            name="attend_back",
        )(meta, *blocks, *grads, lse, mixed, cosine, sine)
    )


def shards_halves(
    clean,
    noise,
    levels,
    lengths,
    order,
    step,
    w_attn,
    m_attn,
    v_attn,
    w_mlp,
    m_mlp,
    v_mlp,
    w_mod,
    m_mod,
    v_mod,
    w_io,
    m_io,
    v_io,
    vectors,
    m_vec,
    v_vec,
):
    bfloat = jnp.bfloat16
    single = jnp.float32
    ctx_index = lax.axis_index("ctx")
    tp_index = lax.axis_index("tp")
    member = ctx_index % 4
    device = jnp.stack([ctx_index, tp_index]).astype(jnp.int32)

    front_shard = call_prepare(w_attn, w_io, vectors)
    token_shard = call_tokens(after(device, front_shard), clean, noise)
    pieces = gather_swaps(token_shard)
    front_pieces = lax.all_gather(front_shard, "ctx", axis=0)
    front_meta, attend_meta, row_levels = call_place(
        after(device, pieces[1]), lengths, order, levels
    )

    count = step[0].astype(single)
    fixes = jnp.stack([1.0 / (1.0 - beta_one**count), 1.0 / (1.0 - beta_two**count)])

    half_dim = D // 2
    column = ctx_index * 128 + jnp.arange(128, dtype=jnp.int32)
    frequency = jnp.exp(-math.log(10000.0) * (column % half_dim).astype(single) / half_dim)
    angle = row_levels.astype(single)[:, None] * frequency[None, :]
    cond = jax.nn.silu(jnp.where(column[None, :] < half_dim, jnp.cos(angle), jnp.sin(angle)))
    cond_low = cond.astype(bfloat)
    cond_slots = cond_low[:32]
    quarter_cols = 6 * D // 4
    mod_cols = lax.dynamic_slice_in_dim(w_mod, tp_index * quarter_cols, quarter_cols, 1)
    mod_part = jnp.dot(cond_slots, mod_cols.astype(bfloat), preferred_element_type=single)
    mod_held = reduce_along_x(mod_part.reshape(8, 4, quarter_cols), ctx_index, single)
    mod_own = reduce_along_z(mod_held, ctx_index, single)
    mod_quarters = reorder_four(spread_frames(mod_own), tp_index)
    mod_all = jnp.concatenate(mod_quarters, axis=1)
    mod_rel = jnp.stack(reorder_four([mod_all[k] for k in range(4)], tp_index))
    mod_rel = mod_rel.reshape(4, 6, D)

    time_pairs = HD // 8
    side_pairs = (HD // 2 - time_pairs) // 2

    def frequencies(count):
        return 10000.0 ** (-jnp.arange(count, dtype=single) / count)

    patch = jnp.arange(PATCHES, dtype=jnp.int32)
    half_position = attend_meta[2:].astype(single)
    time_angle = half_position[:, None] * frequencies(time_pairs)[None, :]
    height_angle = frequencies(side_pairs)[:, None] * (patch // GRID).astype(single)[None, :]
    width_angle = frequencies(side_pairs)[:, None] * (patch % GRID).astype(single)[None, :]
    side_angle = jnp.concatenate([height_angle, width_angle], axis=0)

    def full_table(time_part, side_part):
        return jnp.concatenate(
            [
                jnp.broadcast_to(time_part[:, :, None], (HALF_SLOTS, time_pairs, PATCHES)),
                jnp.broadcast_to(side_part[None], (HALF_SLOTS, 2 * side_pairs, PATCHES)),
            ],
            axis=1,
        )

    cosine = full_table(jnp.cos(time_angle), jnp.cos(side_angle))
    sine = full_table(jnp.sin(time_angle), jnp.sin(side_angle))
    signal_scale, noise_scale, weight = plan(row_levels)
    weight_sum = PATCHES * jnp.sum(weight[:32])
    token_scales = jnp.concatenate([signal_scale[64:68], noise_scale[64:68]])
    loss_scales = jnp.stack([weight[64], 2.0 / clean.shape[1] * weight[64] / weight_sum])

    front_meta = after(front_meta, mod_rel, cosine, sine, token_scales, loss_scales, fixes)
    quarters = spread_frames(call_pick(front_meta, pieces))
    front_all, mid_all, hidden_frames, resid_in, *head_blocks, noisy_low, target, mod_own = (
        call_front(front_meta, token_scales, front_pieces, quarters, mod_rel, cosine, sine)
    )
    hidden_one = hidden_frames.reshape(4 * PATCHES, D)

    out_w = mid_all[:, :256]

    def exchange(blocks):
        return [blocks[0]] + [swap(blocks[k], "ctx", k) for k in (1, 2, 3)]

    head_in = exchange(head_blocks)
    mlp_shard = after(w_mlp.astype(bfloat), head_in[1], head_in[2])
    mlp_w = lax.all_gather(mlp_shard, "ctx", axis=1, tiled=True)
    mixed_blocks, lse, mixed = call_attend(attend_meta, head_in)
    mix_low = jnp.concatenate(reorder_four(exchange(mixed_blocks), member), axis=0)

    def project(left, right, dims):
        pairs = []
        for base in (2 * PATCHES, 0):
            part = lax.dot_general(
                left[:, base : base + 2 * PATCHES], right, dims, preferred_element_type=single
            )
            pairs.append((part[:PATCHES], part[PATCHES:].astype(bfloat)))
        return pairs[1], pairs[0]

    near, far = project(mix_low, out_w, (((0,), (1,)), ((), ())))
    attn_out, resid_mid, hidden_own = row_call(
        middle_kernel,
        "middle",
        (frame_f32(), frame_f32(), frame_low()),
        *sum_frames(near, sum_across(far)),
        resid_in,
        mod_own,
    )
    hidden_list = spread_frames(hidden_own)
    wide = (2 * PATCHES, w_mlp.shape[2])
    wide_low = jax.ShapeDtypeStruct(wide, bfloat)
    far = call_mlp(mlp_kernel, "mlp", (wide_low, wide_low), *hidden_list[2:], mlp_w)
    across = sum_across(far)
    near = call_mlp(
        mlp_kernel,
        "mlp",
        (wide_low, wide_low),
        after(hidden_list[0], across),
        hidden_list[1],
        mlp_w,
    )
    active, slope = (near[2], far[2]), (near[3], far[3])
    grad_own, grad_three, head_rows, grad_gate_two, error_part = row_call(
        loss_kernel,
        "loss",
        (
            frame_low(),
            frame_f32(),
            jax.ShapeDtypeStruct((136, D), single),
            jax.ShapeDtypeStruct((1, D), single),
            jax.ShapeDtypeStruct((1, 128), single),
        ),
        loss_scales,
        *sum_frames(near[:2], across),
        resid_mid,
        mod_own,
        mid_all,
        target,
        smem=1,
    )
    grad_list = [grad_own, swap(grad_own, "tp", 1)]
    near = call_mlp(mlp_back_kernel, "mlp_back", (wide_low,), *grad_list, mlp_w, slope[0])
    grad_across = after(swap(grad_own, "tp", 2), near[0])
    grad_list += [grad_across, swap(grad_across, "tp", 1)]
    far = call_mlp(
        mlp_back_kernel,
        "mlp_back",
        (wide_low,),
        *grad_list[2:],
        mlp_w,
        slope[1],
    )
    across = sum_across(far)
    weight_grad = call_weight_grad(
        hidden_list, grad_list, (near[2], after(far[2], across)), active
    )
    grad_low, grad_mid, rows_two = row_call(
        second_kernel,
        "second",
        (frame_low(), frame_f32(), jax.ShapeDtypeStruct((3, D), single)),
        *sum_frames(near[:2], across),
        after(resid_mid, weight_grad),
        mod_own,
        grad_three,
        attn_out,
    )
    back_list = spread_frames(grad_low)
    grad_attn_low = jnp.concatenate(back_list, axis=0)
    grad_mix = lax.dot_general(
        out_w, grad_attn_low, (((0,), (1,)), ((), ())), preferred_element_type=single
    ).astype(bfloat)
    grad_blocks = reorder_four([grad_mix[HD * k : HD * k + HD] for k in range(4)], member)
    grad_in_blocks = exchange(grad_blocks)
    out_held, out_away = call_head_grad(device, mix_low, after(grad_attn_low, grad_mix))
    out_came = swap(out_away, "ctx", 1)
    grad_in_blocks[0] = after(grad_in_blocks[0], out_held)
    scattered = lax.psum_scatter(
        after(weight_grad, grad_low), "ctx", scatter_dimension=0, tiled=True
    )
    back_blocks = call_attend_back(attend_meta, head_in, grad_in_blocks, lse, mixed, cosine, sine)
    grad_qkv, *parts = call_qkv_back(attend_meta, exchange(back_blocks), front_all)
    near, far = parts[:2], parts[2:]
    across = sum_across(far)
    first_terms = sum_frames(near, across)
    qkv_held, qkv_away = call_head_grad(device, after(grad_qkv, across), hidden_one)
    qkv_came = swap(qkv_away, "ctx", 1)
    group_f32 = jax.ShapeDtypeStruct((IO_ROWS, D), single)
    group_low = jax.ShapeDtypeStruct((IO_ROWS, D), bfloat)
    mod_rows, *io_parts, _ = row_call(
        first_kernel,
        "first",
        (
            jax.ShapeDtypeStruct((MOD_ROWS, 128), bfloat),
            group_f32,
            group_low,
            group_f32,
            group_low,
            jax.ShapeDtypeStruct((4 * IO_ROWS, D), single),
        ),
        device,
        *first_terms,
        after(resid_in, qkv_held),
        mod_own,
        grad_mid,
        noisy_low,
        rows_two,
        grad_gate_two,
        head_rows,
        smem=1,
    )
    io_held, io_away = row_call(
        side_kernel,
        "side",
        (
            jax.ShapeDtypeStruct((4, IO_ROWS, 128), single),
            jax.ShapeDtypeStruct((4 * IO_ROWS + MOD_ROWS, 128), bfloat),
        ),
        device,
        *sum_frames(io_parts[:2], sum_across(io_parts[2:])),
        mod_rows,
        smem=1,
    )
    z_rows = jax.ShapeDtypeStruct((ATTN_ROWS + IO_ROWS + 2 * MOD_ROWS, 128), bfloat)
    qkv_own, io_own, *z_pieces = row_call(
        merge_kernel,
        "merge",
        (
            jax.ShapeDtypeStruct((ATTN_ROWS, 128), single),
            jax.ShapeDtypeStruct((IO_ROWS, 128), single),
            jax.ShapeDtypeStruct((2 * MOD_ROWS, 128), bfloat),
            z_rows,
            z_rows,
            z_rows,
        ),
        device,
        qkv_held,
        qkv_came,
        out_held,
        out_came,
        io_held,
        swap(io_away, "ctx", 1),
        mod_rows,
        smem=1,
    )
    red_attn, spread = row_call(
        finish_kernel,
        "finish",
        (
            jax.ShapeDtypeStruct((4, 128, 256), single),
            jax.ShapeDtypeStruct((8 * MOD_ROWS + 2 * IO_ROWS + 16, 128), bfloat),
        ),
        qkv_own,
        io_own,
        z_pieces[0],
        *(swap(piece, "ctx", 2 * bit) for bit, piece in zip((1, 2, 3), z_pieces[1:])),
        row_call(square_kernel, "square", (jax.ShapeDtypeStruct((1, 128), single),), scattered)[0],
        error_part,
    )
    all_rows, red_vec, io_grad, square = call_mod_grad(device, cond_low, spread_frames(spread))
    terms = sum_terms(square)
    loaded = call_preload((w_mod, m_mod, v_mod), terms[0])
    updated = call_adam(
        fixes,
        terms,
        (red_attn, scattered, cond_low, all_rows),
        (w_io, m_io, v_io, io_grad[: 2 * 128].reshape(2, 128, 128)),
        (vectors, m_vec, v_vec, red_vec),
        ((w_attn, m_attn, v_attn), (w_mlp, m_mlp, v_mlp), loaded),
    )
    return (updated[21][1, 64] / weight_sum, updated[21][0, 0], *updated[:21])


def solution(mesh):
    halves = mesh.shape["ctx"] == 8 and mesh.shape["tp"] == 4
    placed = (
        P("ctx", None),
        P("ctx", None),
        P(),
        P(),
        P(),
        P(),
        P(None, "ctx", "tp"),
        P(None, "ctx", "tp"),
        P(None, "ctx", "tp"),
        P(None, "ctx", "tp"),
        P(None, "ctx", "tp"),
        P(None, "ctx", "tp"),
        P("ctx", None),
        P("ctx", None),
        P("ctx", None),
        P(None, None, "ctx"),
        P(None, None, "ctx"),
        P(None, None, "ctx"),
        P(None, "ctx"),
        P(None, "ctx"),
        P(None, "ctx"),
    )
    return jax.shard_map(
        shards_halves if halves else shards,
        mesh=mesh,
        in_specs=placed,
        out_specs=(
            P(),
            P(),
            P(None, "ctx", "tp"),
            P(None, "ctx", "tp"),
            P(None, "ctx", "tp"),
            P(None, "ctx", "tp"),
            P(None, "ctx", "tp"),
            P(None, "ctx", "tp"),
            P(None, "ctx", "tp"),
            P(None, "ctx", "tp"),
            P("ctx", None),
            P("ctx", None),
            P("ctx", None),
            P("ctx", None),
            P(None, None, "ctx"),
            P(None, None, "ctx"),
            P(None, "ctx"),
            P(None, "ctx"),
            P(None, None, "ctx"),
            P(None, "ctx"),
            P(None, "ctx"),
            P(None, "ctx"),
            P(None, "ctx"),
        ),
        check_vma=False,
    )
```

```python
import functools
import math

import jax
import jax.numpy as jnp
from jax import lax
from jax.experimental import pallas as pl
from jax.experimental.pallas import tpu as pltpu
from jax.sharding import PartitionSpec as P

D = 1024
HD = 64
GRID = 16
PATCHES = 256
LEVELS = 1000


ln_eps = 1e-06
snr_limit = 5.0
clip_limit = 0.001
beta_one = 0.9
beta_two = 0.999
adam_eps = 1e-08
rate_matrix = 0.05
rate_vector = 0.3
decay_rate = 0.1
neg_large = -1e30


def clip_starts(frame_ids, lengths):
    clip_ends = jnp.cumsum(lengths)
    before = (clip_ends[None, :] <= frame_ids[:, None]).astype(jnp.int32)
    return jnp.sum(before * lengths[None, :], axis=1)


def plan(levels):
    fraction = (levels.astype(jnp.float32) + 1.0) / (LEVELS + 1.0)
    signal_scale = jnp.cos(0.5 * math.pi * fraction)
    noise_scale = jnp.sin(0.5 * math.pi * fraction)
    snr_value = signal_scale * signal_scale / (noise_scale * noise_scale)
    weight = jnp.minimum(snr_value, snr_limit) / (snr_value + 1.0)
    return (signal_scale, noise_scale, weight)


def condition(levels, width):
    half_dim = width // 2
    frequency = jnp.exp(-math.log(10000.0) * jnp.arange(half_dim, dtype=jnp.float32) / half_dim)
    angle_tab = levels.astype(jnp.float32)[:, None] * frequency[None, :]
    return jax.nn.silu(jnp.concatenate([jnp.cos(angle_tab), jnp.sin(angle_tab)], axis=1))


def rope_tables(time_pos, height_pos, width_pos, head_dim):
    pair_count = head_dim // 2
    time_pairs = head_dim // 8
    height_pairs = (pair_count - time_pairs) // 2
    width_pairs = pair_count - time_pairs - height_pairs

    def angles(position, count):
        frequency = 10000.0 ** (-jnp.arange(count, dtype=jnp.float32) / count)
        return position.astype(jnp.float32)[:, None] * frequency[None, :]

    angle_tab = jnp.concatenate(
        [
            angles(time_pos, time_pairs),
            angles(height_pos, height_pairs),
            angles(width_pos, width_pairs),
        ],
        axis=1,
    )
    return (jnp.cos(angle_tab), jnp.sin(angle_tab))


def rotate(values, cosine, sine):
    half_dim = values.shape[-1] // 2
    first_half = values[..., :half_dim]
    second_half = values[..., half_dim:]
    cosine = cosine[:, None, :]
    sine = sine[:, None, :]
    return jnp.concatenate(
        [first_half * cosine - second_half * sine, second_half * cosine + first_half * sine],
        axis=-1,
    )


def rotate_back(grads, cosine, sine):
    half_dim = grads.shape[-1] // 2
    first_half = grads[..., :half_dim]
    second_half = grads[..., half_dim:]
    cosine = cosine[:, None, :]
    sine = sine[:, None, :]
    return jnp.concatenate(
        [first_half * cosine + second_half * sine, second_half * cosine - first_half * sine],
        axis=-1,
    )


def layer_norm(values):
    centred = values - jnp.mean(values, axis=-1, keepdims=True)
    inv_std = lax.rsqrt(jnp.mean(centred * centred, axis=-1, keepdims=True) + ln_eps)
    return (centred * inv_std, inv_std)


def norm_back(grad_in, normed, inv_std):
    mean_grad = jnp.mean(grad_in, axis=-1, keepdims=True)
    mean_proj = jnp.mean(grad_in * normed, axis=-1, keepdims=True)
    return inv_std * (grad_in - mean_grad - normed * mean_proj)


def gelu_slope(values):
    return 0.5 * (1.0 + lax.erf(values / math.sqrt(2.0))) + values * jnp.exp(
        -0.5 * values * values
    ) / math.sqrt(2.0 * math.pi)


def stretch_mask(query_stretch, key_stretch, stretch_frames, lengths):
    offsets = jnp.arange(stretch_frames, dtype=jnp.int32)
    query_frames = query_stretch * stretch_frames + offsets
    key_frames = key_stretch * stretch_frames + offsets
    starts = clip_starts(query_frames, lengths)
    return (key_frames[None, :] <= query_frames[:, None]) & (key_frames[None, :] >= starts[:, None])


def expand_mask(allowed):
    return jnp.repeat(jnp.repeat(allowed, PATCHES, axis=0), PATCHES, axis=1)


def online_step(current, query_block, key_block, value_block, keep, scale):
    run_max, run_sum, run_acc = current
    scores = (
        jnp.einsum("qhe,khe->hqk", query_block, key_block, preferred_element_type=jnp.float32)
        * scale
    )
    scores = jnp.where(keep[None], scores, neg_large)
    new_max = jnp.maximum(run_max, jnp.max(scores, axis=-1))
    probs = jnp.where(keep[None], jnp.exp(scores - new_max[..., None]), 0.0)
    shrink = jnp.exp(run_max - new_max)
    run_sum = run_sum * shrink + jnp.sum(probs, axis=-1)
    added = jnp.einsum(
        "hqk,khe->qhe", probs.astype(jnp.bfloat16), value_block, preferred_element_type=jnp.float32
    )
    run_acc = run_acc * jnp.transpose(shrink)[:, :, None] + added
    return (new_max, run_sum, run_acc)


def pair_grads(
    query_block, grad_block, lse_block, delta_block, key_block, value_block, keep, scale
):
    scores = (
        jnp.einsum("qhe,khe->hqk", query_block, key_block, preferred_element_type=jnp.float32)
        * scale
    )
    probs = jnp.where(keep[None], jnp.exp(scores - lse_block[..., None]), 0.0)
    grad_probs = jnp.einsum(
        "qhe,khe->hqk", grad_block, value_block, preferred_element_type=jnp.float32
    )
    grad_scores = (probs * (grad_probs - delta_block[..., None])).astype(jnp.bfloat16)
    grad_query = (
        jnp.einsum("hqk,khe->qhe", grad_scores, key_block, preferred_element_type=jnp.float32)
        * scale
    )
    grad_key = (
        jnp.einsum("hqk,qhe->khe", grad_scores, query_block, preferred_element_type=jnp.float32)
        * scale
    )
    grad_value = jnp.einsum(
        "hqk,qhe->khe", probs.astype(jnp.bfloat16), grad_block, preferred_element_type=jnp.float32
    )
    return (grad_query, grad_key, grad_value)


def adam(weight_now, first_mom, second_mom, grad, factor, count, rate, decay):
    grad = grad * factor
    first_mom = beta_one * first_mom + (1.0 - beta_one) * grad
    second_mom = beta_two * second_mom + (1.0 - beta_two) * grad * grad
    first_hat = first_mom / (1.0 - beta_one**count)
    second_hat = second_mom / (1.0 - beta_two**count)
    updated = weight_now - rate * (
        first_hat / (jnp.sqrt(second_hat) + adam_eps) + decay * weight_now
    )
    return (updated, first_mom, second_mom, updated.astype(jnp.bfloat16))


def shards(
    clean,
    noise,
    levels,
    lengths,
    order,
    step,
    w_attn,
    m_attn,
    v_attn,
    w_mlp,
    m_mlp,
    v_mlp,
    w_mod,
    m_mod,
    v_mod,
    w_io,
    m_io,
    v_io,
    vectors,
    m_vec,
    v_vec,
):
    ctx_count = lax.axis_size("ctx")
    ctx_index = lax.axis_index("ctx")
    tp_index = lax.axis_index("tp")
    tok_rows = clean.shape[0]
    feat_dim = clean.shape[1]
    frames_dev = tok_rows // PATCHES
    stretch_frames = frames_dev // 2
    stretch_rows = stretch_frames * PATCHES
    scale = HD ** (-0.5)
    bfloat = jnp.bfloat16
    single = jnp.float32
    attn_w, mlp_w, mod_w, io_w, vec_low = (
        lax.all_gather(w_attn.astype(bfloat), "ctx", axis=1, tiled=True),
        lax.all_gather(w_mlp.astype(bfloat), "ctx", axis=1, tiled=True),
        lax.all_gather(w_mod.astype(bfloat), "ctx", axis=0, tiled=True),
        lax.all_gather(w_io.astype(bfloat), "ctx", axis=2, tiled=True),
        lax.all_gather(vectors.astype(bfloat), "ctx", axis=1, tiled=True),
    )
    vec_w = vec_low.astype(single)
    local_width = attn_w.shape[2]
    heads_dev = local_width // HD
    frame_count = levels.shape[0]
    local_stretches = lax.dynamic_slice_in_dim(order, 2 * ctx_index, 2, 0)
    frame_ids = (
        local_stretches[:, None] * stretch_frames
        + jnp.arange(stretch_frames, dtype=jnp.int32)[None, :]
    ).reshape(frames_dev)
    table_hit = frame_ids[:, None] == jnp.arange(frame_count, dtype=jnp.int32)[None, :]
    frame_levels = jnp.sum(jnp.where(table_hit, levels[None, :], 0), axis=1)
    starts = clip_starts(frame_ids, lengths)
    signal_scale, noise_scale, weight = plan(frame_levels)
    signal_col = signal_scale[:, None, None]
    noise_col = noise_scale[:, None, None]
    clean_full = clean.astype(single).reshape(frames_dev, PATCHES, feat_dim)
    noise_full = noise.astype(single).reshape(frames_dev, PATCHES, feat_dim)
    noisy = signal_col * clean_full + noise_col * noise_full
    target = signal_col * noise_full - noise_col * clean_full
    noisy_low = noisy.reshape(tok_rows, feat_dim).astype(bfloat)
    embedded = jnp.dot(noisy_low, io_w[0], preferred_element_type=single) + vec_w[6]
    cond_low = condition(frame_levels, D).astype(bfloat)
    modulate = (
        jnp.dot(cond_low, mod_w, preferred_element_type=single) + vec_w[:6].reshape(6 * D)
    ).reshape(frames_dev, 6, 1, D)
    patch_ids = jnp.arange(PATCHES, dtype=jnp.int32)
    time_pos = jnp.repeat(frame_ids - starts, PATCHES)
    height_pos = jnp.tile(patch_ids // GRID, frames_dev)
    width_pos = jnp.tile(patch_ids % GRID, frames_dev)
    cosine, sine = rope_tables(time_pos, height_pos, width_pos, HD)
    resid_in = embedded.reshape(frames_dev, PATCHES, D)
    normed_one, inv_one = layer_norm(resid_in)
    hidden_one = (
        (normed_one * (1.0 + modulate[:, 1]) + modulate[:, 0]).reshape(tok_rows, D).astype(bfloat)
    )
    query_pre = jnp.dot(hidden_one, attn_w[0], preferred_element_type=single).reshape(
        tok_rows, heads_dev, HD
    )
    key_pre = jnp.dot(hidden_one, attn_w[1], preferred_element_type=single).reshape(
        tok_rows, heads_dev, HD
    )
    query_low = rotate(query_pre, cosine, sine).astype(bfloat)
    key_low = rotate(key_pre, cosine, sine).astype(bfloat)
    value_low = (
        jnp.dot(hidden_one, attn_w[2], preferred_element_type=single)
        .astype(bfloat)
        .reshape(tok_rows, heads_dev, HD)
    )
    query_stretches = query_low.reshape(2, stretch_rows, heads_dev, HD)
    init_state = (
        jnp.full((2, heads_dev, stretch_rows), neg_large, single),
        jnp.zeros((2, heads_dev, stretch_rows), single),
        jnp.zeros((2, stretch_rows, heads_dev, HD), single),
    )
    key_flat = key_low.reshape(tok_rows, local_width)
    value_flat = value_low.reshape(tok_rows, local_width)
    carry_state = init_state
    key_piece = lax.all_gather(key_flat, "ctx", axis=0, tiled=True)
    value_piece = lax.all_gather(value_flat, "ctx", axis=0, tiled=True)

    def per_stretch(block_num, carry_state):
        key_block = lax.dynamic_slice_in_dim(
            key_piece, block_num * stretch_rows, stretch_rows, 0
        ).reshape(stretch_rows, heads_dev, HD)
        value_block = lax.dynamic_slice_in_dim(
            value_piece, block_num * stretch_rows, stretch_rows, 0
        ).reshape(stretch_rows, heads_dev, HD)
        key_stretch = lax.dynamic_index_in_dim(order, block_num, 0, keepdims=False)
        updated = []
        for half_num in range(2):
            allowed = stretch_mask(local_stretches[half_num], key_stretch, stretch_frames, lengths)
            current = (carry_state[0][half_num], carry_state[1][half_num], carry_state[2][half_num])
            current = lax.cond(
                jnp.any(allowed),
                lambda cur, keep_mask: online_step(
                    cur,
                    query_stretches[half_num],
                    key_block,
                    value_block,
                    expand_mask(keep_mask),
                    scale,
                ),
                lambda cur, keep_mask: cur,
                current,
                allowed,
            )
            updated.append(current)
        return tuple((jnp.stack([updated[0][member], updated[1][member]]) for member in range(3)))

    run_max, run_sum, run_acc = lax.fori_loop(
        0, key_piece.shape[0] // stretch_rows, per_stretch, carry_state
    )
    mix_rows = (run_acc / jnp.transpose(run_sum, (0, 2, 1))[..., None]).reshape(
        tok_rows, heads_dev, HD
    )
    lse_stretches = run_max + jnp.log(run_sum)
    mix_low = mix_rows.reshape(tok_rows, local_width).astype(bfloat)
    attn_out = lax.psum(
        jnp.einsum("rh,dh->rd", mix_low, attn_w[3], preferred_element_type=single).astype(
            jnp.bfloat16
        ),
        "tp",
    ).astype(jnp.float32)
    attn_full = attn_out.reshape(frames_dev, PATCHES, D)
    resid_mid = resid_in + modulate[:, 2] * attn_full
    normed_two, inv_two = layer_norm(resid_mid)
    hidden_two = (
        (normed_two * (1.0 + modulate[:, 4]) + modulate[:, 3]).reshape(tok_rows, D).astype(bfloat)
    )
    upward = jnp.dot(hidden_two, mlp_w[0], preferred_element_type=single)
    activ_low = jax.nn.gelu(upward, approximate=False).astype(bfloat)
    mlp_out = lax.psum(
        jnp.einsum("rf,df->rd", activ_low, mlp_w[1], preferred_element_type=single).astype(
            jnp.bfloat16
        ),
        "tp",
    ).astype(jnp.float32)
    mlp_full = mlp_out.reshape(frames_dev, PATCHES, D)
    resid_out = resid_mid + modulate[:, 5] * mlp_full
    normed_three, inv_three = layer_norm(resid_out)
    final_low = (normed_three * vec_w[7]).reshape(tok_rows, D).astype(bfloat)
    pred = jnp.einsum("rd,pd->rp", final_low, io_w[1], preferred_element_type=single)
    diff = pred.reshape(frames_dev, PATCHES, feat_dim) - target
    error = jnp.mean(diff * diff, axis=2)
    weight_sum, error_sum = lax.psum(
        (PATCHES * jnp.sum(weight), jnp.sum(weight[:, None] * error)), "ctx"
    )
    loss_value = error_sum / weight_sum
    grad_pred = (
        (2.0 / feat_dim * weight[:, None, None] * diff / weight_sum)
        .reshape(tok_rows, feat_dim)
        .astype(bfloat)
    )
    grad_head = jnp.einsum("rp,rd->pd", grad_pred, final_low, preferred_element_type=single)
    grad_final = jnp.einsum("rp,pd->rd", grad_pred, io_w[1], preferred_element_type=single).reshape(
        frames_dev, PATCHES, D
    )
    grad_gain = jnp.sum(grad_final * normed_three, axis=(0, 1))
    grad_three = norm_back(grad_final * vec_w[7], normed_three, inv_three)
    grad_mlp_low = (modulate[:, 5] * grad_three).reshape(tok_rows, D).astype(bfloat)
    grad_gate_two = jnp.sum(grad_three * mlp_full, axis=1)
    grad_activ = jnp.einsum("rd,df->rf", grad_mlp_low, mlp_w[1], preferred_element_type=single)
    grad_down = jnp.einsum("rd,rf->df", grad_mlp_low, activ_low, preferred_element_type=single)
    grad_up_low = (grad_activ * gelu_slope(upward)).astype(bfloat)
    grad_up = jnp.einsum("rd,rf->df", hidden_two, grad_up_low, preferred_element_type=single)
    grad_hidden_two = lax.psum(
        jnp.einsum("rf,df->rd", grad_up_low, mlp_w[0], preferred_element_type=single).astype(
            jnp.bfloat16
        ),
        "tp",
    ).astype(jnp.float32)
    grad_hidden_two = grad_hidden_two.reshape(frames_dev, PATCHES, D)
    grad_shift_two = jnp.sum(grad_hidden_two, axis=1)
    grad_scale_two = jnp.sum(grad_hidden_two * normed_two, axis=1)
    grad_mid = grad_three + norm_back(grad_hidden_two * (1.0 + modulate[:, 4]), normed_two, inv_two)
    grad_attn_low = (modulate[:, 2] * grad_mid).reshape(tok_rows, D).astype(bfloat)
    grad_gate_one = jnp.sum(grad_mid * attn_full, axis=1)
    grad_outproj = jnp.einsum("rd,rh->dh", grad_attn_low, mix_low, preferred_element_type=single)
    grad_mix_low = jnp.einsum(
        "rd,dh->rh", grad_attn_low, attn_w[3], preferred_element_type=single
    ).astype(bfloat)
    delta_rows = jnp.sum(
        grad_mix_low.astype(single).reshape(tok_rows, heads_dev, HD) * mix_rows, axis=2
    )
    grad_stretches = grad_mix_low.reshape(2, stretch_rows, heads_dev, HD)
    delta_stretches = jnp.transpose(delta_rows.reshape(2, stretch_rows, heads_dev), (0, 2, 1))

    def span_back(key_block, value_block, key_stretch, grad_query_acc):
        key_sum = jnp.zeros((stretch_rows, heads_dev, HD), single)
        value_sum = jnp.zeros((stretch_rows, heads_dev, HD), single)
        query_parts = []
        for half_num in range(2):
            allowed = stretch_mask(local_stretches[half_num], key_stretch, stretch_frames, lengths)
            result = lax.cond(
                jnp.any(allowed),
                lambda keep_mask: pair_grads(
                    query_stretches[half_num],
                    grad_stretches[half_num],
                    lse_stretches[half_num],
                    delta_stretches[half_num],
                    key_block,
                    value_block,
                    expand_mask(keep_mask),
                    scale,
                ),
                lambda keep_mask: (jnp.zeros((stretch_rows, heads_dev, HD), single),) * 3,
                allowed,
            )
            query_parts.append(grad_query_acc[half_num] + result[0])
            key_sum = key_sum + result[1]
            value_sum = value_sum + result[2]
        return (
            jnp.stack(query_parts),
            key_sum.reshape(stretch_rows, local_width),
            value_sum.reshape(stretch_rows, local_width),
        )

    init_back = (
        jnp.zeros((2, stretch_rows, heads_dev, HD), single),
        jnp.zeros((ctx_count * tok_rows, local_width), single),
        jnp.zeros((ctx_count * tok_rows, local_width), single),
    )
    carry_state = init_back
    fold_key_piece = lax.all_gather(key_flat, "ctx", axis=0, tiled=True)
    fold_value_piece = lax.all_gather(value_flat, "ctx", axis=0, tiled=True)

    def per_stretch(block_num, carry_state):
        grad_query_acc, grad_keys_all, grad_values_all = carry_state
        key_block = lax.dynamic_slice_in_dim(
            fold_key_piece, block_num * stretch_rows, stretch_rows, 0
        ).reshape(stretch_rows, heads_dev, HD)
        value_block = lax.dynamic_slice_in_dim(
            fold_value_piece, block_num * stretch_rows, stretch_rows, 0
        ).reshape(stretch_rows, heads_dev, HD)
        key_stretch = lax.dynamic_index_in_dim(order, block_num, 0, keepdims=False)
        grad_query_acc, key_sum, value_sum = span_back(
            key_block, value_block, key_stretch, grad_query_acc
        )
        place = block_num * stretch_rows
        grad_keys_all = lax.dynamic_update_slice_in_dim(grad_keys_all, key_sum, place, 0)
        grad_values_all = lax.dynamic_update_slice_in_dim(grad_values_all, value_sum, place, 0)
        return (grad_query_acc, grad_keys_all, grad_values_all)

    grad_query_acc, grad_keys_all, grad_values_all = lax.fori_loop(
        0, fold_key_piece.shape[0] // stretch_rows, per_stretch, carry_state
    )
    grad_keys, grad_values = (
        lax.psum_scatter(
            grad_keys_all.astype(jnp.bfloat16), "ctx", scatter_dimension=0, tiled=True
        ).astype(jnp.float32),
        lax.psum_scatter(
            grad_values_all.astype(jnp.bfloat16), "ctx", scatter_dimension=0, tiled=True
        ).astype(jnp.float32),
    )
    grad_query = grad_query_acc.reshape(tok_rows, local_width)
    query_back = (
        rotate_back(grad_query.reshape(tok_rows, heads_dev, HD), cosine, sine)
        .reshape(tok_rows, local_width)
        .astype(bfloat)
    )
    key_back = (
        rotate_back(grad_keys.reshape(tok_rows, heads_dev, HD), cosine, sine)
        .reshape(tok_rows, local_width)
        .astype(bfloat)
    )
    value_back = grad_values.astype(bfloat)
    grad_wq = jnp.einsum("rd,rh->dh", hidden_one, query_back, preferred_element_type=single)
    grad_wk = jnp.einsum("rd,rh->dh", hidden_one, key_back, preferred_element_type=single)
    grad_wv = jnp.einsum("rd,rh->dh", hidden_one, value_back, preferred_element_type=single)
    partial_one = (
        jnp.einsum("rh,dh->rd", query_back, attn_w[0], preferred_element_type=single)
        + jnp.einsum("rh,dh->rd", key_back, attn_w[1], preferred_element_type=single)
        + jnp.einsum("rh,dh->rd", value_back, attn_w[2], preferred_element_type=single)
    )
    grad_hidden_one = (
        lax.psum(partial_one.astype(jnp.bfloat16), "tp")
        .astype(jnp.float32)
        .reshape(frames_dev, PATCHES, D)
    )
    grad_shift_one = jnp.sum(grad_hidden_one, axis=1)
    grad_scale_one = jnp.sum(grad_hidden_one * normed_one, axis=1)
    grad_in = grad_mid + norm_back(grad_hidden_one * (1.0 + modulate[:, 1]), normed_one, inv_one)
    grad_mod = jnp.stack(
        [
            grad_shift_one,
            grad_scale_one,
            grad_gate_one,
            grad_shift_two,
            grad_scale_two,
            grad_gate_two,
        ],
        axis=1,
    )
    grad_mod_w = jnp.einsum(
        "fd,fc->dc",
        cond_low,
        grad_mod.reshape(frames_dev, 6 * D).astype(bfloat),
        preferred_element_type=single,
    )
    grad_in_low = grad_in.reshape(tok_rows, D).astype(bfloat)
    grad_embed = jnp.einsum("rp,rd->pd", noisy_low, grad_in_low, preferred_element_type=single)
    grad_vec = jnp.concatenate(
        [jnp.sum(grad_mod, axis=0), jnp.sum(grad_in, axis=(0, 1))[None], grad_gain[None]], axis=0
    )
    grad_attn = jnp.stack([grad_wq, grad_wk, grad_wv, grad_outproj])
    grad_mlp = jnp.stack([grad_up, grad_down])
    grad_io = jnp.stack([grad_embed, grad_head])
    red_attn, red_mlp, red_mod, red_io, red_vec = (
        lax.psum_scatter(
            grad_attn.astype(jnp.bfloat16), "ctx", scatter_dimension=1, tiled=True
        ).astype(jnp.float32),
        lax.psum_scatter(
            grad_mlp.astype(jnp.bfloat16), "ctx", scatter_dimension=1, tiled=True
        ).astype(jnp.float32),
        lax.psum_scatter(
            grad_mod_w.astype(jnp.bfloat16), "ctx", scatter_dimension=0, tiled=True
        ).astype(jnp.float32),
        lax.psum_scatter(
            grad_io.astype(jnp.bfloat16), "ctx", scatter_dimension=2, tiled=True
        ).astype(jnp.float32),
        lax.psum_scatter(
            grad_vec.astype(jnp.bfloat16), "ctx", scatter_dimension=1, tiled=True
        ).astype(jnp.float32),
    )
    shared_sq = jnp.sum(red_mod * red_mod) + jnp.sum(red_io * red_io) + jnp.sum(red_vec * red_vec)
    own_sq = (
        jnp.sum(red_attn * red_attn)
        + jnp.sum(red_mlp * red_mlp)
        + jnp.where(tp_index == 0, shared_sq, 0.0)
    )
    grad_norm = jnp.sqrt(lax.psum(own_sq, ("ctx", "tp")))
    factor = jnp.minimum(1.0, clip_limit / (grad_norm + 1e-06))
    count = step[0].astype(single)
    attn_new = adam(w_attn, m_attn, v_attn, red_attn, factor, count, rate_matrix, decay_rate)
    mlp_new = adam(w_mlp, m_mlp, v_mlp, red_mlp, factor, count, rate_matrix, decay_rate)
    mod_new = adam(w_mod, m_mod, v_mod, red_mod, factor, count, rate_matrix, decay_rate)
    io_new = adam(w_io, m_io, v_io, red_io, factor, count, rate_matrix, decay_rate)
    vec_new = adam(vectors, m_vec, v_vec, red_vec, factor, count, rate_vector, 0.0)
    return (
        loss_value,
        grad_norm,
        attn_new[0],
        attn_new[1],
        attn_new[2],
        attn_new[3],
        mlp_new[0],
        mlp_new[1],
        mlp_new[2],
        mlp_new[3],
        mod_new[0],
        mod_new[1],
        mod_new[2],
        mod_new[3],
        io_new[0],
        io_new[1],
        io_new[2][0],
        io_new[2][1],
        io_new[3],
        vec_new[0],
        vec_new[1],
        vec_new[2],
        vec_new[3],
    )


HALF_SLOTS = 16
QKV_ROWS = 768
ATTN_ROWS = 1024
FRONT_ROWS = 912
TOKEN_ROWS = 512
IO_ROWS = 80
MOD_ROWS = 48
NT = (((1,), (1,)), ((), ()))
TN = (((0,), (0,)), ((), ()))


def swap(values, axis, bit):
    size = 8 if axis == "ctx" else 4
    return lax.ppermute(values, axis, [(i, i ^ bit) for i in range(size)])


def after(values, *others):
    return lax.optimization_barrier((values,) + others)[0]


def gather_swaps(shard):
    along_x = swap(shard, "ctx", 1)
    along_z = [swap(shard, "ctx", bit) for bit in (2, 4, 6)]
    return [shard, along_x, *along_z, swap(jnp.concatenate(along_z, axis=0), "ctx", 1)]


def reduce_blocks(blocks, ctx_index, wire):
    return reduce_along_z(reduce_along_x(blocks, ctx_index, wire), ctx_index, wire)


def reduce_along_x(blocks, ctx_index, wire):
    x = ctx_index % 2
    pairs = blocks.reshape((4, 2) + blocks.shape[1:])
    first, second = pairs[:, 0], pairs[:, 1]
    even = x == 0
    away = jnp.where(even, second, first).astype(wire)
    return jnp.where(even, first, second) + swap(away, "ctx", 1).astype(jnp.float32)


def pieces_along_z(held, ctx_index, wire):
    z = ctx_index // 2
    low = held.astype(wire)
    came = []
    for bit in (1, 2, 3):
        piece = lax.dynamic_index_in_dim(low, z ^ bit, 0, keepdims=False)
        came.append(swap(piece, "ctx", 2 * bit))
    return lax.dynamic_index_in_dim(held, z, 0, keepdims=False), came


def reduce_along_z(held, ctx_index, wire):
    total, came = pieces_along_z(held, ctx_index, wire)
    for piece in came:
        total = total + piece.astype(jnp.float32)
    return total


def spread_frames(own):
    core = swap(own, "tp", 1)
    across = swap(own, "tp", 2)
    return [own, core, across, swap(across, "tp", 1)]


def sum_across(far):
    return (far[0] + swap(far[1], "tp", 1).astype(jnp.float32)).astype(jnp.bfloat16)


def sum_frames(near, across):
    return near[0], swap(near[1], "tp", 1), swap(across, "tp", 2)


def reorder_four(items, index):
    low_bit = (index & 1) == 1
    high_bit = (index & 2) == 2
    once = [jnp.where(low_bit, items[k ^ 1], items[k]) for k in range(4)]
    return [jnp.where(high_bit, once[k ^ 2], once[k]) for k in range(4)]


def sum_terms(values):
    values = values + swap(values, "ctx", 1)
    return [values] + [swap(values, "ctx", bit) for bit in (2, 4, 6)]


def token_kernel(meta, clean, noise, ring):
    for frame in range(4):
        rows = pl.ds(pl.multiple_of(256 * frame + 64 * meta[1], 64), 64)
        ring[128 * frame : 128 * frame + 64, :] = clean[rows, :]
        ring[128 * frame + 64 : 128 * frame + 128, :] = noise[rows, :]


def prepare_kernel(w_attn, w_io, vectors, front):
    for part in range(3):
        front[256 * part : 256 * part + 256, :] = w_attn[part].T.astype(jnp.bfloat16)
    base = QKV_ROWS
    front[base : base + 128, :] = w_io[0].astype(jnp.bfloat16)
    front[base + 128 : base + 144, :] = jnp.concatenate(
        [vectors[...], jnp.zeros((8, 128), jnp.float32)], axis=0
    ).astype(jnp.bfloat16)
    for part in range(2):
        base = FRONT_ROWS + 128 * part
        front[base : base + 128, :] = w_attn[3, :, 128 * part : 128 * part + 128].astype(
            jnp.bfloat16
        )
    front[FRONT_ROWS + 256 : FRONT_ROWS + 384, :] = w_io[1].T.astype(jnp.bfloat16)


def vmem_specs(count):
    return [pl.BlockSpec(memory_space=pltpu.VMEM)] * count


def smem_specs(count):
    return [pl.BlockSpec(memory_space=pltpu.SMEM)] * count


def call_tokens(device, clean, noise):
    return pl.pallas_call(
        token_kernel,
        out_shape=jax.ShapeDtypeStruct((TOKEN_ROWS, 128), jnp.bfloat16),
        in_specs=smem_specs(1) + vmem_specs(2),
        out_specs=vmem_specs(1)[0],
        name="tokens",
    )(device, clean, noise)


def call_prepare(w_attn, w_io, vectors):
    return pl.pallas_call(
        prepare_kernel,
        out_shape=jax.ShapeDtypeStruct((FRONT_ROWS + 384, 128), jnp.bfloat16),
        in_specs=vmem_specs(3),
        out_specs=vmem_specs(1)[0],
        name="prepare",
    )(w_attn, w_io, vectors)


def place_kernel(device, lengths, order, levels, front, attend, rows, inverse, stored, position, level):
    ctx, tp = device[0], device[1]
    frames, stretches, clips = levels.shape[0], order.shape[0], lengths.shape[0]
    per_stretch = frames // stretches
    half = frames // 2

    def per_stretch_place(place, carry):
        inverse[order[place]] = place
        return carry

    lax.fori_loop(0, stretches, per_stretch_place, 0)

    def per_frame(frame, counts):
        long_count, short_count = counts
        begin, start, length = jnp.int32(0), jnp.int32(0), jnp.int32(0)
        for clip in range(clips):
            size = lengths[clip]
            inside = (frame >= begin) & (frame < begin + size)
            start = jnp.where(inside, begin, start)
            length = jnp.where(inside, size, length)
            begin = begin + size
        is_long = length == half
        slot = jnp.where(is_long, long_count, half + short_count)
        stored[slot] = inverse[lax.div(frame, jnp.int32(per_stretch))] * per_stretch + lax.rem(
            frame, jnp.int32(per_stretch)
        )
        position[slot] = frame - start
        level[slot] = levels[frame]
        grown = is_long.astype(jnp.int32)
        return (long_count + grown, short_count + 1 - grown)

    lax.fori_loop(0, frames, per_frame, (jnp.int32(0), jnp.int32(0)))

    member = ctx & 3
    for k in range(4):
        front[8 + k] = 4 * member + (tp ^ k)
        front[12 + k] = member ^ k
        at = stored[4 * ctx + (tp ^ k)]
        front[16 + k] = ((at >> 2) ^ ctx) * 4 + (at & 3)
        front[20 + k] = tp ^ k
    for k in range(8):
        front[k] = 0
    attend[0] = member
    attend[1] = tp
    base = lax.div(ctx, jnp.int32(4)) * half

    def per_slot(slot, carry):
        attend[2 + slot] = position[base + slot]
        return carry

    lax.fori_loop(0, half, per_slot, 0)

    def per_row(row, carry):
        rows[row] = level[row]
        rows[frames + row] = level[4 * (ctx ^ (row & 7)) + (row >> 3)]
        return carry

    lax.fori_loop(0, frames, per_row, 0)
    for k in range(8):
        rows[2 * frames + k] = level[4 * ctx + (tp ^ (k & 3))]


def call_place(device, lengths, order, levels):
    frames = levels.shape[0]
    return pl.pallas_call(
        place_kernel,
        out_shape=(
            jax.ShapeDtypeStruct((24,), jnp.int32),
            jax.ShapeDtypeStruct((2 + frames // 2,), jnp.int32),
            jax.ShapeDtypeStruct((2 * frames + 8,), jnp.int32),
        ),
        in_specs=smem_specs(4),
        out_specs=smem_specs(3),
        scratch_shapes=[pltpu.SMEM((order.shape[0],), jnp.int32)]
        + [pltpu.SMEM((frames,), jnp.int32)] * 3,
        name="place",
    )(device, lengths, order, levels)


def pick_kernel(meta, *refs):
    out, sems = refs[6:]
    places = [(refs[0], 0), (refs[1], 0)]
    for bit in range(3):
        places += [(refs[2 + bit], 0), (refs[5], TOKEN_ROWS * bit)]
    for frame in range(4):
        wanted = meta[16 + frame]
        for place, (source, base) in enumerate(places):

            @pl.when((wanted >> 2) == place)
            def _():
                start = pl.multiple_of(base + (wanted & 3) * 128, 128)
                pltpu.make_async_copy(
                    source.at[pl.ds(start, 128), :],
                    out.at[128 * frame : 128 * frame + 128, :],
                    sems.at[frame],
                ).start()

    for frame in range(4):
        pltpu.make_async_copy(
            refs[0].at[0:128, :], out.at[128 * frame : 128 * frame + 128, :], sems.at[frame]
        ).wait()


def hbm_specs(count):
    return [pl.BlockSpec(memory_space=pltpu.HBM)] * count


def call_pick(meta, pieces):
    return pl.pallas_call(
        pick_kernel,
        out_shape=jax.ShapeDtypeStruct((TOKEN_ROWS, 128), jnp.bfloat16),
        in_specs=smem_specs(1) + hbm_specs(6),
        out_specs=vmem_specs(1)[0],
        scratch_shapes=[pltpu.SemaphoreType.DMA((4,))],
        compiler_params=pltpu.CompilerParams(vmem_limit_bytes=56 * 2**20),
        name="pick",
    )(meta, *pieces)


def centred_norm(values):
    centred = values - jnp.mean(values, axis=-1, keepdims=True)
    inv_std = lax.rsqrt(jnp.mean(centred * centred, axis=-1, keepdims=True) + ln_eps)
    return centred * inv_std, inv_std


def front_kernel(meta, scales, *refs):
    pieces, quarters = refs[0], refs[1:5]
    mod, cosine, sine = refs[5:8]
    weights_out, mid_out, hidden_out, resid_out = refs[8:12]
    head_outs = refs[12:16]
    noisy_out, target_out, mod_out = refs[16:19]
    tokens, heads, weights, mid, hidden, resid, target, mod_own, held, sems, out_sems = refs[19:]
    spans = (slice(QKV_ROWS, FRONT_ROWS + 384), slice(0, QKV_ROWS))
    copies = [
        [
            pltpu.make_async_copy(
                pieces.at[place, span, :], held.at[place, span, :], sems.at[place, index]
            )
            for place in range(8)
        ]
        for index, span in enumerate(spans)
    ]
    for copy in copies[0] + copies[1]:
        copy.start()
    for source in range(4):
        rows = pl.ds(pl.multiple_of(meta[20 + source] * 64, 64), 64)
        for frame in range(4):
            base = 128 * (frame ^ source)
            clean = quarters[source][base : base + 64, :].astype(jnp.float32)
            noise = quarters[source][base + 64 : base + 128, :].astype(jnp.float32)
            mixed = scales[frame] * clean + scales[4 + frame] * noise
            tokens[frame, rows, :] = mixed.astype(jnp.bfloat16)
            if frame == 0:
                target[rows, :] = scales[0] * noise - scales[4] * clean
    outs = [
        pltpu.make_async_copy(tokens.at[0], noisy_out, out_sems.at[0]),
        pltpu.make_async_copy(target, target_out, out_sems.at[1]),
        pltpu.make_async_copy(weights, weights_out, out_sems.at[2]),
        pltpu.make_async_copy(resid, resid_out, out_sems.at[3]),
    ] + [
        pltpu.make_async_copy(hidden.at[frame], hidden_out.at[frame], out_sems.at[4 + frame])
        for frame in range(4)
    ]
    outs.append(pltpu.make_async_copy(mod_own, mod_out, out_sems.at[8]))
    outs.append(pltpu.make_async_copy(mid, mid_out, out_sems.at[9]))
    for place in range(8):
        copies[0][place].wait()
        block = slice(128 * place, 128 * place + 128)
        weights[QKV_ROWS:FRONT_ROWS, block] = held[place, QKV_ROWS:FRONT_ROWS, :]
        for part in range(3):
            base = FRONT_ROWS + 128 * part
            mid[block, 128 * part : 128 * part + 128] = held[place, base : base + 128, :]
    for index in (0, 1, 9):
        outs[index].start()
    embed = weights[QKV_ROWS : QKV_ROWS + 128, :]
    vec_rows = weights[QKV_ROWS + 128 : FRONT_ROWS, :].astype(jnp.float32)
    mod_own[0:6, :] = mod[0] + vec_rows[0:6]
    mod_own[6:8, :] = vec_rows[6:8]
    outs[8].start()
    for frame in range(4):
        values = jnp.dot(tokens[frame], embed, preferred_element_type=jnp.float32) + vec_rows[6:7]
        if frame == 0:
            resid[...] = values
            outs[3].start()
        normed, _ = centred_norm(values)
        shift = mod[frame, 0:1, :] + vec_rows[0:1]
        scale = mod[frame, 1:2, :] + vec_rows[1:2]
        low = (normed * (1.0 + scale) + shift).astype(jnp.bfloat16)
        hidden[frame] = low
        outs[4 + frame].start()
    for place in range(8):
        copies[1][place].wait()
        weights[0:QKV_ROWS, 128 * place : 128 * place + 128] = held[place, 0:QKV_ROWS, :]
    outs[2].start()
    for frame in range(4):
        mixed = lax.dot_general(
            weights[0:QKV_ROWS, :], hidden[frame], NT, preferred_element_type=jnp.float32
        )
        cos_now = cosine[meta[8 + frame]]
        sin_now = sine[meta[8 + frame]]
        cols = slice(256 * frame, 256 * frame + 256)
        for head in range(4):
            where_to = head
            for part in range(2):
                base = 256 * part + 64 * head
                upper = mixed[base : base + 32]
                lower = mixed[base + 32 : base + 64]
                heads[where_to, 64 * part : 64 * part + 32, cols] = (
                    upper * cos_now - lower * sin_now
                ).astype(jnp.bfloat16)
                heads[where_to, 64 * part + 32 : 64 * part + 64, cols] = (
                    lower * cos_now + upper * sin_now
                ).astype(jnp.bfloat16)
            base = 512 + 64 * head
            heads[where_to, 128:192, cols] = mixed[base : base + 64].astype(jnp.bfloat16)
    for k in range(4):
        outs.append(pltpu.make_async_copy(heads.at[meta[12 + k]], head_outs[k], out_sems.at[10 + k]))
        outs[10 + k].start()
    for copy in outs:
        copy.wait()


def call_front(meta, scales, pieces, quarters, mod, cosine, sine):
    return pl.pallas_call(
        front_kernel,
        out_shape=(
            jax.ShapeDtypeStruct((FRONT_ROWS, D), jnp.bfloat16),
            jax.ShapeDtypeStruct((D, 384), jnp.bfloat16),
            jax.ShapeDtypeStruct((4, PATCHES, D), jnp.bfloat16),
            jax.ShapeDtypeStruct((PATCHES, D), jnp.float32),
        )
        + (jax.ShapeDtypeStruct((192, 4 * PATCHES), jnp.bfloat16),) * 4
        + (
            jax.ShapeDtypeStruct((PATCHES, 128), jnp.bfloat16),
            jax.ShapeDtypeStruct((PATCHES, 128), jnp.float32),
            jax.ShapeDtypeStruct((8, D), jnp.float32),
        ),
        in_specs=smem_specs(2) + hbm_specs(1) + vmem_specs(7),
        out_specs=hbm_specs(11),
        scratch_shapes=[
            pltpu.VMEM((4, PATCHES, 128), jnp.bfloat16),
            pltpu.VMEM((4, 192, 4 * PATCHES), jnp.bfloat16),
            pltpu.VMEM((FRONT_ROWS, D), jnp.bfloat16),
            pltpu.VMEM((D, 384), jnp.bfloat16),
            pltpu.VMEM((4, PATCHES, D), jnp.bfloat16),
            pltpu.VMEM((PATCHES, D), jnp.float32),
            pltpu.VMEM((PATCHES, 128), jnp.float32),
            pltpu.VMEM((8, D), jnp.float32),
            pltpu.VMEM((8, FRONT_ROWS + 384, 128), jnp.bfloat16),
            pltpu.SemaphoreType.DMA((8, 2)),
            pltpu.SemaphoreType.DMA((14,)),
        ],
        compiler_params=pltpu.CompilerParams(vmem_limit_bytes=52 * 2**20),
        cost_estimate=pl.CostEstimate(flops=2 * 10**9, bytes_accessed=10**7, transcendentals=0),
        name="front",
    )(meta, scales, pieces, *quarters, mod, cosine, sine)


def total_own(held, came, across):
    return held[...] + came[...].astype(jnp.float32) + across[...].astype(jnp.float32)


def middle_kernel(held, came, across, resid, mod, attn_out, resid_mid, hidden):
    total = total_own(held, came, across)
    attn_out[...] = total.astype(jnp.bfloat16)
    values = resid[...] + mod[2:3, :] * total
    resid_mid[...] = values
    normed, _ = centred_norm(values)
    hidden[...] = (normed * (1.0 + mod[4:5, :]) + mod[3:4, :]).astype(jnp.bfloat16)


def row_call(kernel, name, outs, *operands, smem=0):
    return pl.pallas_call(
        kernel,
        out_shape=tuple(outs),
        in_specs=smem_specs(smem) + vmem_specs(len(operands) - smem),
        out_specs=vmem_specs(len(outs)),
        compiler_params=pltpu.CompilerParams(vmem_limit_bytes=16 * 2**20),
        cost_estimate=pl.CostEstimate(flops=10**9, bytes_accessed=4 * 10**6, transcendentals=0),
        name=name,
    )(*operands)


def frame_f32():
    return jax.ShapeDtypeStruct((PATCHES, D), jnp.float32)


def frame_low():
    return jax.ShapeDtypeStruct((PATCHES, D), jnp.bfloat16)


def back_through_norm(grad, normed, inv_std):
    mean_grad = jnp.mean(grad, axis=-1, keepdims=True)
    mean_proj = jnp.mean(grad * normed, axis=-1, keepdims=True)
    return inv_std * (grad - mean_grad - normed * mean_proj)


def column_sum(values):
    return jnp.sum(values, axis=0, keepdims=True)


def loss_kernel(
    scales, held, came, across, resid_mid, mod, mid, target, grad_low, grad_three, io_rows, gate, error
):
    mlp_out = total_own(held, came, across)
    values = resid_mid[...] + mod[5:6, :] * mlp_out
    normed, inv_std = centred_norm(values)
    gain = mod[7:8, :]
    final = (normed * gain).astype(jnp.bfloat16)
    head = mid[:, 256:384]
    pred = jnp.dot(final, head, preferred_element_type=jnp.float32)
    diff = pred - target[...]
    per_token = jnp.sum(diff * diff, axis=1, keepdims=True)
    error[...] = jnp.broadcast_to(
        scales[0] * jnp.sum(per_token, axis=0, keepdims=True) / diff.shape[1], error.shape
    )
    grad_pred = (scales[1] * diff).astype(jnp.bfloat16)
    grad_final = lax.dot_general(grad_pred, head, NT, preferred_element_type=jnp.float32)
    grad_gain = column_sum(grad_final * normed)
    grad = back_through_norm(grad_final * gain, normed, inv_std)
    grad_three[...] = grad
    grad_low[...] = (mod[5:6, :] * grad).astype(jnp.bfloat16)
    gate[...] = column_sum(grad * mlp_out)
    io_rows[0:128, :] = lax.dot_general(grad_pred, final, TN, preferred_element_type=jnp.float32)
    io_rows[128:136, :] = jnp.concatenate([grad_gain, jnp.zeros((7, D), jnp.float32)], axis=0)


def second_kernel(
    held, came, across, resid_mid, mod, grad_three, attn_out, grad_low, grad_mid, rows
):
    grad_hidden = total_own(held, came, across)
    normed, inv_std = centred_norm(resid_mid[...])
    grad = grad_three[...] + back_through_norm(grad_hidden * (1.0 + mod[4:5, :]), normed, inv_std)
    grad_mid[...] = grad
    grad_low[...] = (mod[2:3, :] * grad).astype(jnp.bfloat16)
    rows[0:1, :] = column_sum(grad * attn_out[...].astype(jnp.float32))
    rows[1:2, :] = column_sum(grad_hidden)
    rows[2:3, :] = column_sum(grad_hidden * normed)


def first_kernel(
    device,
    held,
    came,
    across,
    resid,
    mod,
    grad_mid,
    noisy,
    rows_two,
    gate_two,
    head_rows,
    mod_rows,
    near_held,
    near_away,
    far_held,
    far_away,
    io_rows,
):
    grad_hidden = total_own(held, came, across)
    normed, inv_std = centred_norm(resid[...])
    grad = grad_mid[...] + back_through_norm(grad_hidden * (1.0 + mod[1:2, :]), normed, inv_std)
    rows = [
        column_sum(grad_hidden),
        column_sum(grad_hidden * normed),
        rows_two[0:1, :],
        rows_two[1:2, :],
        rows_two[2:3, :],
        gate_two[...],
    ]
    blocks = [row[:, 128 * k : 128 * k + 128] for row in rows for k in range(8)]
    mod_rows[...] = jnp.concatenate(blocks, axis=0).astype(jnp.bfloat16)
    io_rows[0:128, :] = lax.dot_general(
        noisy[...], grad.astype(jnp.bfloat16), TN, preferred_element_type=jnp.float32
    )
    io_rows[128:256, :] = head_rows[0:128, :]
    io_rows[256:264, :] = jnp.concatenate(
        [column_sum(grad), head_rows[128:129, :], jnp.zeros((6, D), jnp.float32)], axis=0
    )
    io_rows[264:320, :] = jnp.zeros((56, D), jnp.float32)
    for k, out in enumerate((near_held, near_away, far_held, far_away)):
        group = pl.ds(pl.multiple_of(IO_ROWS * (device[1] ^ k), 16), IO_ROWS)
        out[...] = io_rows[group, :].astype(out.dtype)


def side_kernel(device, held, came, across, mod_rows, keep, away):
    total = total_own(held, came, across)
    side = device[0] & 1
    for block in range(8):
        piece = total[:, 128 * block : 128 * block + 128]

        @pl.when(side == block % 2)
        def _():
            keep[block // 2] = piece

        @pl.when(side != block % 2)
        def _():
            away[IO_ROWS * (block // 2) : IO_ROWS * (block // 2) + IO_ROWS, :] = piece.astype(
                jnp.bfloat16
            )

    away[4 * IO_ROWS :, :] = mod_rows[...]


def merge_kernel(
    device, held, came, out_held, out_came, io_held, io_came, mod_rows, own, io_own, *outs
):
    z = device[0] >> 1
    for bit in range(4):
        total = jnp.concatenate(
            [
                held[z ^ bit] + came[z ^ bit].astype(jnp.float32),
                out_held[z ^ bit] + out_came[z ^ bit].astype(jnp.float32),
            ],
            axis=0,
        )
        rows = pl.ds(pl.multiple_of(IO_ROWS * (z ^ bit), 16), IO_ROWS)
        io_total = io_held[z ^ bit] + io_came[rows, :].astype(jnp.float32)
        if bit == 0:
            own[...] = total
            io_own[...] = io_total
        else:
            out = outs[bit]
            out[0:ATTN_ROWS, :] = total.astype(jnp.bfloat16)
            out[ATTN_ROWS : ATTN_ROWS + IO_ROWS, :] = io_total.astype(jnp.bfloat16)
            base = ATTN_ROWS + IO_ROWS
            out[base : base + MOD_ROWS, :] = mod_rows[...]
            out[base + MOD_ROWS : base + 2 * MOD_ROWS, :] = io_came[4 * IO_ROWS :, :]
    outs[0][0:MOD_ROWS, :] = mod_rows[...]
    outs[0][MOD_ROWS : 2 * MOD_ROWS, :] = io_came[4 * IO_ROWS :, :]


def mod_grad_kernel(device, cond, *refs):
    parts = refs[:4]
    rows_out, vector, io_grad, square, rows = refs[4:]
    base = 8 * MOD_ROWS + 2 * IO_ROWS
    terms = []
    for index in range(4):
        owner = device[1] ^ index
        block = parts[index][0 : 8 * MOD_ROWS, :].astype(jnp.float32)
        for frame in range(8):
            for k in range(MOD_ROWS):
                at = MOD_ROWS * frame + k
                rows[owner, frame : frame + 1, 128 * k : 128 * k + 128] = block[at : at + 1, :]
        group = pl.ds(pl.multiple_of(IO_ROWS * owner, 16), IO_ROWS)
        high = parts[index][8 * MOD_ROWS : 8 * MOD_ROWS + IO_ROWS, :].astype(jnp.float32)
        rest = parts[index][8 * MOD_ROWS + IO_ROWS : base, :].astype(jnp.float32)
        io_grad[group, :] = high + rest
        terms.append(column_sum(parts[index][base : base + 16, :].astype(jnp.float32)))
    total = jnp.zeros((1, 1), jnp.float32)
    for index in range(6):
        cols = slice(D * index, D * index + D)
        low = rows[:, :, cols].reshape(32, D)
        rows_out[:, cols] = low.astype(jnp.bfloat16)
        part = lax.dot_general(
            cond[32:64, :], low.astype(jnp.bfloat16), TN, preferred_element_type=jnp.float32
        )
        total = total + jnp.sum(column_sum(part * part), axis=1, keepdims=True)
        own = pl.ds(pl.multiple_of(D * index + 128 * device[0], 128), 128)
        vector[index : index + 1, :] = column_sum(rows[:, :, own].reshape(32, 128))
    vector[6:8, :] = io_grad[256:258, :]
    mixed = vector[0:6, :]
    total = total + jnp.sum(column_sum(mixed * mixed), axis=1, keepdims=True)
    left = lax.broadcasted_iota(jnp.int32, (1, 128), 1) < 64
    square[...] = ((terms[0] + terms[1]) + (terms[2] + terms[3])) + jnp.where(left, total, 0.0)


def call_mod_grad(device, cond, parts):
    return pl.pallas_call(
        mod_grad_kernel,
        out_shape=(
            jax.ShapeDtypeStruct((32, 6 * D), jnp.bfloat16),
            jax.ShapeDtypeStruct((8, 128), jnp.float32),
            jax.ShapeDtypeStruct((4 * IO_ROWS, 128), jnp.float32),
            jax.ShapeDtypeStruct((1, 128), jnp.float32),
        ),
        in_specs=smem_specs(1) + vmem_specs(5),
        out_specs=vmem_specs(4),
        scratch_shapes=[pltpu.VMEM((4, 8, 6 * D), jnp.float32)],
        compiler_params=pltpu.CompilerParams(vmem_limit_bytes=12 * 2**20),
        cost_estimate=pl.CostEstimate(flops=10**8, bytes_accessed=4 * 10**6, transcendentals=0),
        name="mod_grad",
    )(device, cond, *parts)


def mlp_kernel(first, second, weights, held, away, active, slope):
    for frame, source in enumerate((first, second)):
        rows = slice(256 * frame, 256 * frame + 256)
        upward = jnp.dot(source[...], weights[0], preferred_element_type=jnp.float32)
        inner = 0.5 * (1.0 + lax.erf(upward * (1.0 / math.sqrt(2.0))))
        low = (upward * inner).astype(jnp.bfloat16)
        active[rows, :] = low
        change = inner + upward * jnp.exp(-0.5 * upward * upward) * (
            1.0 / math.sqrt(2.0 * math.pi)
        )
        slope[rows, :] = change.astype(jnp.bfloat16)
        part = lax.dot_general(low, weights[1], NT, preferred_element_type=jnp.float32)
        if frame:
            away[...] = part.astype(jnp.bfloat16)
        else:
            held[...] = part


def mlp_back_kernel(first, second, weights, slope, held, away, grad_up):
    for frame, source in enumerate((first, second)):
        rows = slice(256 * frame, 256 * frame + 256)
        grad = jnp.dot(source[...], weights[1], preferred_element_type=jnp.float32)
        low = (grad * slope[rows, :].astype(jnp.float32)).astype(jnp.bfloat16)
        grad_up[rows, :] = low
        part = lax.dot_general(low, weights[0], NT, preferred_element_type=jnp.float32)
        if frame:
            away[...] = part.astype(jnp.bfloat16)
        else:
            held[...] = part


def call_mlp(kernel, name, outs, *operands):
    return pl.pallas_call(
        kernel,
        out_shape=(frame_f32(), frame_low()) + outs,
        in_specs=vmem_specs(len(operands)),
        out_specs=vmem_specs(2 + len(outs)),
        compiler_params=pltpu.CompilerParams(vmem_limit_bytes=16 * 2**20),
        cost_estimate=pl.CostEstimate(
            flops=4 * 10**9, bytes_accessed=2 * 10**7, transcendentals=10**6
        ),
        name=name,
    )(*operands)


def weight_grad_kernel(*refs):
    hidden, grads = refs[:4], refs[4:8]
    grad_up, active = refs[8:10], refs[10:12]
    result, out, sems = refs[12:]
    width = active[0].shape[1]
    copies = []
    for index, (left, right) in enumerate(((hidden, grad_up), (grads, active))):
        total = jnp.zeros((D, width), jnp.float32)
        for frame in range(4):
            rows = slice(256 * (frame % 2), 256 * (frame % 2) + 256)
            total = total + lax.dot_general(
                left[frame][...],
                right[frame // 2][rows, :],
                TN,
                preferred_element_type=jnp.float32,
            )
        out[index] = total.astype(jnp.bfloat16)
        copies.append(
            pltpu.make_async_copy(
                out.at[index], result.at[:, width * index : width * index + width], sems.at[index]
            )
        )
        copies[index].start()
    for copy in copies:
        copy.wait()


def call_weight_grad(hidden, grads, grad_up, active):
    operands = (*hidden, *grads, *grad_up, *active)
    return pl.pallas_call(
        weight_grad_kernel,
        out_shape=jax.ShapeDtypeStruct((D, 2 * active[0].shape[1]), jnp.bfloat16),
        in_specs=vmem_specs(len(operands)),
        out_specs=hbm_specs(1)[0],
        scratch_shapes=[
            pltpu.VMEM((2, D, active[0].shape[1]), jnp.bfloat16),
            pltpu.SemaphoreType.DMA((2,)),
        ],
        compiler_params=pltpu.CompilerParams(vmem_limit_bytes=20 * 2**20),
        cost_estimate=pl.CostEstimate(flops=5 * 10**9, bytes_accessed=2 * 10**7, transcendentals=0),
        name="weight_grad",
    )(*operands)


def side_blocks(device, total, held, away):
    side = device[0] & 1
    for z in range(4):
        held[z] = total[:, pl.ds(pl.multiple_of(256 * z + 128 * side, 128), 128)]
        away[z] = total[:, pl.ds(pl.multiple_of(256 * z + 128 * (1 - side), 128), 128)].astype(
            jnp.bfloat16
        )


def head_grad_kernel(device, left, right, held, away, total):
    total[...] = jnp.dot(left[...], right[...], preferred_element_type=jnp.float32)
    side_blocks(device, total, held, away)


def call_head_grad(device, left, right):
    rows = left.shape[0]
    return pl.pallas_call(
        head_grad_kernel,
        out_shape=(
            jax.ShapeDtypeStruct((4, rows, 128), jnp.float32),
            jax.ShapeDtypeStruct((4, rows, 128), jnp.bfloat16),
        ),
        in_specs=smem_specs(1) + vmem_specs(2),
        out_specs=vmem_specs(2),
        scratch_shapes=[pltpu.VMEM((rows, D), jnp.float32)],
        compiler_params=pltpu.CompilerParams(vmem_limit_bytes=12 * 2**20),
        cost_estimate=pl.CostEstimate(flops=2 * 10**9, bytes_accessed=10**7, transcendentals=0),
        name="head_grad",
    )(device, left, right)


def qkv_back_kernel(meta, *refs):
    blocks, weights = refs[:4], refs[4]
    grads, near_held, near_away, far_held, far_away = refs[5:]
    for k in range(4):
        head = meta[0] ^ k
        for part in range(3):
            rows = pl.ds(pl.multiple_of(256 * part + 64 * head, 64), 64)
            grads[rows, :] = blocks[k][64 * part : 64 * part + 64, :]
    for frame, out in ((2, far_held), (3, far_away), (0, near_held), (1, near_away)):
        part = lax.dot_general(
            grads[:, 256 * frame : 256 * frame + 256],
            weights[0:QKV_ROWS, :],
            TN,
            preferred_element_type=jnp.float32,
        )
        out[...] = part.astype(out.dtype)


def call_qkv_back(meta, blocks, weights):
    return row_call(
        qkv_back_kernel,
        "qkv_back",
        (
            jax.ShapeDtypeStruct((QKV_ROWS, 4 * PATCHES), jnp.bfloat16),
            frame_f32(),
            frame_low(),
            frame_f32(),
            frame_low(),
        ),
        meta,
        *blocks,
        weights,
        smem=1,
    )


def adam_step(weight_now, first_mom, second_mom, grad, scale, rate, decay):
    factor, first_fix, second_fix = scale
    grad = grad * factor
    first_mom = beta_one * first_mom + (1.0 - beta_one) * grad
    second_mom = beta_two * second_mom + (1.0 - beta_two) * grad * grad
    second_hat = second_mom * second_fix
    updated = weight_now - rate * (
        first_mom * first_fix / (second_hat * lax.rsqrt(second_hat) + adam_eps)
        + decay * weight_now
    )
    return updated, first_mom, second_mom, updated.astype(jnp.bfloat16)


def preload_kernel(*refs):
    sources, targets, sems = refs[:3], refs[4:7], refs[7]
    copies = [
        pltpu.make_async_copy(sources[k], targets[k], sems.at[k]) for k in range(3)
    ]
    for copy in copies:
        copy.start()
    for copy in copies:
        copy.wait()


def call_preload(arrays, values):
    return pl.pallas_call(
        preload_kernel,
        out_shape=tuple(jax.ShapeDtypeStruct(a.shape, a.dtype) for a in arrays),
        in_specs=hbm_specs(3) + vmem_specs(1),
        out_specs=vmem_specs(3),
        scratch_shapes=[pltpu.SemaphoreType.DMA((3,))],
        compiler_params=pltpu.CompilerParams(vmem_limit_bytes=4 * 2**20),
        cost_estimate=pl.CostEstimate(flops=10**6, bytes_accessed=10**7, transcendentals=0),
        name="preload",
    )(*arrays, values)


def adam_kernel(*refs):
    fixes, sums = refs[0], refs[1:5]
    attn_grad, mlp_grad, cond, mod_rows = refs[5:9]
    io_in, vec_in = refs[9:13], refs[13:17]
    groups = [refs[17 + 3 * k : 20 + 3 * k] for k in range(3)]
    outs = [refs[26 + 4 * k : 30 + 4 * k] for k in range(3)]
    io_out, vec_out, norm_out = refs[38:43], refs[43:47], refs[47]
    held, slots, low_slots, in_sems, sems = refs[48:]
    depth = held.shape[0]
    tasks = []
    for k in (1, 0, 2):
        width = groups[k][0].shape[-1]
        for lead in range(groups[k][0].shape[0] if k < 2 else 1):
            for col in range(0, width, 1024):
                tasks.append((k, lead, col, min(1024, width - col)))

    def fetches(number):
        k, lead, col, span = tasks[number]
        cut = ((lead,) if k < 2 else ()) + (slice(None), slice(col, col + span))
        slot = number % depth
        if k == 2:
            return []
        return [
            pltpu.make_async_copy(
                groups[k][index].at[cut], held.at[slot, index, :, 0:span], in_sems.at[slot, index]
            )
            for index in range(3)
        ]

    for number in range(min(depth, len(tasks))):
        for copy in fetches(number):
            copy.start()
    total = (sums[0][...] + sums[1][...]) + (sums[2][...] + sums[3][...])
    norm = jnp.sqrt(total)
    norm_out[0:1, :] = norm
    norm_out[1:2, :] = total
    factor = jnp.minimum(1.0, clip_limit / (norm[:, 0:1] + 1e-06))
    scale = (factor, fixes[0], fixes[1])
    results = adam_step(*(ref[...] for ref in io_in), scale, rate_matrix, decay_rate)
    io_out[0][...] = results[0]
    io_out[1][...] = results[1]
    io_out[2][...] = results[2][0]
    io_out[3][...] = results[2][1]
    io_out[4][...] = results[3]
    results = adam_step(*(ref[...] for ref in vec_in), scale, rate_vector, 0.0)
    for out, result in zip(vec_out, results):
        out[...] = result
    running = {}
    for number, (k, lead, col, span) in enumerate(tasks):
        slot = number % depth
        for copy in fetches(number):
            copy.wait()
        for copy in running.pop(number - depth, ()):
            copy.wait()
        cut = ((lead,) if k < 2 else ()) + (slice(None), slice(col, col + span))
        if k == 0:
            grad = attn_grad[lead]
        elif k == 1:
            base = groups[1][0].shape[-1] * lead + col
            grad = mlp_grad[:, base : base + span].astype(jnp.float32)
        else:
            grad = lax.dot_general(
                cond[32:64, :],
                mod_rows[:, col : col + span],
                TN,
                preferred_element_type=jnp.float32,
            )
        if k == 2:
            values = [ref[:, col : col + span] for ref in groups[2]]
        else:
            values = [held[slot, index, :, 0:span] for index in range(3)]
        results = adam_step(*values, grad, scale, rate_matrix, decay_rate)
        copies = []
        for index, result in enumerate(results):
            source = low_slots.at[slot] if index == 3 else slots.at[slot, index]
            source = source.at[:, 0:span]
            source[...] = result
            copies.append(
                pltpu.make_async_copy(source, outs[k][index].at[cut], sems.at[slot, index])
            )
            copies[index].start()
        running[number] = copies
        if number + depth < len(tasks):
            for copy in fetches(number + depth):
                copy.start()
    for copies in running.values():
        for copy in copies:
            copy.wait()


def call_adam(fixes, sums, grads, io_group, vec_group, groups):
    held = [array for group in groups for array in group]
    inside = [*sums, *grads, *io_group, *vec_group]

    def results(group):
        low = jax.ShapeDtypeStruct(group[0].shape, jnp.bfloat16)
        return (jax.ShapeDtypeStruct(group[0].shape, jnp.float32),) * 3 + (low,)

    io_like = results(io_group)
    half = jax.ShapeDtypeStruct(io_group[0].shape[1:], jnp.float32)
    out_shape = sum((results(group) for group in groups), ())
    out_shape = out_shape + io_like[:2] + (half, half) + io_like[3:] + results(vec_group)
    out_shape = out_shape + (jax.ShapeDtypeStruct((2, 128), jnp.float32),)
    return pl.pallas_call(
        adam_kernel,
        out_shape=out_shape,
        in_specs=smem_specs(1) + vmem_specs(len(inside)) + hbm_specs(6) + vmem_specs(3),
        out_specs=hbm_specs(12) + vmem_specs(10),
        scratch_shapes=[
            pltpu.VMEM((6, 3, 128, 1024), jnp.float32),
            pltpu.VMEM((6, 3, 128, 1024), jnp.float32),
            pltpu.VMEM((6, 128, 1024), jnp.bfloat16),
            pltpu.SemaphoreType.DMA((6, 3)),
            pltpu.SemaphoreType.DMA((6, 4)),
        ],
        compiler_params=pltpu.CompilerParams(vmem_limit_bytes=28 * 2**20),
        cost_estimate=pl.CostEstimate(flops=10**7, bytes_accessed=2 * 10**7, transcendentals=0),
        name="adam",
    )(fixes, *inside, *held)


def square_kernel(scattered, square):
    rest = scattered[...].astype(jnp.float32)
    square[...] = jnp.broadcast_to(
        jnp.sum(column_sum(rest * rest), axis=1, keepdims=True), square.shape
    )


def finish_kernel(*refs):
    own, io_own, mod_own, pieces = refs[0], refs[1], refs[2], refs[3:6]
    rest, error, grad, spread = refs[6:]
    total = own[...]
    io_total = io_own[...]
    spread[0 : 2 * MOD_ROWS, :] = mod_own[...]
    for index, piece in enumerate(pieces):
        total = total + piece[0:ATTN_ROWS, :].astype(jnp.float32)
        base = ATTN_ROWS + IO_ROWS
        io_total = io_total + piece[ATTN_ROWS:base, :].astype(jnp.float32)
        spread[2 * MOD_ROWS * (index + 1) : 2 * MOD_ROWS * (index + 2), :] = piece[base:, :]
    high = io_total.astype(jnp.bfloat16)
    base = 8 * MOD_ROWS
    spread[base : base + IO_ROWS, :] = high
    base = base + IO_ROWS
    spread[base : base + IO_ROWS, :] = (io_total - high.astype(jnp.float32)).astype(jnp.bfloat16)
    for part in range(4):
        grad[part] = total[256 * part : 256 * part + 256].T
    squares = rest[:, 0:1]
    for values in (total, io_total):
        squares = squares + jnp.sum(column_sum(values * values), axis=1, keepdims=True)
    left = lax.broadcasted_iota(jnp.int32, (1, 128), 1) < 64
    value = jnp.where(left, squares, error[...])
    terms = []
    for _ in range(3):
        terms.append(value.astype(jnp.bfloat16).astype(jnp.float32))
        value = value - terms[-1]
    spread[base + IO_ROWS :, :] = jnp.concatenate(
        terms + [jnp.zeros((13, 128), jnp.float32)], axis=0
    ).astype(jnp.bfloat16)


def turn(block):
    return block.astype(jnp.float32).T.astype(jnp.bfloat16)


def query_rows(meta, pair):
    first = 2 * pair
    start_first = first - meta[2 + first]
    start_second = first + 1 - meta[3 + first]
    left = lax.broadcasted_iota(jnp.int32, (1, 2 * PATCHES), 1) < PATCHES
    upto = jnp.where(left, first, first + 1)
    since = jnp.where(left, start_first, start_second)
    return jnp.minimum(start_first, start_second), since, upto


def attend_kernel(meta, *refs):
    blocks = refs[:4]
    outs = refs[4:8]
    lse, mixed, query, key, value, scores = refs[8:]
    for member in range(4):
        for frame in range(4):
            slot = 4 * (meta[0] ^ member) + (meta[1] ^ frame)
            cols = slice(256 * frame, 256 * frame + 256)
            lanes = pl.ds(pl.multiple_of((slot % 2) * 256, 256), 256)
            query[slot // 2, :, lanes] = blocks[member][0:64, cols] * 0.125
            key[slot // 2, lanes, :] = turn(blocks[member][64:128, cols])
            value[slot // 2, :, lanes] = blocks[member][128:192, cols]

    def per_pair(pair, carry):
        low, since, upto = query_rows(meta, pair)
        wanted = query[pair]

        def first_pass(keys, top):
            both = jnp.dot(key[keys], wanted, preferred_element_type=jnp.float32)
            for side in range(2):
                slot = 2 * keys + side
                bias = jnp.where((slot >= since) & (slot <= upto), 0.0, neg_large)
                part = both[256 * side : 256 * side + 256] + bias
                scores[keys, 256 * side : 256 * side + 256, :] = part
                top = jnp.maximum(top, jnp.max(part.reshape(32, 8, 2 * PATCHES), axis=0))
            return top

        tops = lax.fori_loop(
            low // 2, pair + 1, first_pass, jnp.full((8, 2 * PATCHES), neg_large, jnp.float32)
        )
        top = jnp.max(tops, axis=0, keepdims=True)

        def second_pass(keys, state):
            total, acc = state
            probs = jnp.exp(scores[keys] - top)
            total = total + jnp.sum(probs.reshape(64, 8, 2 * PATCHES), axis=0)
            acc = acc + jnp.dot(
                value[keys], probs.astype(jnp.bfloat16), preferred_element_type=jnp.float32
            )
            return (total, acc)

        totals, acc = lax.fori_loop(
            low // 2,
            pair + 1,
            second_pass,
            (
                jnp.zeros((8, 2 * PATCHES), jnp.float32),
                jnp.zeros((HD, 2 * PATCHES), jnp.float32),
            ),
        )
        total = jnp.sum(totals, axis=0, keepdims=True)
        lse[pair] = top + jnp.log(total)
        mixed[pair] = acc / total
        return carry

    lax.fori_loop(0, 8, per_pair, 0)
    for member in range(4):
        for frame in range(4):
            slot = 4 * (meta[0] ^ member) + (meta[1] ^ frame)
            lanes = pl.ds(pl.multiple_of((slot % 2) * 256, 256), 256)
            outs[member][:, 256 * frame : 256 * frame + 256] = mixed[slot // 2, :, lanes].astype(
                jnp.bfloat16
            )


def call_attend(meta, blocks):
    vmem = pl.BlockSpec()
    result = pl.pallas_call(
        attend_kernel,
        out_shape=tuple(jax.ShapeDtypeStruct((HD, 4 * PATCHES), jnp.bfloat16) for _ in range(4))
        + (
            jax.ShapeDtypeStruct((8, 1, 2 * PATCHES), jnp.float32),
            jax.ShapeDtypeStruct((8, HD, 2 * PATCHES), jnp.float32),
        ),
        in_specs=[pl.BlockSpec(memory_space=pltpu.SMEM)] + [vmem] * 4,
        out_specs=(vmem,) * 6,
        scratch_shapes=[
            pltpu.VMEM((8, HD, 2 * PATCHES), jnp.bfloat16),
            pltpu.VMEM((8, 2 * PATCHES, HD), jnp.bfloat16),
            pltpu.VMEM((8, HD, 2 * PATCHES), jnp.bfloat16),
            pltpu.VMEM((8, 2 * PATCHES, 2 * PATCHES), jnp.float32),
        ],
        compiler_params=pltpu.CompilerParams(vmem_limit_bytes=48 * 2**20),
        cost_estimate=pl.CostEstimate(flops=9 * 10**9, bytes_accessed=5 * 10**6, transcendentals=10**7),
        name="attend",
    )(meta, *blocks)
    return list(result[:4]), result[4], result[5]


def attend_back_kernel(meta, *refs):
    blocks = refs[:4]
    grads = refs[4:8]
    lse, mixed, cosine, sine = refs[8:12]
    outs = refs[12:16]
    query, key, key_flat, value_flat, grad, sum_key, sum_value, sum_query = refs[16:]
    for member in range(4):
        for frame in range(4):
            slot = 4 * (meta[0] ^ member) + (meta[1] ^ frame)
            cols = slice(256 * frame, 256 * frame + 256)
            place = pl.ds(pl.multiple_of((slot % 2) * 256, 256), 256)
            part = blocks[member][0:64, cols] * 0.125
            query[slot // 2, :, place] = part
            part = blocks[member][64:128, cols]
            key[slot // 2, :, place] = part
            key_flat[slot // 2, place, :] = turn(part)
            value_flat[slot // 2, place, :] = turn(blocks[member][128:192, cols])
            part = grads[member][:, cols]
            grad[slot // 2, :, place] = part
    sum_key[...] = jnp.zeros_like(sum_key)
    sum_value[...] = jnp.zeros_like(sum_value)

    def per_pair(pair, carry):
        low, since, upto = query_rows(meta, pair)
        wanted = query[pair]
        wanted_grad = grad[pair]
        delta = jnp.sum(wanted_grad.astype(jnp.float32) * mixed[pair], axis=0, keepdims=True)
        level = lse[pair]

        def per_keys(keys, acc):
            scores = jnp.dot(key_flat[keys], wanted, preferred_element_type=jnp.float32)
            grad_probs = jnp.dot(
                value_flat[keys], wanted_grad, preferred_element_type=jnp.float32
            )
            low_probs, low_scores = [], []
            for side in range(2):
                rows = slice(256 * side, 256 * side + 256)
                slot = 2 * keys + side
                bias = jnp.where((slot >= since) & (slot <= upto), -level, neg_large)
                probs = jnp.exp(scores[rows] + bias)
                low_probs.append(probs.astype(jnp.bfloat16))
                low_scores.append((probs * (grad_probs[rows] - delta)).astype(jnp.bfloat16))
            all_probs = jnp.concatenate(low_probs, axis=0)
            all_scores = jnp.concatenate(low_scores, axis=0)
            sum_value[keys] += lax.dot_general(
                wanted_grad, all_probs, NT, preferred_element_type=jnp.float32
            )
            sum_key[keys] += lax.dot_general(
                wanted, all_scores, NT, preferred_element_type=jnp.float32
            )
            return acc + jnp.dot(key[keys], all_scores, preferred_element_type=jnp.float32)

        sum_query[pair] = lax.fori_loop(
            low // 2, pair + 1, per_keys, jnp.zeros((HD, 2 * PATCHES), jnp.float32)
        )
        return carry

    lax.fori_loop(0, 8, per_pair, 0)
    for member in range(4):
        for frame in range(4):
            slot = 4 * (meta[0] ^ member) + (meta[1] ^ frame)
            cols = slice(256 * frame, 256 * frame + 256)
            place = pl.ds(pl.multiple_of((slot % 2) * 256, 256), 256)
            cos_now = cosine[slot]
            sin_now = sine[slot]
            for base, part in (
                (0, sum_query[slot // 2, :, place] * 0.125),
                (64, sum_key[slot // 2, :, place]),
            ):
                upper = part[0:32]
                lower = part[32:64]
                outs[member][base : base + 32, cols] = (
                    upper * cos_now + lower * sin_now
                ).astype(jnp.bfloat16)
                outs[member][base + 32 : base + 64, cols] = (
                    lower * cos_now - upper * sin_now
                ).astype(jnp.bfloat16)
            outs[member][128:192, cols] = sum_value[slot // 2, :, place].astype(jnp.bfloat16)


def call_attend_back(meta, blocks, grads, lse, mixed, cosine, sine):
    vmem = pl.BlockSpec()
    flat_pair = pltpu.VMEM((8, 2 * PATCHES, HD), jnp.bfloat16)
    turned_pair = pltpu.VMEM((8, HD, 2 * PATCHES), jnp.bfloat16)
    wide = pltpu.VMEM((8, HD, 2 * PATCHES), jnp.float32)
    return list(
        pl.pallas_call(
            attend_back_kernel,
            out_shape=tuple(
                jax.ShapeDtypeStruct((192, 4 * PATCHES), jnp.bfloat16) for _ in range(4)
            ),
            in_specs=[pl.BlockSpec(memory_space=pltpu.SMEM)] + [vmem] * 12,
            out_specs=(vmem,) * 4,
            scratch_shapes=[
                turned_pair,
                turned_pair,
                flat_pair,
                flat_pair,
                turned_pair,
                wide,
                wide,
                pltpu.VMEM((8, HD, 2 * PATCHES), jnp.float32),
            ],
            compiler_params=pltpu.CompilerParams(vmem_limit_bytes=48 * 2**20),
            cost_estimate=pl.CostEstimate(
                flops=30 * 10**9, bytes_accessed=10**7, transcendentals=10**7
            ),
            name="attend_back",
        )(meta, *blocks, *grads, lse, mixed, cosine, sine)
    )


def shards_halves(
    clean,
    noise,
    levels,
    lengths,
    order,
    step,
    w_attn,
    m_attn,
    v_attn,
    w_mlp,
    m_mlp,
    v_mlp,
    w_mod,
    m_mod,
    v_mod,
    w_io,
    m_io,
    v_io,
    vectors,
    m_vec,
    v_vec,
):
    bfloat = jnp.bfloat16
    single = jnp.float32
    ctx_index = lax.axis_index("ctx")
    tp_index = lax.axis_index("tp")
    member = ctx_index % 4
    device = jnp.stack([ctx_index, tp_index]).astype(jnp.int32)

    front_shard = call_prepare(w_attn, w_io, vectors)
    token_shard = call_tokens(after(device, front_shard), clean, noise)
    pieces = gather_swaps(token_shard)
    front_pieces = lax.all_gather(front_shard, "ctx", axis=0)
    front_meta, attend_meta, row_levels = call_place(
        after(device, pieces[1]), lengths, order, levels
    )

    count = step[0].astype(single)
    fixes = jnp.stack([1.0 / (1.0 - beta_one**count), 1.0 / (1.0 - beta_two**count)])

    half_dim = D // 2
    column = ctx_index * 128 + jnp.arange(128, dtype=jnp.int32)
    frequency = jnp.exp(-math.log(10000.0) * (column % half_dim).astype(single) / half_dim)
    angle = row_levels.astype(single)[:, None] * frequency[None, :]
    cond = jax.nn.silu(jnp.where(column[None, :] < half_dim, jnp.cos(angle), jnp.sin(angle)))
    cond_low = cond.astype(bfloat)
    cond_slots = cond_low[:32]
    quarter_cols = 6 * D // 4
    mod_cols = lax.dynamic_slice_in_dim(w_mod, tp_index * quarter_cols, quarter_cols, 1)
    mod_part = jnp.dot(cond_slots, mod_cols.astype(bfloat), preferred_element_type=single)
    mod_held = reduce_along_x(mod_part.reshape(8, 4, quarter_cols), ctx_index, single)
    mod_own = reduce_along_z(mod_held, ctx_index, single)
    mod_quarters = reorder_four(spread_frames(mod_own), tp_index)
    mod_all = jnp.concatenate(mod_quarters, axis=1)
    mod_rel = jnp.stack(reorder_four([mod_all[k] for k in range(4)], tp_index))
    mod_rel = mod_rel.reshape(4, 6, D)

    time_pairs = HD // 8
    side_pairs = (HD // 2 - time_pairs) // 2

    def frequencies(count):
        return 10000.0 ** (-jnp.arange(count, dtype=single) / count)

    patch = jnp.arange(PATCHES, dtype=jnp.int32)
    half_position = attend_meta[2:].astype(single)
    time_angle = half_position[:, None] * frequencies(time_pairs)[None, :]
    height_angle = frequencies(side_pairs)[:, None] * (patch // GRID).astype(single)[None, :]
    width_angle = frequencies(side_pairs)[:, None] * (patch % GRID).astype(single)[None, :]
    side_angle = jnp.concatenate([height_angle, width_angle], axis=0)

    def full_table(time_part, side_part):
        return jnp.concatenate(
            [
                jnp.broadcast_to(time_part[:, :, None], (HALF_SLOTS, time_pairs, PATCHES)),
                jnp.broadcast_to(side_part[None], (HALF_SLOTS, 2 * side_pairs, PATCHES)),
            ],
            axis=1,
        )

    cosine = full_table(jnp.cos(time_angle), jnp.cos(side_angle))
    sine = full_table(jnp.sin(time_angle), jnp.sin(side_angle))
    signal_scale, noise_scale, weight = plan(row_levels)
    weight_sum = PATCHES * jnp.sum(weight[:32])
    token_scales = jnp.concatenate([signal_scale[64:68], noise_scale[64:68]])
    loss_scales = jnp.stack([weight[64], 2.0 / clean.shape[1] * weight[64] / weight_sum])

    front_meta = after(front_meta, mod_rel, cosine, sine, token_scales, loss_scales, fixes)
    quarters = spread_frames(call_pick(front_meta, pieces))
    front_all, mid_all, hidden_frames, resid_in, *head_blocks, noisy_low, target, mod_own = (
        call_front(front_meta, token_scales, front_pieces, quarters, mod_rel, cosine, sine)
    )
    hidden_one = hidden_frames.reshape(4 * PATCHES, D)

    out_w = mid_all[:, :256]

    def exchange(blocks):
        return [blocks[0]] + [swap(blocks[k], "ctx", k) for k in (1, 2, 3)]

    head_in = exchange(head_blocks)
    mlp_shard = after(w_mlp.astype(bfloat), head_in[1], head_in[2])
    mlp_w = lax.all_gather(mlp_shard, "ctx", axis=1, tiled=True)
    mixed_blocks, lse, mixed = call_attend(attend_meta, head_in)
    mix_low = jnp.concatenate(reorder_four(exchange(mixed_blocks), member), axis=0)

    def project(left, right, dims):
        pairs = []
        for base in (2 * PATCHES, 0):
            part = lax.dot_general(
                left[:, base : base + 2 * PATCHES], right, dims, preferred_element_type=single
            )
            pairs.append((part[:PATCHES], part[PATCHES:].astype(bfloat)))
        return pairs[1], pairs[0]

    near, far = project(mix_low, out_w, (((0,), (1,)), ((), ())))
    attn_out, resid_mid, hidden_own = row_call(
        middle_kernel,
        "middle",
        (frame_low(), frame_f32(), frame_low()),
        *sum_frames(near, sum_across(far)),
        resid_in,
        mod_own,
    )
    hidden_list = spread_frames(hidden_own)
    wide = (2 * PATCHES, w_mlp.shape[2])
    wide_low = jax.ShapeDtypeStruct(wide, bfloat)
    far = call_mlp(mlp_kernel, "mlp", (wide_low, wide_low), *hidden_list[2:], mlp_w)
    across = sum_across(far)
    near = call_mlp(
        mlp_kernel,
        "mlp",
        (wide_low, wide_low),
        after(hidden_list[0], across),
        hidden_list[1],
        mlp_w,
    )
    active, slope = (near[2], far[2]), (near[3], far[3])
    grad_own, grad_three, head_rows, grad_gate_two, error_part = row_call(
        loss_kernel,
        "loss",
        (
            frame_low(),
            frame_f32(),
            jax.ShapeDtypeStruct((136, D), single),
            jax.ShapeDtypeStruct((1, D), single),
            jax.ShapeDtypeStruct((1, 128), single),
        ),
        loss_scales,
        *sum_frames(near[:2], across),
        resid_mid,
        mod_own,
        mid_all,
        target,
        smem=1,
    )
    grad_list = [grad_own, swap(grad_own, "tp", 1)]
    near = call_mlp(mlp_back_kernel, "mlp_back", (wide_low,), *grad_list, mlp_w, slope[0])
    grad_across = after(swap(grad_own, "tp", 2), near[0])
    grad_list += [grad_across, swap(grad_across, "tp", 1)]
    far = call_mlp(
        mlp_back_kernel,
        "mlp_back",
        (wide_low,),
        *grad_list[2:],
        mlp_w,
        slope[1],
    )
    across = sum_across(far)
    weight_grad = call_weight_grad(
        hidden_list, grad_list, (near[2], after(far[2], across)), active
    )
    grad_low, grad_mid, rows_two = row_call(
        second_kernel,
        "second",
        (frame_low(), frame_f32(), jax.ShapeDtypeStruct((3, D), single)),
        *sum_frames(near[:2], across),
        after(resid_mid, weight_grad),
        mod_own,
        grad_three,
        attn_out,
    )
    back_list = spread_frames(grad_low)
    grad_attn_low = jnp.concatenate(back_list, axis=0)
    grad_mix = lax.dot_general(
        out_w, grad_attn_low, (((0,), (1,)), ((), ())), preferred_element_type=single
    ).astype(bfloat)
    grad_blocks = reorder_four([grad_mix[HD * k : HD * k + HD] for k in range(4)], member)
    grad_in_blocks = exchange(grad_blocks)
    out_held, out_away = call_head_grad(device, mix_low, after(grad_attn_low, grad_mix))
    out_came = swap(out_away, "ctx", 1)
    grad_in_blocks[0] = after(grad_in_blocks[0], out_held)
    scattered = lax.psum_scatter(
        after(weight_grad, grad_low), "ctx", scatter_dimension=0, tiled=True
    )
    back_blocks = call_attend_back(attend_meta, head_in, grad_in_blocks, lse, mixed, cosine, sine)
    grad_qkv, *parts = call_qkv_back(attend_meta, exchange(back_blocks), front_all)
    near, far = parts[:2], parts[2:]
    across = sum_across(far)
    first_terms = sum_frames(near, across)
    qkv_held, qkv_away = call_head_grad(device, after(grad_qkv, across), hidden_one)
    qkv_came = swap(qkv_away, "ctx", 1)
    group_f32 = jax.ShapeDtypeStruct((IO_ROWS, D), single)
    group_low = jax.ShapeDtypeStruct((IO_ROWS, D), bfloat)
    mod_rows, *io_parts, _ = row_call(
        first_kernel,
        "first",
        (
            jax.ShapeDtypeStruct((MOD_ROWS, 128), bfloat),
            group_f32,
            group_low,
            group_f32,
            group_low,
            jax.ShapeDtypeStruct((4 * IO_ROWS, D), single),
        ),
        device,
        *first_terms,
        after(resid_in, qkv_held),
        mod_own,
        grad_mid,
        noisy_low,
        rows_two,
        grad_gate_two,
        head_rows,
        smem=1,
    )
    io_held, io_away = row_call(
        side_kernel,
        "side",
        (
            jax.ShapeDtypeStruct((4, IO_ROWS, 128), single),
            jax.ShapeDtypeStruct((4 * IO_ROWS + MOD_ROWS, 128), bfloat),
        ),
        device,
        *sum_frames(io_parts[:2], sum_across(io_parts[2:])),
        mod_rows,
        smem=1,
    )
    z_rows = jax.ShapeDtypeStruct((ATTN_ROWS + IO_ROWS + 2 * MOD_ROWS, 128), bfloat)
    qkv_own, io_own, *z_pieces = row_call(
        merge_kernel,
        "merge",
        (
            jax.ShapeDtypeStruct((ATTN_ROWS, 128), single),
            jax.ShapeDtypeStruct((IO_ROWS, 128), single),
            jax.ShapeDtypeStruct((2 * MOD_ROWS, 128), bfloat),
            z_rows,
            z_rows,
            z_rows,
        ),
        device,
        qkv_held,
        qkv_came,
        out_held,
        out_came,
        io_held,
        swap(io_away, "ctx", 1),
        mod_rows,
        smem=1,
    )
    red_attn, spread = row_call(
        finish_kernel,
        "finish",
        (
            jax.ShapeDtypeStruct((4, 128, 256), single),
            jax.ShapeDtypeStruct((8 * MOD_ROWS + 2 * IO_ROWS + 16, 128), bfloat),
        ),
        qkv_own,
        io_own,
        z_pieces[0],
        *(swap(piece, "ctx", 2 * bit) for bit, piece in zip((1, 2, 3), z_pieces[1:])),
        row_call(square_kernel, "square", (jax.ShapeDtypeStruct((1, 128), single),), scattered)[0],
        error_part,
    )
    all_rows, red_vec, io_grad, square = call_mod_grad(device, cond_low, spread_frames(spread))
    terms = sum_terms(square)
    loaded = call_preload((w_mod, m_mod, v_mod), terms[0])
    updated = call_adam(
        fixes,
        terms,
        (red_attn, scattered, cond_low, all_rows),
        (w_io, m_io, v_io, io_grad[: 2 * 128].reshape(2, 128, 128)),
        (vectors, m_vec, v_vec, red_vec),
        ((w_attn, m_attn, v_attn), (w_mlp, m_mlp, v_mlp), loaded),
    )
    return (updated[21][1, 64] / weight_sum, updated[21][0, 0], *updated[:21])


def solution(mesh):
    halves = mesh.shape["ctx"] == 8 and mesh.shape["tp"] == 4
    placed = (
        P("ctx", None),
        P("ctx", None),
        P(),
        P(),
        P(),
        P(),
        P(None, "ctx", "tp"),
        P(None, "ctx", "tp"),
        P(None, "ctx", "tp"),
        P(None, "ctx", "tp"),
        P(None, "ctx", "tp"),
        P(None, "ctx", "tp"),
        P("ctx", None),
        P("ctx", None),
        P("ctx", None),
        P(None, None, "ctx"),
        P(None, None, "ctx"),
        P(None, None, "ctx"),
        P(None, "ctx"),
        P(None, "ctx"),
        P(None, "ctx"),
    )
    return jax.shard_map(
        shards_halves if halves else shards,
        mesh=mesh,
        in_specs=placed,
        out_specs=(
            P(),
            P(),
            P(None, "ctx", "tp"),
            P(None, "ctx", "tp"),
            P(None, "ctx", "tp"),
            P(None, "ctx", "tp"),
            P(None, "ctx", "tp"),
            P(None, "ctx", "tp"),
            P(None, "ctx", "tp"),
            P(None, "ctx", "tp"),
            P("ctx", None),
            P("ctx", None),
            P("ctx", None),
            P("ctx", None),
            P(None, None, "ctx"),
            P(None, None, "ctx"),
            P(None, "ctx"),
            P(None, "ctx"),
            P(None, None, "ctx"),
            P(None, "ctx"),
            P(None, "ctx"),
            P(None, "ctx"),
            P(None, "ctx"),
        ),
        check_vma=False,
    )
```

```python
import functools
import math

import jax
import jax.numpy as jnp
from jax import lax
from jax.experimental import pallas as pl
from jax.experimental.pallas import tpu as pltpu
from jax.sharding import PartitionSpec as P

D = 1024
HD = 64
GRID = 16
PATCHES = 256
LEVELS = 1000


ln_eps = 1e-06
snr_limit = 5.0
clip_limit = 0.001
beta_one = 0.9
beta_two = 0.999
adam_eps = 1e-08
rate_matrix = 0.05
rate_vector = 0.3
decay_rate = 0.1
neg_large = -1e30


def clip_starts(frame_ids, lengths):
    clip_ends = jnp.cumsum(lengths)
    before = (clip_ends[None, :] <= frame_ids[:, None]).astype(jnp.int32)
    return jnp.sum(before * lengths[None, :], axis=1)


def plan(levels):
    fraction = (levels.astype(jnp.float32) + 1.0) / (LEVELS + 1.0)
    signal_scale = jnp.cos(0.5 * math.pi * fraction)
    noise_scale = jnp.sin(0.5 * math.pi * fraction)
    snr_value = signal_scale * signal_scale / (noise_scale * noise_scale)
    weight = jnp.minimum(snr_value, snr_limit) / (snr_value + 1.0)
    return (signal_scale, noise_scale, weight)


def condition(levels, width):
    half_dim = width // 2
    frequency = jnp.exp(-math.log(10000.0) * jnp.arange(half_dim, dtype=jnp.float32) / half_dim)
    angle_tab = levels.astype(jnp.float32)[:, None] * frequency[None, :]
    return jax.nn.silu(jnp.concatenate([jnp.cos(angle_tab), jnp.sin(angle_tab)], axis=1))


def rope_tables(time_pos, height_pos, width_pos, head_dim):
    pair_count = head_dim // 2
    time_pairs = head_dim // 8
    height_pairs = (pair_count - time_pairs) // 2
    width_pairs = pair_count - time_pairs - height_pairs

    def angles(position, count):
        frequency = 10000.0 ** (-jnp.arange(count, dtype=jnp.float32) / count)
        return position.astype(jnp.float32)[:, None] * frequency[None, :]

    angle_tab = jnp.concatenate(
        [
            angles(time_pos, time_pairs),
            angles(height_pos, height_pairs),
            angles(width_pos, width_pairs),
        ],
        axis=1,
    )
    return (jnp.cos(angle_tab), jnp.sin(angle_tab))


def rotate(values, cosine, sine):
    half_dim = values.shape[-1] // 2
    first_half = values[..., :half_dim]
    second_half = values[..., half_dim:]
    cosine = cosine[:, None, :]
    sine = sine[:, None, :]
    return jnp.concatenate(
        [first_half * cosine - second_half * sine, second_half * cosine + first_half * sine],
        axis=-1,
    )


def rotate_back(grads, cosine, sine):
    half_dim = grads.shape[-1] // 2
    first_half = grads[..., :half_dim]
    second_half = grads[..., half_dim:]
    cosine = cosine[:, None, :]
    sine = sine[:, None, :]
    return jnp.concatenate(
        [first_half * cosine + second_half * sine, second_half * cosine - first_half * sine],
        axis=-1,
    )


def layer_norm(values):
    centred = values - jnp.mean(values, axis=-1, keepdims=True)
    inv_std = lax.rsqrt(jnp.mean(centred * centred, axis=-1, keepdims=True) + ln_eps)
    return (centred * inv_std, inv_std)


def norm_back(grad_in, normed, inv_std):
    mean_grad = jnp.mean(grad_in, axis=-1, keepdims=True)
    mean_proj = jnp.mean(grad_in * normed, axis=-1, keepdims=True)
    return inv_std * (grad_in - mean_grad - normed * mean_proj)


def gelu_slope(values):
    return 0.5 * (1.0 + lax.erf(values / math.sqrt(2.0))) + values * jnp.exp(
        -0.5 * values * values
    ) / math.sqrt(2.0 * math.pi)


def stretch_mask(query_stretch, key_stretch, stretch_frames, lengths):
    offsets = jnp.arange(stretch_frames, dtype=jnp.int32)
    query_frames = query_stretch * stretch_frames + offsets
    key_frames = key_stretch * stretch_frames + offsets
    starts = clip_starts(query_frames, lengths)
    return (key_frames[None, :] <= query_frames[:, None]) & (key_frames[None, :] >= starts[:, None])


def expand_mask(allowed):
    return jnp.repeat(jnp.repeat(allowed, PATCHES, axis=0), PATCHES, axis=1)


def online_step(current, query_block, key_block, value_block, keep, scale):
    run_max, run_sum, run_acc = current
    scores = (
        jnp.einsum("qhe,khe->hqk", query_block, key_block, preferred_element_type=jnp.float32)
        * scale
    )
    scores = jnp.where(keep[None], scores, neg_large)
    new_max = jnp.maximum(run_max, jnp.max(scores, axis=-1))
    probs = jnp.where(keep[None], jnp.exp(scores - new_max[..., None]), 0.0)
    shrink = jnp.exp(run_max - new_max)
    run_sum = run_sum * shrink + jnp.sum(probs, axis=-1)
    added = jnp.einsum(
        "hqk,khe->qhe", probs.astype(jnp.bfloat16), value_block, preferred_element_type=jnp.float32
    )
    run_acc = run_acc * jnp.transpose(shrink)[:, :, None] + added
    return (new_max, run_sum, run_acc)


def pair_grads(
    query_block, grad_block, lse_block, delta_block, key_block, value_block, keep, scale
):
    scores = (
        jnp.einsum("qhe,khe->hqk", query_block, key_block, preferred_element_type=jnp.float32)
        * scale
    )
    probs = jnp.where(keep[None], jnp.exp(scores - lse_block[..., None]), 0.0)
    grad_probs = jnp.einsum(
        "qhe,khe->hqk", grad_block, value_block, preferred_element_type=jnp.float32
    )
    grad_scores = (probs * (grad_probs - delta_block[..., None])).astype(jnp.bfloat16)
    grad_query = (
        jnp.einsum("hqk,khe->qhe", grad_scores, key_block, preferred_element_type=jnp.float32)
        * scale
    )
    grad_key = (
        jnp.einsum("hqk,qhe->khe", grad_scores, query_block, preferred_element_type=jnp.float32)
        * scale
    )
    grad_value = jnp.einsum(
        "hqk,qhe->khe", probs.astype(jnp.bfloat16), grad_block, preferred_element_type=jnp.float32
    )
    return (grad_query, grad_key, grad_value)


def adam(weight_now, first_mom, second_mom, grad, factor, count, rate, decay):
    grad = grad * factor
    first_mom = beta_one * first_mom + (1.0 - beta_one) * grad
    second_mom = beta_two * second_mom + (1.0 - beta_two) * grad * grad
    first_hat = first_mom / (1.0 - beta_one**count)
    second_hat = second_mom / (1.0 - beta_two**count)
    updated = weight_now - rate * (
        first_hat / (jnp.sqrt(second_hat) + adam_eps) + decay * weight_now
    )
    return (updated, first_mom, second_mom, updated.astype(jnp.bfloat16))


def shards(
    clean,
    noise,
    levels,
    lengths,
    order,
    step,
    w_attn,
    m_attn,
    v_attn,
    w_mlp,
    m_mlp,
    v_mlp,
    w_mod,
    m_mod,
    v_mod,
    w_io,
    m_io,
    v_io,
    vectors,
    m_vec,
    v_vec,
):
    ctx_count = lax.axis_size("ctx")
    ctx_index = lax.axis_index("ctx")
    tp_index = lax.axis_index("tp")
    tok_rows = clean.shape[0]
    feat_dim = clean.shape[1]
    frames_dev = tok_rows // PATCHES
    stretch_frames = frames_dev // 2
    stretch_rows = stretch_frames * PATCHES
    scale = HD ** (-0.5)
    bfloat = jnp.bfloat16
    single = jnp.float32
    attn_w, mlp_w, mod_w, io_w, vec_low = (
        lax.all_gather(w_attn.astype(bfloat), "ctx", axis=1, tiled=True),
        lax.all_gather(w_mlp.astype(bfloat), "ctx", axis=1, tiled=True),
        lax.all_gather(w_mod.astype(bfloat), "ctx", axis=0, tiled=True),
        lax.all_gather(w_io.astype(bfloat), "ctx", axis=2, tiled=True),
        lax.all_gather(vectors.astype(bfloat), "ctx", axis=1, tiled=True),
    )
    vec_w = vec_low.astype(single)
    local_width = attn_w.shape[2]
    heads_dev = local_width // HD
    frame_count = levels.shape[0]
    local_stretches = lax.dynamic_slice_in_dim(order, 2 * ctx_index, 2, 0)
    frame_ids = (
        local_stretches[:, None] * stretch_frames
        + jnp.arange(stretch_frames, dtype=jnp.int32)[None, :]
    ).reshape(frames_dev)
    table_hit = frame_ids[:, None] == jnp.arange(frame_count, dtype=jnp.int32)[None, :]
    frame_levels = jnp.sum(jnp.where(table_hit, levels[None, :], 0), axis=1)
    starts = clip_starts(frame_ids, lengths)
    signal_scale, noise_scale, weight = plan(frame_levels)
    signal_col = signal_scale[:, None, None]
    noise_col = noise_scale[:, None, None]
    clean_full = clean.astype(single).reshape(frames_dev, PATCHES, feat_dim)
    noise_full = noise.astype(single).reshape(frames_dev, PATCHES, feat_dim)
    noisy = signal_col * clean_full + noise_col * noise_full
    target = signal_col * noise_full - noise_col * clean_full
    noisy_low = noisy.reshape(tok_rows, feat_dim).astype(bfloat)
    embedded = jnp.dot(noisy_low, io_w[0], preferred_element_type=single) + vec_w[6]
    cond_low = condition(frame_levels, D).astype(bfloat)
    modulate = (
        jnp.dot(cond_low, mod_w, preferred_element_type=single) + vec_w[:6].reshape(6 * D)
    ).reshape(frames_dev, 6, 1, D)
    patch_ids = jnp.arange(PATCHES, dtype=jnp.int32)
    time_pos = jnp.repeat(frame_ids - starts, PATCHES)
    height_pos = jnp.tile(patch_ids // GRID, frames_dev)
    width_pos = jnp.tile(patch_ids % GRID, frames_dev)
    cosine, sine = rope_tables(time_pos, height_pos, width_pos, HD)
    resid_in = embedded.reshape(frames_dev, PATCHES, D)
    normed_one, inv_one = layer_norm(resid_in)
    hidden_one = (
        (normed_one * (1.0 + modulate[:, 1]) + modulate[:, 0]).reshape(tok_rows, D).astype(bfloat)
    )
    query_pre = jnp.dot(hidden_one, attn_w[0], preferred_element_type=single).reshape(
        tok_rows, heads_dev, HD
    )
    key_pre = jnp.dot(hidden_one, attn_w[1], preferred_element_type=single).reshape(
        tok_rows, heads_dev, HD
    )
    query_low = rotate(query_pre, cosine, sine).astype(bfloat)
    key_low = rotate(key_pre, cosine, sine).astype(bfloat)
    value_low = (
        jnp.dot(hidden_one, attn_w[2], preferred_element_type=single)
        .astype(bfloat)
        .reshape(tok_rows, heads_dev, HD)
    )
    query_stretches = query_low.reshape(2, stretch_rows, heads_dev, HD)
    init_state = (
        jnp.full((2, heads_dev, stretch_rows), neg_large, single),
        jnp.zeros((2, heads_dev, stretch_rows), single),
        jnp.zeros((2, stretch_rows, heads_dev, HD), single),
    )
    key_flat = key_low.reshape(tok_rows, local_width)
    value_flat = value_low.reshape(tok_rows, local_width)
    carry_state = init_state
    key_piece = lax.all_gather(key_flat, "ctx", axis=0, tiled=True)
    value_piece = lax.all_gather(value_flat, "ctx", axis=0, tiled=True)

    def per_stretch(block_num, carry_state):
        key_block = lax.dynamic_slice_in_dim(
            key_piece, block_num * stretch_rows, stretch_rows, 0
        ).reshape(stretch_rows, heads_dev, HD)
        value_block = lax.dynamic_slice_in_dim(
            value_piece, block_num * stretch_rows, stretch_rows, 0
        ).reshape(stretch_rows, heads_dev, HD)
        key_stretch = lax.dynamic_index_in_dim(order, block_num, 0, keepdims=False)
        updated = []
        for half_num in range(2):
            allowed = stretch_mask(local_stretches[half_num], key_stretch, stretch_frames, lengths)
            current = (carry_state[0][half_num], carry_state[1][half_num], carry_state[2][half_num])
            current = lax.cond(
                jnp.any(allowed),
                lambda cur, keep_mask: online_step(
                    cur,
                    query_stretches[half_num],
                    key_block,
                    value_block,
                    expand_mask(keep_mask),
                    scale,
                ),
                lambda cur, keep_mask: cur,
                current,
                allowed,
            )
            updated.append(current)
        return tuple((jnp.stack([updated[0][member], updated[1][member]]) for member in range(3)))

    run_max, run_sum, run_acc = lax.fori_loop(
        0, key_piece.shape[0] // stretch_rows, per_stretch, carry_state
    )
    mix_rows = (run_acc / jnp.transpose(run_sum, (0, 2, 1))[..., None]).reshape(
        tok_rows, heads_dev, HD
    )
    lse_stretches = run_max + jnp.log(run_sum)
    mix_low = mix_rows.reshape(tok_rows, local_width).astype(bfloat)
    attn_out = lax.psum(
        jnp.einsum("rh,dh->rd", mix_low, attn_w[3], preferred_element_type=single).astype(
            jnp.bfloat16
        ),
        "tp",
    ).astype(jnp.float32)
    attn_full = attn_out.reshape(frames_dev, PATCHES, D)
    resid_mid = resid_in + modulate[:, 2] * attn_full
    normed_two, inv_two = layer_norm(resid_mid)
    hidden_two = (
        (normed_two * (1.0 + modulate[:, 4]) + modulate[:, 3]).reshape(tok_rows, D).astype(bfloat)
    )
    upward = jnp.dot(hidden_two, mlp_w[0], preferred_element_type=single)
    activ_low = jax.nn.gelu(upward, approximate=False).astype(bfloat)
    mlp_out = lax.psum(
        jnp.einsum("rf,df->rd", activ_low, mlp_w[1], preferred_element_type=single).astype(
            jnp.bfloat16
        ),
        "tp",
    ).astype(jnp.float32)
    mlp_full = mlp_out.reshape(frames_dev, PATCHES, D)
    resid_out = resid_mid + modulate[:, 5] * mlp_full
    normed_three, inv_three = layer_norm(resid_out)
    final_low = (normed_three * vec_w[7]).reshape(tok_rows, D).astype(bfloat)
    pred = jnp.einsum("rd,pd->rp", final_low, io_w[1], preferred_element_type=single)
    diff = pred.reshape(frames_dev, PATCHES, feat_dim) - target
    error = jnp.mean(diff * diff, axis=2)
    weight_sum, error_sum = lax.psum(
        (PATCHES * jnp.sum(weight), jnp.sum(weight[:, None] * error)), "ctx"
    )
    loss_value = error_sum / weight_sum
    grad_pred = (
        (2.0 / feat_dim * weight[:, None, None] * diff / weight_sum)
        .reshape(tok_rows, feat_dim)
        .astype(bfloat)
    )
    grad_head = jnp.einsum("rp,rd->pd", grad_pred, final_low, preferred_element_type=single)
    grad_final = jnp.einsum("rp,pd->rd", grad_pred, io_w[1], preferred_element_type=single).reshape(
        frames_dev, PATCHES, D
    )
    grad_gain = jnp.sum(grad_final * normed_three, axis=(0, 1))
    grad_three = norm_back(grad_final * vec_w[7], normed_three, inv_three)
    grad_mlp_low = (modulate[:, 5] * grad_three).reshape(tok_rows, D).astype(bfloat)
    grad_gate_two = jnp.sum(grad_three * mlp_full, axis=1)
    grad_activ = jnp.einsum("rd,df->rf", grad_mlp_low, mlp_w[1], preferred_element_type=single)
    grad_down = jnp.einsum("rd,rf->df", grad_mlp_low, activ_low, preferred_element_type=single)
    grad_up_low = (grad_activ * gelu_slope(upward)).astype(bfloat)
    grad_up = jnp.einsum("rd,rf->df", hidden_two, grad_up_low, preferred_element_type=single)
    grad_hidden_two = lax.psum(
        jnp.einsum("rf,df->rd", grad_up_low, mlp_w[0], preferred_element_type=single).astype(
            jnp.bfloat16
        ),
        "tp",
    ).astype(jnp.float32)
    grad_hidden_two = grad_hidden_two.reshape(frames_dev, PATCHES, D)
    grad_shift_two = jnp.sum(grad_hidden_two, axis=1)
    grad_scale_two = jnp.sum(grad_hidden_two * normed_two, axis=1)
    grad_mid = grad_three + norm_back(grad_hidden_two * (1.0 + modulate[:, 4]), normed_two, inv_two)
    grad_attn_low = (modulate[:, 2] * grad_mid).reshape(tok_rows, D).astype(bfloat)
    grad_gate_one = jnp.sum(grad_mid * attn_full, axis=1)
    grad_outproj = jnp.einsum("rd,rh->dh", grad_attn_low, mix_low, preferred_element_type=single)
    grad_mix_low = jnp.einsum(
        "rd,dh->rh", grad_attn_low, attn_w[3], preferred_element_type=single
    ).astype(bfloat)
    delta_rows = jnp.sum(
        grad_mix_low.astype(single).reshape(tok_rows, heads_dev, HD) * mix_rows, axis=2
    )
    grad_stretches = grad_mix_low.reshape(2, stretch_rows, heads_dev, HD)
    delta_stretches = jnp.transpose(delta_rows.reshape(2, stretch_rows, heads_dev), (0, 2, 1))

    def span_back(key_block, value_block, key_stretch, grad_query_acc):
        key_sum = jnp.zeros((stretch_rows, heads_dev, HD), single)
        value_sum = jnp.zeros((stretch_rows, heads_dev, HD), single)
        query_parts = []
        for half_num in range(2):
            allowed = stretch_mask(local_stretches[half_num], key_stretch, stretch_frames, lengths)
            result = lax.cond(
                jnp.any(allowed),
                lambda keep_mask: pair_grads(
                    query_stretches[half_num],
                    grad_stretches[half_num],
                    lse_stretches[half_num],
                    delta_stretches[half_num],
                    key_block,
                    value_block,
                    expand_mask(keep_mask),
                    scale,
                ),
                lambda keep_mask: (jnp.zeros((stretch_rows, heads_dev, HD), single),) * 3,
                allowed,
            )
            query_parts.append(grad_query_acc[half_num] + result[0])
            key_sum = key_sum + result[1]
            value_sum = value_sum + result[2]
        return (
            jnp.stack(query_parts),
            key_sum.reshape(stretch_rows, local_width),
            value_sum.reshape(stretch_rows, local_width),
        )

    init_back = (
        jnp.zeros((2, stretch_rows, heads_dev, HD), single),
        jnp.zeros((ctx_count * tok_rows, local_width), single),
        jnp.zeros((ctx_count * tok_rows, local_width), single),
    )
    carry_state = init_back
    fold_key_piece = lax.all_gather(key_flat, "ctx", axis=0, tiled=True)
    fold_value_piece = lax.all_gather(value_flat, "ctx", axis=0, tiled=True)

    def per_stretch(block_num, carry_state):
        grad_query_acc, grad_keys_all, grad_values_all = carry_state
        key_block = lax.dynamic_slice_in_dim(
            fold_key_piece, block_num * stretch_rows, stretch_rows, 0
        ).reshape(stretch_rows, heads_dev, HD)
        value_block = lax.dynamic_slice_in_dim(
            fold_value_piece, block_num * stretch_rows, stretch_rows, 0
        ).reshape(stretch_rows, heads_dev, HD)
        key_stretch = lax.dynamic_index_in_dim(order, block_num, 0, keepdims=False)
        grad_query_acc, key_sum, value_sum = span_back(
            key_block, value_block, key_stretch, grad_query_acc
        )
        place = block_num * stretch_rows
        grad_keys_all = lax.dynamic_update_slice_in_dim(grad_keys_all, key_sum, place, 0)
        grad_values_all = lax.dynamic_update_slice_in_dim(grad_values_all, value_sum, place, 0)
        return (grad_query_acc, grad_keys_all, grad_values_all)

    grad_query_acc, grad_keys_all, grad_values_all = lax.fori_loop(
        0, fold_key_piece.shape[0] // stretch_rows, per_stretch, carry_state
    )
    grad_keys, grad_values = (
        lax.psum_scatter(
            grad_keys_all.astype(jnp.bfloat16), "ctx", scatter_dimension=0, tiled=True
        ).astype(jnp.float32),
        lax.psum_scatter(
            grad_values_all.astype(jnp.bfloat16), "ctx", scatter_dimension=0, tiled=True
        ).astype(jnp.float32),
    )
    grad_query = grad_query_acc.reshape(tok_rows, local_width)
    query_back = (
        rotate_back(grad_query.reshape(tok_rows, heads_dev, HD), cosine, sine)
        .reshape(tok_rows, local_width)
        .astype(bfloat)
    )
    key_back = (
        rotate_back(grad_keys.reshape(tok_rows, heads_dev, HD), cosine, sine)
        .reshape(tok_rows, local_width)
        .astype(bfloat)
    )
    value_back = grad_values.astype(bfloat)
    grad_wq = jnp.einsum("rd,rh->dh", hidden_one, query_back, preferred_element_type=single)
    grad_wk = jnp.einsum("rd,rh->dh", hidden_one, key_back, preferred_element_type=single)
    grad_wv = jnp.einsum("rd,rh->dh", hidden_one, value_back, preferred_element_type=single)
    partial_one = (
        jnp.einsum("rh,dh->rd", query_back, attn_w[0], preferred_element_type=single)
        + jnp.einsum("rh,dh->rd", key_back, attn_w[1], preferred_element_type=single)
        + jnp.einsum("rh,dh->rd", value_back, attn_w[2], preferred_element_type=single)
    )
    grad_hidden_one = (
        lax.psum(partial_one.astype(jnp.bfloat16), "tp")
        .astype(jnp.float32)
        .reshape(frames_dev, PATCHES, D)
    )
    grad_shift_one = jnp.sum(grad_hidden_one, axis=1)
    grad_scale_one = jnp.sum(grad_hidden_one * normed_one, axis=1)
    grad_in = grad_mid + norm_back(grad_hidden_one * (1.0 + modulate[:, 1]), normed_one, inv_one)
    grad_mod = jnp.stack(
        [
            grad_shift_one,
            grad_scale_one,
            grad_gate_one,
            grad_shift_two,
            grad_scale_two,
            grad_gate_two,
        ],
        axis=1,
    )
    grad_mod_w = jnp.einsum(
        "fd,fc->dc",
        cond_low,
        grad_mod.reshape(frames_dev, 6 * D).astype(bfloat),
        preferred_element_type=single,
    )
    grad_in_low = grad_in.reshape(tok_rows, D).astype(bfloat)
    grad_embed = jnp.einsum("rp,rd->pd", noisy_low, grad_in_low, preferred_element_type=single)
    grad_vec = jnp.concatenate(
        [jnp.sum(grad_mod, axis=0), jnp.sum(grad_in, axis=(0, 1))[None], grad_gain[None]], axis=0
    )
    grad_attn = jnp.stack([grad_wq, grad_wk, grad_wv, grad_outproj])
    grad_mlp = jnp.stack([grad_up, grad_down])
    grad_io = jnp.stack([grad_embed, grad_head])
    red_attn, red_mlp, red_mod, red_io, red_vec = (
        lax.psum_scatter(
            grad_attn.astype(jnp.bfloat16), "ctx", scatter_dimension=1, tiled=True
        ).astype(jnp.float32),
        lax.psum_scatter(
            grad_mlp.astype(jnp.bfloat16), "ctx", scatter_dimension=1, tiled=True
        ).astype(jnp.float32),
        lax.psum_scatter(
            grad_mod_w.astype(jnp.bfloat16), "ctx", scatter_dimension=0, tiled=True
        ).astype(jnp.float32),
        lax.psum_scatter(
            grad_io.astype(jnp.bfloat16), "ctx", scatter_dimension=2, tiled=True
        ).astype(jnp.float32),
        lax.psum_scatter(
            grad_vec.astype(jnp.bfloat16), "ctx", scatter_dimension=1, tiled=True
        ).astype(jnp.float32),
    )
    shared_sq = jnp.sum(red_mod * red_mod) + jnp.sum(red_io * red_io) + jnp.sum(red_vec * red_vec)
    own_sq = (
        jnp.sum(red_attn * red_attn)
        + jnp.sum(red_mlp * red_mlp)
        + jnp.where(tp_index == 0, shared_sq, 0.0)
    )
    grad_norm = jnp.sqrt(lax.psum(own_sq, ("ctx", "tp")))
    factor = jnp.minimum(1.0, clip_limit / (grad_norm + 1e-06))
    count = step[0].astype(single)
    attn_new = adam(w_attn, m_attn, v_attn, red_attn, factor, count, rate_matrix, decay_rate)
    mlp_new = adam(w_mlp, m_mlp, v_mlp, red_mlp, factor, count, rate_matrix, decay_rate)
    mod_new = adam(w_mod, m_mod, v_mod, red_mod, factor, count, rate_matrix, decay_rate)
    io_new = adam(w_io, m_io, v_io, red_io, factor, count, rate_matrix, decay_rate)
    vec_new = adam(vectors, m_vec, v_vec, red_vec, factor, count, rate_vector, 0.0)
    return (
        loss_value,
        grad_norm,
        attn_new[0],
        attn_new[1],
        attn_new[2],
        attn_new[3],
        mlp_new[0],
        mlp_new[1],
        mlp_new[2],
        mlp_new[3],
        mod_new[0],
        mod_new[1],
        mod_new[2],
        mod_new[3],
        io_new[0],
        io_new[1],
        io_new[2][0],
        io_new[2][1],
        io_new[3],
        vec_new[0],
        vec_new[1],
        vec_new[2],
        vec_new[3],
    )


HALF_SLOTS = 16
QKV_ROWS = 768
ATTN_ROWS = 1024
FRONT_ROWS = 912
TOKEN_ROWS = 512
IO_ROWS = 80
MOD_ROWS = 48
NT = (((1,), (1,)), ((), ()))
TN = (((0,), (0,)), ((), ()))


def swap(values, axis, bit):
    size = 8 if axis == "ctx" else 4
    return lax.ppermute(values, axis, [(i, i ^ bit) for i in range(size)])


def after(values, *others):
    return lax.optimization_barrier((values,) + others)[0]


def gather_swaps(shard):
    along_x = swap(shard, "ctx", 1)
    along_z = [swap(shard, "ctx", bit) for bit in (2, 4, 6)]
    return [shard, along_x, *along_z, swap(jnp.concatenate(along_z, axis=0), "ctx", 1)]


def reduce_blocks(blocks, ctx_index, wire):
    return reduce_along_z(reduce_along_x(blocks, ctx_index, wire), ctx_index, wire)


def reduce_along_x(blocks, ctx_index, wire):
    x = ctx_index % 2
    pairs = blocks.reshape((4, 2) + blocks.shape[1:])
    first, second = pairs[:, 0], pairs[:, 1]
    even = x == 0
    away = jnp.where(even, second, first).astype(wire)
    return jnp.where(even, first, second) + swap(away, "ctx", 1).astype(jnp.float32)


def pieces_along_z(held, ctx_index, wire):
    z = ctx_index // 2
    low = held.astype(wire)
    came = []
    for bit in (1, 2, 3):
        piece = lax.dynamic_index_in_dim(low, z ^ bit, 0, keepdims=False)
        came.append(swap(piece, "ctx", 2 * bit))
    return lax.dynamic_index_in_dim(held, z, 0, keepdims=False), came


def reduce_along_z(held, ctx_index, wire):
    total, came = pieces_along_z(held, ctx_index, wire)
    for piece in came:
        total = total + piece.astype(jnp.float32)
    return total


def spread_frames(own):
    core = swap(own, "tp", 1)
    across = swap(own, "tp", 2)
    return [own, core, across, swap(across, "tp", 1)]


def sum_across(far):
    return (far[0] + swap(far[1], "tp", 1).astype(jnp.float32)).astype(jnp.bfloat16)


def sum_frames(near, across):
    return near[0], swap(near[1], "tp", 1), swap(across, "tp", 2)


def reorder_four(items, index):
    low_bit = (index & 1) == 1
    high_bit = (index & 2) == 2
    once = [jnp.where(low_bit, items[k ^ 1], items[k]) for k in range(4)]
    return [jnp.where(high_bit, once[k ^ 2], once[k]) for k in range(4)]


def sum_terms(values):
    values = values + swap(values, "ctx", 1)
    return [values] + [swap(values, "ctx", bit) for bit in (2, 4, 6)]


def token_kernel(meta, clean, noise, ring):
    for frame in range(4):
        rows = pl.ds(pl.multiple_of(256 * frame + 64 * meta[1], 64), 64)
        ring[128 * frame : 128 * frame + 64, :] = clean[rows, :]
        ring[128 * frame + 64 : 128 * frame + 128, :] = noise[rows, :]


def prepare_kernel(w_attn, w_io, vectors, front):
    for part in range(3):
        front[256 * part : 256 * part + 256, :] = w_attn[part].T.astype(jnp.bfloat16)
    base = QKV_ROWS
    front[base : base + 128, :] = w_io[0].astype(jnp.bfloat16)
    front[base + 128 : base + 144, :] = jnp.concatenate(
        [vectors[...], jnp.zeros((8, 128), jnp.float32)], axis=0
    ).astype(jnp.bfloat16)
    for part in range(2):
        base = FRONT_ROWS + 128 * part
        front[base : base + 128, :] = w_attn[3, :, 128 * part : 128 * part + 128].astype(
            jnp.bfloat16
        )
    front[FRONT_ROWS + 256 : FRONT_ROWS + 384, :] = w_io[1].T.astype(jnp.bfloat16)


def vmem_specs(count):
    return [pl.BlockSpec(memory_space=pltpu.VMEM)] * count


def smem_specs(count):
    return [pl.BlockSpec(memory_space=pltpu.SMEM)] * count


def call_tokens(device, clean, noise):
    return pl.pallas_call(
        token_kernel,
        out_shape=jax.ShapeDtypeStruct((TOKEN_ROWS, 128), jnp.bfloat16),
        in_specs=smem_specs(1) + vmem_specs(2),
        out_specs=vmem_specs(1)[0],
        name="tokens",
    )(device, clean, noise)


def call_prepare(w_attn, w_io, vectors):
    return pl.pallas_call(
        prepare_kernel,
        out_shape=jax.ShapeDtypeStruct((FRONT_ROWS + 384, 128), jnp.bfloat16),
        in_specs=vmem_specs(3),
        out_specs=vmem_specs(1)[0],
        name="prepare",
    )(w_attn, w_io, vectors)


def place_kernel(device, lengths, order, levels, front, attend, rows, inverse, stored, position, level):
    ctx, tp = device[0], device[1]
    frames, stretches, clips = levels.shape[0], order.shape[0], lengths.shape[0]
    per_stretch = frames // stretches
    half = frames // 2

    def per_stretch_place(place, carry):
        inverse[order[place]] = place
        return carry

    lax.fori_loop(0, stretches, per_stretch_place, 0)

    def per_frame(frame, counts):
        long_count, short_count = counts
        begin, start, length = jnp.int32(0), jnp.int32(0), jnp.int32(0)
        for clip in range(clips):
            size = lengths[clip]
            inside = (frame >= begin) & (frame < begin + size)
            start = jnp.where(inside, begin, start)
            length = jnp.where(inside, size, length)
            begin = begin + size
        is_long = length == half
        slot = jnp.where(is_long, long_count, half + short_count)
        stored[slot] = inverse[lax.div(frame, jnp.int32(per_stretch))] * per_stretch + lax.rem(
            frame, jnp.int32(per_stretch)
        )
        position[slot] = frame - start
        level[slot] = levels[frame]
        grown = is_long.astype(jnp.int32)
        return (long_count + grown, short_count + 1 - grown)

    lax.fori_loop(0, frames, per_frame, (jnp.int32(0), jnp.int32(0)))

    member = ctx & 3
    for k in range(4):
        front[8 + k] = 4 * member + (tp ^ k)
        front[12 + k] = member ^ k
        at = stored[4 * ctx + (tp ^ k)]
        front[16 + k] = ((at >> 2) ^ ctx) * 4 + (at & 3)
        front[20 + k] = tp ^ k
    for k in range(8):
        front[k] = 0
    attend[0] = member
    attend[1] = tp
    base = lax.div(ctx, jnp.int32(4)) * half

    def per_slot(slot, carry):
        attend[2 + slot] = position[base + slot]
        return carry

    lax.fori_loop(0, half, per_slot, 0)

    def per_row(row, carry):
        rows[row] = level[row]
        rows[frames + row] = level[4 * (ctx ^ (row & 7)) + (row >> 3)]
        return carry

    lax.fori_loop(0, frames, per_row, 0)
    for k in range(8):
        rows[2 * frames + k] = level[4 * ctx + (tp ^ (k & 3))]


def call_place(device, lengths, order, levels):
    frames = levels.shape[0]
    return pl.pallas_call(
        place_kernel,
        out_shape=(
            jax.ShapeDtypeStruct((24,), jnp.int32),
            jax.ShapeDtypeStruct((2 + frames // 2,), jnp.int32),
            jax.ShapeDtypeStruct((2 * frames + 8,), jnp.int32),
        ),
        in_specs=smem_specs(4),
        out_specs=smem_specs(3),
        scratch_shapes=[pltpu.SMEM((order.shape[0],), jnp.int32)]
        + [pltpu.SMEM((frames,), jnp.int32)] * 3,
        name="place",
    )(device, lengths, order, levels)


def pick_kernel(meta, *refs):
    out, sems = refs[6:]
    places = [(refs[0], 0), (refs[1], 0)]
    for bit in range(3):
        places += [(refs[2 + bit], 0), (refs[5], TOKEN_ROWS * bit)]
    for frame in range(4):
        wanted = meta[16 + frame]
        for place, (source, base) in enumerate(places):

            @pl.when((wanted >> 2) == place)
            def _():
                start = pl.multiple_of(base + (wanted & 3) * 128, 128)
                pltpu.make_async_copy(
                    source.at[pl.ds(start, 128), :],
                    out.at[128 * frame : 128 * frame + 128, :],
                    sems.at[frame],
                ).start()

    for frame in range(4):
        pltpu.make_async_copy(
            refs[0].at[0:128, :], out.at[128 * frame : 128 * frame + 128, :], sems.at[frame]
        ).wait()


def hbm_specs(count):
    return [pl.BlockSpec(memory_space=pltpu.HBM)] * count


def call_pick(meta, pieces):
    return pl.pallas_call(
        pick_kernel,
        out_shape=jax.ShapeDtypeStruct((TOKEN_ROWS, 128), jnp.bfloat16),
        in_specs=smem_specs(1) + hbm_specs(6),
        out_specs=vmem_specs(1)[0],
        scratch_shapes=[pltpu.SemaphoreType.DMA((4,))],
        compiler_params=pltpu.CompilerParams(vmem_limit_bytes=56 * 2**20),
        name="pick",
    )(meta, *pieces)


def centred_norm(values):
    centred = values - jnp.mean(values, axis=-1, keepdims=True)
    inv_std = lax.rsqrt(jnp.mean(centred * centred, axis=-1, keepdims=True) + ln_eps)
    return centred * inv_std, inv_std


def front_kernel(meta, scales, *refs):
    pieces, quarters = refs[0], refs[1:5]
    mod, cosine, sine = refs[5:8]
    weights_out, mid_out, hidden_out, resid_out = refs[8:12]
    head_outs = refs[12:16]
    noisy_out, target_out, mod_out = refs[16:19]
    tokens, heads, weights, mid, hidden, resid, target, mod_own, held, sems, out_sems = refs[19:]
    spans = (slice(QKV_ROWS, FRONT_ROWS + 384), slice(0, QKV_ROWS))
    copies = [
        [
            pltpu.make_async_copy(
                pieces.at[place, span, :], held.at[place, span, :], sems.at[place, index]
            )
            for place in range(8)
        ]
        for index, span in enumerate(spans)
    ]
    for copy in copies[0] + copies[1]:
        copy.start()
    for source in range(4):
        rows = pl.ds(pl.multiple_of(meta[20 + source] * 64, 64), 64)
        for frame in range(4):
            base = 128 * (frame ^ source)
            clean = quarters[source][base : base + 64, :].astype(jnp.float32)
            noise = quarters[source][base + 64 : base + 128, :].astype(jnp.float32)
            mixed = scales[frame] * clean + scales[4 + frame] * noise
            tokens[frame, rows, :] = mixed.astype(jnp.bfloat16)
            if frame == 0:
                target[rows, :] = scales[0] * noise - scales[4] * clean
    outs = [
        pltpu.make_async_copy(tokens.at[0], noisy_out, out_sems.at[0]),
        pltpu.make_async_copy(target, target_out, out_sems.at[1]),
        pltpu.make_async_copy(weights, weights_out, out_sems.at[2]),
        pltpu.make_async_copy(resid, resid_out, out_sems.at[3]),
    ] + [
        pltpu.make_async_copy(hidden.at[frame], hidden_out.at[frame], out_sems.at[4 + frame])
        for frame in range(4)
    ]
    outs.append(pltpu.make_async_copy(mod_own, mod_out, out_sems.at[8]))
    outs.append(pltpu.make_async_copy(mid, mid_out, out_sems.at[9]))
    for place in range(8):
        copies[0][place].wait()
        block = slice(128 * place, 128 * place + 128)
        weights[QKV_ROWS:FRONT_ROWS, block] = held[place, QKV_ROWS:FRONT_ROWS, :]
        for part in range(3):
            base = FRONT_ROWS + 128 * part
            mid[block, 128 * part : 128 * part + 128] = held[place, base : base + 128, :]
    for index in (0, 1, 9):
        outs[index].start()
    embed = weights[QKV_ROWS : QKV_ROWS + 128, :]
    vec_rows = weights[QKV_ROWS + 128 : FRONT_ROWS, :].astype(jnp.float32)
    mod_own[0:6, :] = mod[0] + vec_rows[0:6]
    mod_own[6:8, :] = vec_rows[6:8]
    outs[8].start()
    for frame in range(4):
        values = jnp.dot(tokens[frame], embed, preferred_element_type=jnp.float32) + vec_rows[6:7]
        if frame == 0:
            resid[...] = values
            outs[3].start()
        normed, _ = centred_norm(values)
        shift = mod[frame, 0:1, :] + vec_rows[0:1]
        scale = mod[frame, 1:2, :] + vec_rows[1:2]
        low = (normed * (1.0 + scale) + shift).astype(jnp.bfloat16)
        hidden[frame] = low
        outs[4 + frame].start()
    for place in range(8):
        copies[1][place].wait()
        weights[0:QKV_ROWS, 128 * place : 128 * place + 128] = held[place, 0:QKV_ROWS, :]
    outs[2].start()
    for frame in range(4):
        mixed = lax.dot_general(
            weights[0:QKV_ROWS, :], hidden[frame], NT, preferred_element_type=jnp.float32
        )
        cos_now = cosine[meta[8 + frame]]
        sin_now = sine[meta[8 + frame]]
        cols = slice(256 * frame, 256 * frame + 256)
        for head in range(4):
            where_to = head
            for part in range(2):
                base = 256 * part + 64 * head
                upper = mixed[base : base + 32]
                lower = mixed[base + 32 : base + 64]
                heads[where_to, 64 * part : 64 * part + 32, cols] = (
                    upper * cos_now - lower * sin_now
                ).astype(jnp.bfloat16)
                heads[where_to, 64 * part + 32 : 64 * part + 64, cols] = (
                    lower * cos_now + upper * sin_now
                ).astype(jnp.bfloat16)
            base = 512 + 64 * head
            heads[where_to, 128:192, cols] = mixed[base : base + 64].astype(jnp.bfloat16)
    for k in range(4):
        outs.append(pltpu.make_async_copy(heads.at[meta[12 + k]], head_outs[k], out_sems.at[10 + k]))
        outs[10 + k].start()
    for copy in outs:
        copy.wait()


def call_front(meta, scales, pieces, quarters, mod, cosine, sine):
    return pl.pallas_call(
        front_kernel,
        out_shape=(
            jax.ShapeDtypeStruct((FRONT_ROWS, D), jnp.bfloat16),
            jax.ShapeDtypeStruct((D, 384), jnp.bfloat16),
            jax.ShapeDtypeStruct((4, PATCHES, D), jnp.bfloat16),
            jax.ShapeDtypeStruct((PATCHES, D), jnp.float32),
        )
        + (jax.ShapeDtypeStruct((192, 4 * PATCHES), jnp.bfloat16),) * 4
        + (
            jax.ShapeDtypeStruct((PATCHES, 128), jnp.bfloat16),
            jax.ShapeDtypeStruct((PATCHES, 128), jnp.float32),
            jax.ShapeDtypeStruct((8, D), jnp.float32),
        ),
        in_specs=smem_specs(2) + hbm_specs(1) + vmem_specs(7),
        out_specs=hbm_specs(11),
        scratch_shapes=[
            pltpu.VMEM((4, PATCHES, 128), jnp.bfloat16),
            pltpu.VMEM((4, 192, 4 * PATCHES), jnp.bfloat16),
            pltpu.VMEM((FRONT_ROWS, D), jnp.bfloat16),
            pltpu.VMEM((D, 384), jnp.bfloat16),
            pltpu.VMEM((4, PATCHES, D), jnp.bfloat16),
            pltpu.VMEM((PATCHES, D), jnp.float32),
            pltpu.VMEM((PATCHES, 128), jnp.float32),
            pltpu.VMEM((8, D), jnp.float32),
            pltpu.VMEM((8, FRONT_ROWS + 384, 128), jnp.bfloat16),
            pltpu.SemaphoreType.DMA((8, 2)),
            pltpu.SemaphoreType.DMA((14,)),
        ],
        compiler_params=pltpu.CompilerParams(vmem_limit_bytes=52 * 2**20),
        cost_estimate=pl.CostEstimate(flops=2 * 10**9, bytes_accessed=10**7, transcendentals=0),
        name="front",
    )(meta, scales, pieces, *quarters, mod, cosine, sine)


def total_own(held, came, across):
    return held[...] + came[...].astype(jnp.float32) + across[...].astype(jnp.float32)


def middle_kernel(held, came, across, resid, mod, attn_out, resid_mid, hidden):
    total = total_own(held, came, across)
    attn_out[...] = total.astype(jnp.bfloat16)
    values = resid[...] + mod[2:3, :] * total
    resid_mid[...] = values
    normed, _ = centred_norm(values)
    hidden[...] = (normed * (1.0 + mod[4:5, :]) + mod[3:4, :]).astype(jnp.bfloat16)


def row_call(kernel, name, outs, *operands, smem=0, inside=None):
    return pl.pallas_call(
        kernel,
        out_shape=tuple(outs),
        in_specs=smem_specs(smem) + (inside or vmem_specs)(len(operands) - smem),
        out_specs=vmem_specs(len(outs)),
        compiler_params=pltpu.CompilerParams(vmem_limit_bytes=32 * 2**20 if inside else 16 * 2**20),
        cost_estimate=pl.CostEstimate(flops=10**9, bytes_accessed=4 * 10**6, transcendentals=0),
        name=name,
    )(*operands)


def plain_specs(count):
    return [pl.BlockSpec()] * count


def frame_f32():
    return jax.ShapeDtypeStruct((PATCHES, D), jnp.float32)


def frame_low():
    return jax.ShapeDtypeStruct((PATCHES, D), jnp.bfloat16)


def back_through_norm(grad, normed, inv_std):
    mean_grad = jnp.mean(grad, axis=-1, keepdims=True)
    mean_proj = jnp.mean(grad * normed, axis=-1, keepdims=True)
    return inv_std * (grad - mean_grad - normed * mean_proj)


def column_sum(values):
    return jnp.sum(values, axis=0, keepdims=True)


def loss_kernel(
    scales, held, came, across, resid_mid, mod, mid, target, grad_low, grad_three, io_rows, gate, error
):
    mlp_out = total_own(held, came, across)
    values = resid_mid[...] + mod[5:6, :] * mlp_out
    normed, inv_std = centred_norm(values)
    gain = mod[7:8, :]
    final = (normed * gain).astype(jnp.bfloat16)
    head = mid[:, 256:384]
    pred = jnp.dot(final, head, preferred_element_type=jnp.float32)
    diff = pred - target[...]
    per_token = jnp.sum(diff * diff, axis=1, keepdims=True)
    error[...] = jnp.broadcast_to(
        scales[0] * jnp.sum(per_token, axis=0, keepdims=True) / diff.shape[1], error.shape
    )
    grad_pred = (scales[1] * diff).astype(jnp.bfloat16)
    grad_final = lax.dot_general(grad_pred, head, NT, preferred_element_type=jnp.float32)
    grad_gain = column_sum(grad_final * normed)
    grad = back_through_norm(grad_final * gain, normed, inv_std)
    grad_three[...] = grad
    grad_low[...] = (mod[5:6, :] * grad).astype(jnp.bfloat16)
    gate[...] = column_sum(grad * mlp_out)
    io_rows[0:128, :] = lax.dot_general(grad_pred, final, TN, preferred_element_type=jnp.float32)
    io_rows[128:136, :] = jnp.concatenate([grad_gain, jnp.zeros((7, D), jnp.float32)], axis=0)


def second_kernel(
    held, came, across, resid_mid, mod, grad_three, attn_out, grad_low, grad_mid, rows
):
    grad_hidden = total_own(held, came, across)
    normed, inv_std = centred_norm(resid_mid[...])
    grad = grad_three[...] + back_through_norm(grad_hidden * (1.0 + mod[4:5, :]), normed, inv_std)
    grad_mid[...] = grad
    grad_low[...] = (mod[2:3, :] * grad).astype(jnp.bfloat16)
    rows[0:1, :] = column_sum(grad * attn_out[...].astype(jnp.float32))
    rows[1:2, :] = column_sum(grad_hidden)
    rows[2:3, :] = column_sum(grad_hidden * normed)


def first_kernel(
    device,
    held,
    came,
    across,
    resid,
    mod,
    grad_mid,
    noisy,
    rows_two,
    gate_two,
    head_rows,
    mod_rows,
    near_held,
    near_away,
    far_held,
    far_away,
    io_rows,
):
    grad_hidden = total_own(held, came, across)
    normed, inv_std = centred_norm(resid[...])
    grad = grad_mid[...] + back_through_norm(grad_hidden * (1.0 + mod[1:2, :]), normed, inv_std)
    rows = [
        column_sum(grad_hidden),
        column_sum(grad_hidden * normed),
        rows_two[0:1, :],
        rows_two[1:2, :],
        rows_two[2:3, :],
        gate_two[...],
    ]
    blocks = [row[:, 128 * k : 128 * k + 128] for row in rows for k in range(8)]
    mod_rows[...] = jnp.concatenate(blocks, axis=0).astype(jnp.bfloat16)
    io_rows[0:128, :] = lax.dot_general(
        noisy[...], grad.astype(jnp.bfloat16), TN, preferred_element_type=jnp.float32
    )
    io_rows[128:256, :] = head_rows[0:128, :]
    io_rows[256:264, :] = jnp.concatenate(
        [column_sum(grad), head_rows[128:129, :], jnp.zeros((6, D), jnp.float32)], axis=0
    )
    io_rows[264:320, :] = jnp.zeros((56, D), jnp.float32)
    for k, out in enumerate((near_held, near_away, far_held, far_away)):
        group = pl.ds(pl.multiple_of(IO_ROWS * (device[1] ^ k), 16), IO_ROWS)
        out[...] = io_rows[group, :].astype(out.dtype)


def side_kernel(device, held, came, across, mod_rows, keep, away):
    total = total_own(held, came, across)
    side = device[0] & 1
    for block in range(8):
        piece = total[:, 128 * block : 128 * block + 128]

        @pl.when(side == block % 2)
        def _():
            keep[block // 2] = piece

        @pl.when(side != block % 2)
        def _():
            away[IO_ROWS * (block // 2) : IO_ROWS * (block // 2) + IO_ROWS, :] = piece.astype(
                jnp.bfloat16
            )

    away[4 * IO_ROWS :, :] = mod_rows[...]


def merge_kernel(
    device, held, came, out_held, out_came, io_held, io_came, mod_rows, own, io_own, *outs
):
    z = device[0] >> 1
    for bit in range(4):
        total = jnp.concatenate(
            [
                held[z ^ bit] + came[z ^ bit].astype(jnp.float32),
                out_held[z ^ bit] + out_came[z ^ bit].astype(jnp.float32),
            ],
            axis=0,
        )
        rows = pl.ds(pl.multiple_of(IO_ROWS * (z ^ bit), 16), IO_ROWS)
        io_total = io_held[z ^ bit] + io_came[rows, :].astype(jnp.float32)
        if bit == 0:
            own[...] = total
            io_own[...] = io_total
        else:
            out = outs[bit]
            out[0:ATTN_ROWS, :] = total.astype(jnp.bfloat16)
            out[ATTN_ROWS : ATTN_ROWS + IO_ROWS, :] = io_total.astype(jnp.bfloat16)
            base = ATTN_ROWS + IO_ROWS
            out[base : base + MOD_ROWS, :] = mod_rows[...]
            out[base + MOD_ROWS : base + 2 * MOD_ROWS, :] = io_came[4 * IO_ROWS :, :]
    outs[0][0:MOD_ROWS, :] = mod_rows[...]
    outs[0][MOD_ROWS : 2 * MOD_ROWS, :] = io_came[4 * IO_ROWS :, :]


def mod_grad_kernel(device, cond, *refs):
    parts = refs[:4]
    rows_out, vector, io_grad, square, rows = refs[4:]
    base = 8 * MOD_ROWS + 2 * IO_ROWS
    terms = []
    for index in range(4):
        owner = device[1] ^ index
        block = parts[index][0 : 8 * MOD_ROWS, :].astype(jnp.float32)
        for frame in range(8):
            for k in range(MOD_ROWS):
                at = MOD_ROWS * frame + k
                rows[owner, frame : frame + 1, 128 * k : 128 * k + 128] = block[at : at + 1, :]
        group = pl.ds(pl.multiple_of(IO_ROWS * owner, 16), IO_ROWS)
        high = parts[index][8 * MOD_ROWS : 8 * MOD_ROWS + IO_ROWS, :].astype(jnp.float32)
        rest = parts[index][8 * MOD_ROWS + IO_ROWS : base, :].astype(jnp.float32)
        io_grad[group, :] = high + rest
        terms.append(column_sum(parts[index][base : base + 16, :].astype(jnp.float32)))
    total = jnp.zeros((1, 1), jnp.float32)
    for index in range(6):
        cols = slice(D * index, D * index + D)
        low = rows[:, :, cols].reshape(32, D)
        rows_out[:, cols] = low.astype(jnp.bfloat16)
        part = lax.dot_general(
            cond[32:64, :], low.astype(jnp.bfloat16), TN, preferred_element_type=jnp.float32
        )
        total = total + jnp.sum(column_sum(part * part), axis=1, keepdims=True)
        own = pl.ds(pl.multiple_of(D * index + 128 * device[0], 128), 128)
        vector[index : index + 1, :] = column_sum(rows[:, :, own].reshape(32, 128))
    vector[6:8, :] = io_grad[256:258, :]
    mixed = vector[0:6, :]
    total = total + jnp.sum(column_sum(mixed * mixed), axis=1, keepdims=True)
    left = lax.broadcasted_iota(jnp.int32, (1, 128), 1) < 64
    square[...] = ((terms[0] + terms[1]) + (terms[2] + terms[3])) + jnp.where(left, total, 0.0)


def call_mod_grad(device, cond, parts):
    return pl.pallas_call(
        mod_grad_kernel,
        out_shape=(
            jax.ShapeDtypeStruct((32, 6 * D), jnp.bfloat16),
            jax.ShapeDtypeStruct((8, 128), jnp.float32),
            jax.ShapeDtypeStruct((4 * IO_ROWS, 128), jnp.float32),
            jax.ShapeDtypeStruct((1, 128), jnp.float32),
        ),
        in_specs=smem_specs(1) + vmem_specs(5),
        out_specs=vmem_specs(4),
        scratch_shapes=[pltpu.VMEM((4, 8, 6 * D), jnp.float32)],
        compiler_params=pltpu.CompilerParams(vmem_limit_bytes=12 * 2**20),
        cost_estimate=pl.CostEstimate(flops=10**8, bytes_accessed=4 * 10**6, transcendentals=0),
        name="mod_grad",
    )(device, cond, *parts)


def mlp_kernel(first, second, weights, held, away, active, slope):
    for frame, source in enumerate((first, second)):
        rows = slice(256 * frame, 256 * frame + 256)
        upward = jnp.dot(source[...], weights[0], preferred_element_type=jnp.float32)
        inner = 0.5 * (1.0 + lax.erf(upward * (1.0 / math.sqrt(2.0))))
        low = (upward * inner).astype(jnp.bfloat16)
        active[rows, :] = low
        change = inner + upward * jnp.exp(-0.5 * upward * upward) * (
            1.0 / math.sqrt(2.0 * math.pi)
        )
        slope[rows, :] = change.astype(jnp.bfloat16)
        part = lax.dot_general(low, weights[1], NT, preferred_element_type=jnp.float32)
        if frame:
            away[...] = part.astype(jnp.bfloat16)
        else:
            held[...] = part


def mlp_back_kernel(first, second, weights, slope, held, away, grad_up):
    for frame, source in enumerate((first, second)):
        rows = slice(256 * frame, 256 * frame + 256)
        grad = jnp.dot(source[...], weights[1], preferred_element_type=jnp.float32)
        low = (grad * slope[rows, :].astype(jnp.float32)).astype(jnp.bfloat16)
        grad_up[rows, :] = low
        part = lax.dot_general(low, weights[0], NT, preferred_element_type=jnp.float32)
        if frame:
            away[...] = part.astype(jnp.bfloat16)
        else:
            held[...] = part


def call_mlp(kernel, name, outs, *operands):
    return pl.pallas_call(
        kernel,
        out_shape=(frame_f32(), frame_low()) + outs,
        in_specs=vmem_specs(len(operands)),
        out_specs=vmem_specs(2 + len(outs)),
        compiler_params=pltpu.CompilerParams(vmem_limit_bytes=16 * 2**20),
        cost_estimate=pl.CostEstimate(
            flops=4 * 10**9, bytes_accessed=2 * 10**7, transcendentals=10**6
        ),
        name=name,
    )(*operands)


def weight_grad_kernel(*refs):
    hidden, grads = refs[:4], refs[4:8]
    grad_up, active = refs[8:10], refs[10:12]
    result, out, sems = refs[12:]
    width = active[0].shape[1]
    copies = []
    for index, (left, right) in enumerate(((hidden, grad_up), (grads, active))):
        total = jnp.zeros((D, width), jnp.float32)
        for frame in range(4):
            rows = slice(256 * (frame % 2), 256 * (frame % 2) + 256)
            total = total + lax.dot_general(
                left[frame][...],
                right[frame // 2][rows, :],
                TN,
                preferred_element_type=jnp.float32,
            )
        out[index] = total.astype(jnp.bfloat16)
        copies.append(
            pltpu.make_async_copy(
                out.at[index], result.at[:, width * index : width * index + width], sems.at[index]
            )
        )
        copies[index].start()
    for copy in copies:
        copy.wait()


def call_weight_grad(hidden, grads, grad_up, active):
    operands = (*hidden, *grads, *grad_up, *active)
    return pl.pallas_call(
        weight_grad_kernel,
        out_shape=jax.ShapeDtypeStruct((D, 2 * active[0].shape[1]), jnp.bfloat16),
        in_specs=vmem_specs(len(operands)),
        out_specs=hbm_specs(1)[0],
        scratch_shapes=[
            pltpu.VMEM((2, D, active[0].shape[1]), jnp.bfloat16),
            pltpu.SemaphoreType.DMA((2,)),
        ],
        compiler_params=pltpu.CompilerParams(vmem_limit_bytes=20 * 2**20),
        cost_estimate=pl.CostEstimate(flops=5 * 10**9, bytes_accessed=2 * 10**7, transcendentals=0),
        name="weight_grad",
    )(*operands)


def side_blocks(device, total, held, away):
    side = device[0] & 1
    for z in range(4):
        held[z] = total[:, pl.ds(pl.multiple_of(256 * z + 128 * side, 128), 128)]
        away[z] = total[:, pl.ds(pl.multiple_of(256 * z + 128 * (1 - side), 128), 128)].astype(
            jnp.bfloat16
        )


def head_grad_kernel(device, left, right, held, away, total):
    total[...] = jnp.dot(left[...], right[...], preferred_element_type=jnp.float32)
    side_blocks(device, total, held, away)


def call_head_grad(device, left, right):
    rows = left.shape[0]
    return pl.pallas_call(
        head_grad_kernel,
        out_shape=(
            jax.ShapeDtypeStruct((4, rows, 128), jnp.float32),
            jax.ShapeDtypeStruct((4, rows, 128), jnp.bfloat16),
        ),
        in_specs=smem_specs(1) + vmem_specs(2),
        out_specs=vmem_specs(2),
        scratch_shapes=[pltpu.VMEM((rows, D), jnp.float32)],
        compiler_params=pltpu.CompilerParams(vmem_limit_bytes=12 * 2**20),
        cost_estimate=pl.CostEstimate(flops=2 * 10**9, bytes_accessed=10**7, transcendentals=0),
        name="head_grad",
    )(device, left, right)


def qkv_back_kernel(meta, *refs):
    blocks, weights = refs[:4], refs[4]
    grads, near_held, near_away, far_held, far_away = refs[5:]
    for k in range(4):
        head = meta[0] ^ k
        for part in range(3):
            rows = pl.ds(pl.multiple_of(256 * part + 64 * head, 64), 64)
            grads[rows, :] = blocks[k][64 * part : 64 * part + 64, :]
    for frame, out in ((2, far_held), (3, far_away), (0, near_held), (1, near_away)):
        part = lax.dot_general(
            grads[:, 256 * frame : 256 * frame + 256],
            weights[0:QKV_ROWS, :],
            TN,
            preferred_element_type=jnp.float32,
        )
        out[...] = part.astype(out.dtype)


def call_qkv_back(meta, blocks, weights):
    return row_call(
        qkv_back_kernel,
        "qkv_back",
        (
            jax.ShapeDtypeStruct((QKV_ROWS, 4 * PATCHES), jnp.bfloat16),
            frame_f32(),
            frame_low(),
            frame_f32(),
            frame_low(),
        ),
        meta,
        *blocks,
        weights,
        smem=1,
    )


def adam_step(weight_now, first_mom, second_mom, grad, scale, rate, decay):
    factor, first_fix, second_fix = scale
    grad = grad * factor
    first_mom = beta_one * first_mom + (1.0 - beta_one) * grad
    second_mom = beta_two * second_mom + (1.0 - beta_two) * grad * grad
    second_hat = second_mom * second_fix
    updated = weight_now - rate * (
        first_mom * first_fix / (second_hat * lax.rsqrt(second_hat) + adam_eps)
        + decay * weight_now
    )
    return updated, first_mom, second_mom, updated.astype(jnp.bfloat16)


def preload_kernel(*refs):
    sources, targets, sems = refs[:3], refs[4:7], refs[7]
    copies = [
        pltpu.make_async_copy(sources[k], targets[k], sems.at[k]) for k in range(3)
    ]
    for copy in copies:
        copy.start()
    for copy in copies:
        copy.wait()


def call_preload(arrays, values):
    return pl.pallas_call(
        preload_kernel,
        out_shape=tuple(jax.ShapeDtypeStruct(a.shape, a.dtype) for a in arrays),
        in_specs=hbm_specs(3) + vmem_specs(1),
        out_specs=vmem_specs(3),
        scratch_shapes=[pltpu.SemaphoreType.DMA((3,))],
        compiler_params=pltpu.CompilerParams(vmem_limit_bytes=4 * 2**20),
        cost_estimate=pl.CostEstimate(flops=10**6, bytes_accessed=10**7, transcendentals=0),
        name="preload",
    )(*arrays, values)


def adam_kernel(*refs):
    fixes, sums = refs[0], refs[1:5]
    attn_grad, mlp_grad, cond, mod_rows = refs[5:9]
    io_in, vec_in = refs[9:13], refs[13:17]
    groups = [refs[17 + 3 * k : 20 + 3 * k] for k in range(3)]
    outs = [refs[26 + 4 * k : 30 + 4 * k] for k in range(3)]
    io_out, vec_out, norm_out = refs[38:43], refs[43:47], refs[47]
    held, slots, low_slots, in_sems, sems = refs[48:]
    depth = held.shape[0]
    tasks = []
    for k in (1, 0, 2):
        width = groups[k][0].shape[-1]
        for lead in range(groups[k][0].shape[0] if k < 2 else 1):
            for col in range(0, width, 1024):
                tasks.append((k, lead, col, min(1024, width - col)))

    def fetches(number):
        k, lead, col, span = tasks[number]
        cut = ((lead,) if k < 2 else ()) + (slice(None), slice(col, col + span))
        slot = number % depth
        if k == 2:
            return []
        return [
            pltpu.make_async_copy(
                groups[k][index].at[cut], held.at[slot, index, :, 0:span], in_sems.at[slot, index]
            )
            for index in range(3)
        ]

    for number in range(min(depth, len(tasks))):
        for copy in fetches(number):
            copy.start()
    total = (sums[0][...] + sums[1][...]) + (sums[2][...] + sums[3][...])
    norm = jnp.sqrt(total)
    norm_out[0:1, :] = norm
    norm_out[1:2, :] = total
    factor = jnp.minimum(1.0, clip_limit / (norm[:, 0:1] + 1e-06))
    scale = (factor, fixes[0], fixes[1])
    results = adam_step(*(ref[...] for ref in io_in), scale, rate_matrix, decay_rate)
    io_out[0][...] = results[0]
    io_out[1][...] = results[1]
    io_out[2][...] = results[2][0]
    io_out[3][...] = results[2][1]
    io_out[4][...] = results[3]
    results = adam_step(*(ref[...] for ref in vec_in), scale, rate_vector, 0.0)
    for out, result in zip(vec_out, results):
        out[...] = result
    running = {}
    for number, (k, lead, col, span) in enumerate(tasks):
        slot = number % depth
        for copy in fetches(number):
            copy.wait()
        for copy in running.pop(number - depth, ()):
            copy.wait()
        cut = ((lead,) if k < 2 else ()) + (slice(None), slice(col, col + span))
        if k == 0:
            grad = attn_grad[lead]
        elif k == 1:
            base = groups[1][0].shape[-1] * lead + col
            grad = mlp_grad[:, base : base + span].astype(jnp.float32)
        else:
            grad = lax.dot_general(
                cond[32:64, :],
                mod_rows[:, col : col + span],
                TN,
                preferred_element_type=jnp.float32,
            )
        if k == 2:
            values = [ref[:, col : col + span] for ref in groups[2]]
        else:
            values = [held[slot, index, :, 0:span] for index in range(3)]
        results = adam_step(*values, grad, scale, rate_matrix, decay_rate)
        copies = []
        for index, result in enumerate(results):
            source = low_slots.at[slot] if index == 3 else slots.at[slot, index]
            source = source.at[:, 0:span]
            source[...] = result
            copies.append(
                pltpu.make_async_copy(source, outs[k][index].at[cut], sems.at[slot, index])
            )
            copies[index].start()
        running[number] = copies
        if number + depth < len(tasks):
            for copy in fetches(number + depth):
                copy.start()
    for copies in running.values():
        for copy in copies:
            copy.wait()


def call_adam(fixes, sums, grads, io_group, vec_group, groups):
    held = [array for group in groups for array in group]
    inside = [*sums, *grads, *io_group, *vec_group]

    def results(group):
        low = jax.ShapeDtypeStruct(group[0].shape, jnp.bfloat16)
        return (jax.ShapeDtypeStruct(group[0].shape, jnp.float32),) * 3 + (low,)

    io_like = results(io_group)
    half = jax.ShapeDtypeStruct(io_group[0].shape[1:], jnp.float32)
    out_shape = sum((results(group) for group in groups), ())
    out_shape = out_shape + io_like[:2] + (half, half) + io_like[3:] + results(vec_group)
    out_shape = out_shape + (jax.ShapeDtypeStruct((2, 128), jnp.float32),)
    return pl.pallas_call(
        adam_kernel,
        out_shape=out_shape,
        in_specs=smem_specs(1) + vmem_specs(len(inside)) + hbm_specs(6) + vmem_specs(3),
        out_specs=hbm_specs(12) + vmem_specs(10),
        scratch_shapes=[
            pltpu.VMEM((6, 3, 128, 1024), jnp.float32),
            pltpu.VMEM((6, 3, 128, 1024), jnp.float32),
            pltpu.VMEM((6, 128, 1024), jnp.bfloat16),
            pltpu.SemaphoreType.DMA((6, 3)),
            pltpu.SemaphoreType.DMA((6, 4)),
        ],
        compiler_params=pltpu.CompilerParams(vmem_limit_bytes=28 * 2**20),
        cost_estimate=pl.CostEstimate(flops=10**7, bytes_accessed=2 * 10**7, transcendentals=0),
        name="adam",
    )(fixes, *inside, *held)


def square_kernel(scattered, square):
    rest = scattered[...].astype(jnp.float32)
    square[...] = jnp.broadcast_to(
        jnp.sum(column_sum(rest * rest), axis=1, keepdims=True), square.shape
    )


def finish_kernel(*refs):
    own, io_own, mod_own, pieces = refs[0], refs[1], refs[2], refs[3:6]
    rest, error, grad, spread = refs[6:]
    total = own[...]
    io_total = io_own[...]
    spread[0 : 2 * MOD_ROWS, :] = mod_own[...]
    for index, piece in enumerate(pieces):
        total = total + piece[0:ATTN_ROWS, :].astype(jnp.float32)
        base = ATTN_ROWS + IO_ROWS
        io_total = io_total + piece[ATTN_ROWS:base, :].astype(jnp.float32)
        spread[2 * MOD_ROWS * (index + 1) : 2 * MOD_ROWS * (index + 2), :] = piece[base:, :]
    high = io_total.astype(jnp.bfloat16)
    base = 8 * MOD_ROWS
    spread[base : base + IO_ROWS, :] = high
    base = base + IO_ROWS
    spread[base : base + IO_ROWS, :] = (io_total - high.astype(jnp.float32)).astype(jnp.bfloat16)
    for part in range(4):
        grad[part] = total[256 * part : 256 * part + 256].T
    squares = rest[:, 0:1]
    for values in (total, io_total):
        squares = squares + jnp.sum(column_sum(values * values), axis=1, keepdims=True)
    left = lax.broadcasted_iota(jnp.int32, (1, 128), 1) < 64
    value = jnp.where(left, squares, error[...])
    terms = []
    for _ in range(3):
        terms.append(value.astype(jnp.bfloat16).astype(jnp.float32))
        value = value - terms[-1]
    spread[base + IO_ROWS :, :] = jnp.concatenate(
        terms + [jnp.zeros((13, 128), jnp.float32)], axis=0
    ).astype(jnp.bfloat16)


def turn(block):
    return block.astype(jnp.float32).T.astype(jnp.bfloat16)


def query_rows(meta, pair):
    first = 2 * pair
    start_first = first - meta[2 + first]
    start_second = first + 1 - meta[3 + first]
    left = lax.broadcasted_iota(jnp.int32, (1, 2 * PATCHES), 1) < PATCHES
    upto = jnp.where(left, first, first + 1)
    since = jnp.where(left, start_first, start_second)
    return jnp.minimum(start_first, start_second), since, upto


def attend_kernel(meta, *refs):
    blocks = refs[:4]
    outs = refs[4:8]
    lse, mixed, query, key, value, scores = refs[8:]
    for member in range(4):
        for frame in range(4):
            slot = 4 * (meta[0] ^ member) + (meta[1] ^ frame)
            cols = slice(256 * frame, 256 * frame + 256)
            lanes = pl.ds(pl.multiple_of((slot % 2) * 256, 256), 256)
            query[slot // 2, :, lanes] = blocks[member][0:64, cols] * 0.125
            key[slot // 2, lanes, :] = turn(blocks[member][64:128, cols])
            value[slot // 2, :, lanes] = blocks[member][128:192, cols]

    def per_pair(pair, carry):
        low, since, upto = query_rows(meta, pair)
        wanted = query[pair]

        def first_pass(keys, top):
            both = jnp.dot(key[keys], wanted, preferred_element_type=jnp.float32)
            for side in range(2):
                slot = 2 * keys + side
                bias = jnp.where((slot >= since) & (slot <= upto), 0.0, neg_large)
                part = both[256 * side : 256 * side + 256] + bias
                scores[keys, 256 * side : 256 * side + 256, :] = part
                top = jnp.maximum(top, jnp.max(part.reshape(32, 8, 2 * PATCHES), axis=0))
            return top

        tops = lax.fori_loop(
            low // 2, pair + 1, first_pass, jnp.full((8, 2 * PATCHES), neg_large, jnp.float32)
        )
        top = jnp.max(tops, axis=0, keepdims=True)

        def second_pass(keys, state):
            total, acc = state
            probs = jnp.exp(scores[keys] - top)
            total = total + jnp.sum(probs.reshape(64, 8, 2 * PATCHES), axis=0)
            acc = acc + jnp.dot(
                value[keys], probs.astype(jnp.bfloat16), preferred_element_type=jnp.float32
            )
            return (total, acc)

        totals, acc = lax.fori_loop(
            low // 2,
            pair + 1,
            second_pass,
            (
                jnp.zeros((8, 2 * PATCHES), jnp.float32),
                jnp.zeros((HD, 2 * PATCHES), jnp.float32),
            ),
        )
        total = jnp.sum(totals, axis=0, keepdims=True)
        lse[pair] = top + jnp.log(total)
        mixed[pair] = acc / total
        return carry

    lax.fori_loop(0, 8, per_pair, 0)
    for member in range(4):
        for frame in range(4):
            slot = 4 * (meta[0] ^ member) + (meta[1] ^ frame)
            lanes = pl.ds(pl.multiple_of((slot % 2) * 256, 256), 256)
            outs[member][:, 256 * frame : 256 * frame + 256] = mixed[slot // 2, :, lanes].astype(
                jnp.bfloat16
            )


def call_attend(meta, blocks):
    vmem = pl.BlockSpec()
    result = pl.pallas_call(
        attend_kernel,
        out_shape=tuple(jax.ShapeDtypeStruct((HD, 4 * PATCHES), jnp.bfloat16) for _ in range(4))
        + (
            jax.ShapeDtypeStruct((8, 1, 2 * PATCHES), jnp.float32),
            jax.ShapeDtypeStruct((8, HD, 2 * PATCHES), jnp.float32),
        ),
        in_specs=[pl.BlockSpec(memory_space=pltpu.SMEM)] + [vmem] * 4,
        out_specs=(vmem,) * 6,
        scratch_shapes=[
            pltpu.VMEM((8, HD, 2 * PATCHES), jnp.bfloat16),
            pltpu.VMEM((8, 2 * PATCHES, HD), jnp.bfloat16),
            pltpu.VMEM((8, HD, 2 * PATCHES), jnp.bfloat16),
            pltpu.VMEM((8, 2 * PATCHES, 2 * PATCHES), jnp.float32),
        ],
        compiler_params=pltpu.CompilerParams(vmem_limit_bytes=48 * 2**20),
        cost_estimate=pl.CostEstimate(flops=9 * 10**9, bytes_accessed=5 * 10**6, transcendentals=10**7),
        name="attend",
    )(meta, *blocks)
    return list(result[:4]), result[4], result[5]


def attend_back_kernel(meta, *refs):
    blocks = refs[:4]
    grads = refs[4:8]
    lse, mixed, cosine, sine = refs[8:12]
    outs = refs[12:16]
    query, key, key_flat, value_flat, grad, sum_key, sum_value, sum_query = refs[16:]
    for member in range(4):
        for frame in range(4):
            slot = 4 * (meta[0] ^ member) + (meta[1] ^ frame)
            cols = slice(256 * frame, 256 * frame + 256)
            place = pl.ds(pl.multiple_of((slot % 2) * 256, 256), 256)
            part = blocks[member][0:64, cols] * 0.125
            query[slot // 2, :, place] = part
            part = blocks[member][64:128, cols]
            key[slot // 2, :, place] = part
            key_flat[slot // 2, place, :] = turn(part)
            value_flat[slot // 2, place, :] = turn(blocks[member][128:192, cols])
            part = grads[member][:, cols]
            grad[slot // 2, :, place] = part
    sum_key[...] = jnp.zeros_like(sum_key)
    sum_value[...] = jnp.zeros_like(sum_value)

    def per_pair(pair, carry):
        low, since, upto = query_rows(meta, pair)
        wanted = query[pair]
        wanted_grad = grad[pair]
        delta = jnp.sum(wanted_grad.astype(jnp.float32) * mixed[pair], axis=0, keepdims=True)
        level = lse[pair]

        def per_keys(keys, acc):
            scores = jnp.dot(key_flat[keys], wanted, preferred_element_type=jnp.float32)
            grad_probs = jnp.dot(
                value_flat[keys], wanted_grad, preferred_element_type=jnp.float32
            )
            low_probs, low_scores = [], []
            for side in range(2):
                rows = slice(256 * side, 256 * side + 256)
                slot = 2 * keys + side
                bias = jnp.where((slot >= since) & (slot <= upto), -level, neg_large)
                probs = jnp.exp(scores[rows] + bias)
                low_probs.append(probs.astype(jnp.bfloat16))
                low_scores.append((probs * (grad_probs[rows] - delta)).astype(jnp.bfloat16))
            all_probs = jnp.concatenate(low_probs, axis=0)
            all_scores = jnp.concatenate(low_scores, axis=0)
            sum_value[keys] += lax.dot_general(
                wanted_grad, all_probs, NT, preferred_element_type=jnp.float32
            )
            sum_key[keys] += lax.dot_general(
                wanted, all_scores, NT, preferred_element_type=jnp.float32
            )
            return acc + jnp.dot(key[keys], all_scores, preferred_element_type=jnp.float32)

        sum_query[pair] = lax.fori_loop(
            low // 2, pair + 1, per_keys, jnp.zeros((HD, 2 * PATCHES), jnp.float32)
        )
        return carry

    lax.fori_loop(0, 8, per_pair, 0)
    for member in range(4):
        for frame in range(4):
            slot = 4 * (meta[0] ^ member) + (meta[1] ^ frame)
            cols = slice(256 * frame, 256 * frame + 256)
            place = pl.ds(pl.multiple_of((slot % 2) * 256, 256), 256)
            cos_now = cosine[slot]
            sin_now = sine[slot]
            for base, part in (
                (0, sum_query[slot // 2, :, place] * 0.125),
                (64, sum_key[slot // 2, :, place]),
            ):
                upper = part[0:32]
                lower = part[32:64]
                outs[member][base : base + 32, cols] = (
                    upper * cos_now + lower * sin_now
                ).astype(jnp.bfloat16)
                outs[member][base + 32 : base + 64, cols] = (
                    lower * cos_now - upper * sin_now
                ).astype(jnp.bfloat16)
            outs[member][128:192, cols] = sum_value[slot // 2, :, place].astype(jnp.bfloat16)


def call_attend_back(meta, blocks, grads, lse, mixed, cosine, sine):
    vmem = pl.BlockSpec()
    flat_pair = pltpu.VMEM((8, 2 * PATCHES, HD), jnp.bfloat16)
    turned_pair = pltpu.VMEM((8, HD, 2 * PATCHES), jnp.bfloat16)
    wide = pltpu.VMEM((8, HD, 2 * PATCHES), jnp.float32)
    return list(
        pl.pallas_call(
            attend_back_kernel,
            out_shape=tuple(
                jax.ShapeDtypeStruct((192, 4 * PATCHES), jnp.bfloat16) for _ in range(4)
            ),
            in_specs=[pl.BlockSpec(memory_space=pltpu.SMEM)] + [vmem] * 12,
            out_specs=(vmem,) * 4,
            scratch_shapes=[
                turned_pair,
                turned_pair,
                flat_pair,
                flat_pair,
                turned_pair,
                wide,
                wide,
                pltpu.VMEM((8, HD, 2 * PATCHES), jnp.float32),
            ],
            compiler_params=pltpu.CompilerParams(vmem_limit_bytes=48 * 2**20),
            cost_estimate=pl.CostEstimate(
                flops=30 * 10**9, bytes_accessed=10**7, transcendentals=10**7
            ),
            name="attend_back",
        )(meta, *blocks, *grads, lse, mixed, cosine, sine)
    )


def shards_halves(
    clean,
    noise,
    levels,
    lengths,
    order,
    step,
    w_attn,
    m_attn,
    v_attn,
    w_mlp,
    m_mlp,
    v_mlp,
    w_mod,
    m_mod,
    v_mod,
    w_io,
    m_io,
    v_io,
    vectors,
    m_vec,
    v_vec,
):
    bfloat = jnp.bfloat16
    single = jnp.float32
    ctx_index = lax.axis_index("ctx")
    tp_index = lax.axis_index("tp")
    member = ctx_index % 4
    device = jnp.stack([ctx_index, tp_index]).astype(jnp.int32)

    front_shard = call_prepare(w_attn, w_io, vectors)
    token_shard = call_tokens(after(device, front_shard), clean, noise)
    pieces = gather_swaps(token_shard)
    front_pieces = lax.all_gather(front_shard, "ctx", axis=0)
    front_meta, attend_meta, row_levels = call_place(
        after(device, pieces[1]), lengths, order, levels
    )

    count = step[0].astype(single)
    fixes = jnp.stack([1.0 / (1.0 - beta_one**count), 1.0 / (1.0 - beta_two**count)])

    half_dim = D // 2
    column = ctx_index * 128 + jnp.arange(128, dtype=jnp.int32)
    frequency = jnp.exp(-math.log(10000.0) * (column % half_dim).astype(single) / half_dim)
    angle = row_levels.astype(single)[:, None] * frequency[None, :]
    cond = jax.nn.silu(jnp.where(column[None, :] < half_dim, jnp.cos(angle), jnp.sin(angle)))
    cond_low = cond.astype(bfloat)
    cond_slots = cond_low[:32]
    quarter_cols = 6 * D // 4
    mod_cols = lax.dynamic_slice_in_dim(w_mod, tp_index * quarter_cols, quarter_cols, 1)
    mod_part = jnp.dot(cond_slots, mod_cols.astype(bfloat), preferred_element_type=single)
    mod_held = reduce_along_x(mod_part.reshape(8, 4, quarter_cols), ctx_index, single)
    mod_own = reduce_along_z(mod_held, ctx_index, single)
    mod_quarters = reorder_four(spread_frames(mod_own), tp_index)
    mod_all = jnp.concatenate(mod_quarters, axis=1)
    mod_rel = jnp.stack(reorder_four([mod_all[k] for k in range(4)], tp_index))
    mod_rel = mod_rel.reshape(4, 6, D)

    time_pairs = HD // 8
    side_pairs = (HD // 2 - time_pairs) // 2

    def frequencies(count):
        return 10000.0 ** (-jnp.arange(count, dtype=single) / count)

    patch = jnp.arange(PATCHES, dtype=jnp.int32)
    half_position = attend_meta[2:].astype(single)
    time_angle = half_position[:, None] * frequencies(time_pairs)[None, :]
    height_angle = frequencies(side_pairs)[:, None] * (patch // GRID).astype(single)[None, :]
    width_angle = frequencies(side_pairs)[:, None] * (patch % GRID).astype(single)[None, :]
    side_angle = jnp.concatenate([height_angle, width_angle], axis=0)

    def full_table(time_part, side_part):
        return jnp.concatenate(
            [
                jnp.broadcast_to(time_part[:, :, None], (HALF_SLOTS, time_pairs, PATCHES)),
                jnp.broadcast_to(side_part[None], (HALF_SLOTS, 2 * side_pairs, PATCHES)),
            ],
            axis=1,
        )

    cosine = full_table(jnp.cos(time_angle), jnp.cos(side_angle))
    sine = full_table(jnp.sin(time_angle), jnp.sin(side_angle))
    signal_scale, noise_scale, weight = plan(row_levels)
    weight_sum = PATCHES * jnp.sum(weight[:32])
    token_scales = jnp.concatenate([signal_scale[64:68], noise_scale[64:68]])
    loss_scales = jnp.stack([weight[64], 2.0 / clean.shape[1] * weight[64] / weight_sum])

    front_meta = after(front_meta, mod_rel, cosine, sine, token_scales, loss_scales, fixes)
    quarters = spread_frames(call_pick(front_meta, pieces))
    front_all, mid_all, hidden_frames, resid_in, *head_blocks, noisy_low, target, mod_own = (
        call_front(front_meta, token_scales, front_pieces, quarters, mod_rel, cosine, sine)
    )
    hidden_one = hidden_frames.reshape(4 * PATCHES, D)

    out_w = mid_all[:, :256]

    def exchange(blocks):
        return [blocks[0]] + [swap(blocks[k], "ctx", k) for k in (1, 2, 3)]

    head_in = exchange(head_blocks)
    mlp_shard = after(w_mlp.astype(bfloat), head_in[1], head_in[2])
    mlp_w = lax.all_gather(mlp_shard, "ctx", axis=1, tiled=True)
    mixed_blocks, lse, mixed = call_attend(attend_meta, head_in)
    mix_low = jnp.concatenate(reorder_four(exchange(mixed_blocks), member), axis=0)

    def project(left, right, dims):
        pairs = []
        for base in (2 * PATCHES, 0):
            part = lax.dot_general(
                left[:, base : base + 2 * PATCHES], right, dims, preferred_element_type=single
            )
            pairs.append((part[:PATCHES], part[PATCHES:].astype(bfloat)))
        return pairs[1], pairs[0]

    near, far = project(mix_low, out_w, (((0,), (1,)), ((), ())))
    attn_out, resid_mid, hidden_own = row_call(
        middle_kernel,
        "middle",
        (frame_low(), frame_f32(), frame_low()),
        *sum_frames(near, sum_across(far)),
        resid_in,
        mod_own,
    )
    hidden_list = spread_frames(hidden_own)
    wide = (2 * PATCHES, w_mlp.shape[2])
    wide_low = jax.ShapeDtypeStruct(wide, bfloat)
    far = call_mlp(mlp_kernel, "mlp", (wide_low, wide_low), *hidden_list[2:], mlp_w)
    across = sum_across(far)
    near = call_mlp(
        mlp_kernel,
        "mlp",
        (wide_low, wide_low),
        after(hidden_list[0], across),
        hidden_list[1],
        mlp_w,
    )
    active, slope = (near[2], far[2]), (near[3], far[3])
    grad_own, grad_three, head_rows, grad_gate_two, error_part = row_call(
        loss_kernel,
        "loss",
        (
            frame_low(),
            frame_f32(),
            jax.ShapeDtypeStruct((136, D), single),
            jax.ShapeDtypeStruct((1, D), single),
            jax.ShapeDtypeStruct((1, 128), single),
        ),
        loss_scales,
        *sum_frames(near[:2], across),
        resid_mid,
        mod_own,
        mid_all,
        target,
        smem=1,
    )
    grad_list = [grad_own, swap(grad_own, "tp", 1)]
    near = call_mlp(mlp_back_kernel, "mlp_back", (wide_low,), *grad_list, mlp_w, slope[0])
    grad_across = after(swap(grad_own, "tp", 2), near[0])
    grad_list += [grad_across, swap(grad_across, "tp", 1)]
    far = call_mlp(
        mlp_back_kernel,
        "mlp_back",
        (wide_low,),
        *grad_list[2:],
        mlp_w,
        slope[1],
    )
    across = sum_across(far)
    weight_grad = call_weight_grad(
        hidden_list, grad_list, (near[2], after(far[2], across)), active
    )
    grad_low, grad_mid, rows_two = row_call(
        second_kernel,
        "second",
        (frame_low(), frame_f32(), jax.ShapeDtypeStruct((3, D), single)),
        *sum_frames(near[:2], across),
        after(resid_mid, weight_grad),
        mod_own,
        grad_three,
        attn_out,
        inside=plain_specs,
    )
    back_list = spread_frames(grad_low)
    grad_attn_low = jnp.concatenate(back_list, axis=0)
    grad_mix = lax.dot_general(
        out_w, grad_attn_low, (((0,), (1,)), ((), ())), preferred_element_type=single
    ).astype(bfloat)
    grad_blocks = reorder_four([grad_mix[HD * k : HD * k + HD] for k in range(4)], member)
    grad_in_blocks = exchange(grad_blocks)
    out_held, out_away = call_head_grad(device, mix_low, after(grad_attn_low, grad_mix))
    out_came = swap(out_away, "ctx", 1)
    grad_in_blocks[0] = after(grad_in_blocks[0], out_held)
    scattered = lax.psum_scatter(
        after(weight_grad, grad_low), "ctx", scatter_dimension=0, tiled=True
    )
    back_blocks = call_attend_back(attend_meta, head_in, grad_in_blocks, lse, mixed, cosine, sine)
    grad_qkv, *parts = call_qkv_back(attend_meta, exchange(back_blocks), front_all)
    near, far = parts[:2], parts[2:]
    across = sum_across(far)
    first_terms = sum_frames(near, across)
    qkv_held, qkv_away = call_head_grad(device, after(grad_qkv, across), hidden_one)
    qkv_came = swap(qkv_away, "ctx", 1)
    group_f32 = jax.ShapeDtypeStruct((IO_ROWS, D), single)
    group_low = jax.ShapeDtypeStruct((IO_ROWS, D), bfloat)
    mod_rows, *io_parts, _ = row_call(
        first_kernel,
        "first",
        (
            jax.ShapeDtypeStruct((MOD_ROWS, 128), bfloat),
            group_f32,
            group_low,
            group_f32,
            group_low,
            jax.ShapeDtypeStruct((4 * IO_ROWS, D), single),
        ),
        device,
        *first_terms,
        after(resid_in, qkv_held),
        mod_own,
        grad_mid,
        noisy_low,
        rows_two,
        grad_gate_two,
        head_rows,
        smem=1,
    )
    io_held, io_away = row_call(
        side_kernel,
        "side",
        (
            jax.ShapeDtypeStruct((4, IO_ROWS, 128), single),
            jax.ShapeDtypeStruct((4 * IO_ROWS + MOD_ROWS, 128), bfloat),
        ),
        device,
        *sum_frames(io_parts[:2], sum_across(io_parts[2:])),
        mod_rows,
        smem=1,
    )
    z_rows = jax.ShapeDtypeStruct((ATTN_ROWS + IO_ROWS + 2 * MOD_ROWS, 128), bfloat)
    qkv_own, io_own, *z_pieces = row_call(
        merge_kernel,
        "merge",
        (
            jax.ShapeDtypeStruct((ATTN_ROWS, 128), single),
            jax.ShapeDtypeStruct((IO_ROWS, 128), single),
            jax.ShapeDtypeStruct((2 * MOD_ROWS, 128), bfloat),
            z_rows,
            z_rows,
            z_rows,
        ),
        device,
        qkv_held,
        qkv_came,
        out_held,
        out_came,
        io_held,
        swap(io_away, "ctx", 1),
        mod_rows,
        smem=1,
    )
    red_attn, spread = row_call(
        finish_kernel,
        "finish",
        (
            jax.ShapeDtypeStruct((4, 128, 256), single),
            jax.ShapeDtypeStruct((8 * MOD_ROWS + 2 * IO_ROWS + 16, 128), bfloat),
        ),
        qkv_own,
        io_own,
        z_pieces[0],
        *(swap(piece, "ctx", 2 * bit) for bit, piece in zip((1, 2, 3), z_pieces[1:])),
        row_call(square_kernel, "square", (jax.ShapeDtypeStruct((1, 128), single),), scattered)[0],
        error_part,
    )
    all_rows, red_vec, io_grad, square = call_mod_grad(device, cond_low, spread_frames(spread))
    terms = sum_terms(square)
    loaded = call_preload((w_mod, m_mod, v_mod), terms[0])
    updated = call_adam(
        fixes,
        terms,
        (red_attn, scattered, cond_low, all_rows),
        (w_io, m_io, v_io, io_grad[: 2 * 128].reshape(2, 128, 128)),
        (vectors, m_vec, v_vec, red_vec),
        ((w_attn, m_attn, v_attn), (w_mlp, m_mlp, v_mlp), loaded),
    )
    return (updated[21][1, 64] / weight_sum, updated[21][0, 0], *updated[:21])


def solution(mesh):
    halves = mesh.shape["ctx"] == 8 and mesh.shape["tp"] == 4
    placed = (
        P("ctx", None),
        P("ctx", None),
        P(),
        P(),
        P(),
        P(),
        P(None, "ctx", "tp"),
        P(None, "ctx", "tp"),
        P(None, "ctx", "tp"),
        P(None, "ctx", "tp"),
        P(None, "ctx", "tp"),
        P(None, "ctx", "tp"),
        P("ctx", None),
        P("ctx", None),
        P("ctx", None),
        P(None, None, "ctx"),
        P(None, None, "ctx"),
        P(None, None, "ctx"),
        P(None, "ctx"),
        P(None, "ctx"),
        P(None, "ctx"),
    )
    return jax.shard_map(
        shards_halves if halves else shards,
        mesh=mesh,
        in_specs=placed,
        out_specs=(
            P(),
            P(),
            P(None, "ctx", "tp"),
            P(None, "ctx", "tp"),
            P(None, "ctx", "tp"),
            P(None, "ctx", "tp"),
            P(None, "ctx", "tp"),
            P(None, "ctx", "tp"),
            P(None, "ctx", "tp"),
            P(None, "ctx", "tp"),
            P("ctx", None),
            P("ctx", None),
            P("ctx", None),
            P("ctx", None),
            P(None, None, "ctx"),
            P(None, None, "ctx"),
            P(None, "ctx"),
            P(None, "ctx"),
            P(None, None, "ctx"),
            P(None, "ctx"),
            P(None, "ctx"),
            P(None, "ctx"),
            P(None, "ctx"),
        ),
        check_vma=False,
    )
```
